32 devices in a mesh: seq: 4 (over x, core), exp: 8 (over z, y).
Axes of the slice: x: 2, y: 2, z: 4, core: 2. Of those that a mesh axis runs over, the one named last changes fastest.
Arguments:
- tokens: bfloat16 [2, 8, 512, 1024], P(None, 'exp', 'seq'), may hold values from -3 to 3
- queries: bfloat16 [2, 8, 512, 1024], P(None, 'exp', 'seq'), may hold values from -6 to 6
- key_rows: bfloat16 [2, 8, 512, 1024], P(None, 'exp', 'seq'), may hold values from -6 to 6
- value_rows: bfloat16 [2, 8, 512, 1024], P(None, 'exp', 'seq'), may hold values from -6 to 6
- segments: int32 [2, 8, 512], P(None, 'exp', 'seq'), may hold values from 0 to 3, never falling along the last dimension, each value on 1 to 256 neighbouring positions
- bias_table: float32 [16, 32], replicated, may hold values from -3 to 5
- out_proj: bfloat16 [1024, 1024], replicated, may hold values from -0.75 to 0.75
- router: bfloat16 [1024, 8], replicated, may hold values from -0.1875 to 0.1875
- gate_weight: bfloat16 [8, 1024, 1408], P('exp'), may hold values from -0.1875 to 0.1875
- up_weight: bfloat16 [8, 1024, 1408], P('exp'), may hold values from -0.1875 to 0.1875
- down_weight: bfloat16 [8, 1408, 1024], P('exp'), may hold values from -0.15625 to 0.15625
- old_table: int32 [8], replicated, may hold values from 0 to 7, each once
- new_table: int32 [8], replicated, may hold values from 0 to 7, as said below
- routes_one: int32 [8, 512, 2], P('exp', 'seq'), may hold values from 0 to 7, all different within a row; in each aligned block of 128 rows (0 to 127, 128 to 255, ..., all dimensions but the last counted through in order) at most 40 rows name the same one
- routes_two: int32 [8, 512, 2], P('exp', 'seq'), may hold values from 0 to 7, all different within a row; in each aligned block of 128 rows (0 to 127, 128 to 255, ..., all dimensions but the last counted through in order) at most 40 rows name the same one
Outputs:
- layer_out: bfloat16 [2, 8, 512, 1024], P(None, 'exp', 'seq')
The draws below stay inside these ranges and needn't reach their ends.
Inputs may be any that keep to these rules, and one draw needn't show every extreme that they name: `old_table`: each position holds a different expert. `new_table`: no expert is served at more than 2 slots, and at least one expert at exactly 2. `routes_one`: the 2 entries of a token differ; in the rows of one device no expert is named more than 40 times, and in some device's rows one is named exactly 40 times. `routes_two`: the 2 entries of a token differ; in the rows of one device no slot is named more than 40 times, and in some device's rows one is named exactly 40 times.
All inputs are finite; a program needn't handle non-finite values.
Results may differ from the reference program's by a relative error of at most 0.006.
Values may be sent and summed in bfloat16 or wider, within the bound.
No kernel may reach another device: no remote copies, remote signals or barrier semaphores. Data moves between devices by JAX's collectives and lax.ppermute only.
A program may use at most 128 MiB of HBM per device.

```python
import math
import jax
import jax.numpy as jnp
import numpy as np
from jax import lax

D = 1024
HEADS = 16
HEAD_DIM = 64
FFW = 1408
TOP = 2
WIN_BLOCKS = 4
NBUCK = 32
DOCS = 4
TOK_DEV = 128
EXPERTS = 8
GROUPS = 8
SEQLEN = 512
CAP = 40
N_SEQ = 4
N_EXP = 8


def query_key_pair(key):
    shape = (2, GROUPS, SEQLEN, HEADS * HEAD_DIM)
    queries = jnp.clip(jax.random.normal(jax.random.fold_in(key, 101), shape, jnp.float32), -5.0, 5.0)
    key_rows = jnp.clip(jax.random.normal(jax.random.fold_in(key, 102), shape, jnp.float32), -5.0, 5.0)
    return (queries, key_rows)


def draw_queries(key, part):
    return query_key_pair(key)[0].astype(jnp.bfloat16)


def draw_key_rows(key, part):
    return query_key_pair(key)[1].astype(jnp.bfloat16)


def draw_new_table(key, part):
    ordering = jax.random.permutation(jax.random.fold_in(key, 201), EXPERTS).astype(jnp.int32)
    chosen_spots = jax.random.permutation(jax.random.fold_in(key, 202), EXPERTS).astype(jnp.int32)
    doubled = max(1, EXPERTS // 4)
    return ordering.at[chosen_spots[:doubled]].set(ordering[chosen_spots[doubled:2 * doubled]])


def steps_of(rng, extent, cuts, low, high):
    factor_of, own = 1.0, jax.random.fold_in(rng, 6)
    for dim, blocks in cuts:
        heights = jnp.exp(jax.random.uniform(jax.random.fold_in(own, dim), (blocks,), jnp.float32, low / len(cuts), high / len(cuts)))
        factor_of = factor_of * jnp.repeat(heights, extent[dim] // blocks).reshape([-1 if axis == dim else 1 for axis in range(len(extent))])
    return factor_of


def split_up(count, total, bound, lean):
    loads = [(1 << 20) // math.isqrt(standing ** lean) + 1 for standing in range(2, count + 1)]
    rest, holding = total - bound - (count - 1), [1] * (count - 1)
    while rest > 0:
        movable = [i for i in range(count - 1) if holding[i] < bound]
        pool, budget = sum([loads[i] for i in movable]), rest
        for i in movable:
            addition = min(bound - holding[i], max(1, budget * loads[i] // pool), rest)
            holding[i] = holding[i] + addition
            rest = rest - addition
    return np.array([bound] + holding)


def uneven_parts(rng, amount, total, bound, slope):
    if amount == 2:
        one = jax.random.randint(rng, (), max(1, total - bound), min(bound, total - 1) + 1)
        return jnp.stack([one, total - one])
    tallies = jnp.asarray(split_up(amount, total, bound, slope), jnp.int32)
    couples = (amount - 1) // 2
    giver, receiver = tallies[1:1 + 2 * couples:2], tallies[2:2 + 2 * couples:2]
    margin = jnp.minimum(giver - 1, bound - receiver)
    moved = jax.random.randint(jax.random.fold_in(rng, 1), (couples,), 0, 1 << 20) % (margin + 1)
    tallies = tallies.at[1:1 + 2 * couples:2].set(giver - moved).at[2:2 + 2 * couples:2].set(receiver + moved)
    return tallies[jax.random.permutation(jax.random.fold_in(rng, 2), amount)]


def assign_block(key, own, number, rows, count, top, reach, skew):
    sequence = jax.random.permutation(key, count)
    crowded, common = portions_of(count, rows * top, reach, skew, True), portions_of(count, rows * top, reach, skew, False)
    places = jnp.arange(count)

    def named(lengths, offset_by):
        used = int((lengths > 0).sum())
        fixed = max(1, used // 4)
        moved = fixed + (places - fixed + offset_by * (used - fixed)) % max(1, count - fixed)
        return jnp.zeros((count,), jnp.int32).at[sequence[jnp.where(places < fixed, places, moved)]].set(jnp.asarray(lengths, jnp.int32))

    lengths = jnp.where(number % 4 == 0, named(crowded, number // 4), named(common, number - number // 4 - 1))
    mixed = jax.random.permutation(jax.random.fold_in(own, 3), count)
    donor, taker = mixed[0:count // 2 * 2:2], mixed[1:count // 2 * 2:2]
    margin = jnp.minimum(lengths[donor] - 1, reach - lengths[taker]) // 2
    margin = jnp.where((donor == sequence[0]) | (taker == sequence[0]) | (lengths[taker] == 0), 0, jnp.maximum(margin, 0))
    moved = jax.random.randint(jax.random.fold_in(own, 4), (count // 2,), 0, 1 << 20) % (margin + 1)
    lengths = lengths.at[donor].add(-moved).at[taker].add(moved)
    items = jnp.searchsorted(jnp.cumsum(lengths), jnp.arange(rows * top), side="right").astype(jnp.int32)
    grid = items.reshape(top, rows).T
    grid = grid[jax.random.permutation(jax.random.fold_in(own, 1), rows)]
    offset_by = jax.random.randint(jax.random.fold_in(own, 2), (rows, 1), 0, top)
    return jnp.take_along_axis(grid, (jnp.arange(top)[None, :] + offset_by) % top, axis=1)


def portions_of(number_of, total, most, skew, full):
    weights = [(1 << 20) // math.isqrt(grade ** skew) + 1 for grade in range(1, number_of + 1)]
    largest = most if full else min(most, max(-(-total // number_of), total * weights[0] // sum(weights)))
    least = 1 if total - largest >= number_of - 1 else 0
    counts, rest = [largest] + [least] * (number_of - 1), total - largest - least * (number_of - 1)
    while rest > 0:
        free = [i for i in range(1, number_of) if counts[i] < largest] or [i for i in range(1, number_of) if counts[i] < most]
        mass, budget = sum([weights[i] for i in free]), rest
        for i in free:
            addition = min(most - counts[i], max(1, budget * weights[i] // mass), rest)
            counts[i] = counts[i] + addition
            rest = rest - addition
    return np.array(counts)


def gaussian(own_key, shape, width, most, pieces=(), kind=jnp.bfloat16):
    drawn = jax.random.normal(own_key, shape, jnp.float32) * width
    if len(pieces) > 0:
        drawn = steps_of(own_key, shape, pieces, -0.22, 0.18) * drawn
    return jnp.clip(drawn, min=-most, max=most).astype(kind)


def setup_inputs(seed: int = 0) -> dict:
    splits = jax.random.split(jax.random.key(seed), 16)
    tokens = gaussian(splits[0], (2, GROUPS, SEQLEN, D), 0.5, 3.0, ((1, 8), (2, 4)))
    queries = draw_queries(jax.random.fold_in(splits[15], 71), 0)
    key_rows = draw_key_rows(jax.random.fold_in(splits[15], 71), 0)
    value_rows = gaussian(splits[3], (2, GROUPS, SEQLEN, HEADS * HEAD_DIM), 1.0, 6.0, ((1, 8), (2, 4)))
    segments = jax.vmap(lambda own: jnp.searchsorted(jnp.cumsum(uneven_parts(own, DOCS, SEQLEN, SEQLEN // 2, 2)), jnp.arange(SEQLEN), side="right"))(jax.random.split(splits[4], 2 * GROUPS)).reshape((2, GROUPS, SEQLEN)).astype(jnp.int32)
    bias_table = jnp.clip(jax.random.uniform(splits[5], (HEADS, NBUCK), jnp.float32, -3.0, 5.0), -3.0, 5.0)
    out_proj = gaussian(splits[6], (HEADS * HEAD_DIM, D), HEAD_DIM ** -0.5, 0.75)
    router = gaussian(splits[7], (D, EXPERTS), D ** -0.5, 0.1875)
    gate_weight = gaussian(splits[8], (EXPERTS, D, FFW), D ** -0.5, 0.1875, ((0, 8),))
    up_weight = gaussian(splits[9], (EXPERTS, D, FFW), D ** -0.5, 0.1875, ((0, 8),))
    down_weight = gaussian(splits[10], (EXPERTS, FFW, D), FFW ** -0.5, 0.15625, ((0, 8),))
    old_table = jax.random.permutation(splits[11], EXPERTS).astype(jnp.int32)
    new_table = draw_new_table(jax.random.fold_in(splits[15], 71), 0)
    routes_one_keys = jax.random.split(jax.random.fold_in(splits[13], 1), GROUPS * SEQLEN // TOK_DEV)
    routes_one_turns = jax.random.permutation(jax.random.fold_in(splits[13], 3), GROUPS * SEQLEN // TOK_DEV)
    routes_one = jax.vmap(lambda own, number: assign_block(jax.random.fold_in(splits[13], 2), own, number, TOK_DEV, EXPERTS, TOP, CAP, 2))(routes_one_keys, routes_one_turns).reshape((GROUPS, SEQLEN, TOP))
    routes_two_keys = jax.random.split(jax.random.fold_in(splits[14], 1), GROUPS * SEQLEN // TOK_DEV)
    routes_two_turns = jax.random.permutation(jax.random.fold_in(splits[14], 3), GROUPS * SEQLEN // TOK_DEV)
    routes_two = jax.vmap(lambda own, number: assign_block(jax.random.fold_in(splits[14], 2), own, number, TOK_DEV, EXPERTS, TOP, CAP, 1))(routes_two_keys, routes_two_turns).reshape((GROUPS, SEQLEN, TOP))
    return dict(tokens=tokens, queries=queries, key_rows=key_rows, value_rows=value_rows, segments=segments, bias_table=bias_table, out_proj=out_proj, router=router, gate_weight=gate_weight, up_weight=up_weight, down_weight=down_weight, old_table=old_table, new_table=new_table, routes_one=routes_one, routes_two=routes_two)


score_scale = 0.125
epsilon = 1e-06
masked_score = -1e+30

def bit_length(distance):
    counted = jnp.zeros_like(distance)
    for exponent in range(NBUCK - 2):
        counted = counted + (distance >= 1 << exponent).astype(jnp.int32)
    return counted

def attend_rows(queries, key_rows, value_rows, segments, bias_table):
    window_len = WIN_BLOCKS * TOK_DEV
    model_width = HEADS * HEAD_DIM

    def one_group(group_args):
        group_queries, group_keys, group_values, group_segments = group_args
        row_starts = jnp.searchsorted(group_segments, group_segments, side='left').astype(jnp.int32)
        padded_keys = jnp.concatenate([jnp.zeros((window_len, model_width), group_keys.dtype), group_keys], axis=0)
        padded_values = jnp.concatenate([jnp.zeros((window_len, model_width), group_values.dtype), group_values], axis=0)

        def one_block(block_index):
            block_start = block_index * TOK_DEV
            query_block = lax.dynamic_slice_in_dim(group_queries, block_start, TOK_DEV, 0)
            key_block = lax.dynamic_slice_in_dim(padded_keys, block_start, window_len + TOK_DEV, 0)
            value_block = lax.dynamic_slice_in_dim(padded_values, block_start, window_len + TOK_DEV, 0)
            block_starts = lax.dynamic_slice_in_dim(row_starts, block_start, TOK_DEV, 0)
            positions = block_start + jnp.arange(TOK_DEV, dtype=jnp.int32)
            key_pos = block_start - window_len + jnp.arange(window_len + TOK_DEV, dtype=jnp.int32)
            distance = positions[:, None] - key_pos[None, :]
            query_heads = query_block.reshape(TOK_DEV, HEADS, HEAD_DIM).astype(jnp.float32)
            key_heads = key_block.reshape(window_len + TOK_DEV, HEADS, HEAD_DIM).astype(jnp.float32)
            value_heads = value_block.reshape(window_len + TOK_DEV, HEADS, HEAD_DIM).astype(jnp.float32)
            sink_key = group_keys[block_starts].reshape(TOK_DEV, HEADS, HEAD_DIM).astype(jnp.float32)
            sink_value = group_values[block_starts].reshape(TOK_DEV, HEADS, HEAD_DIM).astype(jnp.float32)
            window_bias = jnp.take(bias_table, bit_length(jnp.maximum(distance, 0)), axis=1)
            scores = jnp.einsum('qhd,khd->hqk', query_heads, key_heads) * score_scale + window_bias
            visible = (key_pos[None, :] >= block_starts[:, None]) & (distance >= 0) & (distance < window_len)
            scores = jnp.where(visible[None], scores, masked_score)
            sink_scores = jnp.einsum('qhd,qhd->hq', query_heads, sink_key) * score_scale + bias_table[:, NBUCK - 1][:, None]
            sink_visible = positions - block_starts >= window_len
            sink_scores = jnp.where(sink_visible[None], sink_scores, masked_score)
            row_peak = jnp.maximum(lax.optimization_barrier(jnp.max(scores, axis=2)), sink_scores)
            weights = jnp.exp(scores - row_peak[:, :, None])
            sink_weight = jnp.exp(sink_scores - row_peak)
            row_total = lax.optimization_barrier(jnp.sum(weights, axis=2)) + sink_weight
            attn_probs = (weights / row_total[:, :, None]).astype(jnp.bfloat16)
            sink_prob = (sink_weight / row_total).astype(jnp.bfloat16)
            context = jnp.einsum('hqk,khd->qhd', attn_probs.astype(jnp.float32), value_heads)
            context = context + jnp.einsum('hq,qhd->qhd', sink_prob.astype(jnp.float32), sink_value)
            return context.reshape(TOK_DEV, model_width).astype(jnp.bfloat16)
        blocks = lax.map(one_block, jnp.arange(N_SEQ, dtype=jnp.int32))
        return blocks.reshape(SEQLEN, model_width)
    return lax.map(one_group, (queries, key_rows, value_rows, segments))

def mixture(normed, logits, chosen, weight_rows, multiple, gate_weight, up_weight, down_weight):
    picked = jnp.take_along_axis(logits, chosen, axis=1)
    first_gate = jax.nn.sigmoid(picked[:, 0] - picked[:, 1])
    gate_pair = jnp.stack([first_gate, 1.0 - first_gate], axis=1)
    pair_rows = weight_rows.reshape(-1)
    pair_count = pair_rows.shape[0]
    limit = multiple * N_SEQ * N_EXP * CAP
    token_of_pair = jnp.arange(pair_count, dtype=jnp.int32) // TOP
    padded_normed = jnp.concatenate([normed, jnp.zeros((1, D), normed.dtype)], axis=0)
    token_pad = jnp.concatenate([token_of_pair, jnp.full((1,), normed.shape[0], jnp.int32)])

    def one_expert(expert_index, outputs):
        picks = jnp.nonzero(pair_rows == expert_index, size=limit, fill_value=pair_count)[0].astype(jnp.int32)
        rows_in = padded_normed[token_pad[picks]]
        gate_part = jnp.dot(rows_in, gate_weight[expert_index], preferred_element_type=jnp.float32)
        up_part = jnp.dot(rows_in, up_weight[expert_index], preferred_element_type=jnp.float32)
        active = (jax.nn.gelu(gate_part, approximate=True) * up_part).astype(jnp.bfloat16)
        expert_out = jnp.dot(active, down_weight[expert_index], preferred_element_type=jnp.float32).astype(jnp.bfloat16)
        return outputs.at[picks].set(expert_out)
    outputs = lax.fori_loop(0, EXPERTS, one_expert, jnp.zeros((pair_count + 1, D), jnp.bfloat16))
    values = outputs[:pair_count].reshape(-1, TOP, D).astype(jnp.float32)
    return lax.optimization_barrier(jnp.sum(values * gate_pair[:, :, None], axis=1))

def reference(tokens, queries, key_rows, value_rows, segments, bias_table, out_proj, router, gate_weight, up_weight, down_weight, old_table, new_table, routes_one, routes_two):
    holder_of = jnp.zeros((EXPERTS,), jnp.int32).at[old_table].set(jnp.arange(EXPERTS, dtype=jnp.int32))
    second_expert = new_table[routes_two]
    batch_plans = ((routes_one, 1), (second_expert, 2))
    results = []
    for batch_index in range(2):
        context = attend_rows(queries[batch_index], key_rows[batch_index], value_rows[batch_index], segments[batch_index], bias_table)
        flat_context = context.reshape(GROUPS * SEQLEN, HEADS * HEAD_DIM)
        hidden = tokens[batch_index].reshape(GROUPS * SEQLEN, D).astype(jnp.float32) + jnp.dot(flat_context, out_proj, preferred_element_type=jnp.float32)
        normed = (hidden * lax.rsqrt(lax.optimization_barrier(jnp.mean(hidden * hidden, axis=1, keepdims=True)) + epsilon)).astype(jnp.bfloat16)
        logits = jnp.dot(normed, router, preferred_element_type=jnp.float32)
        chosen = batch_plans[batch_index][0].reshape(GROUPS * SEQLEN, TOP)
        weight_rows = holder_of[chosen]
        mixed_out = mixture(normed, logits, chosen, weight_rows, batch_plans[batch_index][1], gate_weight, up_weight, down_weight)
        results.append((hidden + mixed_out).astype(jnp.bfloat16).reshape(GROUPS, SEQLEN, D))
    return jnp.stack(results)
```

```python
import functools

import jax
import jax.numpy as jnp
from jax import lax
from jax.experimental import pallas as pl
from jax.experimental.pallas import tpu as pltpu
from jax.sharding import PartitionSpec as P

WIN_BLOCKS = 4
NBUCK = 32
MAX_SLOTS = 2

score_scale = 0.125
epsilon = 1e-06
masked_score = -1e30

f32 = jnp.float32
bf16 = jnp.bfloat16
NT = (((1,), (1,)), ((), ()))
TN = (((0,), (0,)), ((), ()))
VMEM = pl.BlockSpec(memory_space=pltpu.VMEM)
SMEM = pl.BlockSpec(memory_space=pltpu.SMEM)
ANY = pl.BlockSpec(memory_space=pl.ANY)


def iota(shape, dim):
    return lax.broadcasted_iota(jnp.int32, shape, dim)


def passed_along(value, axis, steps):
    count = lax.axis_size(axis)
    return lax.ppermute(value, axis, [(source, source + steps) for source in range(count - steps)])


def merge_starts(former, latter):
    take_latter = (latter[4] > 0) & ((former[4] == 0) | (latter[3] != former[3]))
    return tuple((jnp.where(take_latter, newer, older) for older, newer in zip(former, latter)))


def latest_start(key_rows, value_rows, segments):
    tok_count, model_width = key_rows.shape
    length, index = (lax.axis_size("seq"), lax.axis_index("seq"))
    last_seg = segments[tok_count - 1]
    lead = jnp.sum((segments < last_seg).astype(jnp.int32))
    one = jnp.ones((), jnp.int32)
    found = (key_rows[lead], value_rows[lead], index * tok_count + lead, last_seg, one)
    everything = jax.tree.map(lambda part: lax.all_gather(part, "seq"), found)
    start = jax.tree.map(jnp.zeros_like, found)

    def lap(k, before):
        new = merge_starts(before, jax.tree.map(lambda part: part[k], everything))
        return jax.tree.map(lambda a, b: jnp.where(k < index, a, b), new, before)

    sink_key, sink_value, sink_pos, sink_seg, sink_has = lax.fori_loop(0, length, lap, start)
    block = jnp.zeros((2 * tok_count, model_width), key_rows.dtype)
    block = block.at[0].set(sink_key).at[tok_count].set(sink_value)
    return (block, jnp.stack([sink_pos, sink_seg, sink_has]))


def placements(routes, table, old_table, experts, tok_count, cap):
    chosen, holders = ([], [])
    for c in range(2):
        pick = routes[c : c + 1, :]
        if table is not None:
            pick = sum(jnp.where(pick == s, table[s], 0) for s in range(experts))
        chosen.append(pick)
        holders.append(sum(jnp.where(pick == old_table[x], x, 0) for x in range(experts)))
    expert = iota((experts, tok_count), 0)
    member = (expert == holders[0]) | (expert == holders[1])
    earlier = (iota((tok_count, tok_count), 0) < iota((tok_count, tok_count), 1)).astype(f32)
    rank = jnp.dot(
        member.astype(f32).astype(bf16), earlier.astype(bf16), preferred_element_type=f32
    ).astype(jnp.int32)
    rows = []
    for c in range(2):
        own = jnp.sum(jnp.where(expert == holders[c], rank, 0), axis=0, keepdims=True)
        rows.append(holders[c] * cap + own)
    return (chosen, rows)


def attend_kernel(
    hops, heads, experts, cap, slotted, sinks,
    bias, new_table, old_table, seg, routes, q, k, v, *rest,
):
    moved, rest = (rest[:hops], rest[hops:])
    if sinks:
        sink_block, sink_info, rest = (rest[0], rest[1], rest[2:])
    tokens, proj, router_t, hidden_out, outgoing, gates_out, rows_out, context = rest
    tok_count, width = q.shape
    window = WIN_BLOCKS * tok_count
    index = lax.axis_index("seq")
    grid = (tok_count, tok_count)
    own_seg = seg[pl.ds(index, 1), :]
    seg_col = jnp.broadcast_to(own_seg, grid).T
    visible, spans = ([], [])
    for j in range(hops + 1):
        key_seg = seg[pl.ds(jnp.maximum(index - j, 0), 1), :]
        key_seg = jnp.where(index >= j, key_seg, -1)
        distance = iota(grid, 0) - iota(grid, 1) + tok_count * j
        seen = (seg_col == key_seg) & (distance >= 0) & (distance < window)
        visible.append(jnp.where(seen, 0.0, masked_score))
        low, high = (max(0, tok_count * (j - 1) + 1), min(window, tok_count * (j + 1)) - 1)
        spans.append((distance, low.bit_length(), high.bit_length()))
    if sinks:
        position = index * tok_count + iota(grid, 0)
        seen = (seg_col == sink_info[1]) & (sink_info[2] > 0) & (position - sink_info[0] >= window)
        visible.append(jnp.where(seen & (iota(grid, 1) == 0), 0.0, masked_score))
        spans.append((None, NBUCK - 1, NBUCK - 1))
    lane = iota((tok_count, 128), 1)
    half = width // heads
    for pair in range(heads // 2):
        cols = slice(128 * pair, 128 * pair + 128)
        both = q[:, cols] * score_scale
        even = jnp.where(lane < half, both, jnp.zeros_like(both))
        odd = jnp.where(lane < half, jnp.zeros_like(both), both)
        stacked = jnp.concatenate([even, odd], axis=0)
        blocks = [(k[:, cols], v[:, cols])]
        for ref in moved:
            blocks.append((ref[:tok_count, cols], ref[tok_count:, cols]))
        if sinks:
            blocks.append((sink_block[:tok_count, cols], sink_block[tok_count:, cols]))
        scores = []
        for (keys, _), (distance, low, high), seen in zip(blocks, spans, visible):
            score = lax.dot_general(stacked, keys, NT, preferred_element_type=f32)
            parts = []
            for side in range(2):
                head = 2 * pair + side
                offset = jnp.full(grid, bias[head, low], f32)
                for bucket in range(low + 1, high + 1):
                    offset = jnp.where(distance >= 1 << (bucket - 1), bias[head, bucket], offset)
                parts.append(score[side * tok_count : (side + 1) * tok_count] + (offset + seen))
            scores.append(jnp.concatenate(parts, axis=0))
        peak = functools.reduce(jnp.maximum, scores)
        peak = jnp.max(peak, axis=1, keepdims=True)
        weights = [jnp.exp(score - peak) for score in scores]
        total = jnp.sum(functools.reduce(jnp.add, weights), axis=1, keepdims=True)
        mixed = sum(
            jnp.dot(weight.astype(bf16), values, preferred_element_type=f32)
            for weight, (_, values) in zip(weights, blocks)
        )
        mixed = mixed / total
        context[:, cols] = jnp.where(lane < half, mixed[:tok_count], mixed[tok_count:]).astype(bf16)
    hidden = tokens[...].astype(f32) + jnp.dot(context[...], proj[...], preferred_element_type=f32)
    hidden_out[...] = hidden
    mean = jnp.mean(hidden * hidden, axis=1, keepdims=True)
    normed = (hidden * lax.rsqrt(mean + epsilon)).astype(bf16)
    logits = lax.dot_general(router_t[...], normed, NT, preferred_element_type=f32)
    chosen, rows = placements(
        routes[...], new_table if slotted else None, old_table, experts, tok_count, cap
    )
    expert = iota((experts, tok_count), 0)
    picked = [
        jnp.sum(jnp.where(expert == pick, logits, 0.0), axis=0, keepdims=True) for pick in chosen
    ]
    first = jax.nn.sigmoid(picked[0] - picked[1])
    gates_out[...] = jnp.concatenate([first, 1.0 - first], axis=0)
    rows_out[...] = jnp.concatenate(rows, axis=0)
    place = iota((experts * cap, tok_count), 0)
    plan = jnp.where((place == rows[0]) | (place == rows[1]), 1.0, 0.0).astype(bf16)
    outgoing[...] = jnp.dot(plan, normed, preferred_element_type=f32).astype(bf16)


def ffn_kernel(chunks, tile, rows, gate, up, down, out, gate_v, up_v, down_v, total, sems):
    copies = []
    for n, (begin, size) in enumerate(chunks):
        span = pl.ds(begin, size)
        copies.append((
            pltpu.make_async_copy(gate.at[:, span], gate_v.at[:, span], sems.at[3 * n]),
            pltpu.make_async_copy(up.at[:, span], up_v.at[:, span], sems.at[3 * n + 1]),
            pltpu.make_async_copy(down.at[span, :], down_v.at[span, :], sems.at[3 * n + 2]),
        ))
    for group in copies:
        for copy in group:
            copy.start()
    for n, (begin, size) in enumerate(chunks):
        span = pl.ds(begin, size)
        for copy in copies[n]:
            copy.wait()

        @pl.loop(0, rows.shape[0] // tile)
        def _(m):
            here = pl.ds(pl.multiple_of(m * tile, tile), tile)
            x = rows[here, :]
            gate_part = jnp.dot(x, gate_v[:, span], preferred_element_type=f32)
            up_part = jnp.dot(x, up_v[:, span], preferred_element_type=f32)
            active = (jax.nn.gelu(gate_part, approximate=True) * up_part).astype(bf16)
            part = jnp.dot(active, down_v[span, :], preferred_element_type=f32)
            if n == 0:
                total[here, :] = part
            elif n < len(chunks) - 1:
                total[here, :] += part
            else:
                out[here, :] = (total[here, :] + part).astype(bf16)


def combine_kernel(hidden, gates, rows, returned, out):
    slots, tok_count = (returned.shape[0], hidden.shape[0])
    place = iota((slots, tok_count), 0)
    spread = jnp.where(place == rows[0:1, :], gates[0:1, :], 0.0)
    spread = spread + jnp.where(place == rows[1:2, :], gates[1:2, :], 0.0)
    coarse = spread.astype(bf16)
    fine = (spread - coarse.astype(f32)).astype(bf16)
    values = returned[...]
    mixed = lax.dot_general(coarse, values, TN, preferred_element_type=f32)
    mixed = mixed + lax.dot_general(fine, values, TN, preferred_element_type=f32)
    out[...] = (hidden[...] + mixed).astype(bf16)


def shaped(shape, dtype):
    return jax.ShapeDtypeStruct(shape, dtype)


def local(
    tokens, queries, key_rows, value_rows, segments, bias_table, out_proj, router,
    gate_weight, up_weight, down_weight, old_table, new_table, routes_one, routes_two,
):
    tok_count, width = tokens.shape[2:]
    heads = bias_table.shape[0]
    experts = router.shape[1]
    inner = gate_weight.shape[2]
    seq_len = tok_count * lax.axis_size("seq")
    capacity = tok_count * 2 * 5 // (4 * experts)
    longest = seq_len // 2
    hops = min(WIN_BLOCKS, (longest - 1 + tok_count - 1) // tok_count)
    sinks = seq_len > WIN_BLOCKS * tok_count
    chunks = [(b, min(256, inner - b)) for b in range(0, inner, 256)]
    all_segs = lax.all_gather(segments[:, 0], "seq", axis=1)
    router_t = router.T
    routes = (routes_one[0].T, routes_two[0].T)
    results = [None, None]
    for batch in (1, 0):
        cap = capacity * (MAX_SLOTS if batch else 1)
        q, k, v = (a[batch, 0] for a in (queries, key_rows, value_rows))
        moving = jnp.concatenate([k, v], axis=0)
        moved = []
        for _ in range(hops):
            moving = passed_along(moving, "seq", 1)
            moved.append(moving)
        extra = list(latest_start(k, v, segments[batch, 0])) if sinks else []
        slots = experts * cap
        hidden, outgoing, gates, rows = pl.pallas_call(
            functools.partial(attend_kernel, hops, heads, experts, cap, batch == 1, sinks),
            out_shape=(
                shaped((tok_count, width), f32),
                shaped((slots, width), bf16),
                shaped((2, tok_count), f32),
                shaped((2, tok_count), jnp.int32),
            ),
            in_specs=[SMEM] * 3 + [VMEM] * (5 + hops) + ([VMEM, SMEM] if sinks else []) + [VMEM] * 3,
            out_specs=(VMEM,) * 4,
            scratch_shapes=[pltpu.VMEM((tok_count, width), bf16)],
            compiler_params=pltpu.CompilerParams(vmem_limit_bytes=32 * 2**20),
            cost_estimate=pl.CostEstimate(flops=10**9, bytes_accessed=8 * 10**6, transcendentals=10**6),
        )(
            bias_table, new_table, old_table, all_segs[batch], routes[batch], q, k, v, *moved,
            *extra, tokens[batch, 0], out_proj, router_t,
        )
        received = lax.all_to_all(
            outgoing.reshape(experts, cap, width), "exp", split_axis=0, concat_axis=0, tiled=True
        )
        tile = min(slots, 320)
        answered = pl.pallas_call(
            functools.partial(ffn_kernel, chunks, tile),
            out_shape=shaped((slots, width), bf16),
            in_specs=[VMEM] + [ANY] * 3,
            out_specs=VMEM,
            scratch_shapes=[
                pltpu.VMEM((width, inner), bf16),
                pltpu.VMEM((width, inner), bf16),
                pltpu.VMEM((inner, width), bf16),
                pltpu.VMEM((slots, width), f32),
                pltpu.SemaphoreType.DMA((3 * len(chunks),)),
            ],
            compiler_params=pltpu.CompilerParams(vmem_limit_bytes=40 * 2**20),
            cost_estimate=pl.CostEstimate(
                flops=6 * slots * width * inner, bytes_accessed=10**7, transcendentals=slots * inner
            ),
        )(received.reshape(slots, width), gate_weight[0], up_weight[0], down_weight[0])
        returned = lax.all_to_all(
            answered.reshape(experts, cap, width), "exp", split_axis=0, concat_axis=0, tiled=True
        )
        results[batch] = pl.pallas_call(
            combine_kernel,
            out_shape=shaped((tok_count, width), bf16),
            in_specs=[VMEM] * 4,
            out_specs=VMEM,
            compiler_params=pltpu.CompilerParams(vmem_limit_bytes=32 * 2**20),
            cost_estimate=pl.CostEstimate(flops=10**9, bytes_accessed=3 * 10**6, transcendentals=0),
        )(hidden, gates, rows, returned.reshape(slots, width))
    return jnp.stack(results)[:, None]


def solution(mesh):
    rows = P(None, "exp", "seq", None)
    placed = (
        rows, rows, rows, rows, P(None, "exp", "seq"), P(), P(), P(),
        P("exp", None, None), P("exp", None, None), P("exp", None, None), P(), P(),
        P("exp", "seq", None), P("exp", "seq", None),
    )
    return jax.shard_map(local, mesh=mesh, in_specs=placed, out_specs=rows, check_vma=False)
```

```python
import functools

import jax
import jax.numpy as jnp
from jax import lax
from jax.experimental import pallas as pl
from jax.experimental.pallas import tpu as pltpu
from jax.sharding import PartitionSpec as P

WIN_BLOCKS = 4
NBUCK = 32
MAX_SLOTS = 2
INTS = 8

score_scale = 0.125
epsilon = 1e-06
masked_score = -1e30

f32 = jnp.float32
bf16 = jnp.bfloat16
NT = (((1,), (1,)), ((), ()))
TN = (((0,), (0,)), ((), ()))
VMEM = pl.BlockSpec(memory_space=pltpu.VMEM)
SMEM = pl.BlockSpec(memory_space=pltpu.SMEM)
ANY = pl.BlockSpec(memory_space=pl.ANY)


def iota(shape, dim):
    return lax.broadcasted_iota(jnp.int32, shape, dim)


def shaped(shape, dtype):
    return jax.ShapeDtypeStruct(shape, dtype)


def passed_along(value, axis, steps):
    count = lax.axis_size(axis)
    return lax.ppermute(value, axis, [(source, source + steps) for source in range(count - steps)])


def swapped(value, axis, mask):
    count = lax.axis_size(axis)
    return lax.ppermute(value, axis, [(source, source ^ mask) for source in range(count)])


def merge_starts(former, latter):
    take_latter = (latter[4] > 0) & ((former[4] == 0) | (latter[3] != former[3]))
    return tuple((jnp.where(take_latter, newer, older) for older, newer in zip(former, latter)))


def latest_start(key_rows, value_rows, segments):
    tok_count, model_width = key_rows.shape
    length, index = (lax.axis_size("seq"), lax.axis_index("seq"))
    last_seg = segments[tok_count - 1]
    lead = jnp.sum((segments < last_seg).astype(jnp.int32))
    one = jnp.ones((), jnp.int32)
    found = (key_rows[lead], value_rows[lead], index * tok_count + lead, last_seg, one)
    everything = jax.tree.map(lambda part: lax.all_gather(part, "seq"), found)
    start = jax.tree.map(jnp.zeros_like, found)

    def lap(k, before):
        new = merge_starts(before, jax.tree.map(lambda part: part[k], everything))
        return jax.tree.map(lambda a, b: jnp.where(k < index, a, b), new, before)

    sink_key, sink_value, sink_pos, sink_seg, sink_has = lax.fori_loop(0, length, lap, start)
    block = jnp.zeros((2 * tok_count, model_width), key_rows.dtype)
    block = block.at[0].set(sink_key).at[tok_count].set(sink_value)
    return (block, jnp.stack([sink_pos, sink_seg, sink_has]))


def column_routes(batch, experts, ints, new_table, old_table):
    me = lax.axis_index("exp")
    first = lax.axis_index("seq") * experts
    chosen, holders = ([[], []], [[], []])
    for m in range(experts // 2):
        base = (first + (me ^ (2 * m))) * INTS + 2 + 2 * batch
        for c in range(2):
            pick = ints[pl.ds(base + c, 1), :]
            if batch:
                pick = sum(jnp.where(pick == s, new_table[s], 0) for s in range(experts))
            chosen[c].append(pick)
            holders[c].append(sum(jnp.where(pick == old_table[x], x, 0) for x in range(experts)))
    return (chosen, [jnp.concatenate(rows, axis=0) for rows in holders])


def attend_kernel(
    batch, hops, relayed, heads, experts, sinks,
    bias, new_table, old_table, ints, q, k, v, *rest,
):
    count = 3 if relayed else hops
    moved, rest = (rest[:count], rest[count:])
    if sinks:
        sink_block, sink_info, rest = (rest[0], rest[1], rest[2:])
    tokens, proj, hidden_out, normed_out, places_out, context = rest
    tok_count, width = tokens.shape[2:]
    window = WIN_BLOCKS * tok_count
    index, me = (lax.axis_index("seq"), lax.axis_index("exp"))
    grid = (tok_count, tok_count)

    def seg_row(block):
        return ints[pl.ds((block * experts + me) * INTS + batch, 1), :]

    seg_col = jnp.broadcast_to(seg_row(index), grid).T
    visible, spans = ([], [])
    for j in range(hops + 1):
        key_seg = jnp.where(index >= j, seg_row(jnp.maximum(index - j, 0)), -1)
        distance = iota(grid, 0) - iota(grid, 1) + tok_count * j
        seen = (seg_col == key_seg) & (distance >= 0) & (distance < window)
        visible.append(jnp.where(seen, 0.0, masked_score))
        low, high = (max(0, tok_count * (j - 1) + 1), min(window, tok_count * (j + 1)) - 1)
        spans.append((distance, low.bit_length(), high.bit_length()))
    if sinks:
        position = index * tok_count + iota(grid, 0)
        seen = (seg_col == sink_info[1]) & (sink_info[2] > 0) & (position - sink_info[0] >= window)
        visible.append(jnp.where(seen & (iota(grid, 1) == 0), 0.0, masked_score))
        spans.append((None, NBUCK - 1, NBUCK - 1))
    lane = iota((tok_count, 128), 1)
    half = width // heads
    keys_at, values_at = (slice(0, tok_count), slice(tok_count, 2 * tok_count))
    for pair in range(heads // 2):
        cols = slice(128 * pair, 128 * pair + 128)
        both = q[batch, 0, :, cols] * score_scale
        even = jnp.where(lane < half, both, jnp.zeros_like(both))
        odd = jnp.where(lane < half, jnp.zeros_like(both), both)
        stacked = jnp.concatenate([even, odd], axis=0)
        blocks = [(k[batch, 0, :, cols], v[batch, 0, :, cols])]
        if relayed:
            pairwise, across, relay = moved
            paired = index % 2 == 1
            blocks.append(tuple(
                jnp.where(paired, pairwise[at, cols], relay[at, cols])
                for at in (keys_at, values_at)
            ))
            blocks.append((across[keys_at, cols], across[values_at, cols]))
        else:
            for ref in moved:
                blocks.append((ref[keys_at, cols], ref[values_at, cols]))
        if sinks:
            blocks.append((sink_block[keys_at, cols], sink_block[values_at, cols]))
        scores = []
        for (keys, _), (distance, low, high), seen in zip(blocks, spans, visible):
            score = lax.dot_general(stacked, keys, NT, preferred_element_type=f32)
            parts = []
            for side in range(2):
                head = 2 * pair + side
                offset = jnp.full(grid, bias[head, low], f32)
                for bucket in range(low + 1, high + 1):
                    offset = jnp.where(distance >= 1 << (bucket - 1), bias[head, bucket], offset)
                parts.append(score[side * tok_count : (side + 1) * tok_count] + (offset + seen))
            scores.append(jnp.concatenate(parts, axis=0))
        peak = jnp.max(functools.reduce(jnp.maximum, scores), axis=1, keepdims=True)
        weights = [jnp.exp(score - peak) for score in scores]
        total = jnp.sum(functools.reduce(jnp.add, weights), axis=1, keepdims=True)
        scale = 1.0 / total
        mixed = sum(
            jnp.dot((weight * scale).astype(bf16), values, preferred_element_type=f32)
            for weight, (_, values) in zip(weights, blocks)
        )
        context[:, cols] = jnp.where(lane < half, mixed[:tok_count], mixed[tok_count:]).astype(bf16)
    hidden = tokens[batch, 0].astype(f32) + jnp.dot(
        context[...], proj[...], preferred_element_type=f32
    )
    hidden_out[...] = hidden
    mean = jnp.mean(hidden * hidden, axis=1, keepdims=True)
    normed_out[...] = (hidden * lax.rsqrt(mean + epsilon)).astype(bf16)
    _, holders = column_routes(batch, experts, ints, new_table, old_table)
    member = jnp.concatenate(
        [jnp.where((holders[0] == at) | (holders[1] == at), 1.0, 0.0) for at in (me, me ^ 1)],
        axis=0,
    )
    earlier = jnp.where(iota(grid, 0) < iota(grid, 1), 1.0, 0.0).astype(bf16)
    rank = jnp.dot(member.astype(bf16), earlier, preferred_element_type=f32)
    places_out[...] = jnp.where(member > 0.5, rank.astype(jnp.int32), -1)


def picked_rows(members, cap, first_row, places, blocks):
    tok_count = blocks[0].shape[0]
    at = iota((len(members) * cap, tok_count), 0)
    rows = None
    for n, m in enumerate(members):
        place = places[first_row + m : first_row + m + 1, :]
        place = jnp.where(place >= 0, place + n * cap, -1)
        plan = jnp.where(at == place, 1.0, 0.0).astype(bf16)
        part = jnp.dot(plan, blocks[n][...], preferred_element_type=f32)
        rows = part if rows is None else rows + part
    return rows.astype(bf16)


def pack_kernel(members, cap, columns, places, *rest):
    blocks, out = (rest[:-1], rest[-1])
    out[...] = picked_rows(members, cap, columns, places, blocks)


def expert_chunks(chunks, rows, stores, weights, scratch):
    gate, up, down = weights
    gate_v, up_v, down_v, total, sems = scratch
    copies = []
    for n, (begin, size) in enumerate(chunks):
        span = pl.ds(begin, size)
        copies.append((
            pltpu.make_async_copy(gate.at[0, :, span], gate_v.at[:, span], sems.at[3 * n]),
            pltpu.make_async_copy(up.at[0, :, span], up_v.at[:, span], sems.at[3 * n + 1]),
            pltpu.make_async_copy(down.at[0, span, :], down_v.at[span, :], sems.at[3 * n + 2]),
        ))
    for group in copies:
        for copy in group:
            copy.start()
    yield
    for n, (begin, size) in enumerate(chunks):
        span = pl.ds(begin, size)
        for copy in copies[n]:
            copy.wait()
        x = rows[...]
        gate_part = jnp.dot(x, gate_v[:, span], preferred_element_type=f32)
        up_part = jnp.dot(x, up_v[:, span], preferred_element_type=f32)
        active = (jax.nn.gelu(gate_part, approximate=True) * up_part).astype(bf16)
        part = jnp.dot(active, down_v[span, :], preferred_element_type=f32)
        if n == 0:
            total[...] = part
        elif n < len(chunks) - 1:
            total[...] += part
        else:
            stores((total[...] + part).astype(bf16))
    yield


def near_kernel(
    batch, experts, cap, chunks, new_table, old_table, ints, places, router_t, *rest
):
    columns = experts // 2
    blocks, rest = (rest[:columns], rest[columns:])
    weights, (out, gates_out, rows), scratch = (rest[:3], rest[3:6], rest[6:])

    def stores(value):
        out[...] = value

    steps = expert_chunks(chunks, rows, stores, weights, scratch)
    next(steps)
    rows[...] = picked_rows(range(columns), cap, 0, places, blocks)
    chosen, holders = column_routes(batch, experts, ints, new_table, old_table)
    me = lax.axis_index("exp")
    firsts = []
    for m in range(columns):
        logits = lax.dot_general(router_t[...], blocks[m][...], NT, preferred_element_type=f32)
        expert = iota(logits.shape, 0)
        picked = [
            jnp.sum(jnp.where(expert == chosen[c][m], logits, 0.0), axis=0, keepdims=True)
            for c in range(2)
        ]
        firsts.append(jax.nn.sigmoid(picked[0] - picked[1]))
    first = jnp.concatenate(firsts, axis=0)
    gates_out[...] = jnp.concatenate(
        [
            jnp.where(holders[0] == at, first, 0.0) + jnp.where(holders[1] == at, 1.0 - first, 0.0)
            for at in (me, me ^ 1)
        ],
        axis=0,
    )
    next(steps)


def far_kernel(chunks, low_in, high_in, *rest):
    weights, (low_out, high_out, rows), scratch = (rest[:3], rest[3:6], rest[6:])
    part = low_in.shape[0]

    def stores(value):
        low_out[...] = value[:part]
        high_out[...] = value[part:]

    steps = expert_chunks(chunks, rows, stores, weights, scratch)
    next(steps)
    rows[:part, :] = low_in[...]
    rows[part:, :] = high_in[...]
    next(steps)


def partial_kernel(members, cap, columns, places, gates, near, far, *outs):
    tok_count = places.shape[1]
    for n, m in enumerate(members):
        total = None
        for source, row, base in ((near, m, m * cap), (far, columns + m, n * cap)):
            at = iota((source.shape[0], tok_count), 0)
            place = places[row : row + 1, :]
            place = jnp.where(place >= 0, place + base, -1)
            spread = jnp.where(at == place, gates[row : row + 1, :], 0.0)
            coarse = spread.astype(bf16)
            fine = (spread - coarse.astype(f32)).astype(bf16)
            for half in (coarse, fine):
                term = lax.dot_general(half, source[...], TN, preferred_element_type=f32)
                total = term if total is None else total + term
        outs[n][...] = total.astype(outs[n].dtype)


def fold_kernel(own, *rest):
    total = own[...]
    for ref in rest[:-1]:
        total = total + ref[...].astype(f32)
    rest[-1][...] = total.astype(rest[-1].dtype)


def final_kernel(counts, *refs):
    out = refs[-1]
    at = 0
    for batch, count in enumerate(counts):
        total = refs[at][...]
        for ref in refs[at + 1 : at + count]:
            total = total + ref[...].astype(f32)
        at += count
        out[batch, 0] = total.astype(bf16)


def call(kernel, outs, ins, args, flops=10**7, moved=10**6, scratch=(), limit=32):
    return pl.pallas_call(
        kernel,
        out_shape=outs,
        in_specs=ins,
        out_specs=jax.tree.map(lambda _: VMEM, outs),
        scratch_shapes=list(scratch),
        compiler_params=pltpu.CompilerParams(vmem_limit_bytes=limit * 2**20),
        cost_estimate=pl.CostEstimate(flops=flops, bytes_accessed=moved, transcendentals=0),
    )(*args)


def local(
    tokens, queries, key_rows, value_rows, segments, bias_table, out_proj, router,
    gate_weight, up_weight, down_weight, old_table, new_table, routes_one, routes_two,
):
    tok_count, width = tokens.shape[2:]
    heads = bias_table.shape[0]
    experts = router.shape[1]
    columns = experts // 2
    inner = gate_weight.shape[2]
    seq_size = lax.axis_size("seq")
    seq_len = tok_count * seq_size
    capacity = tok_count * 2 * 5 // (4 * experts)
    longest = seq_len // 2
    hops = min(WIN_BLOCKS, (longest - 1 + tok_count - 1) // tok_count)
    relayed = seq_size == 4 and hops == 2
    sinks = seq_len > WIN_BLOCKS * tok_count
    chunks = [(b, min(256, inner - b)) for b in range(0, inner, 256)]
    weights = (gate_weight, up_weight, down_weight)
    router_t = router.T
    lower, upper = (range(columns // 2), range(columns // 2, columns))
    rows_bf16 = shaped((tok_count, width), bf16)
    rows_f32 = shaped((tok_count, width), f32)

    stacks = {b: jnp.concatenate([key_rows[b, 0], value_rows[b, 0]], axis=0) for b in (1, 0)}
    moved = {}
    for batch in (1, 0):
        moving = stacks[batch]
        if relayed:
            across = swapped(moving, "seq", 2)
            moved[batch] = [swapped(moving, "seq", 1), across, swapped(across, "seq", 1)]
        else:
            moved[batch] = []
            for _ in range(hops):
                moving = passed_along(moving, "seq", 1)
                moved[batch].append(moving)
    mine = jnp.concatenate(
        [segments[:, 0], routes_one[0].T, routes_two[0].T, jnp.zeros((2, tok_count), jnp.int32)]
    )
    ints = lax.all_gather(mine, ("seq", "exp")).reshape(-1, tok_count)

    def scratch_for(slots):
        return (
            pltpu.VMEM((slots, width), bf16),
            pltpu.VMEM((width, inner), bf16),
            pltpu.VMEM((width, inner), bf16),
            pltpu.VMEM((inner, width), bf16),
            pltpu.VMEM((slots, width), f32),
            pltpu.SemaphoreType.DMA((3 * len(chunks),)),
        )

    sums = {}
    for batch in (1, 0):
        cap = capacity * (MAX_SLOTS if batch else 1)
        slots, part = (columns * cap, columns // 2 * cap)
        extra = []
        if sinks:
            extra = latest_start(key_rows[batch, 0], value_rows[batch, 0], segments[batch, 0])
        hidden, normed, places = call(
            functools.partial(attend_kernel, batch, hops, relayed, heads, experts, sinks),
            (rows_f32, rows_bf16, shaped((2 * columns, tok_count), jnp.int32)),
            [SMEM] * 3 + [VMEM] * (4 + len(moved[batch])) + ([VMEM, SMEM] if sinks else [])
            + [VMEM] * 2,
            (bias_table, new_table, old_table, ints, queries, key_rows, value_rows, *moved[batch],
             *extra, tokens, out_proj),
            flops=10**9, moved=8 * 10**6, scratch=[pltpu.VMEM((tok_count, width), bf16)],
        )
        blocks = {0: normed}
        bit = columns // 2
        while bit:
            for m in sorted(blocks):
                blocks[m | bit] = swapped(blocks[m], "exp", 2 * bit)
            bit //= 2
        crossed = []
        for members in (lower, upper):
            packed = call(
                functools.partial(pack_kernel, members, cap, columns),
                shaped((part, width), bf16),
                [VMEM] * (1 + len(members)),
                (places, *(blocks[m] for m in members)),
            )
            crossed.append(swapped(packed, "exp", 1))
        near, gates = call(
            functools.partial(near_kernel, batch, experts, cap, chunks),
            (shaped((slots, width), bf16), shaped((2 * columns, tok_count), f32)),
            [SMEM] * 2 + [VMEM] * (3 + columns) + [ANY] * 3,
            (new_table, old_table, ints, places, router_t, *(blocks[m] for m in range(columns)),
             *weights),
            flops=6 * slots * width * inner, moved=10**7, scratch=scratch_for(slots), limit=56,
        )
        far = call(
            functools.partial(far_kernel, chunks),
            (shaped((part, width), bf16),) * 2,
            [VMEM] * 2 + [ANY] * 3,
            (*crossed, *weights),
            flops=6 * slots * width * inner, moved=10**7, scratch=scratch_for(slots), limit=56,
        )
        totals = {}
        for members, answered in ((upper, far[1]), (lower, far[0])):
            returned = swapped(answered, "exp", 1)
            parts = call(
                functools.partial(partial_kernel, members, cap, columns),
                tuple(rows_bf16 if m % 2 else rows_f32 for m in members),
                [VMEM] * 4,
                (places, gates, near, returned),
            )
            for m, value in zip(members, parts):
                totals[m] = [value]
        bit = 1
        while bit < columns:
            for m in range(columns - bit, 0, -2 * bit):
                value = totals[m][0]
                if len(totals[m]) > 1:
                    value = call(fold_kernel, rows_bf16, [VMEM] * len(totals[m]), totals[m])
                totals[m - bit].append(swapped(value, "exp", 2 * bit))
            bit *= 2
        sums[batch] = [hidden, *totals[0]]
    return call(
        functools.partial(final_kernel, [len(sums[0]), len(sums[1])]),
        shaped((2, 1, tok_count, width), bf16),
        [VMEM] * (len(sums[0]) + len(sums[1])),
        (*sums[0], *sums[1]),
    )


def solution(mesh):
    rows = P(None, "exp", "seq", None)
    placed = (
        rows, rows, rows, rows, P(None, "exp", "seq"), P(), P(), P(),
        P("exp", None, None), P("exp", None, None), P("exp", None, None), P(), P(),
        P("exp", "seq", None), P("exp", "seq", None),
    )
    return jax.shard_map(local, mesh=mesh, in_specs=placed, out_specs=rows, check_vma=False)
```

```python
import functools

import jax
import jax.numpy as jnp
from jax import lax
from jax.experimental import pallas as pl
from jax.experimental.pallas import tpu as pltpu
from jax.sharding import PartitionSpec as P

WIN_BLOCKS = 4
NBUCK = 32
MAX_SLOTS = 2

score_scale = 0.125
epsilon = 1e-06
masked_score = -1e30

f32 = jnp.float32
bf16 = jnp.bfloat16
NT = (((1,), (1,)), ((), ()))
TN = (((0,), (0,)), ((), ()))
VMEM = pl.BlockSpec(memory_space=pltpu.VMEM)
SMEM = pl.BlockSpec(memory_space=pltpu.SMEM)
ANY = pl.BlockSpec(memory_space=pl.ANY)


def iota(shape, dim):
    return lax.broadcasted_iota(jnp.int32, shape, dim)


def shaped(shape, dtype):
    return jax.ShapeDtypeStruct(shape, dtype)


def passed_along(value, axis, steps):
    count = lax.axis_size(axis)
    return lax.ppermute(value, axis, [(source, source + steps) for source in range(count - steps)])


def swapped(value, axis, mask):
    count = lax.axis_size(axis)
    return lax.ppermute(value, axis, [(source, source ^ mask) for source in range(count)])


def behind(value, *earlier):
    return lax.optimization_barrier((value, *earlier))[0]


def merge_starts(former, latter):
    take_latter = (latter[4] > 0) & ((former[4] == 0) | (latter[3] != former[3]))
    return tuple((jnp.where(take_latter, newer, older) for older, newer in zip(former, latter)))


def latest_start(key_rows, value_rows, segments):
    tok_count, model_width = key_rows.shape
    length, index = (lax.axis_size("seq"), lax.axis_index("seq"))
    last_seg = segments[tok_count - 1]
    lead = jnp.sum((segments < last_seg).astype(jnp.int32))
    one = jnp.ones((), jnp.int32)
    found = (key_rows[lead], value_rows[lead], index * tok_count + lead, last_seg, one)
    everything = jax.tree.map(lambda part: lax.all_gather(part, "seq"), found)
    start = jax.tree.map(jnp.zeros_like, found)

    def lap(k, before):
        new = merge_starts(before, jax.tree.map(lambda part: part[k], everything))
        return jax.tree.map(lambda a, b: jnp.where(k < index, a, b), new, before)

    sink_key, sink_value, sink_pos, sink_seg, sink_has = lax.fori_loop(0, length, lap, start)
    block = jnp.zeros((2 * tok_count, model_width), key_rows.dtype)
    block = block.at[0].set(sink_key).at[tok_count].set(sink_value)
    return (block, jnp.stack([sink_pos, sink_seg, sink_has]))


def column_routes(batch, experts, routes, new_table, old_table):
    chosen, holders = ([[], []], [[], []])
    for ref in routes:
        for c in range(2):
            pick = ref[2 * batch + c : 2 * batch + c + 1, :]
            if batch:
                pick = sum(jnp.where(pick == s, new_table[s], 0) for s in range(experts))
            chosen[c].append(pick)
            holders[c].append(sum(jnp.where(pick == old_table[x], x, 0) for x in range(experts)))
    return (chosen, [jnp.concatenate(rows, axis=0) for rows in holders])


def attend_kernel(
    batch, hops, relayed, heads, experts, sinks,
    bias, new_table, old_table, segs, q, k, v, *rest,
):
    count = 3 if relayed else hops
    moved, rest = (rest[:count], rest[count:])
    if sinks:
        sink_block, sink_info, rest = (rest[0], rest[1], rest[2:])
    routes, rest = (rest[: experts // 2], rest[experts // 2 :])
    tokens, proj, hidden_out, normed_out, places_out, context = rest
    tok_count, width = tokens.shape[2:]
    window = WIN_BLOCKS * tok_count
    index, me = (lax.axis_index("seq"), lax.axis_index("exp"))
    grid = (tok_count, tok_count)

    def seg_row(block):
        return segs[pl.ds(2 * block + batch, 1), :]

    seg_col = jnp.broadcast_to(seg_row(index), grid).T
    visible, spans = ([], [])
    for j in range(hops + 1):
        key_seg = jnp.where(index >= j, seg_row(jnp.maximum(index - j, 0)), -1)
        distance = iota(grid, 0) - iota(grid, 1) + tok_count * j
        seen = (seg_col == key_seg) & (distance >= 0) & (distance < window)
        visible.append(jnp.where(seen, 0.0, masked_score))
        low, high = (max(0, tok_count * (j - 1) + 1), min(window, tok_count * (j + 1)) - 1)
        spans.append((distance, low.bit_length(), high.bit_length()))
    if sinks:
        position = index * tok_count + iota(grid, 0)
        seen = (seg_col == sink_info[1]) & (sink_info[2] > 0) & (position - sink_info[0] >= window)
        visible.append(jnp.where(seen & (iota(grid, 1) == 0), 0.0, masked_score))
        spans.append((None, NBUCK - 1, NBUCK - 1))
    lane = iota((tok_count, 128), 1)
    half = width // heads
    keys_at, values_at = (slice(0, tok_count), slice(tok_count, 2 * tok_count))
    for pair in range(heads // 2):
        cols = slice(128 * pair, 128 * pair + 128)
        both = q[batch, 0, :, cols] * score_scale
        even = jnp.where(lane < half, both, jnp.zeros_like(both))
        odd = jnp.where(lane < half, jnp.zeros_like(both), both)
        stacked = jnp.concatenate([even, odd], axis=0)
        blocks = [(k[batch, 0, :, cols], v[batch, 0, :, cols])]
        if relayed:
            pairwise, across, relay = moved
            paired = index % 2 == 1
            blocks.append(tuple(
                jnp.where(paired, pairwise[at, cols], relay[at, cols])
                for at in (keys_at, values_at)
            ))
            blocks.append((across[keys_at, cols], across[values_at, cols]))
        else:
            for ref in moved:
                blocks.append((ref[keys_at, cols], ref[values_at, cols]))
        if sinks:
            blocks.append((sink_block[keys_at, cols], sink_block[values_at, cols]))
        scores = []
        for (keys, _), (distance, low, high), seen in zip(blocks, spans, visible):
            score = lax.dot_general(stacked, keys, NT, preferred_element_type=f32)
            parts = []
            for side in range(2):
                head = 2 * pair + side
                offset = jnp.full(grid, bias[head, low], f32)
                for bucket in range(low + 1, high + 1):
                    offset = jnp.where(distance >= 1 << (bucket - 1), bias[head, bucket], offset)
                parts.append(score[side * tok_count : (side + 1) * tok_count] + (offset + seen))
            scores.append(jnp.concatenate(parts, axis=0))
        peak = jnp.max(functools.reduce(jnp.maximum, scores), axis=1, keepdims=True)
        weights = [jnp.exp(score - peak) for score in scores]
        total = jnp.sum(functools.reduce(jnp.add, weights), axis=1, keepdims=True)
        scale = 1.0 / total
        mixed = sum(
            jnp.dot((weight * scale).astype(bf16), values, preferred_element_type=f32)
            for weight, (_, values) in zip(weights, blocks)
        )
        context[:, cols] = jnp.where(lane < half, mixed[:tok_count], mixed[tok_count:]).astype(bf16)
    hidden = tokens[batch, 0].astype(f32) + jnp.dot(
        context[...], proj[...], preferred_element_type=f32
    )
    hidden_out[...] = hidden
    mean = jnp.mean(hidden * hidden, axis=1, keepdims=True)
    normed_out[...] = (hidden * lax.rsqrt(mean + epsilon)).astype(bf16)
    _, holders = column_routes(batch, experts, routes, new_table, old_table)
    member = jnp.concatenate(
        [jnp.where((holders[0] == at) | (holders[1] == at), 1.0, 0.0) for at in (me, me ^ 1)],
        axis=0,
    )
    earlier = jnp.where(iota(grid, 0) < iota(grid, 1), 1.0, 0.0).astype(bf16)
    rank = jnp.dot(member.astype(bf16), earlier, preferred_element_type=f32)
    places_out[...] = jnp.where(member > 0.5, rank.astype(jnp.int32), -1)


def picked_rows(members, cap, first_row, places, blocks):
    tok_count = blocks[0].shape[0]
    at = iota((len(members) * cap, tok_count), 0)
    plans = []
    for n, m in enumerate(members):
        place = places[first_row + m : first_row + m + 1, :]
        place = jnp.where(place >= 0, place + n * cap, -1)
        plans.append(jnp.where(at == place, 1.0, 0.0).astype(bf16))
    plan = jnp.concatenate(plans, axis=1)
    rows = jnp.concatenate([block[...] for block in blocks], axis=0)
    return jnp.dot(plan, rows, preferred_element_type=f32).astype(bf16)


def stack_kernel(batch, k, v, out, sems):
    tok_count = k.shape[2]
    copies = [
        pltpu.make_async_copy(k.at[batch, 0], out.at[pl.ds(0, tok_count)], sems.at[0]),
        pltpu.make_async_copy(v.at[batch, 0], out.at[pl.ds(tok_count, tok_count)], sems.at[1]),
    ]
    for copy in copies:
        copy.start()
    for copy in copies:
        copy.wait()


def pack_kernel(members, cap, columns, places, *rest):
    blocks, out = (rest[:-1], rest[-1])
    out[...] = picked_rows(members, cap, columns, places, blocks)


def expert_rows(rows, weights, active, stores):
    gate, up, down = weights
    inner, width = down.shape[1:]
    x = rows[...]
    for begin in range(0, inner, 256):
        span = slice(begin, min(inner, begin + 256))
        gate_part = jnp.dot(x, gate[0, :, span], preferred_element_type=f32)
        up_part = jnp.dot(x, up[0, :, span], preferred_element_type=f32)
        active[:, span] = (jax.nn.gelu(gate_part, approximate=True) * up_part).astype(bf16)
    for begin in range(0, width, 256):
        span = slice(begin, begin + 256)
        part = jnp.dot(active[...], down[0, :, span], preferred_element_type=f32)
        stores(span, part.astype(bf16))


def near_kernel(
    batch, experts, cap, new_table, old_table, places, router_t, *rest
):
    columns = experts // 2
    blocks, rest = (rest[:columns], rest[columns:])
    routes, rest = (rest[:columns], rest[columns:])
    weights, (out, gates_out, rows, active) = (rest[:3], rest[3:])

    def stores(span, value):
        out[:, span] = value

    rows[...] = picked_rows(range(columns), cap, 0, places, blocks)
    chosen, holders = column_routes(batch, experts, routes, new_table, old_table)
    me = lax.axis_index("exp")
    firsts = []
    for m in range(columns):
        logits = lax.dot_general(router_t[...], blocks[m][...], NT, preferred_element_type=f32)
        expert = iota(logits.shape, 0)
        picked = [
            jnp.sum(jnp.where(expert == chosen[c][m], logits, 0.0), axis=0, keepdims=True)
            for c in range(2)
        ]
        firsts.append(jax.nn.sigmoid(picked[0] - picked[1]))
    first = jnp.concatenate(firsts, axis=0)
    gates_out[...] = jnp.concatenate(
        [
            jnp.where(holders[0] == at, first, 0.0) + jnp.where(holders[1] == at, 1.0 - first, 0.0)
            for at in (me, me ^ 1)
        ],
        axis=0,
    )
    expert_rows(rows, weights, active, stores)


def far_kernel(low_in, high_in, *rest):
    weights, (low_out, high_out, rows, active) = (rest[:3], rest[3:])
    part = low_in.shape[0]

    def stores(span, value):
        low_out[:, span] = value[:part]
        high_out[:, span] = value[part:]

    rows[:part, :] = low_in[...]
    rows[part:, :] = high_in[...]
    expert_rows(rows, weights, active, stores)


def partial_kernel(members, cap, columns, places, gates, near, far, *outs):
    tok_count = places.shape[1]
    for n, m in enumerate(members):
        total = None
        for source, row, base in ((near, m, m * cap), (far, columns + m, n * cap)):
            at = iota((source.shape[0], tok_count), 0)
            place = places[row : row + 1, :]
            place = jnp.where(place >= 0, place + base, -1)
            spread = jnp.where(at == place, gates[row : row + 1, :], 0.0)
            coarse = spread.astype(bf16)
            fine = (spread - coarse.astype(f32)).astype(bf16)
            for half in (coarse, fine):
                term = lax.dot_general(half, source[...], TN, preferred_element_type=f32)
                total = term if total is None else total + term
        outs[n][...] = total.astype(outs[n].dtype)


def fold_kernel(own, *rest):
    total = own[...]
    for ref in rest[:-1]:
        total = total + ref[...].astype(f32)
    rest[-1][...] = total.astype(rest[-1].dtype)


def final_kernel(counts, *refs):
    out = refs[-1]
    at = 0
    for batch, count in enumerate(counts):
        total = refs[at][...]
        for ref in refs[at + 1 : at + count]:
            total = total + ref[...].astype(f32)
        at += count
        out[batch, 0] = total.astype(bf16)


def local(
    tokens, queries, key_rows, value_rows, segments, bias_table, out_proj, router,
    gate_weight, up_weight, down_weight, old_table, new_table, routes_one, routes_two,
):
    tok_count, width = tokens.shape[2:]
    heads = bias_table.shape[0]
    experts = router.shape[1]
    columns = experts // 2
    inner = gate_weight.shape[2]
    seq_size = lax.axis_size("seq")
    seq_len = tok_count * seq_size
    capacity = tok_count * 2 * 5 // (4 * experts)
    longest = seq_len // 2
    hops = min(WIN_BLOCKS, (longest - 1 + tok_count - 1) // tok_count)
    relayed = seq_size == 4 and hops == 2
    sinks = seq_len > WIN_BLOCKS * tok_count
    weights = (gate_weight, up_weight, down_weight)
    router_t = router.T
    lower, upper = (range(columns // 2), range(columns // 2, columns))
    rows_bf16 = shaped((tok_count, width), bf16)
    rows_f32 = shaped((tok_count, width), f32)
    caps = (capacity, capacity * MAX_SLOTS)
    latest = []

    def call(kernel, outs, ins, args, flops=10**7, moved=10**6, scratch=(), limit=24):
        args = list(args)
        if latest:
            args[-1] = behind(args[-1], latest[0])
        made = pl.pallas_call(
            kernel,
            out_shape=outs,
            in_specs=ins,
            out_specs=jax.tree.map(lambda _: VMEM, outs),
            scratch_shapes=list(scratch),
            compiler_params=pltpu.CompilerParams(vmem_limit_bytes=limit * 2**20),
            cost_estimate=pl.CostEstimate(flops=flops, bytes_accessed=moved, transcendentals=0),
        )(*args)
        latest[:] = jax.tree.leaves(made)[:1]
        return made

    def multicast(own, order=None):
        blocks = {0: own}
        bit = columns // 2
        while bit:
            for m in sorted(blocks):
                blocks[m | bit] = swapped(blocks[m], "exp", 2 * bit)
            bit //= 2
        return blocks

    def stack(batch):
        return call(
            functools.partial(stack_kernel, batch), shaped((2 * tok_count, width), bf16),
            [ANY] * 2, (key_rows, value_rows), scratch=[pltpu.SemaphoreType.DMA((2,))],
        )

    def exchange(moving, before_relay):
        if not relayed:
            moved = []
            for _ in range(hops):
                moving = passed_along(moving, "seq", 1)
                moved.append(moving)
            return moved
        across = swapped(moving, "seq", 2)
        pairwise = swapped(moving, "seq", 1)
        return [pairwise, across, swapped(behind(across, *before_relay), "seq", 1)]

    def attend(batch, moved):
        extra = []
        if sinks:
            extra = latest_start(key_rows[batch, 0], value_rows[batch, 0], segments[batch, 0])
        return call(
            functools.partial(attend_kernel, batch, hops, relayed, heads, experts, sinks),
            (rows_f32, rows_bf16, shaped((2 * columns, tok_count), jnp.int32)),
            [SMEM] * 3 + [VMEM] * (4 + len(moved)) + ([VMEM, SMEM] if sinks else [])
            + [VMEM] * (2 + columns),
            (bias_table, new_table, old_table, segs, queries, key_rows, value_rows, *moved,
             *extra, *routes, tokens, out_proj),
            flops=10**9, moved=8 * 10**6, scratch=[pltpu.VMEM((tok_count, width), bf16)],
        )

    def pack(batch, members, places, blocks):
        cap = caps[batch]
        return call(
            functools.partial(pack_kernel, members, cap, columns),
            shaped((columns // 2 * cap, width), bf16),
            [VMEM] * (1 + len(members)),
            (places, *(blocks[m] for m in members)),
        )

    def scratch_for(slots):
        return (pltpu.VMEM((slots, width), bf16), pltpu.VMEM((slots, inner), bf16))

    def near_rows(batch, places, blocks):
        slots = columns * caps[batch]
        return call(
            functools.partial(near_kernel, batch, experts, caps[batch]),
            (shaped((slots, width), bf16), shaped((2 * columns, tok_count), f32)),
            [SMEM] * 2 + [VMEM] * (5 + 2 * columns),
            (new_table, old_table, places, router_t, *(blocks[m] for m in range(columns)),
             *routes, *weights),
            flops=6 * slots * width * inner, moved=10**7, scratch=scratch_for(slots),
        )

    def far_rows(batch, low_in, high_in):
        slots = columns * caps[batch]
        return call(
            far_kernel,
            (shaped((slots // 2, width), bf16),) * 2,
            [VMEM] * 5,
            (low_in, high_in, *weights),
            flops=6 * slots * width * inner, moved=10**7, scratch=scratch_for(slots),
        )

    def partial(batch, members, places, gates, near, far):
        return dict(zip(members, call(
            functools.partial(partial_kernel, members, caps[batch], columns),
            tuple(rows_bf16 if m % 2 else rows_f32 for m in members),
            [VMEM] * 4,
            (places, gates, near, far),
        )))

    def fold(parts):
        return call(fold_kernel, rows_bf16, [VMEM] * len(parts), parts)

    stacked = stack(1)
    segs = lax.all_gather(segments[:, 0], "seq", tiled=True)
    routes = multicast(jnp.concatenate([routes_one[0].T, routes_two[0].T]))
    routes = [routes[m] for m in range(columns)]
    moved_two = exchange(stacked, (segs, *routes))
    moved_one = exchange(stack(0) if not relayed else behind(stack(0), moved_two[2]), ())
    hidden_two, normed_two, places_two = attend(1, moved_two)
    blocks_two = multicast(normed_two)
    hidden_one, normed_one, places_one = attend(0, moved_one)
    blocks_one = multicast(behind(normed_one, blocks_two[columns // 2]))
    low_two = swapped(pack(1, lower, places_two, blocks_two), "exp", 1)
    high_two = swapped(pack(1, upper, places_two, blocks_two), "exp", 1)
    near_two, gates_two = near_rows(1, places_two, blocks_two)
    low_one = swapped(pack(0, lower, places_one, blocks_one), "exp", 1)
    far_two = far_rows(1, low_two, high_two)
    back_high_two = swapped(far_two[1], "exp", 1)
    high_one = swapped(pack(0, upper, places_one, blocks_one), "exp", 1)
    near_one, gates_one = near_rows(0, places_one, blocks_one)
    far_one = far_rows(0, low_one, high_one)
    back_high_one = swapped(far_one[1], "exp", 1)
    back_low_two = swapped(behind(far_two[0], far_one[1]), "exp", 1)
    back_low_one = swapped(far_one[0], "exp", 1)
    sums_two = partial(1, upper, places_two, gates_two, near_two, back_high_two)
    sums_one = partial(0, upper, places_one, gates_one, near_one, back_high_one)
    totals = {1: {m: [sums_two[m]] for m in upper}, 0: {m: [sums_one[m]] for m in upper}}

    def send_down(batch, members):
        for m in members:
            parts = totals[batch][m]
            value = parts[0] if len(parts) == 1 else fold(parts)
            totals[batch].setdefault(m & (m - 1), []).append(swapped(value, "exp", 2 * (m & -m)))

    def in_turn(members):
        return sorted(members, key=lambda m: (m & -m, -m))

    send_down(1, in_turn(m for m in upper if m % 2))
    send_down(0, in_turn(m for m in upper if m % 2))
    send_down(1, in_turn(m for m in upper if m % 2 == 0))
    sums_two = partial(1, lower, places_two, gates_two, near_two, back_low_two)
    for m in lower:
        totals[1].setdefault(m, []).insert(0, sums_two[m])
    send_down(1, in_turn(m for m in lower if m))
    send_down(0, in_turn(m for m in upper if m % 2 == 0))
    sums_one = partial(0, lower, places_one, gates_one, near_one, back_low_one)
    for m in lower:
        totals[0].setdefault(m, []).insert(0, sums_one[m])
    send_down(0, in_turn(m for m in lower if m))
    ends = ([hidden_one, *totals[0][0]], [hidden_two, *totals[1][0]])
    return call(
        functools.partial(final_kernel, [len(ends[0]), len(ends[1])]),
        shaped((2, 1, tok_count, width), bf16),
        [VMEM] * (len(ends[0]) + len(ends[1])),
        (*ends[0], *ends[1]),
    )


def solution(mesh):
    rows = P(None, "exp", "seq", None)
    placed = (
        rows, rows, rows, rows, P(None, "exp", "seq"), P(), P(), P(),
        P("exp", None, None), P("exp", None, None), P("exp", None, None), P(), P(),
        P("exp", "seq", None), P("exp", "seq", None),
    )
    return jax.shard_map(local, mesh=mesh, in_specs=placed, out_specs=rows, check_vma=False)
```

```python
import functools

import jax
import jax.numpy as jnp
from jax import lax
from jax.experimental import pallas as pl
from jax.experimental.pallas import tpu as pltpu
from jax.sharding import PartitionSpec as P

WIN_BLOCKS = 4
NBUCK = 32
MAX_SLOTS = 2

score_scale = 0.125
epsilon = 1e-06
masked_score = -1e30

f32 = jnp.float32
bf16 = jnp.bfloat16
NT = (((1,), (1,)), ((), ()))
TN = (((0,), (0,)), ((), ()))
VMEM = pl.BlockSpec(memory_space=pltpu.VMEM)
SMEM = pl.BlockSpec(memory_space=pltpu.SMEM)


def iota(shape, dim):
    return lax.broadcasted_iota(jnp.int32, shape, dim)


def shaped(shape, dtype):
    return jax.ShapeDtypeStruct(shape, dtype)


def passed_along(value, axis, steps):
    count = lax.axis_size(axis)
    return lax.ppermute(value, axis, [(source, source + steps) for source in range(count - steps)])


def swapped(value, axis, mask):
    count = lax.axis_size(axis)
    return lax.ppermute(value, axis, [(source, source ^ mask) for source in range(count)])


def behind(value, *earlier):
    return lax.optimization_barrier((value, *earlier))[0]


def merge_starts(former, latter):
    take_latter = (latter[4] > 0) & ((former[4] == 0) | (latter[3] != former[3]))
    return tuple((jnp.where(take_latter, newer, older) for older, newer in zip(former, latter)))


def latest_start(key_rows, value_rows, segments):
    tok_count, model_width = key_rows.shape
    length, index = (lax.axis_size("seq"), lax.axis_index("seq"))
    last_seg = segments[tok_count - 1]
    lead = jnp.sum((segments < last_seg).astype(jnp.int32))
    one = jnp.ones((), jnp.int32)
    found = (key_rows[lead], value_rows[lead], index * tok_count + lead, last_seg, one)
    everything = jax.tree.map(lambda part: lax.all_gather(part, "seq"), found)
    start = jax.tree.map(jnp.zeros_like, found)

    def lap(k, before):
        new = merge_starts(before, jax.tree.map(lambda part: part[k], everything))
        return jax.tree.map(lambda a, b: jnp.where(k < index, a, b), new, before)

    sink_key, sink_value, sink_pos, sink_seg, sink_has = lax.fori_loop(0, length, lap, start)
    block = jnp.zeros((2 * tok_count, model_width), key_rows.dtype)
    block = block.at[0].set(sink_key).at[tok_count].set(sink_value)
    return (block, jnp.stack([sink_pos, sink_seg, sink_has]))


def column_routes(batch, experts, routes, new_table, old_table):
    chosen, holders = ([[], []], [[], []])
    for ref in routes:
        for c in range(2):
            pick = ref[2 * batch + c : 2 * batch + c + 1, :]
            if batch:
                pick = sum(jnp.where(pick == s, new_table[s], 0) for s in range(experts))
            chosen[c].append(pick)
            holders[c].append(sum(jnp.where(pick == old_table[x], x, 0) for x in range(experts)))
    return (chosen, [jnp.concatenate(rows, axis=0) for rows in holders])


def attend_kernel(
    batch, hops, relayed, heads, experts, sinks,
    bias, new_table, old_table, segs, q, k, v, *rest,
):
    count = 3 if relayed else hops
    moved, rest = (rest[:count], rest[count:])
    if sinks:
        sink_block, sink_info, rest = (rest[0], rest[1], rest[2:])
    routes, rest = (rest[: experts // 2], rest[experts // 2 :])
    tokens, proj, hidden_out, normed_out, places_out, context = rest
    tok_count, width = tokens.shape[2:]
    window = WIN_BLOCKS * tok_count
    index, me = (lax.axis_index("seq"), lax.axis_index("exp"))
    grid = (tok_count, tok_count)

    def sent_seg(ref):
        return ref[2 * tok_count : 2 * tok_count + 1, :tok_count].astype(f32)

    own_seg = segs[batch].astype(f32)
    key_segs = [own_seg]
    if relayed:
        pairwise, across, relay = moved
        paired = index % 2 == 1
        key_segs += [jnp.where(paired, sent_seg(pairwise), sent_seg(relay)), sent_seg(across)]
    else:
        key_segs += [sent_seg(ref) for ref in moved]
    seg_col = jnp.broadcast_to(own_seg, grid).T
    visible, spans = ([], [])
    for j, key_seg in enumerate(key_segs):
        key_seg = jnp.where(index >= j, key_seg, -1.0)
        distance = iota(grid, 0) - iota(grid, 1) + tok_count * j
        seen = (seg_col == key_seg) & (distance >= 0) & (distance < window)
        visible.append(jnp.where(seen, 0.0, masked_score))
        low, high = (max(0, tok_count * (j - 1) + 1), min(window, tok_count * (j + 1)) - 1)
        spans.append((distance, low.bit_length(), high.bit_length()))
    if sinks:
        position = index * tok_count + iota(grid, 0)
        seen = (seg_col == sink_info[1].astype(f32)) & (sink_info[2] > 0) & (position - sink_info[0] >= window)
        visible.append(jnp.where(seen & (iota(grid, 1) == 0), 0.0, masked_score))
        spans.append((None, NBUCK - 1, NBUCK - 1))
    lane = iota((tok_count, 128), 1)
    half = width // heads
    keys_at, values_at = (slice(0, tok_count), slice(tok_count, 2 * tok_count))
    for pair in range(heads // 2):
        cols = slice(128 * pair, 128 * pair + 128)
        both = q[batch, 0, :, cols] * score_scale
        even = jnp.where(lane < half, both, jnp.zeros_like(both))
        odd = jnp.where(lane < half, jnp.zeros_like(both), both)
        stacked = jnp.concatenate([even, odd], axis=0)
        blocks = [(k[batch, 0, :, cols], v[batch, 0, :, cols])]
        if relayed:
            blocks.append(tuple(
                jnp.where(paired, pairwise[at, cols], relay[at, cols])
                for at in (keys_at, values_at)
            ))
            blocks.append((across[keys_at, cols], across[values_at, cols]))
        else:
            for ref in moved:
                blocks.append((ref[keys_at, cols], ref[values_at, cols]))
        if sinks:
            blocks.append((sink_block[keys_at, cols], sink_block[values_at, cols]))
        scores = []
        for (keys, _), (distance, low, high), seen in zip(blocks, spans, visible):
            score = lax.dot_general(stacked, keys, NT, preferred_element_type=f32)
            parts = []
            for side in range(2):
                head = 2 * pair + side
                offset = jnp.full(grid, bias[head, low], f32)
                for bucket in range(low + 1, high + 1):
                    offset = jnp.where(distance >= 1 << (bucket - 1), bias[head, bucket], offset)
                parts.append(score[side * tok_count : (side + 1) * tok_count] + (offset + seen))
            scores.append(jnp.concatenate(parts, axis=0))
        peak = jnp.max(functools.reduce(jnp.maximum, scores), axis=1, keepdims=True)
        weights = [jnp.exp(score - peak) for score in scores]
        total = jnp.sum(functools.reduce(jnp.add, weights), axis=1, keepdims=True)
        scale = 1.0 / total
        mixed = sum(
            jnp.dot((weight * scale).astype(bf16), values, preferred_element_type=f32)
            for weight, (_, values) in zip(weights, blocks)
        )
        context[:, cols] = jnp.where(lane < half, mixed[:tok_count], mixed[tok_count:]).astype(bf16)
    hidden = tokens[batch, 0].astype(f32) + jnp.dot(
        context[...], proj[...], preferred_element_type=f32
    )
    hidden_out[...] = hidden
    mean = jnp.mean(hidden * hidden, axis=1, keepdims=True)
    normed_out[...] = (hidden * lax.rsqrt(mean + epsilon)).astype(bf16)
    _, holders = column_routes(batch, experts, routes, new_table, old_table)
    member = jnp.concatenate(
        [jnp.where((holders[0] == at) | (holders[1] == at), 1.0, 0.0) for at in (me, me ^ 1)],
        axis=0,
    )
    earlier = jnp.where(iota(grid, 0) < iota(grid, 1), 1.0, 0.0).astype(bf16)
    rank = jnp.dot(member.astype(bf16), earlier, preferred_element_type=f32)
    places_out[...] = jnp.where(member > 0.5, rank.astype(jnp.int32), -1)


def picked_rows(members, cap, first_row, places, blocks):
    tok_count = blocks[0].shape[0]
    at = iota((len(members) * cap, tok_count), 0)
    plans = []
    for n, m in enumerate(members):
        place = places[first_row + m : first_row + m + 1, :]
        place = jnp.where(place >= 0, place + n * cap, -1)
        plans.append(jnp.where(at == place, 1.0, 0.0).astype(bf16))
    plan = jnp.concatenate(plans, axis=1)
    rows = jnp.concatenate([block[...] for block in blocks], axis=0)
    return jnp.dot(plan, rows, preferred_element_type=f32).astype(bf16)


def pack_kernel(members, cap, columns, places, *rest):
    blocks, out = (rest[:-1], rest[-1])
    out[...] = picked_rows(members, cap, columns, places, blocks)


def expert_rows(rows, weights, active, stores):
    gate, up, down = weights
    inner, width = down.shape[1:]
    x = rows[...]
    for begin in range(0, inner, 256):
        span = slice(begin, min(inner, begin + 256))
        gate_part = jnp.dot(x, gate[0, :, span], preferred_element_type=f32)
        up_part = jnp.dot(x, up[0, :, span], preferred_element_type=f32)
        active[:, span] = (jax.nn.gelu(gate_part, approximate=True) * up_part).astype(bf16)
    for begin in range(0, width, 256):
        span = slice(begin, begin + 256)
        part = jnp.dot(active[...], down[0, :, span], preferred_element_type=f32)
        stores(span, part.astype(bf16))


def near_kernel(
    batch, experts, cap, new_table, old_table, places, router_t, *rest
):
    columns = experts // 2
    blocks, rest = (rest[:columns], rest[columns:])
    routes, rest = (rest[:columns], rest[columns:])
    weights, (out, gates_out, rows, active) = (rest[:3], rest[3:])

    def stores(span, value):
        out[:, span] = value

    rows[...] = picked_rows(range(columns), cap, 0, places, blocks)
    chosen, holders = column_routes(batch, experts, routes, new_table, old_table)
    me = lax.axis_index("exp")
    firsts = []
    for m in range(columns):
        logits = lax.dot_general(router_t[...], blocks[m][...], NT, preferred_element_type=f32)
        expert = iota(logits.shape, 0)
        picked = [
            jnp.sum(jnp.where(expert == chosen[c][m], logits, 0.0), axis=0, keepdims=True)
            for c in range(2)
        ]
        firsts.append(jax.nn.sigmoid(picked[0] - picked[1]))
    first = jnp.concatenate(firsts, axis=0)
    gates_out[...] = jnp.concatenate(
        [
            jnp.where(holders[0] == at, first, 0.0) + jnp.where(holders[1] == at, 1.0 - first, 0.0)
            for at in (me, me ^ 1)
        ],
        axis=0,
    )
    expert_rows(rows, weights, active, stores)


def far_kernel(low_in, high_in, *rest):
    weights, (low_out, high_out, rows, active) = (rest[:3], rest[3:])
    part = low_in.shape[0]

    def stores(span, value):
        low_out[:, span] = value[:part]
        high_out[:, span] = value[part:]

    rows[:part, :] = low_in[...]
    rows[part:, :] = high_in[...]
    expert_rows(rows, weights, active, stores)


def partial_kernel(members, cap, columns, places, gates, near, far, *outs):
    tok_count = places.shape[1]
    for n, m in enumerate(members):
        total = None
        for source, row, base in ((near, m, m * cap), (far, columns + m, n * cap)):
            at = iota((source.shape[0], tok_count), 0)
            place = places[row : row + 1, :]
            place = jnp.where(place >= 0, place + base, -1)
            spread = jnp.where(at == place, gates[row : row + 1, :], 0.0)
            coarse = spread.astype(bf16)
            fine = (spread - coarse.astype(f32)).astype(bf16)
            for half in (coarse, fine):
                term = lax.dot_general(half, source[...], TN, preferred_element_type=f32)
                total = term if total is None else total + term
        outs[n][...] = total.astype(outs[n].dtype)


def fold_kernel(own, *rest):
    total = own[...]
    for ref in rest[:-1]:
        total = total + ref[...].astype(f32)
    rest[-1][...] = total.astype(rest[-1].dtype)


def final_kernel(counts, *refs):
    out = refs[-1]
    at = 0
    for batch, count in enumerate(counts):
        total = refs[at][...]
        for ref in refs[at + 1 : at + count]:
            total = total + ref[...].astype(f32)
        at += count
        out[batch, 0] = total.astype(bf16)


def local(
    tokens, queries, key_rows, value_rows, segments, bias_table, out_proj, router,
    gate_weight, up_weight, down_weight, old_table, new_table, routes_one, routes_two,
):
    tok_count, width = tokens.shape[2:]
    heads = bias_table.shape[0]
    experts = router.shape[1]
    columns = experts // 2
    inner = gate_weight.shape[2]
    seq_size = lax.axis_size("seq")
    seq_len = tok_count * seq_size
    capacity = tok_count * 2 * 5 // (4 * experts)
    longest = seq_len // 2
    hops = min(WIN_BLOCKS, (longest - 1 + tok_count - 1) // tok_count)
    relayed = seq_size == 4 and hops == 2
    sinks = seq_len > WIN_BLOCKS * tok_count
    weights = (gate_weight, up_weight, down_weight)
    router_t = router.T
    lower, upper = (range(columns // 2), range(columns // 2, columns))
    rows_bf16 = shaped((tok_count, width), bf16)
    rows_f32 = shaped((tok_count, width), f32)
    caps = (capacity, capacity * MAX_SLOTS)
    latest, attended = ([], [])

    def call(kernel, outs, ins, args, flops=10**7, moved=10**6, scratch=(), limit=24):
        args = list(args)
        if latest:
            args[-1] = behind(args[-1], latest[0])
        made = pl.pallas_call(
            kernel,
            out_shape=outs,
            in_specs=ins,
            out_specs=jax.tree.map(lambda _: VMEM, outs),
            scratch_shapes=list(scratch),
            compiler_params=pltpu.CompilerParams(vmem_limit_bytes=limit * 2**20),
            cost_estimate=pl.CostEstimate(flops=flops, bytes_accessed=moved, transcendentals=0),
        )(*args)
        latest[:] = jax.tree.leaves(made)[:1]
        return made

    def multicast(own, meanwhile=None):
        blocks = {0: own}
        bit = columns // 2
        while bit:
            for m in sorted(blocks):
                if m == columns // 2 and meanwhile is not None:
                    attended[:] = [meanwhile()]
                    blocks[m] = behind(blocks[m], attended[0][1])
                    meanwhile = None
                blocks[m | bit] = swapped(blocks[m], "exp", 2 * bit)
            bit //= 2
        return blocks

    def stack(batch, keys, values):
        segs = jnp.pad(segments[batch].astype(bf16), ((0, 15), (0, width - tok_count)))
        return jnp.concatenate([keys[batch, 0], values[batch, 0], segs], axis=0)

    def exchange(moving, before_relay=None):
        if not relayed:
            moved = []
            for _ in range(hops):
                moving = passed_along(moving, "seq", 1)
                moved.append(moving)
            return moved
        across = swapped(moving, "seq", 2)
        pairwise = swapped(moving, "seq", 1)
        if before_relay is not None:
            return [pairwise, across, swapped(behind(across, *before_relay), "seq", 1)]
        return [pairwise, across, lax.ppermute(moving, "seq", [(0, 0), (1, 2), (2, 1), (3, 3)])]

    def attend(batch, moved):
        extra = []
        if sinks:
            extra = latest_start(key_rows[batch, 0], value_rows[batch, 0], segments[batch, 0])
        return call(
            functools.partial(attend_kernel, batch, hops, relayed, heads, experts, sinks),
            (rows_f32, rows_bf16, shaped((2 * columns, tok_count), jnp.int32)),
            [SMEM] * 3 + [VMEM] * (4 + len(moved)) + ([VMEM, SMEM] if sinks else [])
            + [VMEM] * (2 + columns),
            (bias_table, new_table, old_table, segments, queries, key_rows, value_rows, *moved,
             *extra, *routes, tokens, out_proj),
            flops=10**9, moved=8 * 10**6, scratch=[pltpu.VMEM((tok_count, width), bf16)],
        )

    def pack(batch, members, places, blocks):
        cap = caps[batch]
        return call(
            functools.partial(pack_kernel, members, cap, columns),
            shaped((columns // 2 * cap, width), bf16),
            [VMEM] * (1 + len(members)),
            (places, *(blocks[m] for m in members)),
        )

    def scratch_for(slots):
        return (pltpu.VMEM((slots, width), bf16), pltpu.VMEM((slots, inner), bf16))

    def near_rows(batch, places, blocks):
        slots = columns * caps[batch]
        return call(
            functools.partial(near_kernel, batch, experts, caps[batch]),
            (shaped((slots, width), bf16), shaped((2 * columns, tok_count), f32)),
            [SMEM] * 2 + [VMEM] * (5 + 2 * columns),
            (new_table, old_table, places, router_t, *(blocks[m] for m in range(columns)),
             *routes, *weights),
            flops=6 * slots * width * inner, moved=10**7, scratch=scratch_for(slots),
        )

    def far_rows(batch, low_in, high_in):
        slots = columns * caps[batch]
        return call(
            far_kernel,
            (shaped((slots // 2, width), bf16),) * 2,
            [VMEM] * 5,
            (low_in, high_in, *weights),
            flops=6 * slots * width * inner, moved=10**7, scratch=scratch_for(slots),
        )

    def partial(batch, members, places, gates, near, far):
        return dict(zip(members, call(
            functools.partial(partial_kernel, members, caps[batch], columns),
            tuple(rows_bf16 if m % 2 else rows_f32 for m in members),
            [VMEM] * 4,
            (places, gates, near, far),
        )))

    def fold(parts):
        return call(fold_kernel, rows_bf16, [VMEM] * len(parts), parts)

    routes = multicast(jnp.concatenate([routes_one[0].T, routes_two[0].T]))
    routes = [routes[m] for m in range(columns)]
    moved_two = exchange(stack(1, key_rows, value_rows), routes)
    keys, values = (key_rows, value_rows)
    if relayed:
        keys, values, _ = lax.optimization_barrier((key_rows, value_rows, moved_two[0]))
    stacked = stack(0, keys, values)
    moved_one = exchange(behind(stacked, moved_two[min(1, hops - 1)]))
    hidden_two, normed_two, places_two = attend(1, moved_two)
    blocks_two = multicast(normed_two, lambda: attend(0, moved_one))
    hidden_one, normed_one, places_one = attended[0]
    blocks_one = multicast(behind(normed_one, blocks_two[columns // 2]))
    low_two = swapped(pack(1, lower, places_two, blocks_two), "exp", 1)
    high_two = swapped(pack(1, upper, places_two, blocks_two), "exp", 1)
    near_two, gates_two = near_rows(1, places_two, blocks_two)
    low_one = swapped(pack(0, lower, places_one, blocks_one), "exp", 1)
    far_two = far_rows(1, low_two, high_two)
    back_high_two = swapped(far_two[1], "exp", 1)
    high_one = swapped(pack(0, upper, places_one, blocks_one), "exp", 1)
    near_one, gates_one = near_rows(0, places_one, blocks_one)
    far_one = far_rows(0, low_one, high_one)
    back_high_one = swapped(far_one[1], "exp", 1)
    back_low_two = swapped(behind(far_two[0], far_one[1]), "exp", 1)
    back_low_one = swapped(far_one[0], "exp", 1)
    sums_two = partial(1, upper, places_two, gates_two, near_two, back_high_two)
    sums_one = partial(0, upper, places_one, gates_one, near_one, back_high_one)
    totals = {1: {m: [sums_two[m]] for m in upper}, 0: {m: [sums_one[m]] for m in upper}}

    def send_down(batch, members):
        for m in members:
            parts = totals[batch][m]
            value = parts[0] if len(parts) == 1 else fold(parts)
            totals[batch].setdefault(m & (m - 1), []).append(swapped(value, "exp", 2 * (m & -m)))

    def in_turn(members):
        return sorted(members, key=lambda m: (m & -m, -m))

    send_down(1, in_turn(m for m in upper if m % 2))
    send_down(0, in_turn(m for m in upper if m % 2))
    send_down(1, in_turn(m for m in upper if m % 2 == 0))
    sums_two = partial(1, lower, places_two, gates_two, near_two, back_low_two)
    for m in lower:
        totals[1].setdefault(m, []).insert(0, sums_two[m])
    send_down(1, in_turn(m for m in lower if m))
    send_down(0, in_turn(m for m in upper if m % 2 == 0))
    sums_one = partial(0, lower, places_one, gates_one, near_one, back_low_one)
    for m in lower:
        totals[0].setdefault(m, []).insert(0, sums_one[m])
    send_down(0, in_turn(m for m in lower if m))
    ends = ([hidden_one, *totals[0][0]], [hidden_two, *totals[1][0]])
    return call(
        functools.partial(final_kernel, [len(ends[0]), len(ends[1])]),
        shaped((2, 1, tok_count, width), bf16),
        [VMEM] * (len(ends[0]) + len(ends[1])),
        (*ends[0], *ends[1]),
    )


def solution(mesh):
    rows = P(None, "exp", "seq", None)
    placed = (
        rows, rows, rows, rows, P(None, "exp", "seq"), P(), P(), P(),
        P("exp", None, None), P("exp", None, None), P("exp", None, None), P(), P(),
        P("exp", "seq", None), P("exp", "seq", None),
    )
    return jax.shard_map(local, mesh=mesh, in_specs=placed, out_specs=rows, check_vma=False)
```

```python
import functools

import jax
import jax.numpy as jnp
from jax import lax
from jax.experimental import pallas as pl
from jax.experimental.pallas import tpu as pltpu
from jax.sharding import PartitionSpec as P

WIN_BLOCKS = 4
NBUCK = 32
MAX_SLOTS = 2

score_scale = 0.125
epsilon = 1e-06
masked_score = -1e30

f32 = jnp.float32
bf16 = jnp.bfloat16
NT = (((1,), (1,)), ((), ()))
TN = (((0,), (0,)), ((), ()))
VMEM = pl.BlockSpec(memory_space=pltpu.VMEM)
SMEM = pl.BlockSpec(memory_space=pltpu.SMEM)


def iota(shape, dim):
    return lax.broadcasted_iota(jnp.int32, shape, dim)


def shaped(shape, dtype):
    return jax.ShapeDtypeStruct(shape, dtype)


def passed_along(value, axis, steps):
    count = lax.axis_size(axis)
    return lax.ppermute(value, axis, [(source, source + steps) for source in range(count - steps)])


def swapped(value, axis, mask):
    count = lax.axis_size(axis)
    return lax.ppermute(value, axis, [(source, source ^ mask) for source in range(count)])


def behind(value, *earlier):
    return lax.optimization_barrier((value, *earlier))[0]


def merge_starts(former, latter):
    take_latter = (latter[4] > 0) & ((former[4] == 0) | (latter[3] != former[3]))
    return tuple((jnp.where(take_latter, newer, older) for older, newer in zip(former, latter)))


def latest_start(key_rows, value_rows, segments):
    tok_count, model_width = key_rows.shape
    length, index = (lax.axis_size("seq"), lax.axis_index("seq"))
    last_seg = segments[tok_count - 1]
    lead = jnp.sum((segments < last_seg).astype(jnp.int32))
    one = jnp.ones((), jnp.int32)
    found = (key_rows[lead], value_rows[lead], index * tok_count + lead, last_seg, one)
    everything = jax.tree.map(lambda part: lax.all_gather(part, "seq"), found)
    start = jax.tree.map(jnp.zeros_like, found)

    def lap(k, before):
        new = merge_starts(before, jax.tree.map(lambda part: part[k], everything))
        return jax.tree.map(lambda a, b: jnp.where(k < index, a, b), new, before)

    sink_key, sink_value, sink_pos, sink_seg, sink_has = lax.fori_loop(0, length, lap, start)
    block = jnp.zeros((2 * tok_count, model_width), key_rows.dtype)
    block = block.at[0].set(sink_key).at[tok_count].set(sink_value)
    return (block, jnp.stack([sink_pos, sink_seg, sink_has]))


def column_routes(experts, routes, new_table, old_table):
    chosen, holders = ([[], []], [[], []])
    for ref in routes:
        for c in range(2):
            slot = ref[c : c + 1, :]
            pick = sum(jnp.where(slot == s, new_table[s], 0) for s in range(experts))
            chosen[c].append(pick)
            holders[c].append(sum(jnp.where(pick == old_table[x], x, 0) for x in range(experts)))
    return (chosen, [jnp.concatenate(rows, axis=0) for rows in holders])


def attended(batch, hops, relayed, heads, sinks, bias, segs, q, k, v, rest, context):
    count = 3 if relayed else hops
    moved, sent, rest = (rest[:count], rest[count : 2 * count], rest[2 * count :])
    if sinks:
        sink_block, sink_info, rest = (rest[0], rest[1], rest[2:])
    tokens, proj = rest
    tok_count, width = tokens.shape[2:]
    window = WIN_BLOCKS * tok_count
    index = lax.axis_index("seq")
    grid = (tok_count, tok_count)

    own_seg = segs[batch]
    key_segs = [own_seg]
    if relayed:
        pairwise, across, relay = moved
        paired = index % 2 == 1
        key_segs += [jnp.where(paired, sent[0][batch], sent[2][batch]), sent[1][batch]]
    else:
        key_segs += [ref[batch] for ref in sent]
    seg_col = jnp.broadcast_to(own_seg, grid).T
    visible, spans = ([], [])
    for j, key_seg in enumerate(key_segs):
        key_seg = jnp.where(index >= j, key_seg, -1)
        distance = iota(grid, 0) - iota(grid, 1) + tok_count * j
        seen = (seg_col == key_seg) & (distance >= 0) & (distance < window)
        visible.append(jnp.where(seen, 0.0, masked_score))
        low, high = (max(0, tok_count * (j - 1) + 1), min(window, tok_count * (j + 1)) - 1)
        spans.append((distance, low.bit_length(), high.bit_length()))
    if sinks:
        position = index * tok_count + iota(grid, 0)
        seen = (seg_col == sink_info[1]) & (sink_info[2] > 0) & (position - sink_info[0] >= window)
        visible.append(jnp.where(seen & (iota(grid, 1) == 0), 0.0, masked_score))
        spans.append((None, NBUCK - 1, NBUCK - 1))
    lane = iota((tok_count, 128), 1)
    half = width // heads
    keys_at, values_at = (slice(0, tok_count), slice(tok_count, 2 * tok_count))
    for pair in range(heads // 2):
        cols = slice(128 * pair, 128 * pair + 128)
        both = q[batch, 0, :, cols] * score_scale
        even = jnp.where(lane < half, both, jnp.zeros_like(both))
        odd = jnp.where(lane < half, jnp.zeros_like(both), both)
        stacked = jnp.concatenate([even, odd], axis=0)
        blocks = [(k[batch, 0, :, cols], v[batch, 0, :, cols])]
        if relayed:
            blocks.append(tuple(
                jnp.where(paired, pairwise[at, cols], relay[at, cols])
                for at in (keys_at, values_at)
            ))
            blocks.append((across[keys_at, cols], across[values_at, cols]))
        else:
            for ref in moved:
                blocks.append((ref[keys_at, cols], ref[values_at, cols]))
        if sinks:
            blocks.append((sink_block[keys_at, cols], sink_block[values_at, cols]))
        scores = []
        for (keys, _), (distance, low, high), seen in zip(blocks, spans, visible):
            score = lax.dot_general(stacked, keys, NT, preferred_element_type=f32)
            parts = []
            for side in range(2):
                head = 2 * pair + side
                offset = jnp.full(grid, bias[head, low], f32)
                for bucket in range(low + 1, high + 1):
                    offset = jnp.where(distance >= 1 << (bucket - 1), bias[head, bucket], offset)
                parts.append(score[side * tok_count : (side + 1) * tok_count] + (offset + seen))
            scores.append(jnp.concatenate(parts, axis=0))
        peak = jnp.max(functools.reduce(jnp.maximum, scores), axis=1, keepdims=True)
        weights = [jnp.exp(score - peak) for score in scores]
        total = jnp.sum(functools.reduce(jnp.add, weights), axis=1, keepdims=True)
        scale = 1.0 / total
        mixed = sum(
            jnp.dot((weight * scale).astype(bf16), values, preferred_element_type=f32)
            for weight, (_, values) in zip(weights, blocks)
        )
        context[:, cols] = jnp.where(lane < half, mixed[:tok_count], mixed[tok_count:]).astype(bf16)
    hidden = tokens[batch, 0].astype(f32) + jnp.dot(
        context[...], proj[...], preferred_element_type=f32
    )
    mean = jnp.mean(hidden * hidden, axis=1, keepdims=True)
    return (hidden, (hidden * lax.rsqrt(mean + epsilon)).astype(bf16))


def ranks(member):
    grid = (member.shape[1], member.shape[1])
    earlier = jnp.where(iota(grid, 0) < iota(grid, 1), 1.0, 0.0).astype(bf16)
    return jnp.dot(member.astype(bf16), earlier, preferred_element_type=f32).astype(jnp.int32)


def attend_column_kernel(options, experts, bias, new_table, old_table, segs, q, k, v, *rest):
    routes, rest = (rest[: experts // 2], rest[experts // 2 :])
    inputs, (hidden_out, normed_out, places_out, context) = (rest[:-4], rest[-4:])
    hidden, normed = attended(1, *options, bias, segs, q, k, v, inputs, context)
    hidden_out[...] = hidden
    normed_out[...] = normed
    me = lax.axis_index("exp")
    _, holders = column_routes(experts, routes, new_table, old_table)
    member = jnp.concatenate(
        [jnp.where((holders[0] == at) | (holders[1] == at), 1.0, 0.0) for at in (me, me ^ 1)],
        axis=0,
    )
    places_out[...] = jnp.where(member > 0.5, ranks(member), -1)


def attend_direct_kernel(options, experts, cap, bias, old_table, routes, router_t, segs, q, k, v, *rest):
    inputs, rest = (rest[: -4 - experts], rest[-4 - experts :])
    outgoing, (hidden_out, gates_out, rows_out, context) = (rest[:experts], rest[experts:])
    hidden, normed = attended(0, *options, bias, segs, q, k, v, inputs, context)
    hidden_out[...] = hidden
    tok_count = hidden.shape[0]
    chosen = [routes[c : c + 1, :] for c in range(2)]
    holders = [sum(jnp.where(c == old_table[x], x, 0) for x in range(experts)) for c in chosen]
    expert = iota((experts, tok_count), 0)
    packet = expert ^ lax.axis_index("exp")
    member = jnp.where((packet == holders[0]) | (packet == holders[1]), 1.0, 0.0)
    place = ranks(member) + expert * cap
    rows = [
        jnp.sum(jnp.where(packet == holder, place, 0), axis=0, keepdims=True) for holder in holders
    ]
    rows_out[...] = jnp.concatenate(rows, axis=0)
    logits = lax.dot_general(router_t[...], normed, NT, preferred_element_type=f32)
    picked = [jnp.sum(jnp.where(expert == c, logits, 0.0), axis=0, keepdims=True) for c in chosen]
    first = jax.nn.sigmoid(picked[0] - picked[1])
    gates_out[...] = jnp.concatenate([first, 1.0 - first], axis=0)
    at = iota((experts * cap, tok_count), 0)
    plan = jnp.where((at == rows[0]) | (at == rows[1]), 1.0, 0.0).astype(bf16)
    packed = jnp.dot(plan, normed, preferred_element_type=f32)
    for m, ref in enumerate(outgoing):
        ref[...] = packed[m * cap : (m + 1) * cap].astype(bf16)


def picked_rows(members, cap, first_row, places, blocks):
    tok_count = blocks[0].shape[0]
    at = iota((len(members) * cap, tok_count), 0)
    plans = []
    for n, m in enumerate(members):
        place = places[first_row + m : first_row + m + 1, :]
        place = jnp.where(place >= 0, place + n * cap, -1)
        plans.append(jnp.where(at == place, 1.0, 0.0).astype(bf16))
    plan = jnp.concatenate(plans, axis=1)
    rows = jnp.concatenate([block[...] for block in blocks], axis=0)
    return jnp.dot(plan, rows, preferred_element_type=f32).astype(bf16)


def pack_kernel(members, cap, columns, places, *rest):
    blocks, out = (rest[:-1], rest[-1])
    out[...] = picked_rows(members, cap, columns, places, blocks)


def expert_rows(rows, weights, active, stores):
    gate, up, down = weights
    inner, width = down.shape[1:]
    x = rows[...]
    for begin in range(0, inner, 256):
        span = slice(begin, min(inner, begin + 256))
        gate_part = jnp.dot(x, gate[0, :, span], preferred_element_type=f32)
        up_part = jnp.dot(x, up[0, :, span], preferred_element_type=f32)
        active[:, span] = (jax.nn.gelu(gate_part, approximate=True) * up_part).astype(bf16)
    for begin in range(0, width, 256):
        span = slice(begin, begin + 256)
        part = jnp.dot(active[...], down[0, :, span], preferred_element_type=f32)
        stores(span, part)


def near_kernel(experts, cap, new_table, old_table, places, router_t, *rest):
    columns = experts // 2
    blocks, rest = (rest[:columns], rest[columns:])
    routes, rest = (rest[:columns], rest[columns:])
    weights, (out, gates_out, rows, active) = (rest[:3], rest[3:])

    def stores(span, value):
        out[:, span] = value.astype(bf16)

    rows[...] = picked_rows(range(columns), cap, 0, places, blocks)
    chosen, holders = column_routes(experts, routes, new_table, old_table)
    me = lax.axis_index("exp")
    firsts = []
    for m in range(columns):
        logits = lax.dot_general(router_t[...], blocks[m][...], NT, preferred_element_type=f32)
        expert = iota(logits.shape, 0)
        picked = [
            jnp.sum(jnp.where(expert == chosen[c][m], logits, 0.0), axis=0, keepdims=True)
            for c in range(2)
        ]
        firsts.append(jax.nn.sigmoid(picked[0] - picked[1]))
    first = jnp.concatenate(firsts, axis=0)
    gates_out[...] = jnp.concatenate(
        [
            jnp.where(holders[0] == at, first, 0.0) + jnp.where(holders[1] == at, 1.0 - first, 0.0)
            for at in (me, me ^ 1)
        ],
        axis=0,
    )
    expert_rows(rows, weights, active, stores)


def far_kernel(low_in, high_in, *rest):
    weights, (low_out, high_out, rows, active) = (rest[:3], rest[3:])
    part = low_in.shape[0]

    def stores(span, value):
        low_out[:, span] = value[:part].astype(bf16)
        high_out[:, span] = value[part:].astype(bf16)

    rows[:part, :] = low_in[...]
    rows[part:, :] = high_in[...]
    expert_rows(rows, weights, active, stores)


def direct_kernel(*refs):
    count = (len(refs) - 5) // 2
    packets, weights, outs = (refs[:count], refs[count : count + 3], refs[count + 3 : -2])
    rows, active = refs[-2:]
    cap = packets[0].shape[0]

    def stores(span, value):
        for m, out in enumerate(outs):
            out[:, span] = value[m * cap : (m + 1) * cap].astype(bf16)

    rows[...] = jnp.concatenate([ref[...].astype(f32) for ref in packets], axis=0).astype(bf16)
    expert_rows(rows, weights, active, stores)


def combine_kernel(hidden, gates, rows, *rest):
    packets, out = (rest[:-1], rest[-1])
    cap = packets[0].shape[0]
    at = iota((len(packets) * cap, hidden.shape[0]), 0)
    spread = jnp.where(at == rows[0:1, :], gates[0:1, :], 0.0)
    spread = spread + jnp.where(at == rows[1:2, :], gates[1:2, :], 0.0)
    coarse = spread.astype(bf16)
    fine = (spread - coarse.astype(f32)).astype(bf16)
    values = jnp.concatenate([ref[...].astype(f32) for ref in packets], axis=0).astype(bf16)
    total = hidden[...]
    for half in (coarse, fine):
        total = total + lax.dot_general(half, values, TN, preferred_element_type=f32)
    out[...] = total


def partial_kernel(members, cap, columns, places, gates, near, far, *outs):
    tok_count = places.shape[1]
    for n, m in enumerate(members):
        total = None
        for source, row, base in ((near, m, m * cap), (far, columns + m, n * cap)):
            at = iota((source.shape[0], tok_count), 0)
            place = places[row : row + 1, :]
            place = jnp.where(place >= 0, place + base, -1)
            spread = jnp.where(at == place, gates[row : row + 1, :], 0.0)
            coarse = spread.astype(bf16)
            fine = (spread - coarse.astype(f32)).astype(bf16)
            for half in (coarse, fine):
                term = lax.dot_general(half, source[...], TN, preferred_element_type=f32)
                total = term if total is None else total + term
        outs[n][...] = total.astype(outs[n].dtype)


def fold_kernel(own, *rest):
    total = own[...]
    for ref in rest[:-1]:
        total = total + ref[...].astype(f32)
    rest[-1][...] = total.astype(rest[-1].dtype)


def final_kernel(counts, *refs):
    out = refs[-1]
    at = 0
    for batch, count in enumerate(counts):
        total = refs[at][...]
        for ref in refs[at + 1 : at + count]:
            total = total + ref[...].astype(f32)
        at += count
        out[batch, 0] = total.astype(bf16)


def local(
    tokens, queries, key_rows, value_rows, segments, bias_table, out_proj, router,
    gate_weight, up_weight, down_weight, old_table, new_table, routes_one, routes_two,
):
    tok_count, width = tokens.shape[2:]
    heads = bias_table.shape[0]
    experts = router.shape[1]
    columns = experts // 2
    inner = gate_weight.shape[2]
    seq_size = lax.axis_size("seq")
    seq_len = tok_count * seq_size
    capacity = tok_count * 2 * 5 // (4 * experts)
    longest = seq_len // 2
    hops = min(WIN_BLOCKS, (longest - 1 + tok_count - 1) // tok_count)
    relayed = seq_size == 4 and hops == 2
    sinks = seq_len > WIN_BLOCKS * tok_count
    weights = (gate_weight, up_weight, down_weight)
    router_t = router.T
    lower, upper = (range(columns // 2), range(columns // 2, columns))
    rows_bf16 = shaped((tok_count, width), bf16)
    rows_f32 = shaped((tok_count, width), f32)
    cap_two = capacity * MAX_SLOTS
    part_two = columns // 2 * cap_two
    latest = []

    def call(kernel, outs, ins, args, flops=10**7, moved=10**6, scratch=(), limit=24):
        args = list(args)
        if latest:
            args[-1] = behind(args[-1], latest[0])
        made = pl.pallas_call(
            kernel,
            out_shape=outs,
            in_specs=ins,
            out_specs=jax.tree.map(lambda _: VMEM, outs),
            scratch_shapes=list(scratch),
            compiler_params=pltpu.CompilerParams(vmem_limit_bytes=limit * 2**20),
            cost_estimate=pl.CostEstimate(flops=flops, bytes_accessed=moved, transcendentals=0),
        )(*args)
        latest[:] = jax.tree.leaves(made)[:1]
        return made

    def multicast(own):
        blocks = {0: own}
        bit = columns // 2
        while bit:
            for m in sorted(blocks):
                blocks[m | bit] = swapped(blocks[m], "exp", 2 * bit)
            bit //= 2
        return blocks

    def stack(batch, keys, values):
        return jnp.concatenate([keys[batch, 0], values[batch, 0]], axis=0)

    def exchange(moving, *before_relay):
        if not relayed:
            moved = []
            for _ in range(hops):
                moving = passed_along(moving, "seq", 1)
                moved.append(moving)
            return moved
        across = swapped(moving, "seq", 2)
        pairwise = swapped(moving, "seq", 1)
        return [pairwise, across, swapped(behind(across, *before_relay), "seq", 1)]

    def options(batch):
        extra = []
        if sinks:
            extra = latest_start(key_rows[batch, 0], value_rows[batch, 0], segments[batch, 0])
        return ((hops, relayed, heads, sinks), extra)

    def attend_column(moved):
        settings, extra = options(1)
        return call(
            functools.partial(attend_column_kernel, settings, experts),
            (rows_f32, rows_bf16, shaped((2 * columns, tok_count), jnp.int32)),
            [SMEM] * 3 + [VMEM] * (4 + columns + 2 * len(moved)) + ([VMEM, SMEM] if sinks else [])
            + [VMEM] * 2,
            (bias_table, new_table, old_table, segments, queries, key_rows, value_rows, *routes,
             *moved, *sent, *extra, tokens, out_proj),
            flops=10**9, moved=8 * 10**6, scratch=[pltpu.VMEM((tok_count, width), bf16)],
        )

    def attend_direct(moved, after):
        settings, extra = options(0)
        return call(
            functools.partial(attend_direct_kernel, settings, experts, capacity),
            (*[shaped((capacity, width), bf16)] * experts, rows_f32, shaped((2, tok_count), f32),
             shaped((2, tok_count), jnp.int32)),
            [SMEM] * 2 + [VMEM] * (6 + 2 * len(moved)) + ([VMEM, SMEM] if sinks else [])
            + [VMEM] * 2,
            (bias_table, old_table, routes_one[0].T, router_t, segments, queries, key_rows,
             value_rows, *moved, *sent, *extra, behind(tokens, after), out_proj),
            flops=10**9, moved=8 * 10**6, scratch=[pltpu.VMEM((tok_count, width), bf16)],
        )

    def scratch_for(slots):
        return (pltpu.VMEM((slots, width), bf16), pltpu.VMEM((slots, inner), bf16))

    def pack(members, places, blocks):
        return call(
            functools.partial(pack_kernel, members, cap_two, columns),
            shaped((part_two, width), bf16),
            [VMEM] * (1 + len(members)),
            (places, *(blocks[m] for m in members)),
        )

    def partial(members, far):
        parts = call(
            functools.partial(partial_kernel, members, cap_two, columns),
            tuple(rows_bf16 if m % 2 else rows_f32 for m in members),
            [VMEM] * 4,
            (places, gates_two, near, far),
        )
        for m, value in zip(members, parts):
            totals.setdefault(m, []).insert(0, value)

    def send_down(members):
        for m in sorted(members, key=lambda m: (m & -m, -m)):
            parts = totals[m]
            value = parts[0]
            if len(parts) > 1:
                value = call(fold_kernel, rows_bf16, [VMEM] * len(parts), parts)
            totals.setdefault(m & (m - 1), []).append(swapped(value, "exp", 2 * (m & -m)))

    routes = multicast(routes_two[0].T)
    routes = [routes[m] for m in range(columns)]
    if relayed:
        sent = [swapped(segments[:, 0], "seq", mask) for mask in (1, 2, 3)]
    else:
        sent = []
        for _ in range(hops):
            sent.append(passed_along(sent[-1] if sent else segments[:, 0], "seq", 1))
    sent = [each[:, None] for each in sent]

    moved_two = exchange(stack(1, key_rows, value_rows), *routes, *sent)
    keys, values = (key_rows, value_rows)
    if relayed:
        keys, values, _ = lax.optimization_barrier((key_rows, value_rows, moved_two[0]))
    stacked = stack(0, keys, values)
    hidden_two, normed_two, places = attend_column(moved_two)
    blocks = multicast(normed_two)
    moved_one = exchange(behind(stacked, normed_two), blocks[columns // 2])
    low_in = swapped(pack(lower, places, blocks), "exp", 1)
    *packets, hidden_one, gates_one, rows_one = attend_direct(moved_one, blocks[columns // 2])
    arrived = [packets[0]] + [None] * (experts - 1)
    for m in range(experts - 1, 0, -1):
        arrived[m] = swapped(packets[m], "exp", m)
    high_in = swapped(pack(upper, places, blocks), "exp", 1)
    slots = columns * cap_two
    near, gates_two = call(
        functools.partial(near_kernel, experts, cap_two),
        (shaped((slots, width), bf16), shaped((2 * columns, tok_count), f32)),
        [SMEM] * 2 + [VMEM] * (5 + 2 * columns),
        (new_table, old_table, places, router_t, *(blocks[m] for m in range(columns)), *routes,
         *weights),
        flops=6 * slots * width * inner, moved=10**7, scratch=scratch_for(slots),
    )
    low_out, high_out = call(
        far_kernel,
        (shaped((part_two, width), bf16),) * 2,
        [VMEM] * 5,
        (low_in, high_in, *weights),
        flops=6 * slots * width * inner, moved=10**7, scratch=scratch_for(slots),
    )
    high_far, low_far = (swapped(high_out, "exp", 1), swapped(low_out, "exp", 1))
    answers = call(
        direct_kernel,
        (shaped((capacity, width), bf16),) * experts,
        [VMEM] * (3 + experts),
        (*arrived, *weights),
        flops=6 * experts * capacity * width * inner, moved=10**7,
        scratch=scratch_for(experts * capacity),
    )
    returned = [answers[0]] + [None] * (experts - 1)
    for m in range(experts - 1, 0, -1):
        returned[m] = swapped(answers[m], "exp", m)
    totals = {}
    partial(upper, high_far)
    send_down(m for m in upper if m % 2)
    partial(lower, low_far)
    send_down(m for m in upper if m % 2 == 0)
    send_down(m for m in lower if m)
    sum_one = call(
        combine_kernel, rows_f32, [VMEM] * (3 + experts), (hidden_one, gates_one, rows_one, *returned)
    )
    ends = (sum_one, hidden_two, *totals[0])
    return call(
        functools.partial(final_kernel, [1, len(ends) - 1]),
        shaped((2, 1, tok_count, width), bf16),
        [VMEM] * len(ends),
        ends,
    )


def solution(mesh):
    rows = P(None, "exp", "seq", None)
    placed = (
        rows, rows, rows, rows, P(None, "exp", "seq"), P(), P(), P(),
        P("exp", None, None), P("exp", None, None), P("exp", None, None), P(), P(),
        P("exp", "seq", None), P("exp", "seq", None),
    )
    return jax.shard_map(local, mesh=mesh, in_specs=placed, out_specs=rows, check_vma=False)
```

```python
import functools

import jax
import jax.numpy as jnp
from jax import lax
from jax.experimental import pallas as pl
from jax.experimental.pallas import tpu as pltpu
from jax.sharding import PartitionSpec as P

WIN_BLOCKS = 4
NBUCK = 32
MAX_SLOTS = 2

score_scale = 0.125
epsilon = 1e-06
masked_score = -1e30

f32 = jnp.float32
bf16 = jnp.bfloat16
NT = (((1,), (1,)), ((), ()))
TN = (((0,), (0,)), ((), ()))
VMEM = pl.BlockSpec(memory_space=pltpu.VMEM)
SMEM = pl.BlockSpec(memory_space=pltpu.SMEM)


def iota(shape, dim):
    return lax.broadcasted_iota(jnp.int32, shape, dim)


def shaped(shape, dtype):
    return jax.ShapeDtypeStruct(shape, dtype)


def passed_along(value, axis, steps):
    count = lax.axis_size(axis)
    return lax.ppermute(value, axis, [(source, source + steps) for source in range(count - steps)])


def swapped(value, axis, mask):
    count = lax.axis_size(axis)
    return lax.ppermute(value, axis, [(source, source ^ mask) for source in range(count)])


def behind(value, *earlier):
    return lax.optimization_barrier((value, *earlier))[0]


def merge_starts(former, latter):
    take_latter = (latter[4] > 0) & ((former[4] == 0) | (latter[3] != former[3]))
    return tuple((jnp.where(take_latter, newer, older) for older, newer in zip(former, latter)))


def latest_start(key_rows, value_rows, segments):
    tok_count, model_width = key_rows.shape
    length, index = (lax.axis_size("seq"), lax.axis_index("seq"))
    last_seg = segments[tok_count - 1]
    lead = jnp.sum((segments < last_seg).astype(jnp.int32))
    one = jnp.ones((), jnp.int32)
    found = (key_rows[lead], value_rows[lead], index * tok_count + lead, last_seg, one)
    everything = jax.tree.map(lambda part: lax.all_gather(part, "seq"), found)
    start = jax.tree.map(jnp.zeros_like, found)

    def lap(k, before):
        new = merge_starts(before, jax.tree.map(lambda part: part[k], everything))
        return jax.tree.map(lambda a, b: jnp.where(k < index, a, b), new, before)

    sink_key, sink_value, sink_pos, sink_seg, sink_has = lax.fori_loop(0, length, lap, start)
    block = jnp.zeros((2 * tok_count, model_width), key_rows.dtype)
    block = block.at[0].set(sink_key).at[tok_count].set(sink_value)
    return (block, jnp.stack([sink_pos, sink_seg, sink_has]))


def column_routes(experts, routes, new_table, old_table):
    chosen, holders = ([[], []], [[], []])
    for ref in routes:
        for c in range(2):
            slot = ref[c : c + 1, :]
            pick = sum(jnp.where(slot == s, new_table[s], 0) for s in range(experts))
            chosen[c].append(pick)
            holders[c].append(sum(jnp.where(pick == old_table[x], x, 0) for x in range(experts)))
    return (chosen, [jnp.concatenate(rows, axis=0) for rows in holders])


def attended(batch, hops, relayed, heads, sinks, bias, segs, q, k, v, rest, context):
    count = 3 if relayed else hops
    moved, sent, rest = (rest[:count], rest[count : 2 * count], rest[2 * count :])
    if sinks:
        sink_block, sink_info, rest = (rest[0], rest[1], rest[2:])
    tokens, proj = rest
    tok_count, width = tokens.shape[2:]
    window = WIN_BLOCKS * tok_count
    index = lax.axis_index("seq")
    grid = (tok_count, tok_count)

    own_seg = segs[batch]
    key_segs = [own_seg]
    if relayed:
        pairwise, across, relay = moved
        paired = index % 2 == 1
        key_segs += [jnp.where(paired, sent[0][batch], sent[2][batch]), sent[1][batch]]
    else:
        key_segs += [ref[batch] for ref in sent]
    seg_col = jnp.broadcast_to(own_seg, grid).T
    visible, spans = ([], [])
    for j, key_seg in enumerate(key_segs):
        key_seg = jnp.where(index >= j, key_seg, -1)
        distance = iota(grid, 0) - iota(grid, 1) + tok_count * j
        seen = (seg_col == key_seg) & (distance >= 0) & (distance < window)
        visible.append(jnp.where(seen, 0.0, masked_score))
        low, high = (max(0, tok_count * (j - 1) + 1), min(window, tok_count * (j + 1)) - 1)
        spans.append((distance, low.bit_length(), high.bit_length()))
    if sinks:
        position = index * tok_count + iota(grid, 0)
        seen = (seg_col == sink_info[1]) & (sink_info[2] > 0) & (position - sink_info[0] >= window)
        visible.append(jnp.where(seen & (iota(grid, 1) == 0), 0.0, masked_score))
        spans.append((None, NBUCK - 1, NBUCK - 1))
    lane = iota((tok_count, 128), 1)
    half = width // heads
    keys_at, values_at = (slice(0, tok_count), slice(tok_count, 2 * tok_count))
    for pair in range(heads // 2):
        cols = slice(128 * pair, 128 * pair + 128)
        both = q[batch, 0, :, cols] * score_scale
        even = jnp.where(lane < half, both, jnp.zeros_like(both))
        odd = jnp.where(lane < half, jnp.zeros_like(both), both)
        stacked = jnp.concatenate([even, odd], axis=0)
        blocks = [(k[batch, 0, :, cols], v[batch, 0, :, cols])]
        if relayed:
            blocks.append(tuple(
                jnp.where(paired, pairwise[at, cols], relay[at, cols])
                for at in (keys_at, values_at)
            ))
            blocks.append((across[keys_at, cols], across[values_at, cols]))
        else:
            for ref in moved:
                blocks.append((ref[keys_at, cols], ref[values_at, cols]))
        if sinks:
            blocks.append((sink_block[keys_at, cols], sink_block[values_at, cols]))
        scores = []
        for (keys, _), (distance, low, high), seen in zip(blocks, spans, visible):
            score = lax.dot_general(stacked, keys, NT, preferred_element_type=f32)
            parts = []
            for side in range(2):
                head = 2 * pair + side
                offset = jnp.full(grid, bias[head, low], f32)
                for bucket in range(low + 1, high + 1):
                    offset = jnp.where(distance >= 1 << (bucket - 1), bias[head, bucket], offset)
                parts.append(score[side * tok_count : (side + 1) * tok_count] + (offset + seen))
            scores.append(jnp.concatenate(parts, axis=0))
        peak = jnp.max(functools.reduce(jnp.maximum, scores), axis=1, keepdims=True)
        weights = [jnp.exp(score - peak) for score in scores]
        total = jnp.sum(functools.reduce(jnp.add, weights), axis=1, keepdims=True)
        scale = 1.0 / total
        mixed = sum(
            jnp.dot((weight * scale).astype(bf16), values, preferred_element_type=f32)
            for weight, (_, values) in zip(weights, blocks)
        )
        context[:, cols] = jnp.where(lane < half, mixed[:tok_count], mixed[tok_count:]).astype(bf16)
    hidden = tokens[batch, 0].astype(f32) + jnp.dot(
        context[...], proj[...], preferred_element_type=f32
    )
    mean = jnp.mean(hidden * hidden, axis=1, keepdims=True)
    return (hidden, (hidden * lax.rsqrt(mean + epsilon)).astype(bf16))


def ranks(member):
    grid = (member.shape[1], member.shape[1])
    earlier = jnp.where(iota(grid, 0) < iota(grid, 1), 1.0, 0.0).astype(bf16)
    return jnp.dot(member.astype(bf16), earlier, preferred_element_type=f32).astype(jnp.int32)


def attend_column_kernel(options, experts, bias, new_table, old_table, segs, q, k, v, *rest):
    routes, rest = (rest[: experts // 2], rest[experts // 2 :])
    inputs, (hidden_out, normed_out, places_out, context) = (rest[:-4], rest[-4:])
    hidden, normed = attended(1, *options, bias, segs, q, k, v, inputs, context)
    hidden_out[...] = hidden
    normed_out[...] = normed
    me = lax.axis_index("exp")
    _, holders = column_routes(experts, routes, new_table, old_table)
    member = jnp.concatenate(
        [jnp.where((holders[0] == at) | (holders[1] == at), 1.0, 0.0) for at in (me, me ^ 1)],
        axis=0,
    )
    places_out[...] = jnp.where(member > 0.5, ranks(member), -1)


def attend_direct_kernel(options, experts, cap, bias, old_table, routes, router_t, segs, q, k, v, *rest):
    inputs, rest = (rest[: -4 - experts], rest[-4 - experts :])
    outgoing, (hidden_out, gates_out, rows_out, context) = (rest[:experts], rest[experts:])
    hidden, normed = attended(0, *options, bias, segs, q, k, v, inputs, context)
    hidden_out[...] = hidden
    tok_count = hidden.shape[0]
    chosen = [routes[c : c + 1, :] for c in range(2)]
    holders = [sum(jnp.where(c == old_table[x], x, 0) for x in range(experts)) for c in chosen]
    expert = iota((experts, tok_count), 0)
    packet = expert ^ lax.axis_index("exp")
    member = jnp.where((packet == holders[0]) | (packet == holders[1]), 1.0, 0.0)
    place = ranks(member) + expert * cap
    rows = [
        jnp.sum(jnp.where(packet == holder, place, 0), axis=0, keepdims=True) for holder in holders
    ]
    rows_out[...] = jnp.concatenate(rows, axis=0)
    logits = lax.dot_general(router_t[...], normed, NT, preferred_element_type=f32)
    picked = [jnp.sum(jnp.where(expert == c, logits, 0.0), axis=0, keepdims=True) for c in chosen]
    first = jax.nn.sigmoid(picked[0] - picked[1])
    gates_out[...] = jnp.concatenate([first, 1.0 - first], axis=0)
    at = iota((experts * cap, tok_count), 0)
    plan = jnp.where((at == rows[0]) | (at == rows[1]), 1.0, 0.0).astype(bf16)
    packed = jnp.dot(plan, normed, preferred_element_type=f32)
    for m, ref in enumerate(outgoing):
        ref[...] = packed[m * cap : (m + 1) * cap].astype(bf16)


def picked_rows(members, cap, first_row, places, blocks):
    tok_count = blocks[0].shape[0]
    at = iota((len(members) * cap, tok_count), 0)
    plans = []
    for n, m in enumerate(members):
        place = places[first_row + m : first_row + m + 1, :]
        place = jnp.where(place >= 0, place + n * cap, -1)
        plans.append(jnp.where(at == place, 1.0, 0.0).astype(bf16))
    plan = jnp.concatenate(plans, axis=1)
    rows = jnp.concatenate([block[...] for block in blocks], axis=0)
    return jnp.dot(plan, rows, preferred_element_type=f32).astype(bf16)


def pack_kernel(members, cap, columns, places, *rest):
    blocks, out = (rest[:-1], rest[-1])
    out[...] = picked_rows(members, cap, columns, places, blocks)


def expert_rows(rows, weights, active, stores):
    gate, up, down = weights
    inner, width = down.shape[1:]
    x = rows[...]
    for begin in range(0, inner, 256):
        span = slice(begin, min(inner, begin + 256))
        gate_part = jnp.dot(x, gate[0, :, span], preferred_element_type=f32)
        up_part = jnp.dot(x, up[0, :, span], preferred_element_type=f32)
        active[:, span] = (jax.nn.gelu(gate_part, approximate=True) * up_part).astype(bf16)
    for begin in range(0, width, 256):
        span = slice(begin, begin + 256)
        part = jnp.dot(active[...], down[0, :, span], preferred_element_type=f32)
        stores(span, part)


def near_kernel(experts, cap, new_table, old_table, places, router_t, *rest):
    columns = experts // 2
    blocks, rest = (rest[:columns], rest[columns:])
    routes, rest = (rest[:columns], rest[columns:])
    weights, (out, gates_out, rows, active) = (rest[:3], rest[3:])

    def stores(span, value):
        out[:, span] = value.astype(bf16)

    rows[...] = picked_rows(range(columns), cap, 0, places, blocks)
    chosen, holders = column_routes(experts, routes, new_table, old_table)
    me = lax.axis_index("exp")
    firsts = []
    for m in range(columns):
        logits = lax.dot_general(router_t[...], blocks[m][...], NT, preferred_element_type=f32)
        expert = iota(logits.shape, 0)
        picked = [
            jnp.sum(jnp.where(expert == chosen[c][m], logits, 0.0), axis=0, keepdims=True)
            for c in range(2)
        ]
        firsts.append(jax.nn.sigmoid(picked[0] - picked[1]))
    first = jnp.concatenate(firsts, axis=0)
    gates_out[...] = jnp.concatenate(
        [
            jnp.where(holders[0] == at, first, 0.0) + jnp.where(holders[1] == at, 1.0 - first, 0.0)
            for at in (me, me ^ 1)
        ],
        axis=0,
    )
    expert_rows(rows, weights, active, stores)


def far_kernel(low_in, high_in, *rest):
    weights, (low_out, high_out, rows, active) = (rest[:3], rest[3:])
    part = low_in.shape[0]

    def stores(span, value):
        low_out[:, span] = value[:part].astype(bf16)
        high_out[:, span] = value[part:].astype(bf16)

    rows[:part, :] = low_in[...]
    rows[part:, :] = high_in[...]
    expert_rows(rows, weights, active, stores)


def direct_kernel(*refs):
    count = (len(refs) - 5) // 2
    packets, weights, outs = (refs[:count], refs[count : count + 3], refs[count + 3 : -2])
    rows, active = refs[-2:]
    cap = packets[0].shape[0]

    def stores(span, value):
        for m, out in enumerate(outs):
            out[:, span] = value[m * cap : (m + 1) * cap].astype(bf16)

    rows[...] = jnp.concatenate([ref[...].astype(f32) for ref in packets], axis=0).astype(bf16)
    expert_rows(rows, weights, active, stores)


def combine_kernel(hidden, gates, rows, *rest):
    packets, out = (rest[:-1], rest[-1])
    cap = packets[0].shape[0]
    at = iota((len(packets) * cap, hidden.shape[0]), 0)
    spread = jnp.where(at == rows[0:1, :], gates[0:1, :], 0.0)
    spread = spread + jnp.where(at == rows[1:2, :], gates[1:2, :], 0.0)
    coarse = spread.astype(bf16)
    fine = (spread - coarse.astype(f32)).astype(bf16)
    values = jnp.concatenate([ref[...].astype(f32) for ref in packets], axis=0).astype(bf16)
    total = hidden[...]
    for half in (coarse, fine):
        total = total + lax.dot_general(half, values, TN, preferred_element_type=f32)
    out[...] = total


def partial_kernel(members, cap, columns, places, gates, near, far, *outs):
    tok_count = places.shape[1]
    for n, m in enumerate(members):
        total = None
        for source, row, base in ((near, m, m * cap), (far, columns + m, n * cap)):
            at = iota((source.shape[0], tok_count), 0)
            place = places[row : row + 1, :]
            place = jnp.where(place >= 0, place + base, -1)
            spread = jnp.where(at == place, gates[row : row + 1, :], 0.0)
            coarse = spread.astype(bf16)
            fine = (spread - coarse.astype(f32)).astype(bf16)
            for half in (coarse, fine):
                term = lax.dot_general(half, source[...], TN, preferred_element_type=f32)
                total = term if total is None else total + term
        outs[n][...] = total.astype(outs[n].dtype)


def fold_kernel(own, *rest):
    total = own[...]
    for ref in rest[:-1]:
        total = total + ref[...].astype(f32)
    rest[-1][...] = total.astype(rest[-1].dtype)


def final_kernel(counts, *refs):
    out = refs[-1]
    at = 0
    for batch, count in enumerate(counts):
        total = refs[at][...]
        for ref in refs[at + 1 : at + count]:
            total = total + ref[...].astype(f32)
        at += count
        out[batch, 0] = total.astype(bf16)


def local(
    tokens, queries, key_rows, value_rows, segments, bias_table, out_proj, router,
    gate_weight, up_weight, down_weight, old_table, new_table, routes_one, routes_two,
):
    tok_count, width = tokens.shape[2:]
    heads = bias_table.shape[0]
    experts = router.shape[1]
    columns = experts // 2
    inner = gate_weight.shape[2]
    seq_size = lax.axis_size("seq")
    seq_len = tok_count * seq_size
    capacity = tok_count * 2 * 5 // (4 * experts)
    longest = seq_len // 2
    hops = min(WIN_BLOCKS, (longest - 1 + tok_count - 1) // tok_count)
    relayed = seq_size == 4 and hops == 2
    sinks = seq_len > WIN_BLOCKS * tok_count
    weights = (gate_weight, up_weight, down_weight)
    router_t = router.T
    lower, upper = (range(columns // 2), range(columns // 2, columns))
    rows_bf16 = shaped((tok_count, width), bf16)
    rows_f32 = shaped((tok_count, width), f32)
    cap_two = capacity * MAX_SLOTS
    part_two = columns // 2 * cap_two
    latest = []

    def call(kernel, outs, ins, args, flops=10**7, moved=10**6, scratch=(), limit=24):
        args = list(args)
        if latest:
            args[-1] = behind(args[-1], latest[0])
        made = pl.pallas_call(
            kernel,
            out_shape=outs,
            in_specs=ins,
            out_specs=jax.tree.map(lambda _: VMEM, outs),
            scratch_shapes=list(scratch),
            compiler_params=pltpu.CompilerParams(vmem_limit_bytes=limit * 2**20),
            cost_estimate=pl.CostEstimate(flops=flops, bytes_accessed=moved, transcendentals=0),
        )(*args)
        latest[:] = jax.tree.leaves(made)[:1]
        return made

    def multicast(own):
        blocks = {0: own}
        bit = columns // 2
        while bit:
            for m in sorted(blocks):
                moving = blocks[m]
                if m:
                    moving = behind(moving, blocks[bit])
                blocks[m | bit] = swapped(moving, "exp", 2 * bit)
            bit //= 2
        return blocks

    def stack(batch, keys, values):
        return jnp.concatenate([keys[batch, 0], values[batch, 0]], axis=0)

    def exchange(moving, *before_relay):
        if not relayed:
            moved = []
            for _ in range(hops):
                moving = passed_along(moving, "seq", 1)
                moved.append(moving)
            return moved
        across = swapped(moving, "seq", 2)
        pairwise = swapped(moving, "seq", 1)
        return [pairwise, across, swapped(behind(across, *before_relay), "seq", 1)]

    def options(batch):
        extra = []
        if sinks:
            extra = latest_start(key_rows[batch, 0], value_rows[batch, 0], segments[batch, 0])
        return ((hops, relayed, heads, sinks), extra)

    def attend_column(moved):
        settings, extra = options(1)
        return call(
            functools.partial(attend_column_kernel, settings, experts),
            (rows_f32, rows_bf16, shaped((2 * columns, tok_count), jnp.int32)),
            [SMEM] * 3 + [VMEM] * (4 + columns + 2 * len(moved)) + ([VMEM, SMEM] if sinks else [])
            + [VMEM] * 2,
            (bias_table, new_table, old_table, segments, queries, key_rows, value_rows, *routes,
             *moved, *sent, *extra, tokens, out_proj),
            flops=10**9, moved=8 * 10**6, scratch=[pltpu.VMEM((tok_count, width), bf16)],
        )

    def attend_direct(moved, after):
        settings, extra = options(0)
        return call(
            functools.partial(attend_direct_kernel, settings, experts, capacity),
            (*[shaped((capacity, width), bf16)] * experts, rows_f32, shaped((2, tok_count), f32),
             shaped((2, tok_count), jnp.int32)),
            [SMEM] * 2 + [VMEM] * (6 + 2 * len(moved)) + ([VMEM, SMEM] if sinks else [])
            + [VMEM] * 2,
            (bias_table, old_table, routes_one[0].T, router_t, segments, queries, key_rows,
             value_rows, *moved, *sent, *extra, behind(tokens, after), out_proj),
            flops=10**9, moved=8 * 10**6, scratch=[pltpu.VMEM((tok_count, width), bf16)],
        )

    def scratch_for(slots):
        return (pltpu.VMEM((slots, width), bf16), pltpu.VMEM((slots, inner), bf16))

    def pack(members, places, blocks):
        return call(
            functools.partial(pack_kernel, members, cap_two, columns),
            shaped((part_two, width), bf16),
            [VMEM] * (1 + len(members)),
            (places, *(blocks[m] for m in members)),
        )

    def partial(members, far):
        parts = call(
            functools.partial(partial_kernel, members, cap_two, columns),
            tuple(rows_bf16 if m % 2 else rows_f32 for m in members),
            [VMEM] * 4,
            (places, gates_two, near, far),
        )
        for m, value in zip(members, parts):
            totals.setdefault(m, []).insert(0, value)

    def send_down(members):
        for m in sorted(members, key=lambda m: (m & -m, -m)):
            parts = totals[m]
            value = parts[0]
            if len(parts) > 1:
                value = call(fold_kernel, rows_bf16, [VMEM] * len(parts), parts)
            totals.setdefault(m & (m - 1), []).append(swapped(value, "exp", 2 * (m & -m)))

    routes = multicast(routes_two[0].T)
    routes = [routes[m] for m in range(columns)]
    if relayed:
        sent = [swapped(segments[:, 0], "seq", mask) for mask in (1, 2, 3)]
    else:
        sent = []
        for _ in range(hops):
            sent.append(passed_along(sent[-1] if sent else segments[:, 0], "seq", 1))
    sent = [each[:, None] for each in sent]

    moved_two = exchange(stack(1, key_rows, value_rows), *routes, *sent)
    keys, values = (key_rows, value_rows)
    if relayed:
        keys, values, _ = lax.optimization_barrier((key_rows, value_rows, moved_two[0]))
    stacked = stack(0, keys, values)
    hidden_two, normed_two, places = attend_column(moved_two)
    blocks = multicast(normed_two)
    moved_one = exchange(behind(stacked, normed_two), blocks[columns // 2])
    low_in = swapped(pack(lower, places, blocks), "exp", 1)
    *packets, hidden_one, gates_one, rows_one = attend_direct(moved_one, blocks[columns // 2])
    arrived = [packets[0]] + [None] * (experts - 1)
    for m in range(experts - 1, 0, -1):
        arrived[m] = swapped(packets[m], "exp", m)
    high_in = swapped(pack(upper, places, blocks), "exp", 1)
    slots = columns * cap_two
    near, gates_two = call(
        functools.partial(near_kernel, experts, cap_two),
        (shaped((slots, width), bf16), shaped((2 * columns, tok_count), f32)),
        [SMEM] * 2 + [VMEM] * (5 + 2 * columns),
        (new_table, old_table, places, router_t, *(blocks[m] for m in range(columns)), *routes,
         *weights),
        flops=6 * slots * width * inner, moved=10**7, scratch=scratch_for(slots),
    )
    low_out, high_out = call(
        far_kernel,
        (shaped((part_two, width), bf16),) * 2,
        [VMEM] * 5,
        (behind(low_in, *arrived[-4:]), high_in, *weights),
        flops=6 * slots * width * inner, moved=10**7, scratch=scratch_for(slots),
    )
    high_far, low_far = (swapped(high_out, "exp", 1), swapped(low_out, "exp", 1))
    answers = call(
        direct_kernel,
        (shaped((capacity, width), bf16),) * experts,
        [VMEM] * (3 + experts),
        (*arrived, *weights),
        flops=6 * experts * capacity * width * inner, moved=10**7,
        scratch=scratch_for(experts * capacity),
    )
    returned = [answers[0]] + [None] * (experts - 1)
    for m in range(experts - 1, 0, -1):
        returned[m] = swapped(answers[m], "exp", m)
    totals = {}
    partial(upper, high_far)
    send_down(m for m in upper if m % 2)
    partial(lower, behind(low_far, *returned[-4:]))
    send_down(m for m in upper if m % 2 == 0)
    send_down(m for m in lower if m)
    sum_one = call(
        combine_kernel, rows_f32, [VMEM] * (3 + experts), (hidden_one, gates_one, rows_one, *returned)
    )
    ends = (sum_one, hidden_two, *totals[0])
    return call(
        functools.partial(final_kernel, [1, len(ends) - 1]),
        shaped((2, 1, tok_count, width), bf16),
        [VMEM] * len(ends),
        ends,
    )


def solution(mesh):
    rows = P(None, "exp", "seq", None)
    placed = (
        rows, rows, rows, rows, P(None, "exp", "seq"), P(), P(), P(),
        P("exp", None, None), P("exp", None, None), P("exp", None, None), P(), P(),
        P("exp", "seq", None), P("exp", "seq", None),
    )
    return jax.shard_map(local, mesh=mesh, in_specs=placed, out_specs=rows, check_vma=False)
```

```python
import functools

import jax
import jax.numpy as jnp
from jax import lax
from jax.experimental import pallas as pl
from jax.experimental.pallas import tpu as pltpu
from jax.sharding import PartitionSpec as P

WIN_BLOCKS = 4
NBUCK = 32
MAX_SLOTS = 2

score_scale = 0.125
epsilon = 1e-06
masked_score = -1e30

f32 = jnp.float32
bf16 = jnp.bfloat16
NT = (((1,), (1,)), ((), ()))
TN = (((0,), (0,)), ((), ()))
VMEM = pl.BlockSpec(memory_space=pltpu.VMEM)
SMEM = pl.BlockSpec(memory_space=pltpu.SMEM)


def iota(shape, dim):
    return lax.broadcasted_iota(jnp.int32, shape, dim)


def shaped(shape, dtype):
    return jax.ShapeDtypeStruct(shape, dtype)


def passed_along(value, axis, steps):
    count = lax.axis_size(axis)
    return lax.ppermute(value, axis, [(source, source + steps) for source in range(count - steps)])


def swapped(value, axis, mask):
    count = lax.axis_size(axis)
    return lax.ppermute(value, axis, [(source, source ^ mask) for source in range(count)])


def behind(value, *earlier):
    return lax.optimization_barrier((value, *earlier))[0]


def merge_starts(former, latter):
    take_latter = (latter[4] > 0) & ((former[4] == 0) | (latter[3] != former[3]))
    return tuple((jnp.where(take_latter, newer, older) for older, newer in zip(former, latter)))


def latest_start(key_rows, value_rows, segments):
    tok_count, model_width = key_rows.shape
    length, index = (lax.axis_size("seq"), lax.axis_index("seq"))
    last_seg = segments[tok_count - 1]
    lead = jnp.sum((segments < last_seg).astype(jnp.int32))
    one = jnp.ones((), jnp.int32)
    found = (key_rows[lead], value_rows[lead], index * tok_count + lead, last_seg, one)
    everything = jax.tree.map(lambda part: lax.all_gather(part, "seq"), found)
    start = jax.tree.map(jnp.zeros_like, found)

    def lap(k, before):
        new = merge_starts(before, jax.tree.map(lambda part: part[k], everything))
        return jax.tree.map(lambda a, b: jnp.where(k < index, a, b), new, before)

    sink_key, sink_value, sink_pos, sink_seg, sink_has = lax.fori_loop(0, length, lap, start)
    block = jnp.zeros((2 * tok_count, model_width), key_rows.dtype)
    block = block.at[0].set(sink_key).at[tok_count].set(sink_value)
    return (block, jnp.stack([sink_pos, sink_seg, sink_has]))


def column_routes(experts, routes, new_table, old_table):
    chosen, holders = ([[], []], [[], []])
    for ref in routes:
        for c in range(2):
            slot = ref[c : c + 1, :]
            pick = sum(jnp.where(slot == s, new_table[s], 0) for s in range(experts))
            chosen[c].append(pick)
            holders[c].append(sum(jnp.where(pick == old_table[x], x, 0) for x in range(experts)))
    return (chosen, [jnp.concatenate(rows, axis=0) for rows in holders])


def attended(batch, hops, relayed, heads, sinks, bias, segs, q, k, v, rest, context):
    count = 3 if relayed else hops
    moved, sent, rest = (rest[:count], rest[count : 2 * count], rest[2 * count :])
    if sinks:
        sink_block, sink_info, rest = (rest[0], rest[1], rest[2:])
    tokens, proj = rest
    tok_count, width = tokens.shape[2:]
    window = WIN_BLOCKS * tok_count
    index = lax.axis_index("seq")
    grid = (tok_count, tok_count)

    own_seg = segs[batch]
    key_segs = [own_seg]
    if relayed:
        pairwise, across, relay = moved
        paired = index % 2 == 1
        key_segs += [jnp.where(paired, sent[0][batch], sent[2][batch]), sent[1][batch]]
    else:
        key_segs += [ref[batch] for ref in sent]
    seg_col = jnp.broadcast_to(own_seg, grid).T
    visible, spans = ([], [])
    for j, key_seg in enumerate(key_segs):
        key_seg = jnp.where(index >= j, key_seg, -1)
        distance = iota(grid, 0) - iota(grid, 1) + tok_count * j
        seen = (seg_col == key_seg) & (distance >= 0) & (distance < window)
        visible.append(jnp.where(seen, 0.0, masked_score))
        low, high = (max(0, tok_count * (j - 1) + 1), min(window, tok_count * (j + 1)) - 1)
        spans.append((distance, low.bit_length(), high.bit_length()))
    if sinks:
        position = index * tok_count + iota(grid, 0)
        seen = (seg_col == sink_info[1]) & (sink_info[2] > 0) & (position - sink_info[0] >= window)
        visible.append(jnp.where(seen & (iota(grid, 1) == 0), 0.0, masked_score))
        spans.append((None, NBUCK - 1, NBUCK - 1))
    lane = iota((tok_count, 128), 1)
    half = width // heads
    keys_at, values_at = (slice(0, tok_count), slice(tok_count, 2 * tok_count))
    for pair in range(heads // 2):
        cols = slice(128 * pair, 128 * pair + 128)
        both = q[batch, 0, :, cols] * score_scale
        even = jnp.where(lane < half, both, jnp.zeros_like(both))
        odd = jnp.where(lane < half, jnp.zeros_like(both), both)
        stacked = jnp.concatenate([even, odd], axis=0)
        blocks = [(k[batch, 0, :, cols], v[batch, 0, :, cols])]
        if relayed:
            blocks.append(tuple(
                jnp.where(paired, pairwise[at, cols], relay[at, cols])
                for at in (keys_at, values_at)
            ))
            blocks.append((across[keys_at, cols], across[values_at, cols]))
        else:
            for ref in moved:
                blocks.append((ref[keys_at, cols], ref[values_at, cols]))
        if sinks:
            blocks.append((sink_block[keys_at, cols], sink_block[values_at, cols]))
        scores = []
        for (keys, _), (distance, low, high), seen in zip(blocks, spans, visible):
            score = lax.dot_general(stacked, keys, NT, preferred_element_type=f32)
            parts = []
            for side in range(2):
                head = 2 * pair + side
                offset = jnp.full(grid, bias[head, low], f32)
                for bucket in range(low + 1, high + 1):
                    offset = jnp.where(distance >= 1 << (bucket - 1), bias[head, bucket], offset)
                parts.append(score[side * tok_count : (side + 1) * tok_count] + (offset + seen))
            scores.append(jnp.concatenate(parts, axis=0))
        peak = jnp.max(functools.reduce(jnp.maximum, scores), axis=1, keepdims=True)
        weights = [jnp.exp(score - peak) for score in scores]
        total = jnp.sum(functools.reduce(jnp.add, weights), axis=1, keepdims=True)
        scale = 1.0 / total
        mixed = sum(
            jnp.dot((weight * scale).astype(bf16), values, preferred_element_type=f32)
            for weight, (_, values) in zip(weights, blocks)
        )
        context[:, cols] = jnp.where(lane < half, mixed[:tok_count], mixed[tok_count:]).astype(bf16)
    hidden = tokens[batch, 0].astype(f32) + jnp.dot(
        context[...], proj[...], preferred_element_type=f32
    )
    mean = jnp.mean(hidden * hidden, axis=1, keepdims=True)
    return (hidden, (hidden * lax.rsqrt(mean + epsilon)).astype(bf16))


def ranks(member):
    grid = (member.shape[1], member.shape[1])
    earlier = jnp.where(iota(grid, 0) < iota(grid, 1), 1.0, 0.0).astype(bf16)
    return jnp.dot(member.astype(bf16), earlier, preferred_element_type=f32).astype(jnp.int32)


def attend_column_kernel(options, experts, bias, new_table, old_table, segs, q, k, v, *rest):
    routes, rest = (rest[: experts // 2], rest[experts // 2 :])
    inputs, (hidden_out, *normed_out, places_out, context) = (rest[:-5], rest[-5:])
    hidden, normed = attended(1, *options, bias, segs, q, k, v, inputs, context)
    hidden_out[...] = hidden
    for ref, span in halves(normed_out):
        ref[...] = normed[:, span]
    me = lax.axis_index("exp")
    _, holders = column_routes(experts, routes, new_table, old_table)
    member = jnp.concatenate(
        [jnp.where((holders[0] == at) | (holders[1] == at), 1.0, 0.0) for at in (me, me ^ 1)],
        axis=0,
    )
    places_out[...] = jnp.where(member > 0.5, ranks(member), -1)


def halves(refs):
    width = refs[0].shape[-1]
    return [(ref, slice(n * width, (n + 1) * width)) for n, ref in enumerate(refs)]


def attend_direct_kernel(options, experts, cap, bias, old_table, routes, router_t, segs, q, k, v, *rest):
    layers = experts // 2
    inputs, rest = (rest[: -4 - layers], rest[-4 - layers :])
    outgoing, (hidden_out, gates_out, rows_out, context) = (rest[:layers], rest[layers:])
    hidden, normed = attended(0, *options, bias, segs, q, k, v, inputs, context)
    hidden_out[...] = hidden
    tok_count = hidden.shape[0]
    chosen = [routes[c : c + 1, :] for c in range(2)]
    holders = [sum(jnp.where(c == old_table[x], x, 0) for x in range(experts)) for c in chosen]
    expert = iota((experts, tok_count), 0)
    packet = expert ^ lax.axis_index("exp")
    member = jnp.where((packet == holders[0]) | (packet == holders[1]), 1.0, 0.0)
    place = ranks(member) + expert * cap
    rows = [
        jnp.sum(jnp.where(packet == holder, place, 0), axis=0, keepdims=True) for holder in holders
    ]
    rows_out[...] = jnp.concatenate(rows, axis=0)
    logits = lax.dot_general(router_t[...], normed, NT, preferred_element_type=f32)
    picked = [jnp.sum(jnp.where(expert == c, logits, 0.0), axis=0, keepdims=True) for c in chosen]
    first = jax.nn.sigmoid(picked[0] - picked[1])
    gates_out[...] = jnp.concatenate([first, 1.0 - first], axis=0)
    at = iota((experts * cap, tok_count), 0)
    plan = jnp.where((at == rows[0]) | (at == rows[1]), 1.0, 0.0).astype(bf16)
    packed = jnp.dot(plan, normed, preferred_element_type=f32)
    for m, ref in enumerate(outgoing):
        ref[...] = packed[2 * m * cap : 2 * (m + 1) * cap].astype(bf16)


def column_plan(columns, cap, first_row, places):
    plans = []
    for m in range(columns):
        place = places[first_row + m : first_row + m + 1, :]
        at = iota((columns * cap, place.shape[1]), 0)
        plans.append(jnp.where(at == jnp.where(place >= 0, place + m * cap, -1), 1.0, 0.0))
    return jnp.concatenate(plans, axis=1).astype(bf16)


def column_rows(gathered):
    layer = lax.axis_index("exp") // 2
    return [gathered[layer ^ m] for m in range(gathered.shape[0])]


def pack_kernel(columns, cap, places, gathered, out):
    plan = column_plan(columns, cap, columns, places)
    rows = jnp.concatenate(column_rows(gathered), axis=0)
    out[...] = jnp.dot(plan, rows, preferred_element_type=f32).astype(bf16)


def crossing_kernel(*refs):
    packets, out = (refs[:-1], refs[-1])
    cap = packets[0].shape[0] // 2
    parts = [ref[...].astype(f32)[cap:] for ref in packets]
    out[...] = jnp.concatenate(parts, axis=0).astype(bf16)


def expert_rows(rows, weights, active, stores):
    gate, up, down = weights
    inner, width = down.shape[1:]
    x = rows[...]
    for begin in range(0, inner, 256):
        span = slice(begin, min(inner, begin + 256))
        gate_part = jnp.dot(x, gate[0, :, span], preferred_element_type=f32)
        up_part = jnp.dot(x, up[0, :, span], preferred_element_type=f32)
        active[:, span] = (jax.nn.gelu(gate_part, approximate=True) * up_part).astype(bf16)
    for begin in range(0, width, 256):
        span = slice(begin, begin + 256)
        part = jnp.dot(active[...], down[0, :, span], preferred_element_type=f32)
        stores(span, part)


def near_kernel(columns, experts, cap, new_table, old_table, places, router_t, *rest):
    gathered, rest = (rest[:2], rest[2:])
    routes, rest = (rest[:columns], rest[columns:])
    weights, (out, gates_out, rows, active) = (rest[:3], rest[3:])

    def stores(span, value):
        out[:, span] = value.astype(bf16)

    plan = column_plan(columns, cap, 0, places)
    logits = None
    for ref, span in halves(gathered):
        each = jnp.concatenate(column_rows(ref), axis=0)
        rows[:, span] = jnp.dot(plan, each, preferred_element_type=f32).astype(bf16)
        part = lax.dot_general(router_t[:, span], each, NT, preferred_element_type=f32)
        logits = part if logits is None else logits + part
    chosen, holders = column_routes(experts, routes, new_table, old_table)
    chosen = [jnp.concatenate(picks, axis=1) for picks in chosen]
    expert = iota(logits.shape, 0)
    picked = [
        jnp.sum(jnp.where(expert == pick, logits, 0.0), axis=0, keepdims=True) for pick in chosen
    ]
    first = jax.nn.sigmoid(picked[0] - picked[1])
    tok_count = places.shape[1]
    first = jnp.concatenate(
        [first[:, m * tok_count : (m + 1) * tok_count] for m in range(columns)], axis=0
    )
    me = lax.axis_index("exp")
    gates_out[...] = jnp.concatenate(
        [
            jnp.where(holders[0] == at, first, 0.0) + jnp.where(holders[1] == at, 1.0 - first, 0.0)
            for at in (me, me ^ 1)
        ],
        axis=0,
    )
    expert_rows(rows, weights, active, stores)


def far_kernel(*refs):
    packets, weights, outs, (rows, active) = (refs[:2], refs[2:5], refs[5:7], refs[7:])

    def stores(span, value):
        for out, half in halves(outs):
            if half.start <= span.start < half.stop:
                out[:, span.start - half.start : span.stop - half.start] = value.astype(bf16)

    for ref, span in halves(packets):
        rows[:, span] = ref[...]
    expert_rows(rows, weights, active, stores)


def direct_kernel(layers, *refs):
    packets, crossed, weights = (refs[:layers], refs[layers], refs[layers + 1 : layers + 4])
    near, far, rows, active = refs[layers + 4 :]
    cap = packets[0].shape[0] // 2
    half = layers * cap

    def stores(span, value):
        near[:, span] = value[:half].astype(bf16)
        far[:, span] = value[half:].astype(bf16)

    parts = [ref[...].astype(f32)[:cap] for ref in packets]
    rows[:half, :] = jnp.concatenate(parts, axis=0).astype(bf16)
    rows[half:, :] = crossed[...]
    expert_rows(rows, weights, active, stores)


def rejoin_kernel(near, far, *outs):
    cap = outs[0].shape[0] // 2
    both = [ref[...].astype(f32) for ref in (near, far)]
    for m, out in enumerate(outs):
        parts = [each[m * cap : (m + 1) * cap] for each in both]
        out[...] = jnp.concatenate(parts, axis=0).astype(bf16)


def combine_kernel(hidden, gates, rows, *rest):
    packets, out = (rest[:-1], rest[-1])
    cap = packets[0].shape[0]
    at = iota((len(packets) * cap, hidden.shape[0]), 0)
    spread = jnp.where(at == rows[0:1, :], gates[0:1, :], 0.0)
    spread = spread + jnp.where(at == rows[1:2, :], gates[1:2, :], 0.0)
    coarse = spread.astype(bf16)
    fine = (spread - coarse.astype(f32)).astype(bf16)
    values = jnp.concatenate([ref[...].astype(f32) for ref in packets], axis=0).astype(bf16)
    total = hidden[...]
    for half in (coarse, fine):
        total = total + lax.dot_general(half, values, TN, preferred_element_type=f32)
    out[...] = total


def partial_kernel(half, columns, cap, places, gates, near, far, out):
    tok_count = places.shape[1]
    layer = lax.axis_index("exp") // 2
    width = far.shape[1]
    span = slice(half * width, (half + 1) * width)
    for m in range(columns):
        total = None
        rows = slice(m * cap, (m + 1) * cap)
        for values, row in ((near[rows, span], m), (far[rows, :], columns + m)):
            at = iota((cap, tok_count), 0)
            spread = jnp.where(at == places[row : row + 1, :], gates[row : row + 1, :], 0.0)
            coarse = spread.astype(bf16)
            fine = (spread - coarse.astype(f32)).astype(bf16)
            for weight in (coarse, fine):
                term = lax.dot_general(weight, values, TN, preferred_element_type=f32)
                total = term if total is None else total + term
        out[layer ^ m] = total.astype(bf16)


def final_kernel(one, hidden, low, high, out):
    out[0, 0] = one[...].astype(bf16)
    for ref, span in halves((low, high)):
        out[1, 0, :, span] = (hidden[:, span] + ref[...].astype(f32)).astype(bf16)


def local(
    tokens, queries, key_rows, value_rows, segments, bias_table, out_proj, router,
    gate_weight, up_weight, down_weight, old_table, new_table, routes_one, routes_two,
):
    tok_count, width = tokens.shape[2:]
    heads = bias_table.shape[0]
    experts = router.shape[1]
    columns = experts // 2
    inner = gate_weight.shape[2]
    seq_size = lax.axis_size("seq")
    seq_len = tok_count * seq_size
    capacity = tok_count * 2 * 5 // (4 * experts)
    longest = seq_len // 2
    hops = min(WIN_BLOCKS, (longest - 1 + tok_count - 1) // tok_count)
    relayed = seq_size == 4 and hops == 2
    sinks = seq_len > WIN_BLOCKS * tok_count
    weights = (gate_weight, up_weight, down_weight)
    router_t = router.T
    groups = [[2 * layer + y for layer in range(columns)] for y in range(2)]
    part_bf16 = shaped((tok_count, width // 2), bf16)
    rows_f32 = shaped((tok_count, width), f32)
    cap_two = capacity * MAX_SLOTS
    slots = columns * cap_two
    packet = shaped((2 * capacity, width), bf16)
    latest = []

    def call(kernel, outs, ins, args, flops=10**7, moved=10**6, scratch=(), limit=24):
        args = list(args)
        if latest:
            args[-1] = behind(args[-1], latest[0])
        made = pl.pallas_call(
            kernel,
            out_shape=outs,
            in_specs=ins,
            out_specs=jax.tree.map(lambda _: VMEM, outs),
            scratch_shapes=list(scratch),
            compiler_params=pltpu.CompilerParams(vmem_limit_bytes=limit * 2**20),
            cost_estimate=pl.CostEstimate(flops=flops, bytes_accessed=moved, transcendentals=0),
        )(*args)
        latest[:] = jax.tree.leaves(made)[:1]
        return made

    def multicast(own):
        blocks = {0: own}
        bit = columns // 2
        while bit:
            for m in sorted(blocks):
                moving = blocks[m]
                if m:
                    moving = behind(moving, blocks[bit])
                blocks[m | bit] = swapped(moving, "exp", 2 * bit)
            bit //= 2
        return blocks

    def stack(batch, keys, values):
        return jnp.concatenate([keys[batch, 0], values[batch, 0]], axis=0)

    def exchange(moving, *before_relay):
        if not relayed:
            moved = []
            for _ in range(hops):
                moving = passed_along(moving, "seq", 1)
                moved.append(moving)
            return moved
        across = swapped(moving, "seq", 2)
        pairwise = swapped(moving, "seq", 1)
        return [pairwise, across, swapped(behind(across, *before_relay), "seq", 1)]

    def options(batch):
        extra = []
        if sinks:
            extra = latest_start(key_rows[batch, 0], value_rows[batch, 0], segments[batch, 0])
        return ((hops, relayed, heads, sinks), extra)

    def attend_column(moved):
        settings, extra = options(1)
        return call(
            functools.partial(attend_column_kernel, settings, experts),
            (rows_f32, part_bf16, part_bf16, shaped((2 * columns, tok_count), jnp.int32)),
            [SMEM] * 3 + [VMEM] * (4 + columns + 2 * len(moved)) + ([VMEM, SMEM] if sinks else [])
            + [VMEM] * 2,
            (bias_table, new_table, old_table, segments, queries, key_rows, value_rows, *routes,
             *moved, *sent, *extra, tokens, out_proj),
            flops=10**9, moved=8 * 10**6, scratch=[pltpu.VMEM((tok_count, width), bf16)],
        )

    def attend_direct(moved):
        settings, extra = options(0)
        return call(
            functools.partial(attend_direct_kernel, settings, experts, capacity),
            (*[packet] * columns, rows_f32, shaped((2, tok_count), f32),
             shaped((2, tok_count), jnp.int32)),
            [SMEM] * 2 + [VMEM] * (6 + 2 * len(moved)) + ([VMEM, SMEM] if sinks else [])
            + [VMEM] * 2,
            (bias_table, old_table, routes_one[0].T, router_t, segments, queries, key_rows,
             value_rows, *moved, *sent, *extra, tokens, out_proj),
            flops=10**9, moved=8 * 10**6, scratch=[pltpu.VMEM((tok_count, width), bf16)],
        )

    def scratch_for(slots):
        return (pltpu.VMEM((slots, width), bf16), pltpu.VMEM((slots, inner), bf16))

    routes = multicast(routes_two[0].T)
    routes = [routes[m] for m in range(columns)]
    if relayed:
        sent = [swapped(segments[:, 0], "seq", mask) for mask in (1, 2, 3)]
    else:
        sent = []
        for _ in range(hops):
            sent.append(passed_along(sent[-1] if sent else segments[:, 0], "seq", 1))
    sent = [each[:, None] for each in sent]

    moved_two = exchange(stack(1, key_rows, value_rows), *routes, *sent)
    keys, values = (key_rows, value_rows)
    if relayed:
        keys, values, _ = lax.optimization_barrier((key_rows, value_rows, moved_two[0]))
    stacked = stack(0, keys, values)
    moved_one = exchange(behind(stacked, moved_two[min(1, hops - 1)]))
    hidden_two, *normed, places = attend_column(moved_two)
    gathered = [lax.all_gather(half, "exp", axis_index_groups=groups) for half in normed]
    *packets, hidden_one, gates_one, rows_one = attend_direct(moved_one)
    arrived = [packets[0]] + [swapped(packets[m], "exp", 2 * m) for m in range(1, columns)]
    crossed_two = []
    for half in gathered:
        packed = call(
            functools.partial(pack_kernel, columns, cap_two), shaped((slots, width // 2), bf16),
            [VMEM] * 2, (places, half),
        )
        crossed_two.append(swapped(packed, "exp", 1))
    crossing = call(
        crossing_kernel, shaped((columns * capacity, width), bf16), [VMEM] * columns, arrived
    )
    crossed_one = swapped(crossing, "exp", 1)
    near, gates_two = call(
        functools.partial(near_kernel, columns, experts, cap_two),
        (shaped((slots, width), bf16), shaped((2 * columns, tok_count), f32)),
        [SMEM] * 2 + [VMEM] * (7 + columns),
        (new_table, old_table, places, router_t, *gathered, *routes, *weights),
        flops=6 * slots * width * inner, moved=10**7, scratch=scratch_for(slots),
    )
    far = call(
        far_kernel,
        (shaped((slots, width // 2), bf16),) * 2,
        [VMEM] * 5,
        (*crossed_two, *weights),
        flops=6 * slots * width * inner, moved=10**7, scratch=scratch_for(slots),
    )
    far = [swapped(half, "exp", 1) for half in far]
    near_one, far_one = call(
        functools.partial(direct_kernel, columns),
        (shaped((columns * capacity, width), bf16),) * 2,
        [VMEM] * (4 + columns),
        (*arrived, crossed_one, *weights),
        flops=6 * experts * capacity * width * inner, moved=10**7,
        scratch=scratch_for(experts * capacity),
    )
    far_one = swapped(far_one, "exp", 1)
    sums = []
    for half, back in enumerate(far):
        part = call(
            functools.partial(partial_kernel, half, columns, cap_two),
            shaped((columns, tok_count, width // 2), bf16),
            [VMEM] * 4,
            (places, gates_two, near, back),
        )
        sums.append(lax.psum_scatter(part, "exp", axis_index_groups=groups))
    answers = call(rejoin_kernel, [packet] * columns, [VMEM] * 2, (near_one, far_one))
    returned = [answers[0]] + [swapped(answers[m], "exp", 2 * m) for m in range(1, columns)]
    sum_one = call(
        combine_kernel, rows_f32, [VMEM] * (3 + columns), (hidden_one, gates_one, rows_one, *returned)
    )
    return call(
        final_kernel, shaped((2, 1, tok_count, width), bf16), [VMEM] * 4,
        (sum_one, hidden_two, *sums),
    )


def solution(mesh):
    rows = P(None, "exp", "seq", None)
    placed = (
        rows, rows, rows, rows, P(None, "exp", "seq"), P(), P(), P(),
        P("exp", None, None), P("exp", None, None), P("exp", None, None), P(), P(),
        P("exp", "seq", None), P("exp", "seq", None),
    )
    return jax.shard_map(local, mesh=mesh, in_specs=placed, out_specs=rows, check_vma=False)
```

```python
import functools

import jax
import jax.numpy as jnp
from jax import lax
from jax.experimental import pallas as pl
from jax.experimental.pallas import tpu as pltpu
from jax.sharding import PartitionSpec as P

WIN_BLOCKS = 4
NBUCK = 32
MAX_SLOTS = 2

score_scale = 0.125
epsilon = 1e-06
masked_score = -1e30

f32 = jnp.float32
bf16 = jnp.bfloat16
NT = (((1,), (1,)), ((), ()))
TN = (((0,), (0,)), ((), ()))
VMEM = pl.BlockSpec(memory_space=pltpu.VMEM)
SMEM = pl.BlockSpec(memory_space=pltpu.SMEM)
ANY = pl.BlockSpec(memory_space=pl.ANY)


def iota(shape, dim):
    return lax.broadcasted_iota(jnp.int32, shape, dim)


def shaped(shape, dtype):
    return jax.ShapeDtypeStruct(shape, dtype)


def passed_along(value, axis, steps):
    count = lax.axis_size(axis)
    return lax.ppermute(value, axis, [(source, source + steps) for source in range(count - steps)])


def swapped(value, axis, mask):
    count = lax.axis_size(axis)
    return lax.ppermute(value, axis, [(source, source ^ mask) for source in range(count)])


def merge_starts(former, latter):
    take_latter = (latter[4] > 0) & ((former[4] == 0) | (latter[3] != former[3]))
    return tuple((jnp.where(take_latter, newer, older) for older, newer in zip(former, latter)))


def latest_start(key_rows, value_rows, segments):
    tok_count, model_width = key_rows.shape
    length, index = (lax.axis_size("seq"), lax.axis_index("seq"))
    last_seg = segments[tok_count - 1]
    lead = jnp.sum((segments < last_seg).astype(jnp.int32))
    one = jnp.ones((), jnp.int32)
    found = (key_rows[lead], value_rows[lead], index * tok_count + lead, last_seg, one)
    everything = jax.tree.map(lambda part: lax.all_gather(part, "seq"), found)
    start = jax.tree.map(jnp.zeros_like, found)

    def lap(k, before):
        new = merge_starts(before, jax.tree.map(lambda part: part[k], everything))
        return jax.tree.map(lambda a, b: jnp.where(k < index, a, b), new, before)

    sink_key, sink_value, sink_pos, sink_seg, sink_has = lax.fori_loop(0, length, lap, start)
    block = jnp.zeros((2 * tok_count, model_width), key_rows.dtype)
    block = block.at[0].set(sink_key).at[tok_count].set(sink_value)
    return (block, jnp.stack([sink_pos, sink_seg, sink_has]))


def column_routes(experts, routes, new_table, old_table):
    chosen, holders = ([[], []], [[], []])
    for ref in routes:
        for c in range(2):
            slot = ref[c : c + 1, :]
            pick = sum(jnp.where(slot == s, new_table[s], 0) for s in range(experts))
            chosen[c].append(pick)
            holders[c].append(sum(jnp.where(pick == old_table[x], x, 0) for x in range(experts)))
    return (chosen, [jnp.concatenate(rows, axis=0) for rows in holders])


def attended(batch, hops, relayed, heads, sinks, bias, segs, q, k, v, rest, context):
    count = 3 if relayed else hops
    moved, sent, rest = (rest[:count], rest[count : 2 * count], rest[2 * count :])
    if sinks:
        sink_block, sink_info, rest = (rest[0], rest[1], rest[2:])
    tokens, proj = rest
    tok_count, width = tokens.shape[2:]
    window = WIN_BLOCKS * tok_count
    index = lax.axis_index("seq")
    grid = (tok_count, tok_count)

    own_seg = segs[batch]
    key_segs = [own_seg]
    if relayed:
        pairwise, across, relay = moved
        paired = index % 2 == 1
        key_segs += [jnp.where(paired, sent[0][batch : batch + 1], sent[2][batch : batch + 1])]
        key_segs.append(sent[1][batch : batch + 1, :])
    else:
        key_segs += [ref[batch : batch + 1, :] for ref in sent]
    seg_col = jnp.broadcast_to(own_seg, grid).T
    visible, spans = ([], [])
    for j, key_seg in enumerate(key_segs):
        key_seg = jnp.where(index >= j, key_seg, -1)
        distance = iota(grid, 0) - iota(grid, 1) + tok_count * j
        seen = (seg_col == key_seg) & (distance >= 0) & (distance < window)
        visible.append(jnp.where(seen, 0.0, masked_score))
        low, high = (max(0, tok_count * (j - 1) + 1), min(window, tok_count * (j + 1)) - 1)
        spans.append((distance, low.bit_length(), high.bit_length()))
    if sinks:
        position = index * tok_count + iota(grid, 0)
        seen = (seg_col == sink_info[1]) & (sink_info[2] > 0) & (position - sink_info[0] >= window)
        visible.append(jnp.where(seen & (iota(grid, 1) == 0), 0.0, masked_score))
        spans.append((None, NBUCK - 1, NBUCK - 1))
    lane = iota((tok_count, 128), 1)
    half = width // heads
    keys_at, values_at = (slice(0, tok_count), slice(tok_count, 2 * tok_count))
    for pair in range(heads // 2):
        cols = slice(128 * pair, 128 * pair + 128)
        both = q[batch, 0, :, cols] * score_scale
        even = jnp.where(lane < half, both, jnp.zeros_like(both))
        odd = jnp.where(lane < half, jnp.zeros_like(both), both)
        stacked = jnp.concatenate([even, odd], axis=0)
        blocks = [(k[batch, 0, :, cols], v[batch, 0, :, cols])]
        if relayed:
            blocks.append(tuple(
                jnp.where(paired, pairwise[at, cols], relay[at, cols])
                for at in (keys_at, values_at)
            ))
            blocks.append((across[keys_at, cols], across[values_at, cols]))
        else:
            for ref in moved:
                blocks.append((ref[keys_at, cols], ref[values_at, cols]))
        if sinks:
            blocks.append((sink_block[keys_at, cols], sink_block[values_at, cols]))
        scores = []
        for (keys, _), (distance, low, high), seen in zip(blocks, spans, visible):
            score = lax.dot_general(stacked, keys, NT, preferred_element_type=f32)
            parts = []
            for side in range(2):
                head = 2 * pair + side
                offset = jnp.full(grid, bias[head, low], f32)
                for bucket in range(low + 1, high + 1):
                    offset = jnp.where(distance >= 1 << (bucket - 1), bias[head, bucket], offset)
                parts.append(score[side * tok_count : (side + 1) * tok_count] + (offset + seen))
            scores.append(jnp.concatenate(parts, axis=0))
        peak = jnp.max(functools.reduce(jnp.maximum, scores), axis=1, keepdims=True)
        weights = [jnp.exp(score - peak) for score in scores]
        total = jnp.sum(functools.reduce(jnp.add, weights), axis=1, keepdims=True)
        scale = 1.0 / total
        mixed = sum(
            jnp.dot((weight * scale).astype(bf16), values, preferred_element_type=f32)
            for weight, (_, values) in zip(weights, blocks)
        )
        context[:, cols] = jnp.where(lane < half, mixed[:tok_count], mixed[tok_count:]).astype(bf16)
    hidden = tokens[batch, 0].astype(f32) + jnp.dot(
        context[...], proj[...], preferred_element_type=f32
    )
    mean = jnp.mean(hidden * hidden, axis=1, keepdims=True)
    return (hidden, (hidden * lax.rsqrt(mean + epsilon)).astype(bf16))


def ranks(member):
    grid = (member.shape[1], member.shape[1])
    earlier = jnp.where(iota(grid, 0) < iota(grid, 1), 1.0, 0.0).astype(bf16)
    return jnp.dot(member.astype(bf16), earlier, preferred_element_type=f32).astype(jnp.int32)


def attend_column_kernel(options, experts, bias, new_table, old_table, segs, q, k, v, *rest):
    routes, rest = (rest[: experts // 2], rest[experts // 2 :])
    inputs, (hidden_out, normed_out, places_out, context) = (rest[:-4], rest[-4:])
    hidden, normed = attended(1, *options, bias, segs, q, k, v, inputs, context)
    hidden_out[...] = hidden
    normed_out[...] = normed
    me = lax.axis_index("exp")
    _, holders = column_routes(experts, routes, new_table, old_table)
    member = jnp.concatenate(
        [jnp.where((holders[0] == at) | (holders[1] == at), 1.0, 0.0) for at in (me, me ^ 1)],
        axis=0,
    )
    places_out[...] = jnp.where(member > 0.5, ranks(member), -1)


def attend_direct_kernel(options, experts, cap, bias, old_table, routes, router_t, segs, q, k, v, *rest):
    layers = experts // 2
    inputs, rest = (rest[: -4 - layers], rest[-4 - layers :])
    outgoing, (hidden_out, gates_out, rows_out, context) = (rest[:layers], rest[layers:])
    hidden, normed = attended(0, *options, bias, segs, q, k, v, inputs, context)
    hidden_out[...] = hidden
    tok_count = hidden.shape[0]
    chosen = [routes[c : c + 1, :] for c in range(2)]
    holders = [sum(jnp.where(c == old_table[x], x, 0) for x in range(experts)) for c in chosen]
    expert = iota((experts, tok_count), 0)
    packet = expert ^ lax.axis_index("exp")
    member = jnp.where((packet == holders[0]) | (packet == holders[1]), 1.0, 0.0)
    place = ranks(member) + expert * cap
    rows = [
        jnp.sum(jnp.where(packet == holder, place, 0), axis=0, keepdims=True) for holder in holders
    ]
    rows_out[...] = jnp.concatenate(rows, axis=0)
    logits = lax.dot_general(router_t[...], normed, NT, preferred_element_type=f32)
    picked = [jnp.sum(jnp.where(expert == c, logits, 0.0), axis=0, keepdims=True) for c in chosen]
    first = jax.nn.sigmoid(picked[0] - picked[1])
    gates_out[...] = jnp.concatenate([first, 1.0 - first], axis=0)
    at = iota((experts * cap, tok_count), 0)
    plan = jnp.where((at == rows[0]) | (at == rows[1]), 1.0, 0.0).astype(bf16)
    packed = jnp.dot(plan, normed, preferred_element_type=f32)
    for m, ref in enumerate(outgoing):
        ref[...] = packed[2 * m * cap : 2 * (m + 1) * cap].astype(bf16)


def picked_rows(members, cap, first_row, places, blocks):
    at = iota((len(members) * cap, blocks[0].shape[0]), 0)
    plans = []
    for n, m in enumerate(members):
        place = places[first_row + m : first_row + m + 1, :]
        place = jnp.where(place >= 0, place + n * cap, -1)
        plans.append(jnp.where(at == place, 1.0, 0.0))
    plan = jnp.concatenate(plans, axis=1).astype(bf16)
    rows = jnp.concatenate([block[...] for block in blocks], axis=0)
    return (jnp.dot(plan, rows, preferred_element_type=f32).astype(bf16), rows)


def pack_kernel(members, cap, columns, places, *rest):
    blocks, out = (rest[:-1], rest[-1])
    out[...], _ = picked_rows(members, cap, columns, places, blocks)


def numbers_kernel(routes, segs, routes_out, segs_out):
    routes_out[...] = routes[...]
    segs_out[...] = segs[:, 0]


def collect_kernel(*refs):
    count = len(refs) // 2
    for ref, out in zip(refs[:count], refs[count:]):
        out[...] = ref[...]


def stack_kernel(k, v, across, out, across_out):
    del across, across_out
    tok_count = k.shape[2]
    out[:tok_count, :] = k[0, 0]
    out[tok_count:, :] = v[0, 0]


def crossing_kernel(*refs):
    packets, out = (refs[:-1], refs[-1])
    cap = packets[0].shape[0] // 2
    parts = [ref[...].astype(f32)[cap:] for ref in packets]
    out[...] = jnp.concatenate(parts, axis=0).astype(bf16)


def expert_rows(rows, weights, active, stores):
    gate, up, down = weights
    inner, width = down.shape[1:]
    x = rows[...]
    for begin in range(0, inner, 256):
        span = slice(begin, min(inner, begin + 256))
        gate_part = jnp.dot(x, gate[0, :, span], preferred_element_type=f32)
        up_part = jnp.dot(x, up[0, :, span], preferred_element_type=f32)
        active[:, span] = (jax.nn.gelu(gate_part, approximate=True) * up_part).astype(bf16)
    for begin in range(0, width, 256):
        span = slice(begin, begin + 256)
        part = jnp.dot(active[...], down[0, :, span], preferred_element_type=f32)
        stores(span, part)


def near_kernel(columns, experts, cap, new_table, old_table, places, router_t, *rest):
    blocks, rest = (rest[:columns], rest[columns:])
    routes, rest = (rest[:columns], rest[columns:])
    weights, (out, gates_out, rows, active) = (rest[:3], rest[3:])

    def stores(span, value):
        out[:, span] = value.astype(bf16)

    rows[...], tokens = picked_rows(range(columns), cap, 0, places, blocks)
    logits = lax.dot_general(router_t[...], tokens, NT, preferred_element_type=f32)
    chosen, holders = column_routes(experts, routes, new_table, old_table)
    chosen = [jnp.concatenate(picks, axis=1) for picks in chosen]
    expert = iota(logits.shape, 0)
    picked = [
        jnp.sum(jnp.where(expert == pick, logits, 0.0), axis=0, keepdims=True) for pick in chosen
    ]
    first = jax.nn.sigmoid(picked[0] - picked[1])
    tok_count = places.shape[1]
    first = jnp.concatenate(
        [first[:, m * tok_count : (m + 1) * tok_count] for m in range(columns)], axis=0
    )
    me = lax.axis_index("exp")
    gates_out[...] = jnp.concatenate(
        [
            jnp.where(holders[0] == at, first, 0.0) + jnp.where(holders[1] == at, 1.0 - first, 0.0)
            for at in (me, me ^ 1)
        ],
        axis=0,
    )
    expert_rows(rows, weights, active, stores)


def far_kernel(low_in, high_in, *rest):
    weights, (low_out, high_out, rows, active) = (rest[:3], rest[3:])
    part = low_in.shape[0]

    def stores(span, value):
        low_out[:, span] = value[:part].astype(bf16)
        high_out[:, span] = value[part:].astype(bf16)

    rows[:part, :] = low_in[...]
    rows[part:, :] = high_in[...]
    expert_rows(rows, weights, active, stores)


def direct_kernel(layers, *refs):
    packets, crossed, weights = (refs[:layers], refs[layers], refs[layers + 1 : layers + 4])
    near, far, rows, active = refs[layers + 4 :]
    cap = packets[0].shape[0] // 2
    half = layers * cap

    def stores(span, value):
        near[:, span] = value[:half].astype(bf16)
        far[:, span] = value[half:].astype(bf16)

    parts = [ref[...].astype(f32)[:cap] for ref in packets]
    rows[:half, :] = jnp.concatenate(parts, axis=0).astype(bf16)
    rows[half:, :] = crossed[...]
    expert_rows(rows, weights, active, stores)


def rejoin_kernel(near, far, *outs):
    cap = outs[0].shape[0] // 2
    both = [ref[...].astype(f32) for ref in (near, far)]
    for m, out in enumerate(outs):
        parts = [each[m * cap : (m + 1) * cap] for each in both]
        out[...] = jnp.concatenate(parts, axis=0).astype(bf16)


def combine_kernel(hidden, gates, rows, *rest):
    packets, out = (rest[:-1], rest[-1])
    cap = packets[0].shape[0]
    at = iota((len(packets) * cap, hidden.shape[0]), 0)
    spread = jnp.where(at == rows[0:1, :], gates[0:1, :], 0.0)
    spread = spread + jnp.where(at == rows[1:2, :], gates[1:2, :], 0.0)
    coarse = spread.astype(bf16)
    fine = (spread - coarse.astype(f32)).astype(bf16)
    values = jnp.concatenate([ref[...].astype(f32) for ref in packets], axis=0).astype(bf16)
    total = hidden[...]
    for half in (coarse, fine):
        total = total + lax.dot_general(half, values, TN, preferred_element_type=f32)
    out[...] = total


def partial_kernel(members, cap, columns, places, gates, near, far, *outs):
    at = iota((cap, places.shape[1]), 0)
    for n, m in enumerate(members):
        total = None
        near_rows = near[m * cap : (m + 1) * cap, :]
        far_rows = far[n * cap : (n + 1) * cap, :]
        for values, row in ((near_rows, m), (far_rows, columns + m)):
            spread = jnp.where(at == places[row : row + 1, :], gates[row : row + 1, :], 0.0)
            coarse = spread.astype(bf16)
            fine = (spread - coarse.astype(f32)).astype(bf16)
            for half in (coarse, fine):
                term = lax.dot_general(half, values, TN, preferred_element_type=f32)
                total = term if total is None else total + term
        outs[n][...] = total.astype(outs[n].dtype)


def fold_kernel(own, *rest):
    total = own[...]
    for ref in rest[:-1]:
        total = total + ref[...].astype(f32)
    rest[-1][...] = total.astype(rest[-1].dtype)


def final_kernel(one, *rest):
    out = rest[-1]
    out[0, 0] = one[...].astype(bf16)
    total = rest[0][...]
    for ref in rest[1:-1]:
        total = total + ref[...].astype(f32)
    out[1, 0] = total.astype(bf16)


def local(
    tokens, queries, key_rows, value_rows, segments, bias_table, out_proj, router,
    gate_weight, up_weight, down_weight, old_table, new_table, routes_one, routes_two,
):
    tok_count, width = tokens.shape[2:]
    heads = bias_table.shape[0]
    experts = router.shape[1]
    columns = experts // 2
    inner = gate_weight.shape[2]
    seq_size = lax.axis_size("seq")
    seq_len = tok_count * seq_size
    capacity = tok_count * 2 * 5 // (4 * experts)
    longest = seq_len // 2
    hops = min(WIN_BLOCKS, (longest - 1 + tok_count - 1) // tok_count)
    relayed = seq_size == 4 and hops == 2
    sinks = seq_len > WIN_BLOCKS * tok_count
    weights = (gate_weight, up_weight, down_weight)
    router_t = router.T
    lower, upper = (range(columns // 2), range(columns // 2, columns))
    rows_bf16 = shaped((tok_count, width), bf16)
    rows_f32 = shaped((tok_count, width), f32)
    cap_two = capacity * MAX_SLOTS
    slots = columns * cap_two
    part_two = slots // 2
    packet = shaped((2 * capacity, width), bf16)
    latest = []

    def call(kernel, outs, ins, args, scratch=(), after=(), aliases=None):
        after = [*after, *latest]
        out_specs = jax.tree.map(lambda _: VMEM, outs)
        if aliases:
            out_specs = (VMEM, ANY)

        def body(*refs):
            kernel(*refs[: len(args)], *refs[len(args) + len(after) :])

        made = pl.pallas_call(
            body,
            out_shape=outs,
            in_specs=ins + [ANY] * len(after),
            out_specs=out_specs,
            scratch_shapes=list(scratch),
            input_output_aliases=aliases or {},
            compiler_params=pltpu.CompilerParams(vmem_limit_bytes=24 * 2**20),
            cost_estimate=pl.CostEstimate(flops=1, bytes_accessed=1, transcendentals=0),
        )(*args, *after)
        latest[:] = jax.tree.leaves(made)[:1]
        return made

    def multicast(own):
        blocks = {0: own}
        bit = columns // 2
        while bit:
            for m in sorted(blocks):
                blocks[m | bit] = swapped(blocks[m], "exp", 2 * bit)
            bit //= 2
        return blocks

    def chained(moving):
        moved = []
        for _ in range(hops):
            moving = passed_along(moving, "seq", 1)
            moved.append(moving)
        return moved

    def options(batch):
        extra = []
        if sinks:
            extra = latest_start(key_rows[batch, 0], value_rows[batch, 0], segments[batch, 0])
        return ((hops, relayed, heads, sinks), extra)

    def attend_column(moved):
        settings, extra = options(1)
        return call(
            functools.partial(attend_column_kernel, settings, experts),
            (rows_f32, rows_bf16, shaped((2 * columns, tok_count), jnp.int32)),
            [SMEM] * 3 + [VMEM] * (4 + columns + 2 * len(moved)) + ([VMEM, SMEM] if sinks else [])
            + [VMEM] * 2,
            (bias_table, new_table, old_table, segments, queries, key_rows, value_rows, *routes,
             *moved, *sent, *extra, tokens, out_proj),
            scratch=[pltpu.VMEM((tok_count, width), bf16)],
        )

    def attend_direct(moved):
        settings, extra = options(0)
        return call(
            functools.partial(attend_direct_kernel, settings, experts, capacity),
            (*[packet] * columns, rows_f32, shaped((2, tok_count), f32),
             shaped((2, tok_count), jnp.int32)),
            [SMEM] * 2 + [VMEM] * (6 + 2 * len(moved)) + ([VMEM, SMEM] if sinks else [])
            + [VMEM] * 2,
            (bias_table, old_table, routes_one[0].T, router_t, segments, queries, key_rows,
             value_rows, *moved, *sent, *extra, tokens, out_proj),
            scratch=[pltpu.VMEM((tok_count, width), bf16)],
        )

    def scratch_for(slots):
        return (pltpu.VMEM((slots, width), bf16), pltpu.VMEM((slots, inner), bf16))

    def pack(members, places, blocks):
        return call(
            functools.partial(pack_kernel, members, cap_two, columns),
            shaped((part_two, width), bf16),
            [VMEM] * (1 + len(members)),
            (places, *(blocks[m] for m in members)),
        )

    def partial(members, far):
        parts = call(
            functools.partial(partial_kernel, members, cap_two, columns),
            tuple(rows_bf16 if m % 2 else rows_f32 for m in members),
            [VMEM] * 4,
            (places, gates_two, near, far),
        )
        for m, value in zip(members, parts):
            totals.setdefault(m, []).insert(0, value)

    def send_down(members):
        for m in sorted(members, key=lambda m: (m & -m, -m)):
            parts = totals[m]
            value = parts[0]
            if len(parts) > 1:
                value = call(fold_kernel, rows_bf16, [VMEM] * len(parts), parts)
            totals.setdefault(m & (m - 1), []).append(swapped(value, "exp", 2 * (m & -m)))

    stacked = jnp.concatenate([key_rows[1, 0], value_rows[1, 0]], axis=0)
    first_hop = swapped(stacked, "seq", 1) if relayed else passed_along(stacked, "seq", 1)
    own_routes, own_segs = call(
        numbers_kernel,
        (shaped((2, tok_count), jnp.int32),) * 2,
        [VMEM] * 2,
        (routes_two[0].T, segments),
        after=[first_hop],
    )
    routes = multicast(own_routes)
    routes = [routes[m] for m in range(columns)]
    if relayed:
        sent = [swapped(own_segs, "seq", mask) for mask in (1, 2, 3)]
        across = swapped(stacked, "seq", 2)
    else:
        sent = chained(own_segs)
        across = first_hop
    count = len(sent)
    *routes, latest_seg = call(
        collect_kernel,
        tuple(shaped((2, tok_count), jnp.int32) for _ in range(columns + 1)),
        [VMEM] * (columns + 1),
        (*routes, sent[-1]),
        after=sent[:-1],
    )
    sent = [*sent[: count - 1], latest_seg]
    stacked, across = call(
        stack_kernel, (shaped((2 * tok_count, width), bf16),) * 2, [VMEM] * 2 + [ANY],
        (key_rows, value_rows, across), aliases={2: 1},
    )
    if relayed:
        moved_one = [
            swapped(stacked, "seq", 1),
            swapped(stacked, "seq", 2),
            lax.ppermute(stacked, "seq", [(0, 0), (1, 2), (2, 1), (3, 3)]),
        ]
        moved_two = [first_hop, across, swapped(across, "seq", 1)]
    else:
        moved_one, moved_two = (chained(stacked), [across])
        while len(moved_two) < hops:
            moved_two.append(passed_along(moved_two[-1], "seq", 1))
    hidden_two, normed_two, places = attend_column(moved_two)
    blocks = multicast(normed_two)
    low_in = swapped(pack(lower, places, blocks), "exp", 1)
    *packets, hidden_one, gates_one, rows_one = attend_direct(moved_one)
    arrived = [packets[0]] + [swapped(packets[m], "exp", 2 * m) for m in range(1, columns)]
    high_in = swapped(pack(upper, places, blocks), "exp", 1)
    near, gates_two = call(
        functools.partial(near_kernel, columns, experts, cap_two),
        (shaped((slots, width), bf16), shaped((2 * columns, tok_count), f32)),
        [SMEM] * 2 + [VMEM] * (5 + 2 * columns),
        (new_table, old_table, places, router_t, *(blocks[m] for m in range(columns)), *routes,
         *weights),
        scratch=scratch_for(slots),
    )
    crossing = call(
        crossing_kernel, shaped((columns * capacity, width), bf16), [VMEM] * columns, arrived
    )
    crossed_one = swapped(crossing, "exp", 1)
    low_out, high_out = call(
        far_kernel,
        (shaped((part_two, width), bf16),) * 2,
        [VMEM] * 5,
        (low_in, high_in, *weights),
        scratch=scratch_for(slots),
    )
    high_far, low_far = (swapped(high_out, "exp", 1), swapped(low_out, "exp", 1))
    near_one, far_one = call(
        functools.partial(direct_kernel, columns),
        (shaped((columns * capacity, width), bf16),) * 2,
        [VMEM] * (4 + columns),
        (*arrived, crossed_one, *weights),
        scratch=scratch_for(experts * capacity),
    )
    far_one = swapped(far_one, "exp", 1)
    totals = {}
    partial(upper, high_far)
    send_down(m for m in upper if m % 2)
    partial(lower, low_far)
    send_down(m for m in upper if m % 2 == 0)
    send_down(m for m in lower if m)
    answers = call(rejoin_kernel, [packet] * columns, [VMEM] * 2, (near_one, far_one))
    returned = [answers[0]] + [swapped(answers[m], "exp", 2 * m) for m in range(1, columns)]
    sum_one = call(
        combine_kernel, rows_f32, [VMEM] * (3 + columns), (hidden_one, gates_one, rows_one, *returned)
    )
    ends = (sum_one, hidden_two, *totals[0])
    return call(
        final_kernel, shaped((2, 1, tok_count, width), bf16), [VMEM] * len(ends), ends
    )


def solution(mesh):
    rows = P(None, "exp", "seq", None)
    placed = (
        rows, rows, rows, rows, P(None, "exp", "seq"), P(), P(), P(),
        P("exp", None, None), P("exp", None, None), P("exp", None, None), P(), P(),
        P("exp", "seq", None), P("exp", "seq", None),
    )
    return jax.shard_map(local, mesh=mesh, in_specs=placed, out_specs=rows, check_vma=False)
```

```python
import functools

import jax
import jax.numpy as jnp
from jax import lax
from jax.experimental import pallas as pl
from jax.experimental.pallas import tpu as pltpu
from jax.sharding import PartitionSpec as P

WIN_BLOCKS = 4
NBUCK = 32
MAX_SLOTS = 2

score_scale = 0.125
epsilon = 1e-06
masked_score = -1e30

f32 = jnp.float32
bf16 = jnp.bfloat16
NT = (((1,), (1,)), ((), ()))
TN = (((0,), (0,)), ((), ()))
VMEM = pl.BlockSpec(memory_space=pltpu.VMEM)
SMEM = pl.BlockSpec(memory_space=pltpu.SMEM)
ANY = pl.BlockSpec(memory_space=pl.ANY)


def iota(shape, dim):
    return lax.broadcasted_iota(jnp.int32, shape, dim)


def shaped(shape, dtype):
    return jax.ShapeDtypeStruct(shape, dtype)


def passed_along(value, axis, steps):
    count = lax.axis_size(axis)
    return lax.ppermute(value, axis, [(source, source + steps) for source in range(count - steps)])


def swapped(value, axis, mask):
    count = lax.axis_size(axis)
    return lax.ppermute(value, axis, [(source, source ^ mask) for source in range(count)])


def merge_starts(former, latter):
    take_latter = (latter[4] > 0) & ((former[4] == 0) | (latter[3] != former[3]))
    return tuple((jnp.where(take_latter, newer, older) for older, newer in zip(former, latter)))


def latest_start(key_rows, value_rows, segments):
    tok_count, model_width = key_rows.shape
    length, index = (lax.axis_size("seq"), lax.axis_index("seq"))
    last_seg = segments[tok_count - 1]
    lead = jnp.sum((segments < last_seg).astype(jnp.int32))
    one = jnp.ones((), jnp.int32)
    found = (key_rows[lead], value_rows[lead], index * tok_count + lead, last_seg, one)
    everything = jax.tree.map(lambda part: lax.all_gather(part, "seq"), found)
    start = jax.tree.map(jnp.zeros_like, found)

    def lap(k, before):
        new = merge_starts(before, jax.tree.map(lambda part: part[k], everything))
        return jax.tree.map(lambda a, b: jnp.where(k < index, a, b), new, before)

    sink_key, sink_value, sink_pos, sink_seg, sink_has = lax.fori_loop(0, length, lap, start)
    block = jnp.zeros((2 * tok_count, model_width), key_rows.dtype)
    block = block.at[0].set(sink_key).at[tok_count].set(sink_value)
    return (block, jnp.stack([sink_pos, sink_seg, sink_has]))


def column_routes(experts, routes, new_table, old_table):
    chosen, holders = ([[], []], [[], []])
    for ref in routes:
        for c in range(2):
            slot = ref[c : c + 1, :]
            pick = sum(jnp.where(slot == s, new_table[s], 0) for s in range(experts))
            chosen[c].append(pick)
            holders[c].append(sum(jnp.where(pick == old_table[x], x, 0) for x in range(experts)))
    return (chosen, [jnp.concatenate(rows, axis=0) for rows in holders])


def attended(batch, hops, relayed, heads, sinks, bias, segs, q, k, v, rest, context):
    count = 3 if relayed else hops
    moved, sent, rest = (rest[:count], rest[count : 2 * count], rest[2 * count :])
    if sinks:
        sink_block, sink_info, rest = (rest[0], rest[1], rest[2:])
    tokens, proj = rest
    tok_count, width = tokens.shape[2:]
    window = WIN_BLOCKS * tok_count
    index = lax.axis_index("seq")
    grid = (tok_count, tok_count)

    own_seg = segs[batch]
    key_segs = [own_seg]
    if relayed:
        pairwise, across, relay = moved
        paired = index % 2 == 1
        key_segs += [jnp.where(paired, sent[0][batch : batch + 1], sent[2][batch : batch + 1])]
        key_segs.append(sent[1][batch : batch + 1, :])
    else:
        key_segs += [ref[batch : batch + 1, :] for ref in sent]
    seg_col = jnp.broadcast_to(own_seg, grid).T
    visible, spans = ([], [])
    for j, key_seg in enumerate(key_segs):
        key_seg = jnp.where(index >= j, key_seg, -1)
        distance = iota(grid, 0) - iota(grid, 1) + tok_count * j
        seen = (seg_col == key_seg) & (distance >= 0) & (distance < window)
        visible.append(jnp.where(seen, 0.0, masked_score))
        low, high = (max(0, tok_count * (j - 1) + 1), min(window, tok_count * (j + 1)) - 1)
        spans.append((distance, low.bit_length(), high.bit_length()))
    if sinks:
        position = index * tok_count + iota(grid, 0)
        seen = (seg_col == sink_info[1]) & (sink_info[2] > 0) & (position - sink_info[0] >= window)
        visible.append(jnp.where(seen & (iota(grid, 1) == 0), 0.0, masked_score))
        spans.append((None, NBUCK - 1, NBUCK - 1))
    lane = iota((tok_count, 128), 1)
    half = width // heads
    keys_at, values_at = (slice(0, tok_count), slice(tok_count, 2 * tok_count))
    for pair in range(heads // 2):
        cols = slice(128 * pair, 128 * pair + 128)
        both = q[batch, 0, :, cols] * score_scale
        even = jnp.where(lane < half, both, jnp.zeros_like(both))
        odd = jnp.where(lane < half, jnp.zeros_like(both), both)
        stacked = jnp.concatenate([even, odd], axis=0)
        blocks = [(k[batch, 0, :, cols], v[batch, 0, :, cols])]
        if relayed:
            blocks.append(tuple(
                jnp.where(paired, pairwise[at, cols], relay[at, cols])
                for at in (keys_at, values_at)
            ))
            blocks.append((across[keys_at, cols], across[values_at, cols]))
        else:
            for ref in moved:
                blocks.append((ref[keys_at, cols], ref[values_at, cols]))
        if sinks:
            blocks.append((sink_block[keys_at, cols], sink_block[values_at, cols]))
        scores = []
        for (keys, _), (distance, low, high), seen in zip(blocks, spans, visible):
            score = lax.dot_general(stacked, keys, NT, preferred_element_type=f32)
            parts = []
            for side in range(2):
                head = 2 * pair + side
                offset = jnp.full(grid, bias[head, low], f32)
                for bucket in range(low + 1, high + 1):
                    offset = jnp.where(distance >= 1 << (bucket - 1), bias[head, bucket], offset)
                parts.append(score[side * tok_count : (side + 1) * tok_count] + (offset + seen))
            scores.append(jnp.concatenate(parts, axis=0))
        peak = jnp.max(functools.reduce(jnp.maximum, scores), axis=1, keepdims=True)
        weights = [jnp.exp(score - peak) for score in scores]
        total = jnp.sum(functools.reduce(jnp.add, weights), axis=1, keepdims=True)
        scale = 1.0 / total
        mixed = sum(
            jnp.dot((weight * scale).astype(bf16), values, preferred_element_type=f32)
            for weight, (_, values) in zip(weights, blocks)
        )
        context[:, cols] = jnp.where(lane < half, mixed[:tok_count], mixed[tok_count:]).astype(bf16)
    hidden = tokens[batch, 0].astype(f32) + jnp.dot(
        context[...], proj[...], preferred_element_type=f32
    )
    mean = jnp.mean(hidden * hidden, axis=1, keepdims=True)
    return (hidden, (hidden * lax.rsqrt(mean + epsilon)).astype(bf16))


def ranks(member):
    grid = (member.shape[1], member.shape[1])
    earlier = jnp.where(iota(grid, 0) < iota(grid, 1), 1.0, 0.0).astype(bf16)
    return jnp.dot(member.astype(bf16), earlier, preferred_element_type=f32).astype(jnp.int32)


def attend_column_kernel(options, experts, bias, new_table, old_table, segs, q, k, v, *rest):
    routes, rest = (rest[: experts // 2], rest[experts // 2 :])
    inputs, (hidden_out, normed_out, places_out, context) = (rest[:-4], rest[-4:])
    hidden, normed = attended(1, *options, bias, segs, q, k, v, inputs, context)
    hidden_out[...] = hidden
    normed_out[...] = normed
    me = lax.axis_index("exp")
    _, holders = column_routes(experts, routes, new_table, old_table)
    member = jnp.concatenate(
        [jnp.where((holders[0] == at) | (holders[1] == at), 1.0, 0.0) for at in (me, me ^ 1)],
        axis=0,
    )
    places_out[...] = jnp.where(member > 0.5, ranks(member), -1)


def attend_direct_kernel(options, experts, cap, bias, old_table, routes, router_t, segs, q, k, v, *rest):
    layers = experts // 2
    inputs, rest = (rest[: -4 - layers], rest[-4 - layers :])
    outgoing, (hidden_out, gates_out, rows_out, context) = (rest[:layers], rest[layers:])
    hidden, normed = attended(0, *options, bias, segs, q, k, v, inputs, context)
    hidden_out[...] = hidden
    tok_count = hidden.shape[0]
    chosen = [routes[c : c + 1, :] for c in range(2)]
    holders = [sum(jnp.where(c == old_table[x], x, 0) for x in range(experts)) for c in chosen]
    expert = iota((experts, tok_count), 0)
    packet = expert ^ lax.axis_index("exp")
    member = jnp.where((packet == holders[0]) | (packet == holders[1]), 1.0, 0.0)
    place = ranks(member) + expert * cap
    rows = [
        jnp.sum(jnp.where(packet == holder, place, 0), axis=0, keepdims=True) for holder in holders
    ]
    rows_out[...] = jnp.concatenate(rows, axis=0)
    logits = lax.dot_general(router_t[...], normed, NT, preferred_element_type=f32)
    picked = [jnp.sum(jnp.where(expert == c, logits, 0.0), axis=0, keepdims=True) for c in chosen]
    first = jax.nn.sigmoid(picked[0] - picked[1])
    gates_out[...] = jnp.concatenate([first, 1.0 - first], axis=0)
    at = iota((experts * cap, tok_count), 0)
    plan = jnp.where((at == rows[0]) | (at == rows[1]), 1.0, 0.0).astype(bf16)
    packed = jnp.dot(plan, normed, preferred_element_type=f32)
    for m, ref in enumerate(outgoing):
        ref[...] = packed[2 * m * cap : 2 * (m + 1) * cap].astype(bf16)


def picked_rows(members, cap, first_row, places, blocks):
    at = iota((len(members) * cap, blocks[0].shape[0]), 0)
    plans = []
    for n, m in enumerate(members):
        place = places[first_row + m : first_row + m + 1, :]
        place = jnp.where(place >= 0, place + n * cap, -1)
        plans.append(jnp.where(at == place, 1.0, 0.0))
    plan = jnp.concatenate(plans, axis=1).astype(bf16)
    rows = jnp.concatenate([block[...] for block in blocks], axis=0)
    return (jnp.dot(plan, rows, preferred_element_type=f32).astype(bf16), rows)


def pack_kernel(members, cap, columns, places, *rest):
    blocks, out = (rest[:-1], rest[-1])
    out[...], _ = picked_rows(members, cap, columns, places, blocks)


def numbers_kernel(routes, segs, routes_out, segs_out):
    routes_out[...] = routes[...]
    segs_out[...] = segs[:, 0]


def collect_kernel(new_table, old_table, *refs):
    del new_table, old_table
    count = len(refs) // 2
    for ref, out in zip(refs[:count], refs[count:]):
        out[...] = ref[...]


def stack_kernel(k, v, across, out, across_out):
    del across, across_out
    tok_count = k.shape[2]
    out[:tok_count, :] = k[1, 0]
    out[tok_count:, :] = v[1, 0]


def crossing_kernel(*refs):
    packets, out = (refs[:-1], refs[-1])
    cap = packets[0].shape[0] // 2
    parts = [ref[...].astype(f32)[cap:] for ref in packets]
    out[...] = jnp.concatenate(parts, axis=0).astype(bf16)


def expert_rows(rows, weights, active, stores):
    gate, up, down = weights
    inner, width = down.shape[1:]
    x = rows[...]
    for begin in range(0, inner, 256):
        span = slice(begin, min(inner, begin + 256))
        gate_part = jnp.dot(x, gate[0, :, span], preferred_element_type=f32)
        up_part = jnp.dot(x, up[0, :, span], preferred_element_type=f32)
        active[:, span] = (jax.nn.gelu(gate_part, approximate=True) * up_part).astype(bf16)
    for begin in range(0, width, 256):
        span = slice(begin, begin + 256)
        part = jnp.dot(active[...], down[0, :, span], preferred_element_type=f32)
        stores(span, part)


def near_kernel(columns, experts, cap, new_table, old_table, places, router_t, *rest):
    blocks, rest = (rest[:columns], rest[columns:])
    routes, rest = (rest[:columns], rest[columns:])
    weights, (_, out, gates_out, _, rows, active) = (rest[:3], rest[3:])

    def stores(span, value):
        out[:, span] = value.astype(bf16)

    rows[...], tokens = picked_rows(range(columns), cap, 0, places, blocks)
    logits = lax.dot_general(router_t[...], tokens, NT, preferred_element_type=f32)
    chosen, holders = column_routes(experts, routes, new_table, old_table)
    chosen = [jnp.concatenate(picks, axis=1) for picks in chosen]
    expert = iota(logits.shape, 0)
    picked = [
        jnp.sum(jnp.where(expert == pick, logits, 0.0), axis=0, keepdims=True) for pick in chosen
    ]
    first = jax.nn.sigmoid(picked[0] - picked[1])
    tok_count = places.shape[1]
    first = jnp.concatenate(
        [first[:, m * tok_count : (m + 1) * tok_count] for m in range(columns)], axis=0
    )
    me = lax.axis_index("exp")
    gates_out[...] = jnp.concatenate(
        [
            jnp.where(holders[0] == at, first, 0.0) + jnp.where(holders[1] == at, 1.0 - first, 0.0)
            for at in (me, me ^ 1)
        ],
        axis=0,
    )
    expert_rows(rows, weights, active, stores)


def far_kernel(low_in, high_in, *rest):
    weights, (low_out, high_out, rows, active) = (rest[:3], rest[3:])
    part = low_in.shape[0]

    def stores(span, value):
        low_out[:, span] = value[:part].astype(bf16)
        high_out[:, span] = value[part:].astype(bf16)

    rows[:part, :] = low_in[...]
    rows[part:, :] = high_in[...]
    expert_rows(rows, weights, active, stores)


def direct_kernel(layers, *refs):
    packets, crossed, weights = (refs[:layers], refs[layers], refs[layers + 1 : layers + 4])
    near, far, rows, active = refs[layers + 4 :]
    cap = packets[0].shape[0] // 2
    half = layers * cap

    def stores(span, value):
        near[:, span] = value[:half].astype(bf16)
        far[:, span] = value[half:].astype(bf16)

    parts = [ref[...].astype(f32)[:cap] for ref in packets]
    rows[:half, :] = jnp.concatenate(parts, axis=0).astype(bf16)
    rows[half:, :] = crossed[...]
    expert_rows(rows, weights, active, stores)


def rejoin_kernel(near, far, *outs):
    cap = outs[0].shape[0] // 2
    both = [ref[...].astype(f32) for ref in (near, far)]
    for m, out in enumerate(outs):
        parts = [each[m * cap : (m + 1) * cap] for each in both]
        out[...] = jnp.concatenate(parts, axis=0).astype(bf16)


def combine_kernel(hidden, gates, rows, *rest):
    packets, out = (rest[:-1], rest[-1])
    cap = packets[0].shape[0]
    at = iota((len(packets) * cap, hidden.shape[0]), 0)
    spread = jnp.where(at == rows[0:1, :], gates[0:1, :], 0.0)
    spread = spread + jnp.where(at == rows[1:2, :], gates[1:2, :], 0.0)
    coarse = spread.astype(bf16)
    fine = (spread - coarse.astype(f32)).astype(bf16)
    values = jnp.concatenate([ref[...].astype(f32) for ref in packets], axis=0).astype(bf16)
    total = hidden[...]
    for half in (coarse, fine):
        total = total + lax.dot_general(half, values, TN, preferred_element_type=f32)
    out[...] = total


def partial_kernel(members, cap, columns, places, gates, near, far, *outs):
    at = iota((cap, places.shape[1]), 0)
    for n, m in enumerate(members):
        total = None
        near_rows = near[m * cap : (m + 1) * cap, :]
        far_rows = far[n * cap : (n + 1) * cap, :]
        for values, row in ((near_rows, m), (far_rows, columns + m)):
            spread = jnp.where(at == places[row : row + 1, :], gates[row : row + 1, :], 0.0)
            coarse = spread.astype(bf16)
            fine = (spread - coarse.astype(f32)).astype(bf16)
            for half in (coarse, fine):
                term = lax.dot_general(half, values, TN, preferred_element_type=f32)
                total = term if total is None else total + term
        outs[n][...] = total.astype(outs[n].dtype)


def fold_kernel(own, *rest):
    total = own[...]
    for ref in rest[:-1]:
        total = total + ref[...].astype(f32)
    rest[-1][...] = total.astype(rest[-1].dtype)


def final_kernel(one, *rest):
    out = rest[-1]
    out[0, 0] = one[...].astype(bf16)
    total = rest[0][...]
    for ref in rest[1:-1]:
        total = total + ref[...].astype(f32)
    out[1, 0] = total.astype(bf16)


def local(
    tokens, queries, key_rows, value_rows, segments, bias_table, out_proj, router,
    gate_weight, up_weight, down_weight, old_table, new_table, routes_one, routes_two,
):
    tok_count, width = tokens.shape[2:]
    heads = bias_table.shape[0]
    experts = router.shape[1]
    columns = experts // 2
    inner = gate_weight.shape[2]
    seq_size = lax.axis_size("seq")
    seq_len = tok_count * seq_size
    capacity = tok_count * 2 * 5 // (4 * experts)
    longest = seq_len // 2
    hops = min(WIN_BLOCKS, (longest - 1 + tok_count - 1) // tok_count)
    relayed = seq_size == 4 and hops == 2
    sinks = seq_len > WIN_BLOCKS * tok_count
    weights = (gate_weight, up_weight, down_weight)
    router_t = router.T
    lower, upper = (range(columns // 2), range(columns // 2, columns))
    rows_bf16 = shaped((tok_count, width), bf16)
    rows_f32 = shaped((tok_count, width), f32)
    cap_two = capacity * MAX_SLOTS
    slots = columns * cap_two
    part_two = slots // 2
    packet = shaped((2 * capacity, width), bf16)
    latest = []

    def call(kernel, outs, ins, args, scratch=(), after=(), aliases=None, work=1):
        after = [*after, *latest]
        out_specs = jax.tree.map(lambda _: VMEM, outs)
        if aliases:
            out_specs = tuple(ANY if n in aliases.values() else VMEM for n in range(len(outs)))

        def body(*refs):
            kernel(*refs[: len(args)], *refs[len(args) + len(after) :])

        made = pl.pallas_call(
            body,
            out_shape=outs,
            in_specs=ins + [ANY] * len(after),
            out_specs=out_specs,
            scratch_shapes=list(scratch),
            input_output_aliases=aliases or {},
            compiler_params=pltpu.CompilerParams(vmem_limit_bytes=24 * 2**20),
            cost_estimate=pl.CostEstimate(flops=work, bytes_accessed=1, transcendentals=0),
        )(*args, *after)
        latest[:] = jax.tree.leaves(made)[:1]
        return made

    def multicast(own):
        blocks = {0: own}
        bit = columns // 2
        while bit:
            for m in sorted(blocks):
                blocks[m | bit] = swapped(blocks[m], "exp", 2 * bit)
            bit //= 2
        return blocks

    def chained(moving):
        moved = []
        for _ in range(hops):
            moving = passed_along(moving, "seq", 1)
            moved.append(moving)
        return moved

    def options(batch):
        extra = []
        if sinks:
            extra = latest_start(key_rows[batch, 0], value_rows[batch, 0], segments[batch, 0])
        return ((hops, relayed, heads, sinks), extra)

    def attend_column(moved):
        settings, extra = options(1)
        return call(
            functools.partial(attend_column_kernel, settings, experts),
            (rows_f32, rows_bf16, shaped((2 * columns, tok_count), jnp.int32)),
            [SMEM] * 3 + [VMEM] * (4 + columns + 2 * len(moved)) + ([VMEM, SMEM] if sinks else [])
            + [VMEM] * 2,
            (bias_table, new_table, old_table, segments, queries, key_rows, value_rows, *routes,
             *moved, *sent, *extra, tokens, out_proj),
            scratch=[pltpu.VMEM((tok_count, width), bf16)],
        )

    def attend_direct(moved):
        settings, extra = options(0)
        return call(
            functools.partial(attend_direct_kernel, settings, experts, capacity),
            (*[packet] * columns, rows_f32, shaped((2, tok_count), f32),
             shaped((2, tok_count), jnp.int32)),
            [SMEM] * 2 + [VMEM] * (6 + 2 * len(moved)) + ([VMEM, SMEM] if sinks else [])
            + [VMEM] * 2,
            (bias_table, old_table, routes_one[0].T, router_t, segments, queries, key_rows,
             value_rows, *moved, *sent, *extra, tokens, out_proj),
            scratch=[pltpu.VMEM((tok_count, width), bf16)],
        )

    def scratch_for(slots):
        return (pltpu.VMEM((slots, width), bf16), pltpu.VMEM((slots, inner), bf16))

    def pack(members, places, blocks):
        return call(
            functools.partial(pack_kernel, members, cap_two, columns),
            shaped((part_two, width), bf16),
            [VMEM] * (1 + len(members)),
            (places, *(blocks[m] for m in members)),
        )

    def partial(members, far):
        parts = call(
            functools.partial(partial_kernel, members, cap_two, columns),
            tuple(rows_bf16 if m % 2 else rows_f32 for m in members),
            [VMEM] * 4,
            (places, gates_two, near, far),
        )
        for m, value in zip(members, parts):
            totals.setdefault(m, []).insert(0, value)

    def send_down(members):
        for m in sorted(members, key=lambda m: (m & -m, -m)):
            parts = totals[m]
            value = parts[0]
            if len(parts) > 1:
                value = call(fold_kernel, rows_bf16, [VMEM] * len(parts), parts)
            totals.setdefault(m & (m - 1), []).append(swapped(value, "exp", 2 * (m & -m)))

    stacked = jnp.concatenate([key_rows[0, 0], value_rows[0, 0]], axis=0)
    first_hop = swapped(stacked, "seq", 1) if relayed else passed_along(stacked, "seq", 1)
    own_routes, own_segs = call(
        numbers_kernel,
        (shaped((2, tok_count), jnp.int32),) * 2,
        [VMEM] * 2,
        (routes_two[0].T, segments),
        after=[first_hop],
    )
    routes = multicast(own_routes)
    if relayed:
        sent = [swapped(own_segs, "seq", mask) for mask in (1, 2, 3)]
        across = swapped(stacked, "seq", 2)
    else:
        sent = chained(own_segs)
        across = first_hop
    *routes, latest_seg = call(
        collect_kernel,
        tuple(shaped((2, tok_count), jnp.int32) for _ in range(columns + 1)),
        [SMEM] * 2 + [VMEM] * (columns + 1),
        (new_table, old_table, *(routes[m] for m in range(columns)), sent[-1]),
        after=sent[:-1],
    )
    sent = [*sent[:-1], latest_seg]
    stacked, across = call(
        stack_kernel, (shaped((2 * tok_count, width), bf16),) * 2, [VMEM] * 2 + [ANY],
        (key_rows, value_rows, across), aliases={2: 1},
    )
    if relayed:
        moved_one = [first_hop, across, swapped(across, "seq", 1)]
        moved_two = [
            swapped(stacked, "seq", 1),
            swapped(stacked, "seq", 2),
            lax.ppermute(stacked, "seq", [(0, 0), (1, 2), (2, 1), (3, 3)]),
        ]
    else:
        moved_one, moved_two = ([across], chained(stacked))
        while len(moved_one) < hops:
            moved_one.append(passed_along(moved_one[-1], "seq", 1))
    *packets, hidden_one, gates_one, rows_one = attend_direct(moved_one)
    arrived = [packets[0]] + [swapped(packets[m], "exp", 2 * m) for m in range(1, columns)]
    hidden_two, normed_two, places = attend_column(moved_two)
    blocks = multicast(normed_two)
    crossing = call(
        crossing_kernel, shaped((columns * capacity, width), bf16), [VMEM] * columns, arrived,
        work=2 * 10**10,
    )
    crossed_one = swapped(crossing, "exp", 1)
    low_in = swapped(pack(lower, places, blocks), "exp", 1)
    near_one, far_one = call(
        functools.partial(direct_kernel, columns),
        (shaped((columns * capacity, width), bf16),) * 2,
        [VMEM] * (4 + columns),
        (*arrived, crossed_one, *weights),
        scratch=scratch_for(experts * capacity),
        after=[blocks[columns // 2]],
    )
    far_one = swapped(far_one, "exp", 1)
    high_in = swapped(pack(upper, places, blocks), "exp", 1)
    answers = call(rejoin_kernel, [packet] * columns, [VMEM] * 2, (near_one, far_one))
    returned = [answers[0]] + [swapped(answers[m], "exp", 2 * m) for m in range(1, columns)]
    low_out, high_out = call(
        far_kernel,
        (shaped((part_two, width), bf16),) * 2,
        [VMEM] * 5,
        (low_in, high_in, *weights),
        scratch=scratch_for(slots),
    )
    high_far = swapped(high_out, "exp", 1)
    near, gates_two, low_out = call(
        functools.partial(near_kernel, columns, experts, cap_two),
        (shaped((slots, width), bf16), shaped((2 * columns, tok_count), f32),
         shaped((part_two, width), bf16)),
        [SMEM] * 2 + [VMEM] * (5 + 2 * columns) + [ANY],
        (new_table, old_table, places, router_t, *(blocks[m] for m in range(columns)), *routes,
         *weights, low_out),
        scratch=scratch_for(slots), work=4 * 10**9, aliases={7 + 2 * columns: 2},
    )
    low_far = swapped(low_out, "exp", 1)
    sum_one = call(
        combine_kernel, rows_f32, [VMEM] * (3 + columns), (hidden_one, gates_one, rows_one, *returned)
    )
    totals = {}
    partial(upper, high_far)
    send_down(m for m in upper if m % 2)
    partial(lower, low_far)
    send_down(m for m in upper if m % 2 == 0)
    send_down(m for m in lower if m)
    ends = (sum_one, hidden_two, *totals[0])
    return call(
        final_kernel, shaped((2, 1, tok_count, width), bf16), [VMEM] * len(ends), ends
    )


def solution(mesh):
    rows = P(None, "exp", "seq", None)
    placed = (
        rows, rows, rows, rows, P(None, "exp", "seq"), P(), P(), P(),
        P("exp", None, None), P("exp", None, None), P("exp", None, None), P(), P(),
        P("exp", "seq", None), P("exp", "seq", None),
    )
    return jax.shard_map(local, mesh=mesh, in_specs=placed, out_specs=rows, check_vma=False)
```

```python
import functools

import jax
import jax.numpy as jnp
from jax import lax
from jax.experimental import pallas as pl
from jax.experimental.pallas import tpu as pltpu
from jax.sharding import PartitionSpec as P

WIN_BLOCKS = 4
NBUCK = 32
MAX_SLOTS = 2

score_scale = 0.125
epsilon = 1e-06
masked_score = -1e30

f32 = jnp.float32
bf16 = jnp.bfloat16
NT = (((1,), (1,)), ((), ()))
TN = (((0,), (0,)), ((), ()))
VMEM = pl.BlockSpec(memory_space=pltpu.VMEM)
SMEM = pl.BlockSpec(memory_space=pltpu.SMEM)
ANY = pl.BlockSpec(memory_space=pl.ANY)


def iota(shape, dim):
    return lax.broadcasted_iota(jnp.int32, shape, dim)


def shaped(shape, dtype):
    return jax.ShapeDtypeStruct(shape, dtype)


def passed_along(value, axis, steps):
    count = lax.axis_size(axis)
    return lax.ppermute(value, axis, [(source, source + steps) for source in range(count - steps)])


def swapped(value, axis, mask):
    count = lax.axis_size(axis)
    return lax.ppermute(value, axis, [(source, source ^ mask) for source in range(count)])


def merge_starts(former, latter):
    take_latter = (latter[4] > 0) & ((former[4] == 0) | (latter[3] != former[3]))
    return tuple((jnp.where(take_latter, newer, older) for older, newer in zip(former, latter)))


def latest_start(key_rows, value_rows, segments):
    tok_count, model_width = key_rows.shape
    length, index = (lax.axis_size("seq"), lax.axis_index("seq"))
    last_seg = segments[tok_count - 1]
    lead = jnp.sum((segments < last_seg).astype(jnp.int32))
    one = jnp.ones((), jnp.int32)
    found = (key_rows[lead], value_rows[lead], index * tok_count + lead, last_seg, one)
    everything = jax.tree.map(lambda part: lax.all_gather(part, "seq"), found)
    start = jax.tree.map(jnp.zeros_like, found)

    def lap(k, before):
        new = merge_starts(before, jax.tree.map(lambda part: part[k], everything))
        return jax.tree.map(lambda a, b: jnp.where(k < index, a, b), new, before)

    sink_key, sink_value, sink_pos, sink_seg, sink_has = lax.fori_loop(0, length, lap, start)
    block = jnp.zeros((2 * tok_count, model_width), key_rows.dtype)
    block = block.at[0].set(sink_key).at[tok_count].set(sink_value)
    return (block, jnp.stack([sink_pos, sink_seg, sink_has]))


def column_routes(experts, routes, new_table, old_table):
    chosen, holders = ([[], []], [[], []])
    for ref in routes:
        for c in range(2):
            slot = ref[c : c + 1, :]
            pick = sum(jnp.where(slot == s, new_table[s], 0) for s in range(experts))
            chosen[c].append(pick)
            holders[c].append(sum(jnp.where(pick == old_table[x], x, 0) for x in range(experts)))
    return (chosen, [jnp.concatenate(rows, axis=0) for rows in holders])


def attended(batch, hops, relayed, heads, sinks, bias, segs, q, k, v, rest, context):
    count = 3 if relayed else hops
    moved, sent, rest = (rest[:count], rest[count : 2 * count], rest[2 * count :])
    if sinks:
        sink_block, sink_info, rest = (rest[0], rest[1], rest[2:])
    tokens, proj = rest
    tok_count, width = tokens.shape[2:]
    window = WIN_BLOCKS * tok_count
    index = lax.axis_index("seq")
    grid = (tok_count, tok_count)

    own_seg = segs[batch]
    key_segs = [own_seg]
    if relayed:
        pairwise, across, relay = moved
        paired = index % 2 == 1
        key_segs += [jnp.where(paired, sent[0][batch : batch + 1], sent[2][batch : batch + 1])]
        key_segs.append(sent[1][batch : batch + 1, :])
    else:
        key_segs += [ref[batch : batch + 1, :] for ref in sent]
    seg_col = jnp.broadcast_to(own_seg, grid).T
    visible, spans = ([], [])
    for j, key_seg in enumerate(key_segs):
        key_seg = jnp.where(index >= j, key_seg, -1)
        distance = iota(grid, 0) - iota(grid, 1) + tok_count * j
        seen = (seg_col == key_seg) & (distance >= 0) & (distance < window)
        visible.append(jnp.where(seen, 0.0, masked_score))
        low, high = (max(0, tok_count * (j - 1) + 1), min(window, tok_count * (j + 1)) - 1)
        spans.append((distance, low.bit_length(), high.bit_length()))
    if sinks:
        position = index * tok_count + iota(grid, 0)
        seen = (seg_col == sink_info[1]) & (sink_info[2] > 0) & (position - sink_info[0] >= window)
        visible.append(jnp.where(seen & (iota(grid, 1) == 0), 0.0, masked_score))
        spans.append((None, NBUCK - 1, NBUCK - 1))
    lane = iota((tok_count, 128), 1)
    half = width // heads
    keys_at, values_at = (slice(0, tok_count), slice(tok_count, 2 * tok_count))
    for pair in range(heads // 2):
        cols = slice(128 * pair, 128 * pair + 128)
        both = q[batch, 0, :, cols] * score_scale
        even = jnp.where(lane < half, both, jnp.zeros_like(both))
        odd = jnp.where(lane < half, jnp.zeros_like(both), both)
        stacked = jnp.concatenate([even, odd], axis=0)
        blocks = [(k[batch, 0, :, cols], v[batch, 0, :, cols])]
        if relayed:
            blocks.append(tuple(
                jnp.where(paired, pairwise[at, cols], relay[at, cols])
                for at in (keys_at, values_at)
            ))
            blocks.append((across[keys_at, cols], across[values_at, cols]))
        else:
            for ref in moved:
                blocks.append((ref[keys_at, cols], ref[values_at, cols]))
        if sinks:
            blocks.append((sink_block[keys_at, cols], sink_block[values_at, cols]))
        scores = []
        for (keys, _), (distance, low, high), seen in zip(blocks, spans, visible):
            score = lax.dot_general(stacked, keys, NT, preferred_element_type=f32)
            parts = []
            for side in range(2):
                head = 2 * pair + side
                offset = jnp.full(grid, bias[head, low], f32)
                for bucket in range(low + 1, high + 1):
                    offset = jnp.where(distance >= 1 << (bucket - 1), bias[head, bucket], offset)
                parts.append(score[side * tok_count : (side + 1) * tok_count] + (offset + seen))
            scores.append(jnp.concatenate(parts, axis=0))
        peak = jnp.max(functools.reduce(jnp.maximum, scores), axis=1, keepdims=True)
        weights = [jnp.exp(score - peak) for score in scores]
        total = jnp.sum(functools.reduce(jnp.add, weights), axis=1, keepdims=True)
        scale = 1.0 / total
        mixed = sum(
            jnp.dot((weight * scale).astype(bf16), values, preferred_element_type=f32)
            for weight, (_, values) in zip(weights, blocks)
        )
        context[:, cols] = jnp.where(lane < half, mixed[:tok_count], mixed[tok_count:]).astype(bf16)
    hidden = tokens[batch, 0].astype(f32) + jnp.dot(
        context[...], proj[...], preferred_element_type=f32
    )
    mean = jnp.mean(hidden * hidden, axis=1, keepdims=True)
    return (hidden, (hidden * lax.rsqrt(mean + epsilon)).astype(bf16))


def ranks(member):
    grid = (member.shape[1], member.shape[1])
    earlier = jnp.where(iota(grid, 0) < iota(grid, 1), 1.0, 0.0).astype(bf16)
    return jnp.dot(member.astype(bf16), earlier, preferred_element_type=f32).astype(jnp.int32)


def attend_column_kernel(options, experts, bias, new_table, old_table, segs, q, k, v, *rest):
    routes, rest = (rest[: experts // 2], rest[experts // 2 :])
    inputs, (hidden_out, normed_out, places_out, context) = (rest[:-4], rest[-4:])
    hidden, normed = attended(1, *options, bias, segs, q, k, v, inputs, context)
    hidden_out[...] = hidden
    normed_out[...] = normed
    me = lax.axis_index("exp")
    _, holders = column_routes(experts, routes, new_table, old_table)
    member = jnp.concatenate(
        [jnp.where((holders[0] == at) | (holders[1] == at), 1.0, 0.0) for at in (me, me ^ 1)],
        axis=0,
    )
    places_out[...] = jnp.where(member > 0.5, ranks(member), -1)


def attend_direct_kernel(options, experts, cap, bias, old_table, routes, router_t, segs, q, k, v, *rest):
    layers = experts // 2
    inputs, rest = (rest[: -4 - layers], rest[-4 - layers :])
    outgoing, (hidden_out, gates_out, rows_out, context) = (rest[:layers], rest[layers:])
    hidden, normed = attended(0, *options, bias, segs, q, k, v, inputs, context)
    hidden_out[...] = hidden
    tok_count = hidden.shape[0]
    chosen = [routes[c : c + 1, :] for c in range(2)]
    holders = [sum(jnp.where(c == old_table[x], x, 0) for x in range(experts)) for c in chosen]
    expert = iota((experts, tok_count), 0)
    packet = expert ^ lax.axis_index("exp")
    member = jnp.where((packet == holders[0]) | (packet == holders[1]), 1.0, 0.0)
    place = ranks(member) + expert * cap
    rows = [
        jnp.sum(jnp.where(packet == holder, place, 0), axis=0, keepdims=True) for holder in holders
    ]
    rows_out[...] = jnp.concatenate(rows, axis=0)
    logits = lax.dot_general(router_t[...], normed, NT, preferred_element_type=f32)
    picked = [jnp.sum(jnp.where(expert == c, logits, 0.0), axis=0, keepdims=True) for c in chosen]
    first = jax.nn.sigmoid(picked[0] - picked[1])
    gates_out[...] = jnp.concatenate([first, 1.0 - first], axis=0)
    at = iota((experts * cap, tok_count), 0)
    plan = jnp.where((at == rows[0]) | (at == rows[1]), 1.0, 0.0).astype(bf16)
    packed = jnp.dot(plan, normed, preferred_element_type=f32)
    for m, ref in enumerate(outgoing):
        ref[...] = packed[2 * m * cap : 2 * (m + 1) * cap].astype(bf16)


def picked_rows(members, cap, first_row, places, blocks):
    at = iota((len(members) * cap, blocks[0].shape[0]), 0)
    plans = []
    for n, m in enumerate(members):
        place = places[first_row + m : first_row + m + 1, :]
        place = jnp.where(place >= 0, place + n * cap, -1)
        plans.append(jnp.where(at == place, 1.0, 0.0))
    plan = jnp.concatenate(plans, axis=1).astype(bf16)
    rows = jnp.concatenate([block[...] for block in blocks], axis=0)
    return (jnp.dot(plan, rows, preferred_element_type=f32).astype(bf16), rows)


def pack_kernel(members, cap, columns, places, *rest):
    blocks, out = (rest[:-1], rest[-1])
    out[...], _ = picked_rows(members, cap, columns, places, blocks)


def numbers_kernel(new_table, old_table, routes_one, routes, segs, routes_out, segs_out):
    del new_table, old_table, routes_one
    routes_out[...] = routes[...]
    segs_out[...] = segs[:, 0]


def collect_kernel(*refs):
    count = len(refs) // 2
    for ref, out in zip(refs[:count], refs[count:]):
        out[...] = ref[...]


def stack_kernel(k, v, across, out, across_out):
    del across, across_out
    tok_count = k.shape[2]
    out[:tok_count, :] = k[0, 0]
    out[tok_count:, :] = v[0, 0]


def crossing_kernel(*refs):
    packets, out = (refs[:-1], refs[-1])
    cap = packets[0].shape[0] // 2
    parts = [ref[...].astype(f32)[cap:] for ref in packets]
    out[...] = jnp.concatenate(parts, axis=0).astype(bf16)


def expert_rows(rows, weights, active, stores):
    gate, up, down = weights
    inner, width = down.shape[1:]
    x = rows[...]
    for begin in range(0, inner, 256):
        span = slice(begin, min(inner, begin + 256))
        gate_part = jnp.dot(x, gate[0, :, span], preferred_element_type=f32)
        up_part = jnp.dot(x, up[0, :, span], preferred_element_type=f32)
        active[:, span] = (jax.nn.gelu(gate_part, approximate=True) * up_part).astype(bf16)
    for begin in range(0, width, 256):
        span = slice(begin, begin + 256)
        part = jnp.dot(active[...], down[0, :, span], preferred_element_type=f32)
        stores(span, part)


def near_kernel(columns, experts, cap, new_table, old_table, places, router_t, *rest):
    blocks, rest = (rest[:columns], rest[columns:])
    routes, rest = (rest[:columns], rest[columns:])
    weights, (_, out, gates_out, _, rows, active) = (rest[:3], rest[3:])

    def stores(span, value):
        out[:, span] = value.astype(bf16)

    rows[...], tokens = picked_rows(range(columns), cap, 0, places, blocks)
    logits = lax.dot_general(router_t[...], tokens, NT, preferred_element_type=f32)
    chosen, holders = column_routes(experts, routes, new_table, old_table)
    chosen = [jnp.concatenate(picks, axis=1) for picks in chosen]
    expert = iota(logits.shape, 0)
    picked = [
        jnp.sum(jnp.where(expert == pick, logits, 0.0), axis=0, keepdims=True) for pick in chosen
    ]
    first = jax.nn.sigmoid(picked[0] - picked[1])
    tok_count = places.shape[1]
    first = jnp.concatenate(
        [first[:, m * tok_count : (m + 1) * tok_count] for m in range(columns)], axis=0
    )
    me = lax.axis_index("exp")
    gates_out[...] = jnp.concatenate(
        [
            jnp.where(holders[0] == at, first, 0.0) + jnp.where(holders[1] == at, 1.0 - first, 0.0)
            for at in (me, me ^ 1)
        ],
        axis=0,
    )
    expert_rows(rows, weights, active, stores)


def far_kernel(low_in, high_in, *rest):
    weights, (low_out, high_out, rows, active) = (rest[:3], rest[3:])
    part = low_in.shape[0]

    def stores(span, value):
        low_out[:, span] = value[:part].astype(bf16)
        high_out[:, span] = value[part:].astype(bf16)

    rows[:part, :] = low_in[...]
    rows[part:, :] = high_in[...]
    expert_rows(rows, weights, active, stores)


def direct_kernel(layers, *refs):
    packets, crossed, weights = (refs[:layers], refs[layers], refs[layers + 1 : layers + 4])
    near, far, rows, active = refs[layers + 4 :]
    cap = packets[0].shape[0] // 2
    half = layers * cap

    def stores(span, value):
        near[:, span] = value[:half].astype(bf16)
        far[:, span] = value[half:].astype(bf16)

    parts = [ref[...].astype(f32)[:cap] for ref in packets]
    rows[:half, :] = jnp.concatenate(parts, axis=0).astype(bf16)
    rows[half:, :] = crossed[...]
    expert_rows(rows, weights, active, stores)


def rejoin_kernel(near, far, *outs):
    cap = outs[0].shape[0] // 2
    both = [ref[...].astype(f32) for ref in (near, far)]
    for m, out in enumerate(outs):
        parts = [each[m * cap : (m + 1) * cap] for each in both]
        out[...] = jnp.concatenate(parts, axis=0).astype(bf16)


def partial_kernel(members, cap, columns, places, gates, near, far, *outs):
    at = iota((cap, places.shape[1]), 0)
    for n, m in enumerate(members):
        total = None
        near_rows = near[m * cap : (m + 1) * cap, :]
        far_rows = far[n * cap : (n + 1) * cap, :]
        for values, row in ((near_rows, m), (far_rows, columns + m)):
            spread = jnp.where(at == places[row : row + 1, :], gates[row : row + 1, :], 0.0)
            coarse = spread.astype(bf16)
            fine = (spread - coarse.astype(f32)).astype(bf16)
            for half in (coarse, fine):
                term = lax.dot_general(half, values, TN, preferred_element_type=f32)
                total = term if total is None else total + term
        outs[n][...] = total.astype(outs[n].dtype)


def fold_kernel(own, *rest):
    total = own[...]
    for ref in rest[:-1]:
        total = total + ref[...].astype(f32)
    rest[-1][...] = total.astype(rest[-1].dtype)


def final_kernel(layers, hidden, gates, rows, *rest):
    packets, ends, out = (rest[:layers], rest[layers:-1], rest[-1])
    at = iota((layers * packets[0].shape[0], hidden.shape[0]), 0)
    spread = jnp.where(at == rows[0:1, :], gates[0:1, :], 0.0)
    spread = spread + jnp.where(at == rows[1:2, :], gates[1:2, :], 0.0)
    coarse = spread.astype(bf16)
    fine = (spread - coarse.astype(f32)).astype(bf16)
    values = jnp.concatenate([ref[...].astype(f32) for ref in packets], axis=0).astype(bf16)
    total = hidden[...]
    for half in (coarse, fine):
        total = total + lax.dot_general(half, values, TN, preferred_element_type=f32)
    out[0, 0] = total.astype(bf16)
    total = ends[0][...]
    for ref in ends[1:]:
        total = total + ref[...].astype(f32)
    out[1, 0] = total.astype(bf16)


def local(
    tokens, queries, key_rows, value_rows, segments, bias_table, out_proj, router,
    gate_weight, up_weight, down_weight, old_table, new_table, routes_one, routes_two,
):
    tok_count, width = tokens.shape[2:]
    heads = bias_table.shape[0]
    experts = router.shape[1]
    columns = experts // 2
    inner = gate_weight.shape[2]
    seq_size = lax.axis_size("seq")
    seq_len = tok_count * seq_size
    capacity = tok_count * 2 * 5 // (4 * experts)
    longest = seq_len // 2
    hops = min(WIN_BLOCKS, (longest - 1 + tok_count - 1) // tok_count)
    relayed = seq_size == 4 and hops == 2
    sinks = seq_len > WIN_BLOCKS * tok_count
    weights = (gate_weight, up_weight, down_weight)
    router_t = router.T
    lower, upper = (range(columns // 2), range(columns // 2, columns))
    rows_bf16 = shaped((tok_count, width), bf16)
    rows_f32 = shaped((tok_count, width), f32)
    cap_two = capacity * MAX_SLOTS
    slots = columns * cap_two
    part_two = slots // 2
    packet = shaped((2 * capacity, width), bf16)
    latest = []

    def call(kernel, outs, ins, args, scratch=(), after=(), aliases=None, work=1):
        after = [*after, *latest]
        out_specs = jax.tree.map(lambda _: VMEM, outs)
        if aliases:
            out_specs = tuple(ANY if n in aliases.values() else VMEM for n in range(len(outs)))

        def body(*refs):
            kernel(*refs[: len(args)], *refs[len(args) + len(after) :])

        made = pl.pallas_call(
            body,
            out_shape=outs,
            in_specs=ins + [ANY] * len(after),
            out_specs=out_specs,
            scratch_shapes=list(scratch),
            input_output_aliases=aliases or {},
            compiler_params=pltpu.CompilerParams(vmem_limit_bytes=24 * 2**20),
            cost_estimate=pl.CostEstimate(flops=work, bytes_accessed=1, transcendentals=0),
        )(*args, *after)
        latest[:] = jax.tree.leaves(made)[:1]
        return made

    def multicast(own):
        blocks = {0: own}
        bit = columns // 2
        while bit:
            for m in sorted(blocks):
                blocks[m | bit] = swapped(blocks[m], "exp", 2 * bit)
            bit //= 2
        return blocks

    def chained(moving):
        moved = []
        for _ in range(hops):
            moving = passed_along(moving, "seq", 1)
            moved.append(moving)
        return moved

    def options(batch):
        extra = []
        if sinks:
            extra = latest_start(key_rows[batch, 0], value_rows[batch, 0], segments[batch, 0])
        return ((hops, relayed, heads, sinks), extra)

    def attend_column(moved):
        settings, extra = options(1)
        return call(
            functools.partial(attend_column_kernel, settings, experts),
            (rows_f32, rows_bf16, shaped((2 * columns, tok_count), jnp.int32)),
            [SMEM] * 3 + [VMEM] * (4 + columns + 2 * len(moved)) + ([VMEM, SMEM] if sinks else [])
            + [VMEM] * 2,
            (bias_table, new_table, old_table, segments, queries, key_rows, value_rows, *routes,
             *moved, *sent, *extra, tokens, out_proj),
            scratch=[pltpu.VMEM((tok_count, width), bf16)],
        )

    def attend_direct(moved):
        settings, extra = options(0)
        return call(
            functools.partial(attend_direct_kernel, settings, experts, capacity),
            (*[packet] * columns, rows_f32, shaped((2, tok_count), f32),
             shaped((2, tok_count), jnp.int32)),
            [SMEM] * 2 + [VMEM] * (6 + 2 * len(moved)) + ([VMEM, SMEM] if sinks else [])
            + [VMEM] * 2,
            (bias_table, old_table, routes_first, router_t, segments, queries, key_rows,
             value_rows, *moved, *sent, *extra, tokens, out_proj),
            scratch=[pltpu.VMEM((tok_count, width), bf16)],
        )

    def scratch_for(slots):
        return (pltpu.VMEM((slots, width), bf16), pltpu.VMEM((slots, inner), bf16))

    def pack(members, places, blocks):
        return call(
            functools.partial(pack_kernel, members, cap_two, columns),
            shaped((part_two, width), bf16),
            [VMEM] * (1 + len(members)),
            (places, *(blocks[m] for m in members)),
        )

    def partial(members, far):
        parts = call(
            functools.partial(partial_kernel, members, cap_two, columns),
            tuple(rows_bf16 if m % 2 else rows_f32 for m in members),
            [VMEM] * 4,
            (places, gates_two, near, far),
        )
        for m, value in zip(members, parts):
            totals.setdefault(m, []).insert(0, value)

    def send_down(members):
        for m in sorted(members, key=lambda m: (m & -m, -m)):
            parts = totals[m]
            value = parts[0]
            if len(parts) > 1:
                value = call(fold_kernel, rows_bf16, [VMEM] * len(parts), parts)
            totals.setdefault(m & (m - 1), []).append(swapped(value, "exp", 2 * (m & -m)))

    stacked = jnp.concatenate([key_rows[1, 0], value_rows[1, 0]], axis=0)
    first_hop = swapped(stacked, "seq", 1) if relayed else passed_along(stacked, "seq", 1)
    routes_first = routes_one[0].T
    own_routes, own_segs = call(
        numbers_kernel,
        (shaped((2, tok_count), jnp.int32),) * 2,
        [SMEM] * 2 + [VMEM] * 3,
        (new_table, old_table, routes_first, routes_two[0].T, segments),
        after=[first_hop],
    )
    routes = multicast(own_routes)
    if relayed:
        sent = [swapped(own_segs, "seq", mask) for mask in (1, 2, 3)]
        across = swapped(stacked, "seq", 2)
    else:
        sent = chained(own_segs)
        across = first_hop
    *routes, latest_seg = call(
        collect_kernel,
        tuple(shaped((2, tok_count), jnp.int32) for _ in range(columns + 1)),
        [VMEM] * (columns + 1),
        (*(routes[m] for m in range(columns)), sent[-1]),
        after=sent[:-1],
    )
    sent = [*sent[:-1], latest_seg]
    stacked, across = call(
        stack_kernel, (shaped((2 * tok_count, width), bf16),) * 2, [VMEM] * 2 + [ANY],
        (key_rows, value_rows, across), aliases={2: 1},
    )
    if relayed:
        moved_two = [first_hop, across, swapped(across, "seq", 1)]
        moved_one = [
            swapped(stacked, "seq", 1),
            swapped(stacked, "seq", 2),
            lax.ppermute(stacked, "seq", [(0, 0), (1, 2), (2, 1), (3, 3)]),
        ]
    else:
        moved_two, moved_one = ([across], chained(stacked))
        while len(moved_two) < hops:
            moved_two.append(passed_along(moved_two[-1], "seq", 1))
    hidden_two, normed_two, places = attend_column(moved_two)
    blocks = multicast(normed_two)
    *packets, hidden_one, gates_one, rows_one = attend_direct(moved_one)
    arrived = [packets[0]] + [swapped(packets[m], "exp", 2 * m) for m in range(1, columns)]
    low_in = swapped(pack(lower, places, blocks), "exp", 1)
    high_in = swapped(pack(upper, places, blocks), "exp", 1)
    crossing = call(
        crossing_kernel, shaped((columns * capacity, width), bf16), [VMEM] * columns, arrived,
        work=2 * 10**10,
    )
    crossed_one = swapped(crossing, "exp", 1)
    low_out, high_out = call(
        far_kernel,
        (shaped((part_two, width), bf16),) * 2,
        [VMEM] * 5,
        (low_in, high_in, *weights),
        scratch=scratch_for(slots),
    )
    high_far = swapped(high_out, "exp", 1)
    near, gates_two, low_out = call(
        functools.partial(near_kernel, columns, experts, cap_two),
        (shaped((slots, width), bf16), shaped((2 * columns, tok_count), f32),
         shaped((part_two, width), bf16)),
        [SMEM] * 2 + [VMEM] * (5 + 2 * columns) + [ANY],
        (new_table, old_table, places, router_t, *(blocks[m] for m in range(columns)), *routes,
         *weights, low_out),
        scratch=scratch_for(slots), work=4 * 10**9, aliases={7 + 2 * columns: 2},
    )
    low_far = swapped(low_out, "exp", 1)
    totals = {}
    partial(upper, high_far)
    send_down(m for m in upper if m % 2)
    near_one, far_one = call(
        functools.partial(direct_kernel, columns),
        (shaped((columns * capacity, width), bf16),) * 2,
        [VMEM] * (4 + columns),
        (*arrived, crossed_one, *weights),
        scratch=scratch_for(experts * capacity),
    )
    far_one = swapped(far_one, "exp", 1)
    send_down(m for m in upper if m % 2 == 0)
    partial(lower, low_far)
    send_down(m for m in lower if m)
    answers = call(rejoin_kernel, [packet] * columns, [VMEM] * 2, (near_one, far_one))
    returned = [answers[0]] + [swapped(answers[m], "exp", 2 * m) for m in range(1, columns)]
    ends = (hidden_two, *totals[0])
    return call(
        functools.partial(final_kernel, columns), shaped((2, 1, tok_count, width), bf16),
        [VMEM] * (3 + columns + len(ends)), (hidden_one, gates_one, rows_one, *returned, *ends),
    )


def solution(mesh):
    rows = P(None, "exp", "seq", None)
    placed = (
        rows, rows, rows, rows, P(None, "exp", "seq"), P(), P(), P(),
        P("exp", None, None), P("exp", None, None), P("exp", None, None), P(), P(),
        P("exp", "seq", None), P("exp", "seq", None),
    )
    return jax.shard_map(local, mesh=mesh, in_specs=placed, out_specs=rows, check_vma=False)
```

```python
import functools

import jax
import jax.numpy as jnp
from jax import lax
from jax.experimental import pallas as pl
from jax.experimental.pallas import tpu as pltpu
from jax.sharding import PartitionSpec as P

WIN_BLOCKS = 4
NBUCK = 32
MAX_SLOTS = 2
ONE_ROW, TWO_ROW, NEW_ROW, OLD_ROW = (2, 4, 6, 7)

score_scale = 0.125
epsilon = 1e-06
masked_score = -1e30

f32 = jnp.float32
bf16 = jnp.bfloat16
NT = (((1,), (1,)), ((), ()))
TN = (((0,), (0,)), ((), ()))
VMEM = pl.BlockSpec(memory_space=pltpu.VMEM)
SMEM = pl.BlockSpec(memory_space=pltpu.SMEM)
ANY = pl.BlockSpec(memory_space=pl.ANY)


def iota(shape, dim):
    return lax.broadcasted_iota(jnp.int32, shape, dim)


def shaped(shape, dtype):
    return jax.ShapeDtypeStruct(shape, dtype)


def passed_along(value, axis, steps):
    count = lax.axis_size(axis)
    return lax.ppermute(value, axis, [(source, source + steps) for source in range(count - steps)])


def swapped(value, axis, mask):
    count = lax.axis_size(axis)
    return lax.ppermute(value, axis, [(source, source ^ mask) for source in range(count)])


def merge_starts(former, latter):
    take_latter = (latter[4] > 0) & ((former[4] == 0) | (latter[3] != former[3]))
    return tuple((jnp.where(take_latter, newer, older) for older, newer in zip(former, latter)))


def latest_start(key_rows, value_rows, segments):
    tok_count, model_width = key_rows.shape
    length, index = (lax.axis_size("seq"), lax.axis_index("seq"))
    last_seg = segments[tok_count - 1]
    lead = jnp.sum((segments < last_seg).astype(jnp.int32))
    one = jnp.ones((), jnp.int32)
    found = (key_rows[lead], value_rows[lead], index * tok_count + lead, last_seg, one)
    everything = jax.tree.map(lambda part: lax.all_gather(part, "seq"), found)
    start = jax.tree.map(jnp.zeros_like, found)

    def lap(k, before):
        new = merge_starts(before, jax.tree.map(lambda part: part[k], everything))
        return jax.tree.map(lambda a, b: jnp.where(k < index, a, b), new, before)

    sink_key, sink_value, sink_pos, sink_seg, sink_has = lax.fori_loop(0, length, lap, start)
    block = jnp.zeros((2 * tok_count, model_width), key_rows.dtype)
    block = block.at[0].set(sink_key).at[tok_count].set(sink_value)
    return (block, jnp.stack([sink_pos, sink_seg, sink_has]))


def table_entry(own, row, entry):
    return own[row : row + 1, entry : entry + 1]


def holder_of(experts, own, pick):
    return sum(
        jnp.where(pick == table_entry(own, OLD_ROW, x), x, 0) for x in range(experts)
    )


def column_routes(experts, routes, own):
    chosen, holders = ([[], []], [[], []])
    for ref in routes:
        for c in range(2):
            slot = ref[c : c + 1, :]
            pick = sum(
                jnp.where(slot == s, table_entry(own, NEW_ROW, s), 0) for s in range(experts)
            )
            chosen[c].append(pick)
            holders[c].append(holder_of(experts, own, pick))
    return (chosen, [jnp.concatenate(rows, axis=0) for rows in holders])


def attended(batch, hops, relayed, heads, sinks, bias, own, q, k, v, rest, context):
    count = 3 if relayed else hops
    moved, sent, rest = (rest[:count], rest[count : 2 * count], rest[2 * count :])
    if sinks:
        sink_block, sink_info, rest = (rest[0], rest[1], rest[2:])
    tokens, proj = rest
    tok_count, width = tokens.shape[2:]
    window = WIN_BLOCKS * tok_count
    index = lax.axis_index("seq")
    grid = (tok_count, tok_count)

    own_seg = own[batch : batch + 1, :]
    key_segs = [own_seg]
    if relayed:
        pairwise, across, relay = moved
        paired = index % 2 == 1
        key_segs += [jnp.where(paired, sent[0][batch : batch + 1], sent[2][batch : batch + 1])]
        key_segs.append(sent[1][batch : batch + 1, :])
    else:
        key_segs += [ref[batch : batch + 1, :] for ref in sent]
    seg_col = jnp.broadcast_to(own_seg, grid).T
    visible, spans = ([], [])
    for j, key_seg in enumerate(key_segs):
        key_seg = jnp.where(index >= j, key_seg, -1)
        distance = iota(grid, 0) - iota(grid, 1) + tok_count * j
        seen = (seg_col == key_seg) & (distance >= 0) & (distance < window)
        visible.append(jnp.where(seen, 0.0, masked_score))
        low, high = (max(0, tok_count * (j - 1) + 1), min(window, tok_count * (j + 1)) - 1)
        spans.append((distance, low.bit_length(), high.bit_length()))
    if sinks:
        position = index * tok_count + iota(grid, 0)
        seen = (seg_col == sink_info[1]) & (sink_info[2] > 0) & (position - sink_info[0] >= window)
        visible.append(jnp.where(seen & (iota(grid, 1) == 0), 0.0, masked_score))
        spans.append((None, NBUCK - 1, NBUCK - 1))
    lane = iota((tok_count, 128), 1)
    half = width // heads
    keys_at, values_at = (slice(0, tok_count), slice(tok_count, 2 * tok_count))
    for pair in range(heads // 2):
        cols = slice(128 * pair, 128 * pair + 128)
        both = q[batch, 0, :, cols] * score_scale
        even = jnp.where(lane < half, both, jnp.zeros_like(both))
        odd = jnp.where(lane < half, jnp.zeros_like(both), both)
        stacked = jnp.concatenate([even, odd], axis=0)
        blocks = [(k[batch, 0, :, cols], v[batch, 0, :, cols])]
        if relayed:
            blocks.append(tuple(
                jnp.where(paired, pairwise[at, cols], relay[at, cols])
                for at in (keys_at, values_at)
            ))
            blocks.append((across[keys_at, cols], across[values_at, cols]))
        else:
            for ref in moved:
                blocks.append((ref[keys_at, cols], ref[values_at, cols]))
        if sinks:
            blocks.append((sink_block[keys_at, cols], sink_block[values_at, cols]))
        scores = []
        for (keys, _), (distance, low, high), seen in zip(blocks, spans, visible):
            score = lax.dot_general(stacked, keys, NT, preferred_element_type=f32)
            parts = []
            for side in range(2):
                head = 2 * pair + side
                offset = jnp.full(grid, bias[head, low], f32)
                for bucket in range(low + 1, high + 1):
                    offset = jnp.where(distance >= 1 << (bucket - 1), bias[head, bucket], offset)
                parts.append(score[side * tok_count : (side + 1) * tok_count] + (offset + seen))
            scores.append(jnp.concatenate(parts, axis=0))
        peak = jnp.max(functools.reduce(jnp.maximum, scores), axis=1, keepdims=True)
        weights = [jnp.exp(score - peak) for score in scores]
        total = jnp.sum(functools.reduce(jnp.add, weights), axis=1, keepdims=True)
        scale = 1.0 / total
        mixed = sum(
            jnp.dot((weight * scale).astype(bf16), values, preferred_element_type=f32)
            for weight, (_, values) in zip(weights, blocks)
        )
        context[:, cols] = jnp.where(lane < half, mixed[:tok_count], mixed[tok_count:]).astype(bf16)
    hidden = tokens[batch, 0].astype(f32) + jnp.dot(
        context[...], proj[...], preferred_element_type=f32
    )
    mean = jnp.mean(hidden * hidden, axis=1, keepdims=True)
    return (hidden, (hidden * lax.rsqrt(mean + epsilon)).astype(bf16))


def ranks(member):
    grid = (member.shape[1], member.shape[1])
    earlier = jnp.where(iota(grid, 0) < iota(grid, 1), 1.0, 0.0).astype(bf16)
    return jnp.dot(member.astype(bf16), earlier, preferred_element_type=f32).astype(jnp.int32)


def attend_column_kernel(options, experts, bias, own, q, k, v, *rest):
    routes, rest = (rest[: experts // 2], rest[experts // 2 :])
    inputs, (hidden_out, normed_out, places_out, context) = (rest[:-4], rest[-4:])
    hidden, normed = attended(1, *options, bias, own, q, k, v, inputs, context)
    hidden_out[...] = hidden
    normed_out[...] = normed
    me = lax.axis_index("exp")
    _, holders = column_routes(experts, routes, own)
    member = jnp.concatenate(
        [jnp.where((holders[0] == at) | (holders[1] == at), 1.0, 0.0) for at in (me, me ^ 1)],
        axis=0,
    )
    places_out[...] = jnp.where(member > 0.5, ranks(member), -1)


def attend_direct_kernel(options, experts, cap, bias, router_t, own, q, k, v, *rest):
    layers = experts // 2
    inputs, rest = (rest[: -4 - layers], rest[-4 - layers :])
    outgoing, (hidden_out, gates_out, rows_out, context) = (rest[:layers], rest[layers:])
    hidden, normed = attended(0, *options, bias, own, q, k, v, inputs, context)
    hidden_out[...] = hidden
    tok_count = hidden.shape[0]
    chosen = [own[ONE_ROW + c : ONE_ROW + c + 1, :] for c in range(2)]
    holders = [holder_of(experts, own, pick) for pick in chosen]
    expert = iota((experts, tok_count), 0)
    packet = expert ^ lax.axis_index("exp")
    member = jnp.where((packet == holders[0]) | (packet == holders[1]), 1.0, 0.0)
    place = ranks(member) + expert * cap
    rows = [
        jnp.sum(jnp.where(packet == holder, place, 0), axis=0, keepdims=True) for holder in holders
    ]
    rows_out[...] = jnp.concatenate(rows, axis=0)
    logits = lax.dot_general(router_t[...], normed, NT, preferred_element_type=f32)
    picked = [jnp.sum(jnp.where(expert == c, logits, 0.0), axis=0, keepdims=True) for c in chosen]
    first = jax.nn.sigmoid(picked[0] - picked[1])
    gates_out[...] = jnp.concatenate([first, 1.0 - first], axis=0)
    at = iota((experts * cap, tok_count), 0)
    plan = jnp.where((at == rows[0]) | (at == rows[1]), 1.0, 0.0).astype(bf16)
    packed = jnp.dot(plan, normed, preferred_element_type=f32)
    for m, ref in enumerate(outgoing):
        ref[...] = packed[2 * m * cap : 2 * (m + 1) * cap].astype(bf16)


def picked_rows(members, cap, first_row, places, blocks):
    at = iota((len(members) * cap, blocks[0].shape[0]), 0)
    plans = []
    for n, m in enumerate(members):
        place = places[first_row + m : first_row + m + 1, :]
        place = jnp.where(place >= 0, place + n * cap, -1)
        plans.append(jnp.where(at == place, 1.0, 0.0))
    plan = jnp.concatenate(plans, axis=1).astype(bf16)
    rows = jnp.concatenate([block[...] for block in blocks], axis=0)
    return (jnp.dot(plan, rows, preferred_element_type=f32).astype(bf16), rows)


def pack_kernel(members, cap, columns, places, *rest):
    blocks, out = (rest[:-1], rest[-1])
    out[...], _ = picked_rows(members, cap, columns, places, blocks)


def numbers_kernel(numbers, own, routes_out, segs_out):
    own[...] = numbers[...]
    routes_out[...] = numbers[TWO_ROW : TWO_ROW + 2, :]
    segs_out[...] = numbers[:2, :]


def collect_kernel(*refs):
    count = len(refs) // 2
    for ref, out in zip(refs[:count], refs[count:]):
        out[...] = ref[...]


def stack_kernel(k, v, across, out, across_out):
    del across, across_out
    tok_count = k.shape[2]
    out[:tok_count, :] = k[0, 0]
    out[tok_count:, :] = v[0, 0]


def crossing_kernel(*refs):
    packets, out = (refs[:-1], refs[-1])
    cap = packets[0].shape[0] // 2
    parts = [ref[...].astype(f32)[cap:] for ref in packets]
    out[...] = jnp.concatenate(parts, axis=0).astype(bf16)


def expert_rows(rows, weights, active, stores):
    gate, up, down = weights
    inner, width = down.shape[1:]
    x = rows[...]
    for begin in range(0, inner, 256):
        span = slice(begin, min(inner, begin + 256))
        gate_part = jnp.dot(x, gate[0, :, span], preferred_element_type=f32)
        up_part = jnp.dot(x, up[0, :, span], preferred_element_type=f32)
        active[:, span] = (jax.nn.gelu(gate_part, approximate=True) * up_part).astype(bf16)
    for begin in range(0, width, 256):
        span = slice(begin, begin + 256)
        part = jnp.dot(active[...], down[0, :, span], preferred_element_type=f32)
        stores(span, part)


def near_kernel(columns, experts, cap, own, places, router_t, *rest):
    blocks, rest = (rest[:columns], rest[columns:])
    routes, rest = (rest[:columns], rest[columns:])
    weights, (_, out, gates_out, _, rows, active) = (rest[:3], rest[3:])

    def stores(span, value):
        out[:, span] = value.astype(bf16)

    rows[...], tokens = picked_rows(range(columns), cap, 0, places, blocks)
    logits = lax.dot_general(router_t[...], tokens, NT, preferred_element_type=f32)
    chosen, holders = column_routes(experts, routes, own)
    chosen = [jnp.concatenate(picks, axis=1) for picks in chosen]
    expert = iota(logits.shape, 0)
    picked = [
        jnp.sum(jnp.where(expert == pick, logits, 0.0), axis=0, keepdims=True) for pick in chosen
    ]
    first = jax.nn.sigmoid(picked[0] - picked[1])
    tok_count = places.shape[1]
    first = jnp.concatenate(
        [first[:, m * tok_count : (m + 1) * tok_count] for m in range(columns)], axis=0
    )
    me = lax.axis_index("exp")
    gates_out[...] = jnp.concatenate(
        [
            jnp.where(holders[0] == at, first, 0.0) + jnp.where(holders[1] == at, 1.0 - first, 0.0)
            for at in (me, me ^ 1)
        ],
        axis=0,
    )
    expert_rows(rows, weights, active, stores)


def far_kernel(low_in, high_in, *rest):
    weights, (low_out, high_out, rows, active) = (rest[:3], rest[3:])
    part = low_in.shape[0]

    def stores(span, value):
        low_out[:, span] = value[:part].astype(bf16)
        high_out[:, span] = value[part:].astype(bf16)

    rows[:part, :] = low_in[...]
    rows[part:, :] = high_in[...]
    expert_rows(rows, weights, active, stores)


def direct_kernel(layers, *refs):
    packets, crossed, weights = (refs[:layers], refs[layers], refs[layers + 1 : layers + 4])
    near, far, rows, active = refs[layers + 4 :]
    cap = packets[0].shape[0] // 2
    half = layers * cap

    def stores(span, value):
        near[:, span] = value[:half].astype(bf16)
        far[:, span] = value[half:].astype(bf16)

    parts = [ref[...].astype(f32)[:cap] for ref in packets]
    rows[:half, :] = jnp.concatenate(parts, axis=0).astype(bf16)
    rows[half:, :] = crossed[...]
    expert_rows(rows, weights, active, stores)


def rejoin_kernel(near, far, *outs):
    cap = outs[0].shape[0] // 2
    both = [ref[...].astype(f32) for ref in (near, far)]
    for m, out in enumerate(outs):
        parts = [each[m * cap : (m + 1) * cap] for each in both]
        out[...] = jnp.concatenate(parts, axis=0).astype(bf16)


def partial_kernel(members, cap, columns, places, gates, near, far, *outs):
    at = iota((cap, places.shape[1]), 0)
    for n, m in enumerate(members):
        total = None
        near_rows = near[m * cap : (m + 1) * cap, :]
        far_rows = far[n * cap : (n + 1) * cap, :]
        for values, row in ((near_rows, m), (far_rows, columns + m)):
            spread = jnp.where(at == places[row : row + 1, :], gates[row : row + 1, :], 0.0)
            coarse = spread.astype(bf16)
            fine = (spread - coarse.astype(f32)).astype(bf16)
            for half in (coarse, fine):
                term = lax.dot_general(half, values, TN, preferred_element_type=f32)
                total = term if total is None else total + term
        outs[n][...] = total.astype(outs[n].dtype)


def fold_kernel(own, *rest):
    total = own[...]
    for ref in rest[:-1]:
        total = total + ref[...].astype(f32)
    rest[-1][...] = total.astype(rest[-1].dtype)


def final_kernel(layers, hidden, gates, rows, *rest):
    packets, ends, out = (rest[:layers], rest[layers:-1], rest[-1])
    at = iota((layers * packets[0].shape[0], hidden.shape[0]), 0)
    spread = jnp.where(at == rows[0:1, :], gates[0:1, :], 0.0)
    spread = spread + jnp.where(at == rows[1:2, :], gates[1:2, :], 0.0)
    coarse = spread.astype(bf16)
    fine = (spread - coarse.astype(f32)).astype(bf16)
    values = jnp.concatenate([ref[...].astype(f32) for ref in packets], axis=0).astype(bf16)
    total = hidden[...]
    for half in (coarse, fine):
        total = total + lax.dot_general(half, values, TN, preferred_element_type=f32)
    out[0, 0] = total.astype(bf16)
    total = ends[0][...]
    for ref in ends[1:]:
        total = total + ref[...].astype(f32)
    out[1, 0] = total.astype(bf16)


def local(
    tokens, queries, key_rows, value_rows, segments, bias_table, out_proj, router,
    gate_weight, up_weight, down_weight, old_table, new_table, routes_one, routes_two,
):
    tok_count, width = tokens.shape[2:]
    heads = bias_table.shape[0]
    experts = router.shape[1]
    columns = experts // 2
    inner = gate_weight.shape[2]
    seq_size = lax.axis_size("seq")
    seq_len = tok_count * seq_size
    capacity = tok_count * 2 * 5 // (4 * experts)
    longest = seq_len // 2
    hops = min(WIN_BLOCKS, (longest - 1 + tok_count - 1) // tok_count)
    relayed = seq_size == 4 and hops == 2
    sinks = seq_len > WIN_BLOCKS * tok_count
    weights = (gate_weight, up_weight, down_weight)
    router_t = router.T
    lower, upper = (range(columns // 2), range(columns // 2, columns))
    rows_bf16 = shaped((tok_count, width), bf16)
    rows_f32 = shaped((tok_count, width), f32)
    cap_two = capacity * MAX_SLOTS
    slots = columns * cap_two
    part_two = slots // 2
    packet = shaped((2 * capacity, width), bf16)
    latest = []

    def call(kernel, outs, ins, args, scratch=(), after=(), aliases=None, work=1):
        after = [*after, *latest]
        out_specs = jax.tree.map(lambda _: VMEM, outs)
        if aliases:
            out_specs = tuple(ANY if n in aliases.values() else VMEM for n in range(len(outs)))

        def body(*refs):
            kernel(*refs[: len(args)], *refs[len(args) + len(after) :])

        made = pl.pallas_call(
            body,
            out_shape=outs,
            in_specs=ins + [ANY] * len(after),
            out_specs=out_specs,
            scratch_shapes=list(scratch),
            input_output_aliases=aliases or {},
            compiler_params=pltpu.CompilerParams(vmem_limit_bytes=24 * 2**20),
            cost_estimate=pl.CostEstimate(flops=work, bytes_accessed=1, transcendentals=0),
        )(*args, *after)
        latest[:] = jax.tree.leaves(made)[:1]
        return made

    def multicast(own):
        blocks = {0: own}
        bit = columns // 2
        while bit:
            for m in sorted(blocks):
                blocks[m | bit] = swapped(blocks[m], "exp", 2 * bit)
            bit //= 2
        return blocks

    def chained(moving):
        moved = []
        for _ in range(hops):
            moving = passed_along(moving, "seq", 1)
            moved.append(moving)
        return moved

    def options(batch):
        extra = []
        if sinks:
            extra = latest_start(key_rows[batch, 0], value_rows[batch, 0], segments[batch, 0])
        return ((hops, relayed, heads, sinks), extra)

    def attend_column(moved):
        settings, extra = options(1)
        return call(
            functools.partial(attend_column_kernel, settings, experts),
            (rows_f32, rows_bf16, shaped((2 * columns, tok_count), jnp.int32)),
            [SMEM] + [VMEM] * (4 + columns + 2 * len(moved)) + ([VMEM, SMEM] if sinks else [])
            + [VMEM] * 2,
            (bias_table, own, queries, key_rows, value_rows, *routes,
             *moved, *sent, *extra, tokens, out_proj),
            scratch=[pltpu.VMEM((tok_count, width), bf16)],
        )

    def attend_direct(moved):
        settings, extra = options(0)
        return call(
            functools.partial(attend_direct_kernel, settings, experts, capacity),
            (*[packet] * columns, rows_f32, shaped((2, tok_count), f32),
             shaped((2, tok_count), jnp.int32)),
            [SMEM] + [VMEM] * (5 + 2 * len(moved)) + ([VMEM, SMEM] if sinks else [])
            + [VMEM] * 2,
            (bias_table, router_t, own, queries, key_rows, value_rows,
              *moved, *sent, *extra, tokens, out_proj),
            scratch=[pltpu.VMEM((tok_count, width), bf16)],
        )

    def scratch_for(slots):
        return (pltpu.VMEM((slots, width), bf16), pltpu.VMEM((slots, inner), bf16))

    def pack(members, places, blocks):
        return call(
            functools.partial(pack_kernel, members, cap_two, columns),
            shaped((part_two, width), bf16),
            [VMEM] * (1 + len(members)),
            (places, *(blocks[m] for m in members)),
        )

    def partial(members, far):
        parts = call(
            functools.partial(partial_kernel, members, cap_two, columns),
            tuple(rows_bf16 if m % 2 else rows_f32 for m in members),
            [VMEM] * 4,
            (places, gates_two, near, far),
        )
        for m, value in zip(members, parts):
            totals.setdefault(m, []).insert(0, value)

    def send_down(members):
        for m in sorted(members, key=lambda m: (m & -m, -m)):
            parts = totals[m]
            value = parts[0]
            if len(parts) > 1:
                value = call(fold_kernel, rows_bf16, [VMEM] * len(parts), parts)
            totals.setdefault(m & (m - 1), []).append(swapped(value, "exp", 2 * (m & -m)))

    stacked = jnp.concatenate([key_rows[1, 0], value_rows[1, 0]], axis=0)
    first_hop = swapped(stacked, "seq", 1) if relayed else passed_along(stacked, "seq", 1)
    tables = [jnp.pad(table, (0, tok_count - experts))[None] for table in (new_table, old_table)]
    numbers = jnp.concatenate([segments[:, 0], routes_one[0].T, routes_two[0].T, *tables])
    own, own_routes, own_segs = call(
        numbers_kernel,
        tuple(shaped((rows, tok_count), jnp.int32) for rows in (8, 2, 2)),
        [VMEM], (numbers,), after=[first_hop],
    )
    routes = multicast(own_routes)
    if relayed:
        sent = [swapped(own_segs, "seq", mask) for mask in (1, 2, 3)]
        across = swapped(stacked, "seq", 2)
    else:
        sent = chained(own_segs)
        across = first_hop
    *routes, latest_seg = call(
        collect_kernel,
        tuple(shaped((2, tok_count), jnp.int32) for _ in range(columns + 1)),
        [VMEM] * (columns + 1),
        (*(routes[m] for m in range(columns)), sent[-1]),
        after=sent[:-1],
    )
    sent = [*sent[:-1], latest_seg]
    stacked, across = call(
        stack_kernel, (shaped((2 * tok_count, width), bf16),) * 2, [VMEM] * 2 + [ANY],
        (key_rows, value_rows, across), aliases={2: 1},
    )
    if relayed:
        moved_two = [first_hop, across, swapped(across, "seq", 1)]
        moved_one = [
            swapped(stacked, "seq", 1),
            swapped(stacked, "seq", 2),
            lax.ppermute(stacked, "seq", [(0, 0), (1, 2), (2, 1), (3, 3)]),
        ]
    else:
        moved_two, moved_one = ([across], chained(stacked))
        while len(moved_two) < hops:
            moved_two.append(passed_along(moved_two[-1], "seq", 1))
    hidden_two, normed_two, places = attend_column(moved_two)
    blocks = multicast(normed_two)
    low_in = swapped(pack(lower, places, blocks), "exp", 1)
    *packets, hidden_one, gates_one, rows_one = attend_direct(moved_one)
    arrived = [packets[0]] + [swapped(packets[m], "exp", 2 * m) for m in range(1, columns)]
    high_in = swapped(pack(upper, places, blocks), "exp", 1)
    low_out, high_out = call(
        far_kernel,
        (shaped((part_two, width), bf16),) * 2,
        [VMEM] * 5,
        (low_in, high_in, *weights),
        scratch=scratch_for(slots),
    )
    high_far = swapped(high_out, "exp", 1)
    near, gates_two, low_out = call(
        functools.partial(near_kernel, columns, experts, cap_two),
        (shaped((slots, width), bf16), shaped((2 * columns, tok_count), f32),
         shaped((part_two, width), bf16)),
        [VMEM] * (6 + 2 * columns) + [ANY],
        (own, places, router_t, *(blocks[m] for m in range(columns)), *routes,
         *weights, low_out),
        scratch=scratch_for(slots), work=4 * 10**9, aliases={6 + 2 * columns: 2},
    )
    low_far = swapped(low_out, "exp", 1)
    crossing = call(
        crossing_kernel, shaped((columns * capacity, width), bf16), [VMEM] * columns, arrived,
        work=2 * 10**10,
    )
    crossed_one = swapped(crossing, "exp", 1)
    totals = {}
    partial(upper, high_far)
    send_down(m for m in upper if m % 2)
    near_one, far_one = call(
        functools.partial(direct_kernel, columns),
        (shaped((columns * capacity, width), bf16),) * 2,
        [VMEM] * (4 + columns),
        (*arrived, crossed_one, *weights),
        scratch=scratch_for(experts * capacity),
    )
    far_one = swapped(far_one, "exp", 1)
    send_down(m for m in upper if m % 2 == 0)
    partial(lower, low_far)
    send_down(m for m in lower if m)
    answers = call(rejoin_kernel, [packet] * columns, [VMEM] * 2, (near_one, far_one))
    returned = [answers[0]] + [swapped(answers[m], "exp", 2 * m) for m in range(1, columns)]
    ends = (hidden_two, *totals[0])
    return call(
        functools.partial(final_kernel, columns), shaped((2, 1, tok_count, width), bf16),
        [VMEM] * (3 + columns + len(ends)), (hidden_one, gates_one, rows_one, *returned, *ends),
    )


def solution(mesh):
    rows = P(None, "exp", "seq", None)
    placed = (
        rows, rows, rows, rows, P(None, "exp", "seq"), P(), P(), P(),
        P("exp", None, None), P("exp", None, None), P("exp", None, None), P(), P(),
        P("exp", "seq", None), P("exp", "seq", None),
    )
    return jax.shard_map(local, mesh=mesh, in_specs=placed, out_specs=rows, check_vma=False)
```

```python
import functools

import jax
import jax.numpy as jnp
from jax import lax
from jax.experimental import pallas as pl
from jax.experimental.pallas import tpu as pltpu
from jax.sharding import PartitionSpec as P

WIN_BLOCKS = 4
NBUCK = 32
MAX_SLOTS = 2
ONE_ROW, TWO_ROW, NEW_ROW, OLD_ROW = (2, 4, 6, 7)

score_scale = 0.125
epsilon = 1e-06
masked_score = -1e30

f32 = jnp.float32
bf16 = jnp.bfloat16
NT = (((1,), (1,)), ((), ()))
TN = (((0,), (0,)), ((), ()))
VMEM = pl.BlockSpec(memory_space=pltpu.VMEM)
SMEM = pl.BlockSpec(memory_space=pltpu.SMEM)
ANY = pl.BlockSpec(memory_space=pl.ANY)


def iota(shape, dim):
    return lax.broadcasted_iota(jnp.int32, shape, dim)


def shaped(shape, dtype):
    return jax.ShapeDtypeStruct(shape, dtype)


def passed_along(value, axis, steps):
    count = lax.axis_size(axis)
    return lax.ppermute(value, axis, [(source, source + steps) for source in range(count - steps)])


def swapped(value, axis, mask):
    count = lax.axis_size(axis)
    return lax.ppermute(value, axis, [(source, source ^ mask) for source in range(count)])


def merge_starts(former, latter):
    take_latter = (latter[4] > 0) & ((former[4] == 0) | (latter[3] != former[3]))
    return tuple((jnp.where(take_latter, newer, older) for older, newer in zip(former, latter)))


def latest_start(key_rows, value_rows, segments):
    tok_count, model_width = key_rows.shape
    length, index = (lax.axis_size("seq"), lax.axis_index("seq"))
    last_seg = segments[tok_count - 1]
    lead = jnp.sum((segments < last_seg).astype(jnp.int32))
    one = jnp.ones((), jnp.int32)
    found = (key_rows[lead], value_rows[lead], index * tok_count + lead, last_seg, one)
    everything = jax.tree.map(lambda part: lax.all_gather(part, "seq"), found)
    start = jax.tree.map(jnp.zeros_like, found)

    def lap(k, before):
        new = merge_starts(before, jax.tree.map(lambda part: part[k], everything))
        return jax.tree.map(lambda a, b: jnp.where(k < index, a, b), new, before)

    sink_key, sink_value, sink_pos, sink_seg, sink_has = lax.fori_loop(0, length, lap, start)
    block = jnp.zeros((2 * tok_count, model_width), key_rows.dtype)
    block = block.at[0].set(sink_key).at[tok_count].set(sink_value)
    return (block, jnp.stack([sink_pos, sink_seg, sink_has]))


def table_entry(own, row, entry):
    return own[row : row + 1, entry : entry + 1]


def holder_of(experts, own, pick):
    return sum(
        jnp.where(pick == table_entry(own, OLD_ROW, x), x, 0) for x in range(experts)
    )


def column_routes(experts, routes, own):
    members = len(routes)
    slots = jnp.concatenate([ref[c : c + 1, :] for c in range(2) for ref in routes], axis=0)
    chosen = sum(jnp.where(slots == s, table_entry(own, NEW_ROW, s), 0) for s in range(experts))
    holders = holder_of(experts, own, chosen)
    return tuple((each[:members], each[members:]) for each in (chosen, holders))


def attended(batch, hops, relayed, heads, sinks, bias, own, q, stack, rest, context):
    count = 3 if relayed else hops
    moved, sent, rest = (rest[:count], rest[count : 2 * count], rest[2 * count :])
    if sinks:
        sink_block, sink_info, rest = (rest[0], rest[1], rest[2:])
    tokens, proj = rest
    tok_count, width = tokens.shape[2:]
    window = WIN_BLOCKS * tok_count
    index = lax.axis_index("seq")
    grid = (tok_count, tok_count)

    own_seg = own[batch : batch + 1, :]
    key_segs = [own_seg]
    if relayed:
        pairwise, across, relay = moved
        paired = index % 2 == 1
        key_segs += [jnp.where(paired, sent[0][batch : batch + 1], sent[2][batch : batch + 1])]
        key_segs.append(sent[1][batch : batch + 1, :])
    else:
        key_segs += [ref[batch : batch + 1, :] for ref in sent]
    seg_col = jnp.broadcast_to(own_seg, grid).T
    visible, spans = ([], [])
    for j, key_seg in enumerate(key_segs):
        key_seg = jnp.where(index >= j, key_seg, -1)
        distance = iota(grid, 0) - iota(grid, 1) + tok_count * j
        seen = (seg_col == key_seg) & (distance >= 0) & (distance < window)
        visible.append(jnp.where(seen, 0.0, masked_score))
        low, high = (max(0, tok_count * (j - 1) + 1), min(window, tok_count * (j + 1)) - 1)
        spans.append((distance, low.bit_length(), high.bit_length()))
    if sinks:
        position = index * tok_count + iota(grid, 0)
        seen = (seg_col == sink_info[1]) & (sink_info[2] > 0) & (position - sink_info[0] >= window)
        visible.append(jnp.where(seen & (iota(grid, 1) == 0), 0.0, masked_score))
        spans.append((None, NBUCK - 1, NBUCK - 1))
    lane = iota((tok_count, 128), 1)
    half = width // heads
    keys_at, values_at = (slice(0, tok_count), slice(tok_count, 2 * tok_count))
    for pair in range(heads // 2):
        cols = slice(128 * pair, 128 * pair + 128)
        both = q[batch, 0, :, cols] * score_scale
        even = jnp.where(lane < half, both, jnp.zeros_like(both))
        odd = jnp.where(lane < half, jnp.zeros_like(both), both)
        stacked = jnp.concatenate([even, odd], axis=0)
        blocks = [(stack[keys_at, cols], stack[values_at, cols])]
        if relayed:
            blocks.append(tuple(
                jnp.where(paired, pairwise[at, cols], relay[at, cols])
                for at in (keys_at, values_at)
            ))
            blocks.append((across[keys_at, cols], across[values_at, cols]))
        else:
            for ref in moved:
                blocks.append((ref[keys_at, cols], ref[values_at, cols]))
        if sinks:
            blocks.append((sink_block[keys_at, cols], sink_block[values_at, cols]))
        scores = []
        for (keys, _), (distance, low, high), seen in zip(blocks, spans, visible):
            score = lax.dot_general(stacked, keys, NT, preferred_element_type=f32)
            parts = []
            for side in range(2):
                head = 2 * pair + side
                offset = jnp.full(grid, bias[head, low], f32)
                for bucket in range(low + 1, high + 1):
                    offset = jnp.where(distance >= 1 << (bucket - 1), bias[head, bucket], offset)
                parts.append(score[side * tok_count : (side + 1) * tok_count] + (offset + seen))
            scores.append(jnp.concatenate(parts, axis=0))
        peak = jnp.max(functools.reduce(jnp.maximum, scores), axis=1, keepdims=True)
        weights = [jnp.exp(score - peak) for score in scores]
        total = jnp.sum(functools.reduce(jnp.add, weights), axis=1, keepdims=True)
        scale = 1.0 / total
        mixed = sum(
            jnp.dot((weight * scale).astype(bf16), values, preferred_element_type=f32)
            for weight, (_, values) in zip(weights, blocks)
        )
        context[:, cols] = jnp.where(lane < half, mixed[:tok_count], mixed[tok_count:]).astype(bf16)
    hidden = tokens[batch, 0].astype(f32) + jnp.dot(
        context[...], proj[...], preferred_element_type=f32
    )
    mean = jnp.mean(hidden * hidden, axis=1, keepdims=True)
    return (hidden, (hidden * lax.rsqrt(mean + epsilon)).astype(bf16))


def ranks(member):
    grid = (member.shape[1], member.shape[1])
    earlier = jnp.where(iota(grid, 0) < iota(grid, 1), 1.0, 0.0).astype(bf16)
    return jnp.dot(member.astype(bf16), earlier, preferred_element_type=f32).astype(jnp.int32)


def attend_column_kernel(options, bias, own, q, stack, *rest):
    inputs, (hidden_out, normed_out, context) = (rest[:-3], rest[-3:])
    hidden, normed = attended(1, *options, bias, own, q, stack, inputs, context)
    hidden_out[...] = hidden
    normed_out[...] = normed


def column_places(experts, routes, own):
    me = lax.axis_index("exp")
    _, holders = column_routes(experts, routes, own)
    member = jnp.concatenate(
        [jnp.where((holders[0] == at) | (holders[1] == at), 1.0, 0.0) for at in (me, me ^ 1)],
        axis=0,
    )
    return jnp.where(member > 0.5, ranks(member), -1)


def attend_direct_kernel(options, experts, cap, bias, router_t, own, q, stack, *rest):
    layers = experts // 2
    inputs, rest = (rest[: -4 - layers], rest[-4 - layers :])
    outgoing, (hidden_out, gates_out, rows_out, context) = (rest[:layers], rest[layers:])
    hidden, normed = attended(0, *options, bias, own, q, stack, inputs, context)
    hidden_out[...] = hidden
    tok_count = hidden.shape[0]
    chosen = [own[ONE_ROW + c : ONE_ROW + c + 1, :] for c in range(2)]
    holders = [holder_of(experts, own, pick) for pick in chosen]
    expert = iota((experts, tok_count), 0)
    packet = expert ^ lax.axis_index("exp")
    member = jnp.where((packet == holders[0]) | (packet == holders[1]), 1.0, 0.0)
    place = ranks(member) + expert * cap
    rows = [
        jnp.sum(jnp.where(packet == holder, place, 0), axis=0, keepdims=True) for holder in holders
    ]
    rows_out[...] = jnp.concatenate(rows, axis=0)
    logits = lax.dot_general(router_t[...], normed, NT, preferred_element_type=f32)
    picked = [jnp.sum(jnp.where(expert == c, logits, 0.0), axis=0, keepdims=True) for c in chosen]
    first = jax.nn.sigmoid(picked[0] - picked[1])
    gates_out[...] = jnp.concatenate([first, 1.0 - first], axis=0)
    at = iota((experts * cap, tok_count), 0)
    plan = jnp.where((at == rows[0]) | (at == rows[1]), 1.0, 0.0).astype(bf16)
    packed = jnp.dot(plan, normed, preferred_element_type=f32)
    for m, ref in enumerate(outgoing):
        ref[...] = packed[2 * m * cap : 2 * (m + 1) * cap].astype(bf16)


def picked_rows(members, cap, first_row, places, blocks):
    at = iota((len(members) * cap, blocks[0].shape[0]), 0)
    plans = []
    for n, m in enumerate(members):
        place = places[first_row + m : first_row + m + 1, :]
        place = jnp.where(place >= 0, place + n * cap, -1)
        plans.append(jnp.where(at == place, 1.0, 0.0))
    plan = jnp.concatenate(plans, axis=1).astype(bf16)
    rows = jnp.concatenate([block[...] for block in blocks], axis=0)
    return (jnp.dot(plan, rows, preferred_element_type=f32).astype(bf16), rows)


def pack_kernel(members, cap, columns, places, *rest):
    blocks, out = (rest[:-1], rest[-1])
    out[...], _ = picked_rows(members, cap, columns, places, blocks)


def first_pack_kernel(members, cap, columns, own, *rest):
    routes, blocks, (places, out) = (rest[:columns], rest[columns:-2], rest[-2:])
    places[...] = column_places(2 * columns, routes, own)
    out[...], _ = picked_rows(members, cap, columns, places, blocks)


def numbers_kernel(numbers, own, routes_out, segs_out):
    own[...] = numbers[...]
    routes_out[...] = numbers[TWO_ROW : TWO_ROW + 2, :]
    segs_out[...] = numbers[:2, :]


def collect_kernel(*refs):
    count = len(refs) // 2
    for ref, out in zip(refs[:count], refs[count:]):
        out[...] = ref[...]


def stage_kernel(k, v, q, tokens, out):
    del q, tokens
    tok_count = k.shape[2]
    out[:tok_count, :] = k[0, 0]
    out[tok_count:, :] = v[0, 0]


def pass_kernel(*refs):
    del refs


def crossing_kernel(*refs):
    packets, out = (refs[:-1], refs[-1])
    cap = packets[0].shape[0] // 2
    parts = [ref[...].astype(f32)[cap:] for ref in packets]
    out[...] = jnp.concatenate(parts, axis=0).astype(bf16)


def expert_rows(rows, weights, active, stores):
    gate, up, down = weights
    inner, width = down.shape[1:]
    x = rows[...]
    for begin in range(0, inner, 256):
        span = slice(begin, min(inner, begin + 256))
        gate_part = jnp.dot(x, gate[0, :, span], preferred_element_type=f32)
        up_part = jnp.dot(x, up[0, :, span], preferred_element_type=f32)
        active[:, span] = (jax.nn.gelu(gate_part, approximate=True) * up_part).astype(bf16)
    for begin in range(0, width, 256):
        span = slice(begin, begin + 256)
        part = jnp.dot(active[...], down[0, :, span], preferred_element_type=f32)
        stores(span, part)


def near_kernel(columns, experts, cap, own, places, router_t, *rest):
    blocks, rest = (rest[:columns], rest[columns:])
    routes, rest = (rest[:columns], rest[columns:])
    weights, (_, out, gates_out, _, rows, active) = (rest[:3], rest[3:])

    def stores(span, value):
        out[:, span] = value.astype(bf16)

    rows[...], tokens = picked_rows(range(columns), cap, 0, places, blocks)
    logits = lax.dot_general(router_t[...], tokens, NT, preferred_element_type=f32)
    chosen, holders = column_routes(experts, routes, own)
    chosen = [
        jnp.concatenate([picks[m : m + 1, :] for m in range(columns)], axis=1) for picks in chosen
    ]
    expert = iota(logits.shape, 0)
    picked = [
        jnp.sum(jnp.where(expert == pick, logits, 0.0), axis=0, keepdims=True) for pick in chosen
    ]
    first = jax.nn.sigmoid(picked[0] - picked[1])
    tok_count = places.shape[1]
    first = jnp.concatenate(
        [first[:, m * tok_count : (m + 1) * tok_count] for m in range(columns)], axis=0
    )
    me = lax.axis_index("exp")
    gates_out[...] = jnp.concatenate(
        [
            jnp.where(holders[0] == at, first, 0.0) + jnp.where(holders[1] == at, 1.0 - first, 0.0)
            for at in (me, me ^ 1)
        ],
        axis=0,
    )
    expert_rows(rows, weights, active, stores)


def far_kernel(low_in, high_in, *rest):
    weights, (low_out, high_out, rows, active) = (rest[:3], rest[3:])
    part = low_in.shape[0]

    def stores(span, value):
        low_out[:, span] = value[:part].astype(bf16)
        high_out[:, span] = value[part:].astype(bf16)

    rows[:part, :] = low_in[...]
    rows[part:, :] = high_in[...]
    expert_rows(rows, weights, active, stores)


def direct_kernel(layers, *refs):
    packets, crossed, weights = (refs[:layers], refs[layers], refs[layers + 1 : layers + 4])
    near, far, rows, active = refs[layers + 4 :]
    cap = packets[0].shape[0] // 2
    half = layers * cap

    def stores(span, value):
        near[:, span] = value[:half].astype(bf16)
        far[:, span] = value[half:].astype(bf16)

    parts = [ref[...].astype(f32)[:cap] for ref in packets]
    rows[:half, :] = jnp.concatenate(parts, axis=0).astype(bf16)
    rows[half:, :] = crossed[...]
    expert_rows(rows, weights, active, stores)


def rejoin_kernel(near, far, *outs):
    cap = outs[0].shape[0] // 2
    both = [ref[...].astype(f32) for ref in (near, far)]
    for m, out in enumerate(outs):
        parts = [each[m * cap : (m + 1) * cap] for each in both]
        out[...] = jnp.concatenate(parts, axis=0).astype(bf16)


def partial_kernel(members, cap, columns, places, gates, near, far, *outs):
    at = iota((cap, places.shape[1]), 0)
    for n, m in enumerate(members):
        total = None
        near_rows = near[m * cap : (m + 1) * cap, :]
        far_rows = far[n * cap : (n + 1) * cap, :]
        for values, row in ((near_rows, m), (far_rows, columns + m)):
            spread = jnp.where(at == places[row : row + 1, :], gates[row : row + 1, :], 0.0)
            coarse = spread.astype(bf16)
            fine = (spread - coarse.astype(f32)).astype(bf16)
            for half in (coarse, fine):
                term = lax.dot_general(half, values, TN, preferred_element_type=f32)
                total = term if total is None else total + term
        outs[n][...] = total.astype(outs[n].dtype)


def fold_kernel(own, *rest):
    total = own[...]
    for ref in rest[:-1]:
        total = total + ref[...].astype(f32)
    rest[-1][...] = total.astype(rest[-1].dtype)


def final_kernel(layers, hidden, gates, rows, *rest):
    packets, ends, out = (rest[:layers], rest[layers:-1], rest[-1])
    at = iota((layers * packets[0].shape[0], hidden.shape[0]), 0)
    spread = jnp.where(at == rows[0:1, :], gates[0:1, :], 0.0)
    spread = spread + jnp.where(at == rows[1:2, :], gates[1:2, :], 0.0)
    coarse = spread.astype(bf16)
    fine = (spread - coarse.astype(f32)).astype(bf16)
    values = jnp.concatenate([ref[...].astype(f32) for ref in packets], axis=0).astype(bf16)
    total = hidden[...]
    for half in (coarse, fine):
        total = total + lax.dot_general(half, values, TN, preferred_element_type=f32)
    out[0, 0] = total.astype(bf16)
    total = ends[0][...]
    for ref in ends[1:]:
        total = total + ref[...].astype(f32)
    out[1, 0] = total.astype(bf16)


def local(
    tokens, queries, key_rows, value_rows, segments, bias_table, out_proj, router,
    gate_weight, up_weight, down_weight, old_table, new_table, routes_one, routes_two,
):
    tok_count, width = tokens.shape[2:]
    heads = bias_table.shape[0]
    experts = router.shape[1]
    columns = experts // 2
    inner = gate_weight.shape[2]
    seq_size = lax.axis_size("seq")
    seq_len = tok_count * seq_size
    capacity = tok_count * 2 * 5 // (4 * experts)
    longest = seq_len // 2
    hops = min(WIN_BLOCKS, (longest - 1 + tok_count - 1) // tok_count)
    relayed = seq_size == 4 and hops == 2
    sinks = seq_len > WIN_BLOCKS * tok_count
    weights = (gate_weight, up_weight, down_weight)
    router_t = router.T
    lower, upper = (range(columns // 2), range(columns // 2, columns))
    rows_bf16 = shaped((tok_count, width), bf16)
    rows_f32 = shaped((tok_count, width), f32)
    cap_two = capacity * MAX_SLOTS
    slots = columns * cap_two
    part_two = slots // 2
    packet = shaped((2 * capacity, width), bf16)
    stack_shape = shaped((2 * tok_count, width), bf16)
    latest = []

    def call(kernel, outs, ins, args, scratch=(), after=(), aliases=None, work=1):
        after = [*after, *latest]
        out_specs = jax.tree.map(lambda _: VMEM, outs)
        if aliases:
            out_specs = tuple(ANY if n in aliases.values() else VMEM for n in range(len(outs)))

        def body(*refs):
            kernel(*refs[: len(args)], *refs[len(args) + len(after) :])

        made = pl.pallas_call(
            body,
            out_shape=outs,
            in_specs=ins + [ANY] * len(after),
            out_specs=out_specs,
            scratch_shapes=list(scratch),
            input_output_aliases=aliases or {},
            compiler_params=pltpu.CompilerParams(vmem_limit_bytes=24 * 2**20),
            cost_estimate=pl.CostEstimate(flops=work, bytes_accessed=1, transcendentals=0),
        )(*args, *after)
        latest[:] = jax.tree.leaves(made)[:1]
        return made

    def multicast(own):
        blocks = {0: own}
        bit = columns // 2
        while bit:
            for m in sorted(blocks):
                blocks[m | bit] = swapped(blocks[m], "exp", 2 * bit)
            bit //= 2
        return blocks

    def chained(moving):
        moved = []
        for _ in range(hops):
            moving = passed_along(moving, "seq", 1)
            moved.append(moving)
        return moved

    def options(batch):
        extra = []
        if sinks:
            extra = latest_start(key_rows[batch, 0], value_rows[batch, 0], segments[batch, 0])
        return ((hops, relayed, heads, sinks), extra)

    def attend_column(moved):
        settings, extra = options(1)
        return call(
            functools.partial(attend_column_kernel, settings),
            (rows_f32, rows_bf16),
            [SMEM] + [VMEM] * (3 + 2 * len(moved)) + ([VMEM, SMEM] if sinks else [])
            + [VMEM] * 2,
            (bias_table, own, queries, stacks[1], *moved, *sent, *extra, tokens, out_proj),
            scratch=[pltpu.VMEM((tok_count, width), bf16)],
        )

    def attend_direct(moved):
        settings, extra = options(0)
        return call(
            functools.partial(attend_direct_kernel, settings, experts, capacity),
            (*[packet] * columns, rows_f32, shaped((2, tok_count), f32),
             shaped((2, tok_count), jnp.int32)),
            [SMEM] + [VMEM] * (4 + 2 * len(moved)) + ([VMEM, SMEM] if sinks else [])
            + [VMEM] * 2,
            (bias_table, router_t, own, queries, stacks[0], *moved, *sent, *extra, tokens,
             out_proj),
            scratch=[pltpu.VMEM((tok_count, width), bf16)],
        )

    def scratch_for(slots):
        return (pltpu.VMEM((slots, width), bf16), pltpu.VMEM((slots, inner), bf16))

    def pack(members, places, blocks):
        return call(
            functools.partial(pack_kernel, members, cap_two, columns),
            shaped((part_two, width), bf16),
            [VMEM] * (1 + len(members)),
            (places, *(blocks[m] for m in members)),
        )

    def partial(members, far):
        parts = call(
            functools.partial(partial_kernel, members, cap_two, columns),
            tuple(rows_bf16 if m % 2 else rows_f32 for m in members),
            [VMEM] * 4,
            (places, gates_two, near, far),
        )
        for m, value in zip(members, parts):
            totals.setdefault(m, []).insert(0, value)

    def send_down(members):
        for m in sorted(members, key=lambda m: (m & -m, -m)):
            parts = totals[m]
            value = parts[0]
            if len(parts) > 1:
                value = call(fold_kernel, rows_bf16, [VMEM] * len(parts), parts)
            totals.setdefault(m & (m - 1), []).append(swapped(value, "exp", 2 * (m & -m)))

    stacked = jnp.concatenate([key_rows[1, 0], value_rows[1, 0]], axis=0)
    first_hop = swapped(stacked, "seq", 1) if relayed else passed_along(stacked, "seq", 1)
    tables = [jnp.pad(table, (0, tok_count - experts))[None] for table in (new_table, old_table)]
    numbers = jnp.concatenate([segments[:, 0], routes_one[0].T, routes_two[0].T, *tables])
    own, own_routes, own_segs = call(
        numbers_kernel,
        tuple(shaped((rows, tok_count), jnp.int32) for rows in (8, 2, 2)),
        [VMEM], (numbers,), after=[first_hop],
    )
    routes = multicast(own_routes)
    if relayed:
        sent = [swapped(own_segs, "seq", mask) for mask in (1, 2, 3)]
        across = swapped(stacked, "seq", 2)
    else:
        sent = chained(own_segs)
        across = first_hop
    stack_one = call(
        stage_kernel, stack_shape, [VMEM] * 4, (key_rows, value_rows, queries, tokens),
        after=[routes[columns // 2]],
    )
    *routes, latest_seg = call(
        collect_kernel,
        tuple(shaped((2, tok_count), jnp.int32) for _ in range(columns + 1)),
        [VMEM] * (columns + 1),
        (*(routes[m] for m in range(columns)), sent[-1]),
        after=sent[:-1],
    )
    sent = [*sent[:-1], latest_seg]
    stack_one, across = call(
        pass_kernel, (stack_shape, stack_shape), [ANY] * 2, (stack_one, across),
        aliases={0: 0, 1: 1},
    )
    stacks = (stack_one, stacked)
    if relayed:
        moved_two = [first_hop, across, swapped(across, "seq", 1)]
        moved_one = [
            swapped(stack_one, "seq", 1),
            swapped(stack_one, "seq", 2),
            lax.ppermute(stack_one, "seq", [(0, 0), (1, 2), (2, 1), (3, 3)]),
        ]
    else:
        moved_two, moved_one = ([across], chained(stack_one))
        while len(moved_two) < hops:
            moved_two.append(passed_along(moved_two[-1], "seq", 1))
    hidden_two, normed_two = attend_column(moved_two)
    blocks = multicast(normed_two)
    places, low_in = call(
        functools.partial(first_pack_kernel, lower, cap_two, columns),
        (shaped((2 * columns, tok_count), jnp.int32), shaped((part_two, width), bf16)),
        [VMEM] * (1 + columns + len(lower)),
        (own, *routes, *(blocks[m] for m in lower)),
    )
    low_in = swapped(low_in, "exp", 1)
    *packets, hidden_one, gates_one, rows_one = attend_direct(moved_one)
    arrived = [packets[0]] + [swapped(packets[m], "exp", 2 * m) for m in range(1, columns)]
    high_in = swapped(pack(upper, places, blocks), "exp", 1)
    low_out, high_out = call(
        far_kernel,
        (shaped((part_two, width), bf16),) * 2,
        [VMEM] * 5,
        (low_in, high_in, *weights),
        scratch=scratch_for(slots),
    )
    high_far = swapped(high_out, "exp", 1)
    crossing = call(
        crossing_kernel, shaped((columns * capacity, width), bf16), [VMEM] * columns, arrived,
        work=2 * 10**10,
    )
    crossed_one = swapped(crossing, "exp", 1)
    near, gates_two, low_out = call(
        functools.partial(near_kernel, columns, experts, cap_two),
        (shaped((slots, width), bf16), shaped((2 * columns, tok_count), f32),
         shaped((part_two, width), bf16)),
        [VMEM] * (6 + 2 * columns) + [ANY],
        (own, places, router_t, *(blocks[m] for m in range(columns)), *routes,
         *weights, low_out),
        scratch=scratch_for(slots), work=4 * 10**9, aliases={6 + 2 * columns: 2},
    )
    low_far = swapped(low_out, "exp", 1)
    totals = {}
    partial(upper, high_far)
    send_down(m for m in upper if m % 2)
    near_one, far_one = call(
        functools.partial(direct_kernel, columns),
        (shaped((columns * capacity, width), bf16),) * 2,
        [VMEM] * (4 + columns),
        (*arrived, crossed_one, *weights),
        scratch=scratch_for(experts * capacity),
    )
    far_one = swapped(far_one, "exp", 1)
    send_down(m for m in upper if m % 2 == 0)
    partial(lower, low_far)
    send_down(m for m in lower if m)
    answers = call(rejoin_kernel, [packet] * columns, [VMEM] * 2, (near_one, far_one))
    returned = [answers[0]] + [swapped(answers[m], "exp", 2 * m) for m in range(1, columns)]
    ends = (hidden_two, *totals[0])
    return call(
        functools.partial(final_kernel, columns), shaped((2, 1, tok_count, width), bf16),
        [VMEM] * (3 + columns + len(ends)), (hidden_one, gates_one, rows_one, *returned, *ends),
    )


def solution(mesh):
    rows = P(None, "exp", "seq", None)
    placed = (
        rows, rows, rows, rows, P(None, "exp", "seq"), P(), P(), P(),
        P("exp", None, None), P("exp", None, None), P("exp", None, None), P(), P(),
        P("exp", "seq", None), P("exp", "seq", None),
    )
    return jax.shard_map(local, mesh=mesh, in_specs=placed, out_specs=rows, check_vma=False)
```

```python
import functools

import jax
import jax.numpy as jnp
from jax import lax
from jax.experimental import pallas as pl
from jax.experimental.pallas import tpu as pltpu
from jax.sharding import PartitionSpec as P

WIN_BLOCKS = 4
NBUCK = 32
MAX_SLOTS = 2
ONE_ROW, TWO_ROW, NEW_ROW, OLD_ROW = (2, 4, 6, 7)

score_scale = 0.125
epsilon = 1e-06
masked_score = -1e30

f32 = jnp.float32
bf16 = jnp.bfloat16
NT = (((1,), (1,)), ((), ()))
TN = (((0,), (0,)), ((), ()))
VMEM = pl.BlockSpec(memory_space=pltpu.VMEM)
SMEM = pl.BlockSpec(memory_space=pltpu.SMEM)
ANY = pl.BlockSpec(memory_space=pl.ANY)


def iota(shape, dim):
    return lax.broadcasted_iota(jnp.int32, shape, dim)


def shaped(shape, dtype):
    return jax.ShapeDtypeStruct(shape, dtype)


def passed_along(value, axis, steps):
    count = lax.axis_size(axis)
    return lax.ppermute(value, axis, [(source, source + steps) for source in range(count - steps)])


def swapped(value, axis, mask):
    count = lax.axis_size(axis)
    return lax.ppermute(value, axis, [(source, source ^ mask) for source in range(count)])


def merge_starts(former, latter):
    take_latter = (latter[4] > 0) & ((former[4] == 0) | (latter[3] != former[3]))
    return tuple((jnp.where(take_latter, newer, older) for older, newer in zip(former, latter)))


def latest_start(key_rows, value_rows, segments):
    tok_count, model_width = key_rows.shape
    length, index = (lax.axis_size("seq"), lax.axis_index("seq"))
    last_seg = segments[tok_count - 1]
    lead = jnp.sum((segments < last_seg).astype(jnp.int32))
    one = jnp.ones((), jnp.int32)
    found = (key_rows[lead], value_rows[lead], index * tok_count + lead, last_seg, one)
    everything = jax.tree.map(lambda part: lax.all_gather(part, "seq"), found)
    start = jax.tree.map(jnp.zeros_like, found)

    def lap(k, before):
        new = merge_starts(before, jax.tree.map(lambda part: part[k], everything))
        return jax.tree.map(lambda a, b: jnp.where(k < index, a, b), new, before)

    sink_key, sink_value, sink_pos, sink_seg, sink_has = lax.fori_loop(0, length, lap, start)
    block = jnp.zeros((2 * tok_count, model_width), key_rows.dtype)
    block = block.at[0].set(sink_key).at[tok_count].set(sink_value)
    return (block, jnp.stack([sink_pos, sink_seg, sink_has]))


def table_entry(own, row, entry):
    return own[row : row + 1, entry : entry + 1]


def holder_of(experts, own, pick):
    return sum(
        jnp.where(pick == table_entry(own, OLD_ROW, x), x, 0) for x in range(experts)
    )


def column_routes(experts, routes, own):
    members = len(routes)
    slots = jnp.concatenate([ref[c : c + 1, :] for c in range(2) for ref in routes], axis=0)
    chosen = sum(jnp.where(slots == s, table_entry(own, NEW_ROW, s), 0) for s in range(experts))
    holders = holder_of(experts, own, chosen)
    return tuple((each[:members], each[members:]) for each in (chosen, holders))


def attended(batch, hops, relayed, heads, sinks, bias, own, q, stack, rest, context):
    count = 3 if relayed else hops
    moved, sent, rest = (rest[:count], rest[count : 2 * count], rest[2 * count :])
    if sinks:
        sink_block, sink_info, rest = (rest[0], rest[1], rest[2:])
    tokens, proj = rest
    tok_count, width = tokens.shape[2:]
    window = WIN_BLOCKS * tok_count
    index = lax.axis_index("seq")
    grid = (tok_count, tok_count)

    own_seg = own[batch : batch + 1, :]
    key_segs = [own_seg]
    if relayed:
        pairwise, across, relay = moved
        paired = index % 2 == 1
        key_segs += [jnp.where(paired, sent[0][batch : batch + 1], sent[2][batch : batch + 1])]
        key_segs.append(sent[1][batch : batch + 1, :])
    else:
        key_segs += [ref[batch : batch + 1, :] for ref in sent]
    seg_col = jnp.broadcast_to(own_seg, grid).T
    visible, spans = ([], [])
    for j, key_seg in enumerate(key_segs):
        key_seg = jnp.where(index >= j, key_seg, -1)
        distance = iota(grid, 0) - iota(grid, 1) + tok_count * j
        seen = (seg_col == key_seg) & (distance >= 0) & (distance < window)
        visible.append(jnp.where(seen, 0.0, masked_score))
        low, high = (max(0, tok_count * (j - 1) + 1), min(window, tok_count * (j + 1)) - 1)
        spans.append((distance, low.bit_length(), high.bit_length()))
    if sinks:
        position = index * tok_count + iota(grid, 0)
        seen = (seg_col == sink_info[1]) & (sink_info[2] > 0) & (position - sink_info[0] >= window)
        visible.append(jnp.where(seen & (iota(grid, 1) == 0), 0.0, masked_score))
        spans.append((None, NBUCK - 1, NBUCK - 1))
    lane = iota((tok_count, 128), 1)
    half = width // heads
    keys_at, values_at = (slice(0, tok_count), slice(tok_count, 2 * tok_count))
    for pair in range(heads // 2):
        cols = slice(128 * pair, 128 * pair + 128)
        both = q[batch, 0, :, cols] * score_scale
        even = jnp.where(lane < half, both, jnp.zeros_like(both))
        odd = jnp.where(lane < half, jnp.zeros_like(both), both)
        stacked = jnp.concatenate([even, odd], axis=0)
        blocks = [(stack[keys_at, cols], stack[values_at, cols])]
        if relayed:
            blocks.append(tuple(
                jnp.where(paired, pairwise[at, cols], relay[at, cols])
                for at in (keys_at, values_at)
            ))
            blocks.append((across[keys_at, cols], across[values_at, cols]))
        else:
            for ref in moved:
                blocks.append((ref[keys_at, cols], ref[values_at, cols]))
        if sinks:
            blocks.append((sink_block[keys_at, cols], sink_block[values_at, cols]))
        scores = []
        for (keys, _), (distance, low, high), seen in zip(blocks, spans, visible):
            score = lax.dot_general(stacked, keys, NT, preferred_element_type=f32)
            parts = []
            for side in range(2):
                head = 2 * pair + side
                offset = jnp.full(grid, bias[head, low], f32)
                for bucket in range(low + 1, high + 1):
                    offset = jnp.where(distance >= 1 << (bucket - 1), bias[head, bucket], offset)
                parts.append(score[side * tok_count : (side + 1) * tok_count] + (offset + seen))
            scores.append(jnp.concatenate(parts, axis=0))
        peak = jnp.max(functools.reduce(jnp.maximum, scores), axis=1, keepdims=True)
        weights = [jnp.exp(score - peak) for score in scores]
        total = jnp.sum(functools.reduce(jnp.add, weights), axis=1, keepdims=True)
        scale = 1.0 / total
        mixed = sum(
            jnp.dot((weight * scale).astype(bf16), values, preferred_element_type=f32)
            for weight, (_, values) in zip(weights, blocks)
        )
        context[:, cols] = jnp.where(lane < half, mixed[:tok_count], mixed[tok_count:]).astype(bf16)
    hidden = tokens[batch, 0].astype(f32) + jnp.dot(
        context[...], proj[...], preferred_element_type=f32
    )
    mean = jnp.mean(hidden * hidden, axis=1, keepdims=True)
    return (hidden, (hidden * lax.rsqrt(mean + epsilon)).astype(bf16))


def ranks(member):
    grid = (member.shape[1], member.shape[1])
    earlier = jnp.where(iota(grid, 0) < iota(grid, 1), 1.0, 0.0).astype(bf16)
    return jnp.dot(member.astype(bf16), earlier, preferred_element_type=f32).astype(jnp.int32)


def attend_column_kernel(options, bias, own, q, stack, *rest):
    inputs, (hidden_out, normed_out, context) = (rest[:-3], rest[-3:])
    hidden, normed = attended(1, *options, bias, own, q, stack, inputs, context)
    hidden_out[...] = hidden
    normed_out[...] = normed


def column_places(experts, routes, own):
    me = lax.axis_index("exp")
    _, holders = column_routes(experts, routes, own)
    member = jnp.concatenate(
        [jnp.where((holders[0] == at) | (holders[1] == at), 1.0, 0.0) for at in (me, me ^ 1)],
        axis=0,
    )
    return jnp.where(member > 0.5, ranks(member), -1)


def attend_direct_kernel(options, experts, cap, bias, router_t, own, q, stack, *rest):
    layers = experts // 2
    inputs, rest = (rest[: -4 - layers], rest[-4 - layers :])
    outgoing, (hidden_out, gates_out, rows_out, context) = (rest[:layers], rest[layers:])
    hidden, normed = attended(0, *options, bias, own, q, stack, inputs, context)
    hidden_out[...] = hidden
    tok_count = hidden.shape[0]
    chosen = [own[ONE_ROW + c : ONE_ROW + c + 1, :] for c in range(2)]
    holders = [holder_of(experts, own, pick) for pick in chosen]
    expert = iota((experts, tok_count), 0)
    packet = expert ^ lax.axis_index("exp")
    member = jnp.where((packet == holders[0]) | (packet == holders[1]), 1.0, 0.0)
    place = ranks(member) + expert * cap
    rows = [
        jnp.sum(jnp.where(packet == holder, place, 0), axis=0, keepdims=True) for holder in holders
    ]
    rows_out[...] = jnp.concatenate(rows, axis=0)
    logits = lax.dot_general(router_t[...], normed, NT, preferred_element_type=f32)
    picked = [jnp.sum(jnp.where(expert == c, logits, 0.0), axis=0, keepdims=True) for c in chosen]
    first = jax.nn.sigmoid(picked[0] - picked[1])
    gates_out[...] = jnp.concatenate([first, 1.0 - first], axis=0)
    at = iota((experts * cap, tok_count), 0)
    plan = jnp.where((at == rows[0]) | (at == rows[1]), 1.0, 0.0).astype(bf16)
    packed = jnp.dot(plan, normed, preferred_element_type=f32)
    for m, ref in enumerate(outgoing):
        ref[...] = packed[2 * m * cap : 2 * (m + 1) * cap].astype(bf16)


def picked_rows(members, cap, first_row, places, blocks):
    at = iota((len(members) * cap, blocks[0].shape[0]), 0)
    plans = []
    for n, m in enumerate(members):
        place = places[first_row + m : first_row + m + 1, :]
        place = jnp.where(place >= 0, place + n * cap, -1)
        plans.append(jnp.where(at == place, 1.0, 0.0))
    plan = jnp.concatenate(plans, axis=1).astype(bf16)
    rows = jnp.concatenate([block[...] for block in blocks], axis=0)
    return (jnp.dot(plan, rows, preferred_element_type=f32).astype(bf16), rows)


def pack_kernel(members, cap, columns, places, *rest):
    blocks, out = (rest[:-1], rest[-1])
    out[...], _ = picked_rows(members, cap, columns, places, blocks)


def first_pack_kernel(members, cap, columns, own, *rest):
    routes, blocks, (places, out) = (rest[:columns], rest[columns:-2], rest[-2:])
    places[...] = column_places(2 * columns, routes, own)
    out[...], _ = picked_rows(members, cap, columns, places, blocks)


def numbers_kernel(numbers, own, routes_out, segs_out):
    own[...] = numbers[...]
    routes_out[...] = numbers[TWO_ROW : TWO_ROW + 2, :]
    segs_out[...] = numbers[:2, :]


def collect_kernel(*refs):
    count = len(refs) // 2
    for ref, out in zip(refs[:count], refs[count:]):
        out[...] = ref[...]


def stage_kernel(k, v, q, tokens, out):
    del q, tokens
    tok_count = k.shape[2]
    out[:tok_count, :] = k[0, 0]
    out[tok_count:, :] = v[0, 0]


def pass_kernel(*refs):
    del refs


def crossing_kernel(*refs):
    packets, out = (refs[:-1], refs[-1])
    cap = packets[0].shape[0] // 2
    parts = [ref[...].astype(f32)[cap:] for ref in packets]
    out[...] = jnp.concatenate(parts, axis=0).astype(bf16)


def expert_rows(rows, weights, active, stores):
    gate, up, down = weights
    inner, width = down.shape[1:]
    x = rows[...]
    for begin in range(0, inner, 256):
        span = slice(begin, min(inner, begin + 256))
        gate_part = jnp.dot(x, gate[0, :, span], preferred_element_type=f32)
        up_part = jnp.dot(x, up[0, :, span], preferred_element_type=f32)
        active[:, span] = (jax.nn.gelu(gate_part, approximate=True) * up_part).astype(bf16)
    for begin in range(0, width, 256):
        span = slice(begin, begin + 256)
        part = jnp.dot(active[...], down[0, :, span], preferred_element_type=f32)
        stores(span, part)


def near_kernel(columns, experts, cap, own, places, router_t, *rest):
    blocks, rest = (rest[:columns], rest[columns:])
    routes, rest = (rest[:columns], rest[columns:])
    weights, (_, out, gates_out, _, rows, active) = (rest[:3], rest[3:])

    def stores(span, value):
        out[:, span] = value.astype(bf16)

    rows[...], tokens = picked_rows(range(columns), cap, 0, places, blocks)
    logits = lax.dot_general(router_t[...], tokens, NT, preferred_element_type=f32)
    chosen, holders = column_routes(experts, routes, own)
    chosen = [
        jnp.concatenate([picks[m : m + 1, :] for m in range(columns)], axis=1) for picks in chosen
    ]
    expert = iota(logits.shape, 0)
    picked = [
        jnp.sum(jnp.where(expert == pick, logits, 0.0), axis=0, keepdims=True) for pick in chosen
    ]
    first = jax.nn.sigmoid(picked[0] - picked[1])
    tok_count = places.shape[1]
    first = jnp.concatenate(
        [first[:, m * tok_count : (m + 1) * tok_count] for m in range(columns)], axis=0
    )
    me = lax.axis_index("exp")
    gates_out[...] = jnp.concatenate(
        [
            jnp.where(holders[0] == at, first, 0.0) + jnp.where(holders[1] == at, 1.0 - first, 0.0)
            for at in (me, me ^ 1)
        ],
        axis=0,
    )
    expert_rows(rows, weights, active, stores)


def far_kernel(low_in, high_in, *rest):
    weights, (low_out, high_out, rows, active) = (rest[:3], rest[3:])
    part = low_in.shape[0]

    def stores(span, value):
        low_out[:, span] = value[:part].astype(bf16)
        high_out[:, span] = value[part:].astype(bf16)

    rows[:part, :] = low_in[...]
    rows[part:, :] = high_in[...]
    expert_rows(rows, weights, active, stores)


def direct_kernel(layers, *refs):
    packets, crossed, weights = (refs[:layers], refs[layers], refs[layers + 1 : layers + 4])
    near, far, rows, active = refs[layers + 4 :]
    cap = packets[0].shape[0] // 2
    half = layers * cap

    def stores(span, value):
        near[:, span] = value[:half].astype(bf16)
        far[:, span] = value[half:].astype(bf16)

    parts = [ref[...].astype(f32)[:cap] for ref in packets]
    rows[:half, :] = jnp.concatenate(parts, axis=0).astype(bf16)
    rows[half:, :] = crossed[...]
    expert_rows(rows, weights, active, stores)


def rejoin_kernel(near, far, *outs):
    cap = outs[0].shape[0] // 2
    both = [ref[...].astype(f32) for ref in (near, far)]
    for m, out in enumerate(outs):
        parts = [each[m * cap : (m + 1) * cap] for each in both]
        out[...] = jnp.concatenate(parts, axis=0).astype(bf16)


def partial_kernel(members, cap, columns, places, gates, near, far, *outs):
    at = iota((cap, places.shape[1]), 0)
    for n, m in enumerate(members):
        total = None
        near_rows = near[m * cap : (m + 1) * cap, :]
        far_rows = far[n * cap : (n + 1) * cap, :]
        for values, row in ((near_rows, m), (far_rows, columns + m)):
            spread = jnp.where(at == places[row : row + 1, :], gates[row : row + 1, :], 0.0)
            coarse = spread.astype(bf16)
            fine = (spread - coarse.astype(f32)).astype(bf16)
            for half in (coarse, fine):
                term = lax.dot_general(half, values, TN, preferred_element_type=f32)
                total = term if total is None else total + term
        outs[n][...] = total.astype(outs[n].dtype)


def fold_kernel(own, *rest):
    total = own[...]
    for ref in rest[:-1]:
        total = total + ref[...].astype(f32)
    rest[-1][...] = total.astype(rest[-1].dtype)


def final_kernel(layers, hidden, gates, rows, *rest):
    packets, ends, out = (rest[:layers], rest[layers:-1], rest[-1])
    at = iota((layers * packets[0].shape[0], hidden.shape[0]), 0)
    spread = jnp.where(at == rows[0:1, :], gates[0:1, :], 0.0)
    spread = spread + jnp.where(at == rows[1:2, :], gates[1:2, :], 0.0)
    coarse = spread.astype(bf16)
    fine = (spread - coarse.astype(f32)).astype(bf16)
    values = jnp.concatenate([ref[...].astype(f32) for ref in packets], axis=0).astype(bf16)
    total = hidden[...]
    for half in (coarse, fine):
        total = total + lax.dot_general(half, values, TN, preferred_element_type=f32)
    out[0, 0] = total.astype(bf16)
    total = ends[0][...]
    for ref in ends[1:]:
        total = total + ref[...].astype(f32)
    out[1, 0] = total.astype(bf16)


def local(
    tokens, queries, key_rows, value_rows, segments, bias_table, out_proj, router,
    gate_weight, up_weight, down_weight, old_table, new_table, routes_one, routes_two,
):
    tok_count, width = tokens.shape[2:]
    heads = bias_table.shape[0]
    experts = router.shape[1]
    columns = experts // 2
    inner = gate_weight.shape[2]
    seq_size = lax.axis_size("seq")
    seq_len = tok_count * seq_size
    capacity = tok_count * 2 * 5 // (4 * experts)
    longest = seq_len // 2
    hops = min(WIN_BLOCKS, (longest - 1 + tok_count - 1) // tok_count)
    relayed = seq_size == 4 and hops == 2
    sinks = seq_len > WIN_BLOCKS * tok_count
    weights = (gate_weight, up_weight, down_weight)
    router_t = router.T
    lower, upper = (range(columns // 2), range(columns // 2, columns))
    rows_bf16 = shaped((tok_count, width), bf16)
    rows_f32 = shaped((tok_count, width), f32)
    cap_two = capacity * MAX_SLOTS
    slots = columns * cap_two
    part_two = slots // 2
    packet = shaped((2 * capacity, width), bf16)
    stack_shape = shaped((2 * tok_count, width), bf16)
    latest = []

    def call(kernel, outs, ins, args, scratch=(), after=(), aliases=None, work=1):
        after = [*after, *latest]
        out_specs = jax.tree.map(lambda _: VMEM, outs)
        if aliases:
            out_specs = tuple(ANY if n in aliases.values() else VMEM for n in range(len(outs)))

        def body(*refs):
            kernel(*refs[: len(args)], *refs[len(args) + len(after) :])

        made = pl.pallas_call(
            body,
            out_shape=outs,
            in_specs=ins + [ANY] * len(after),
            out_specs=out_specs,
            scratch_shapes=list(scratch),
            input_output_aliases=aliases or {},
            compiler_params=pltpu.CompilerParams(vmem_limit_bytes=24 * 2**20),
            cost_estimate=pl.CostEstimate(flops=work, bytes_accessed=1, transcendentals=0),
        )(*args, *after)
        latest[:] = jax.tree.leaves(made)[:1]
        return made

    def multicast(own):
        blocks = {0: own}
        bit = columns // 2
        while bit:
            for m in sorted(blocks):
                blocks[m | bit] = swapped(blocks[m], "exp", 2 * bit)
            bit //= 2
        return blocks

    def chained(moving):
        moved = []
        for _ in range(hops):
            moving = passed_along(moving, "seq", 1)
            moved.append(moving)
        return moved

    def options(batch):
        extra = []
        if sinks:
            extra = latest_start(key_rows[batch, 0], value_rows[batch, 0], segments[batch, 0])
        return ((hops, relayed, heads, sinks), extra)

    def attend_column(moved):
        settings, extra = options(1)
        return call(
            functools.partial(attend_column_kernel, settings),
            (rows_f32, rows_bf16),
            [SMEM] + [VMEM] * (3 + 2 * len(moved)) + ([VMEM, SMEM] if sinks else [])
            + [VMEM] * 2,
            (bias_table, own, queries, stacks[1], *moved, *sent, *extra, tokens, out_proj),
            scratch=[pltpu.VMEM((tok_count, width), bf16)],
        )

    def attend_direct(moved):
        settings, extra = options(0)
        return call(
            functools.partial(attend_direct_kernel, settings, experts, capacity),
            (*[packet] * columns, rows_f32, shaped((2, tok_count), f32),
             shaped((2, tok_count), jnp.int32)),
            [SMEM] + [VMEM] * (4 + 2 * len(moved)) + ([VMEM, SMEM] if sinks else [])
            + [VMEM] * 2,
            (bias_table, router_t, own, queries, stacks[0], *moved, *sent, *extra, tokens,
             out_proj),
            scratch=[pltpu.VMEM((tok_count, width), bf16)],
        )

    def scratch_for(slots):
        return (pltpu.VMEM((slots, width), bf16), pltpu.VMEM((slots, inner), bf16))

    def pack(members, places, blocks):
        return call(
            functools.partial(pack_kernel, members, cap_two, columns),
            shaped((part_two, width), bf16),
            [VMEM] * (1 + len(members)),
            (places, *(blocks[m] for m in members)),
        )

    def partial(members, far):
        parts = call(
            functools.partial(partial_kernel, members, cap_two, columns),
            tuple(rows_bf16 if m % 2 else rows_f32 for m in members),
            [VMEM] * 4,
            (places, gates_two, near, far),
        )
        for m, value in zip(members, parts):
            totals.setdefault(m, []).insert(0, value)

    def send_down(members):
        for m in sorted(members, key=lambda m: (m & -m, -m)):
            parts = totals[m]
            value = parts[0]
            if len(parts) > 1:
                value = call(fold_kernel, rows_bf16, [VMEM] * len(parts), parts)
            totals.setdefault(m & (m - 1), []).append(swapped(value, "exp", 2 * (m & -m)))

    stacked = jnp.concatenate([key_rows[1, 0], value_rows[1, 0]], axis=0)
    first_hop = swapped(stacked, "seq", 1) if relayed else passed_along(stacked, "seq", 1)
    tables = [jnp.pad(table, (0, tok_count - experts))[None] for table in (new_table, old_table)]
    numbers = jnp.concatenate([segments[:, 0], routes_one[0].T, routes_two[0].T, *tables])
    own, own_routes, own_segs = call(
        numbers_kernel,
        tuple(shaped((rows, tok_count), jnp.int32) for rows in (8, 2, 2)),
        [VMEM], (numbers,), after=[first_hop],
    )
    routes = multicast(own_routes)
    if relayed:
        sent = [swapped(own_segs, "seq", mask) for mask in (1, 2, 3)]
        across = swapped(stacked, "seq", 2)
    else:
        sent = chained(own_segs)
        across = first_hop
    stack_one = call(
        stage_kernel, stack_shape, [VMEM] * 4, (key_rows, value_rows, queries, tokens),
        after=[routes[columns // 2]],
    )
    *routes, latest_seg = call(
        collect_kernel,
        tuple(shaped((2, tok_count), jnp.int32) for _ in range(columns + 1)),
        [VMEM] * (columns + 1),
        (*(routes[m] for m in range(columns)), sent[-1]),
        after=sent[:-1],
    )
    sent = [*sent[:-1], latest_seg]
    if relayed:
        moved_two = [first_hop, across, swapped(across, "seq", 1)]
    else:
        moved_two = [across]
        while len(moved_two) < hops:
            moved_two.append(passed_along(moved_two[-1], "seq", 1))
    stacks = [stack_one, stacked]
    hidden_two, normed_two = attend_column(moved_two)
    (stack_one,) = call(
        pass_kernel, (stack_shape,), [ANY], (stack_one,), aliases={0: 0}, after=[across]
    )
    stacks[0] = stack_one
    if relayed:
        moved_one = [
            swapped(stack_one, "seq", 1),
            swapped(stack_one, "seq", 2),
            lax.ppermute(stack_one, "seq", [(0, 0), (1, 2), (2, 1), (3, 3)]),
        ]
    else:
        moved_one = chained(stack_one)
    blocks = multicast(normed_two)
    places, low_in = call(
        functools.partial(first_pack_kernel, lower, cap_two, columns),
        (shaped((2 * columns, tok_count), jnp.int32), shaped((part_two, width), bf16)),
        [VMEM] * (1 + columns + len(lower)),
        (own, *routes, *(blocks[m] for m in lower)),
    )
    low_in = swapped(low_in, "exp", 1)
    high_in = swapped(pack(upper, places, blocks), "exp", 1)
    *packets, hidden_one, gates_one, rows_one = attend_direct(moved_one)
    arrived = [packets[0]] + [swapped(packets[m], "exp", 2 * m) for m in range(1, columns)]
    low_out, high_out = call(
        far_kernel,
        (shaped((part_two, width), bf16),) * 2,
        [VMEM] * 5,
        (low_in, high_in, *weights),
        scratch=scratch_for(slots),
    )
    high_far = swapped(high_out, "exp", 1)
    crossing = call(
        crossing_kernel, shaped((columns * capacity, width), bf16), [VMEM] * columns, arrived,
        work=2 * 10**10,
    )
    crossed_one = swapped(crossing, "exp", 1)
    near, gates_two, low_out = call(
        functools.partial(near_kernel, columns, experts, cap_two),
        (shaped((slots, width), bf16), shaped((2 * columns, tok_count), f32),
         shaped((part_two, width), bf16)),
        [VMEM] * (6 + 2 * columns) + [ANY],
        (own, places, router_t, *(blocks[m] for m in range(columns)), *routes,
         *weights, low_out),
        scratch=scratch_for(slots), work=4 * 10**9, aliases={6 + 2 * columns: 2},
    )
    low_far = swapped(low_out, "exp", 1)
    totals = {}
    partial(upper, high_far)
    send_down(m for m in upper if m % 2)
    near_one, far_one = call(
        functools.partial(direct_kernel, columns),
        (shaped((columns * capacity, width), bf16),) * 2,
        [VMEM] * (4 + columns),
        (*arrived, crossed_one, *weights),
        scratch=scratch_for(experts * capacity),
    )
    far_one = swapped(far_one, "exp", 1)
    send_down(m for m in upper if m % 2 == 0)
    partial(lower, low_far)
    send_down(m for m in lower if m)
    answers = call(rejoin_kernel, [packet] * columns, [VMEM] * 2, (near_one, far_one))
    returned = [answers[0]] + [swapped(answers[m], "exp", 2 * m) for m in range(1, columns)]
    far_part, rest = (totals[0][1], [hidden_two, totals[0][0], *totals[0][2:]])
    ends = (call(fold_kernel, rows_f32, [VMEM] * 2, (rest[0], far_part)), *rest[1:])
    return call(
        functools.partial(final_kernel, columns), shaped((2, 1, tok_count, width), bf16),
        [VMEM] * (3 + columns + len(ends)), (hidden_one, gates_one, rows_one, *returned, *ends),
    )


def solution(mesh):
    rows = P(None, "exp", "seq", None)
    placed = (
        rows, rows, rows, rows, P(None, "exp", "seq"), P(), P(), P(),
        P("exp", None, None), P("exp", None, None), P("exp", None, None), P(), P(),
        P("exp", "seq", None), P("exp", "seq", None),
    )
    return jax.shard_map(local, mesh=mesh, in_specs=placed, out_specs=rows, check_vma=False)
```

```python
import functools

import jax
import jax.numpy as jnp
from jax import lax
from jax.experimental import pallas as pl
from jax.experimental.pallas import tpu as pltpu
from jax.sharding import PartitionSpec as P

WIN_BLOCKS = 4
NBUCK = 32
MAX_SLOTS = 2
ONE_ROW, TWO_ROW, NEW_ROW, OLD_ROW = (2, 4, 6, 7)

score_scale = 0.125
epsilon = 1e-06
masked_score = -1e30

f32 = jnp.float32
bf16 = jnp.bfloat16
NT = (((1,), (1,)), ((), ()))
TN = (((0,), (0,)), ((), ()))
VMEM = pl.BlockSpec(memory_space=pltpu.VMEM)
SMEM = pl.BlockSpec(memory_space=pltpu.SMEM)
ANY = pl.BlockSpec(memory_space=pl.ANY)


def iota(shape, dim):
    return lax.broadcasted_iota(jnp.int32, shape, dim)


def shaped(shape, dtype):
    return jax.ShapeDtypeStruct(shape, dtype)


def passed_along(value, axis, steps):
    count = lax.axis_size(axis)
    return lax.ppermute(value, axis, [(source, source + steps) for source in range(count - steps)])


def swapped(value, axis, mask):
    count = lax.axis_size(axis)
    return lax.ppermute(value, axis, [(source, source ^ mask) for source in range(count)])


def merge_starts(former, latter):
    take_latter = (latter[4] > 0) & ((former[4] == 0) | (latter[3] != former[3]))
    return tuple((jnp.where(take_latter, newer, older) for older, newer in zip(former, latter)))


def latest_start(key_rows, value_rows, segments):
    tok_count, model_width = key_rows.shape
    length, index = (lax.axis_size("seq"), lax.axis_index("seq"))
    last_seg = segments[tok_count - 1]
    lead = jnp.sum((segments < last_seg).astype(jnp.int32))
    one = jnp.ones((), jnp.int32)
    found = (key_rows[lead], value_rows[lead], index * tok_count + lead, last_seg, one)
    everything = jax.tree.map(lambda part: lax.all_gather(part, "seq"), found)
    start = jax.tree.map(jnp.zeros_like, found)

    def lap(k, before):
        new = merge_starts(before, jax.tree.map(lambda part: part[k], everything))
        return jax.tree.map(lambda a, b: jnp.where(k < index, a, b), new, before)

    sink_key, sink_value, sink_pos, sink_seg, sink_has = lax.fori_loop(0, length, lap, start)
    block = jnp.zeros((2 * tok_count, model_width), key_rows.dtype)
    block = block.at[0].set(sink_key).at[tok_count].set(sink_value)
    return (block, jnp.stack([sink_pos, sink_seg, sink_has]))


def table_entry(own, row, entry):
    return own[row : row + 1, entry : entry + 1]


def holder_of(experts, own, pick):
    return sum(
        jnp.where(pick == table_entry(own, OLD_ROW, x), x, 0) for x in range(experts)
    )


def column_routes(experts, routes, own):
    members = len(routes)
    slots = jnp.concatenate([ref[c : c + 1, :] for c in range(2) for ref in routes], axis=0)
    chosen = sum(jnp.where(slots == s, table_entry(own, NEW_ROW, s), 0) for s in range(experts))
    holders = holder_of(experts, own, chosen)
    return tuple((each[:members], each[members:]) for each in (chosen, holders))


def attended(batch, hops, relayed, heads, sinks, bias, own, q, stack, rest, context):
    count = 3 if relayed else hops
    moved, sent, rest = (rest[:count], rest[count : 2 * count], rest[2 * count :])
    if sinks:
        sink_block, sink_info, rest = (rest[0], rest[1], rest[2:])
    tokens, proj = rest
    tok_count, width = tokens.shape[2:]
    window = WIN_BLOCKS * tok_count
    index = lax.axis_index("seq")
    grid = (tok_count, tok_count)

    own_seg = own[batch : batch + 1, :]
    key_segs = [own_seg]
    if relayed:
        pairwise, across, relay = moved
        paired = index % 2 == 1
        key_segs += [jnp.where(paired, sent[0][batch : batch + 1], sent[2][batch : batch + 1])]
        key_segs.append(sent[1][batch : batch + 1, :])
    else:
        key_segs += [ref[batch : batch + 1, :] for ref in sent]
    seg_col = jnp.broadcast_to(own_seg, grid).T
    visible, spans = ([], [])
    for j, key_seg in enumerate(key_segs):
        key_seg = jnp.where(index >= j, key_seg, -1)
        distance = iota(grid, 0) - iota(grid, 1) + tok_count * j
        seen = (seg_col == key_seg) & (distance >= 0) & (distance < window)
        visible.append(jnp.where(seen, 0.0, masked_score))
        low, high = (max(0, tok_count * (j - 1) + 1), min(window, tok_count * (j + 1)) - 1)
        spans.append((distance, low.bit_length(), high.bit_length()))
    if sinks:
        position = index * tok_count + iota(grid, 0)
        seen = (seg_col == sink_info[1]) & (sink_info[2] > 0) & (position - sink_info[0] >= window)
        visible.append(jnp.where(seen & (iota(grid, 1) == 0), 0.0, masked_score))
        spans.append((None, NBUCK - 1, NBUCK - 1))
    lane = iota((tok_count, 128), 1)
    half = width // heads
    keys_at, values_at = (slice(0, tok_count), slice(tok_count, 2 * tok_count))
    for pair in range(heads // 2):
        cols = slice(128 * pair, 128 * pair + 128)
        both = q[batch, 0, :, cols] * score_scale
        even = jnp.where(lane < half, both, jnp.zeros_like(both))
        odd = jnp.where(lane < half, jnp.zeros_like(both), both)
        stacked = jnp.concatenate([even, odd], axis=0)
        blocks = [(stack[keys_at, cols], stack[values_at, cols])]
        if relayed:
            blocks.append(tuple(
                jnp.where(paired, pairwise[at, cols], relay[at, cols])
                for at in (keys_at, values_at)
            ))
            blocks.append((across[keys_at, cols], across[values_at, cols]))
        else:
            for ref in moved:
                blocks.append((ref[keys_at, cols], ref[values_at, cols]))
        if sinks:
            blocks.append((sink_block[keys_at, cols], sink_block[values_at, cols]))
        scores = []
        for (keys, _), (distance, low, high), seen in zip(blocks, spans, visible):
            score = lax.dot_general(stacked, keys, NT, preferred_element_type=f32)
            parts = []
            for side in range(2):
                head = 2 * pair + side
                offset = jnp.full(grid, bias[head, low], f32)
                for bucket in range(low + 1, high + 1):
                    offset = jnp.where(distance >= 1 << (bucket - 1), bias[head, bucket], offset)
                parts.append(score[side * tok_count : (side + 1) * tok_count] + (offset + seen))
            scores.append(jnp.concatenate(parts, axis=0))
        peak = jnp.max(functools.reduce(jnp.maximum, scores), axis=1, keepdims=True)
        weights = [jnp.exp(score - peak) for score in scores]
        total = jnp.sum(functools.reduce(jnp.add, weights), axis=1, keepdims=True)
        scale = 1.0 / total
        mixed = sum(
            jnp.dot((weight * scale).astype(bf16), values, preferred_element_type=f32)
            for weight, (_, values) in zip(weights, blocks)
        )
        context[:, cols] = jnp.where(lane < half, mixed[:tok_count], mixed[tok_count:]).astype(bf16)
    hidden = tokens[batch, 0].astype(f32) + jnp.dot(
        context[...], proj[...], preferred_element_type=f32
    )
    mean = jnp.mean(hidden * hidden, axis=1, keepdims=True)
    return (hidden, (hidden * lax.rsqrt(mean + epsilon)).astype(bf16))


def ranks(member):
    grid = (member.shape[1], member.shape[1])
    earlier = jnp.where(iota(grid, 0) < iota(grid, 1), 1.0, 0.0).astype(bf16)
    return jnp.dot(member.astype(bf16), earlier, preferred_element_type=f32).astype(jnp.int32)


def attend_column_kernel(options, bias, own, q, stack, *rest):
    inputs, (hidden_out, normed_out, context) = (rest[:-3], rest[-3:])
    hidden, normed = attended(1, *options, bias, own, q, stack, inputs, context)
    hidden_out[...] = hidden
    normed_out[...] = normed


def column_places(experts, routes, own):
    me = lax.axis_index("exp")
    _, holders = column_routes(experts, routes, own)
    member = jnp.concatenate(
        [jnp.where((holders[0] == at) | (holders[1] == at), 1.0, 0.0) for at in (me, me ^ 1)],
        axis=0,
    )
    return jnp.where(member > 0.5, ranks(member), -1)


def attend_direct_kernel(options, experts, cap, bias, router_t, own, q, stack, *rest):
    layers = experts // 2
    inputs, rest = (rest[: -4 - layers], rest[-4 - layers :])
    outgoing, (hidden_out, gates_out, rows_out, context) = (rest[:layers], rest[layers:])
    hidden, normed = attended(0, *options, bias, own, q, stack, inputs, context)
    hidden_out[...] = hidden
    tok_count = hidden.shape[0]
    chosen = [own[ONE_ROW + c : ONE_ROW + c + 1, :] for c in range(2)]
    holders = [holder_of(experts, own, pick) for pick in chosen]
    expert = iota((experts, tok_count), 0)
    packet = expert ^ lax.axis_index("exp")
    member = jnp.where((packet == holders[0]) | (packet == holders[1]), 1.0, 0.0)
    place = ranks(member) + expert * cap
    rows = [
        jnp.sum(jnp.where(packet == holder, place, 0), axis=0, keepdims=True) for holder in holders
    ]
    rows_out[...] = jnp.concatenate(rows, axis=0)
    logits = lax.dot_general(router_t[...], normed, NT, preferred_element_type=f32)
    picked = [jnp.sum(jnp.where(expert == c, logits, 0.0), axis=0, keepdims=True) for c in chosen]
    first = jax.nn.sigmoid(picked[0] - picked[1])
    gates_out[...] = jnp.concatenate([first, 1.0 - first], axis=0)
    at = iota((experts * cap, tok_count), 0)
    plan = jnp.where((at == rows[0]) | (at == rows[1]), 1.0, 0.0).astype(bf16)
    packed = jnp.dot(plan, normed, preferred_element_type=f32)
    for m, ref in enumerate(outgoing):
        ref[...] = packed[2 * m * cap : 2 * (m + 1) * cap].astype(bf16)


def picked_rows(members, cap, first_row, places, blocks):
    at = iota((len(members) * cap, blocks[0].shape[0]), 0)
    plans = []
    for n, m in enumerate(members):
        place = places[first_row + m : first_row + m + 1, :]
        place = jnp.where(place >= 0, place + n * cap, -1)
        plans.append(jnp.where(at == place, 1.0, 0.0))
    plan = jnp.concatenate(plans, axis=1).astype(bf16)
    rows = jnp.concatenate([block[...] for block in blocks], axis=0)
    return (jnp.dot(plan, rows, preferred_element_type=f32).astype(bf16), rows)


def pack_kernel(members, cap, columns, places, *rest):
    blocks, out = (rest[:-1], rest[-1])
    out[...], _ = picked_rows(members, cap, columns, places, blocks)


def first_pack_kernel(members, cap, columns, own, *rest):
    routes, blocks, (places, out) = (rest[:columns], rest[columns:-2], rest[-2:])
    places[...] = column_places(2 * columns, routes, own)
    out[...], _ = picked_rows(members, cap, columns, places, blocks)


def numbers_kernel(numbers, own, routes_out, segs_out):
    own[...] = numbers[...]
    routes_out[...] = numbers[TWO_ROW : TWO_ROW + 2, :]
    segs_out[...] = numbers[:2, :]


def collect_kernel(*refs):
    count = len(refs) // 2
    for ref, out in zip(refs[:count], refs[count:]):
        out[...] = ref[...]


def stage_kernel(k, v, q, tokens, out):
    del q, tokens
    tok_count = k.shape[2]
    out[:tok_count, :] = k[0, 0]
    out[tok_count:, :] = v[0, 0]


def pass_kernel(*refs):
    del refs


def crossing_kernel(*refs):
    packets, out = (refs[:-1], refs[-1])
    cap = packets[0].shape[0] // 2
    parts = [ref[...].astype(f32)[cap:] for ref in packets]
    out[...] = jnp.concatenate(parts, axis=0).astype(bf16)


def expert_rows(rows, weights, active, stores):
    gate, up, down = weights
    inner, width = down.shape[1:]
    x = rows[...]
    for begin in range(0, inner, 256):
        span = slice(begin, min(inner, begin + 256))
        gate_part = jnp.dot(x, gate[0, :, span], preferred_element_type=f32)
        up_part = jnp.dot(x, up[0, :, span], preferred_element_type=f32)
        active[:, span] = (jax.nn.gelu(gate_part, approximate=True) * up_part).astype(bf16)
    for begin in range(0, width, 256):
        span = slice(begin, begin + 256)
        part = jnp.dot(active[...], down[0, :, span], preferred_element_type=f32)
        stores(span, part)


def near_kernel(columns, experts, cap, own, places, router_t, *rest):
    blocks, rest = (rest[:columns], rest[columns:])
    routes, rest = (rest[:columns], rest[columns:])
    weights, (_, out, gates_out, _, rows, active) = (rest[:3], rest[3:])

    def stores(span, value):
        out[:, span] = value.astype(bf16)

    rows[...], tokens = picked_rows(range(columns), cap, 0, places, blocks)
    logits = lax.dot_general(router_t[...], tokens, NT, preferred_element_type=f32)
    chosen, holders = column_routes(experts, routes, own)
    chosen = [
        jnp.concatenate([picks[m : m + 1, :] for m in range(columns)], axis=1) for picks in chosen
    ]
    expert = iota(logits.shape, 0)
    picked = [
        jnp.sum(jnp.where(expert == pick, logits, 0.0), axis=0, keepdims=True) for pick in chosen
    ]
    first = jax.nn.sigmoid(picked[0] - picked[1])
    tok_count = places.shape[1]
    first = jnp.concatenate(
        [first[:, m * tok_count : (m + 1) * tok_count] for m in range(columns)], axis=0
    )
    me = lax.axis_index("exp")
    gates_out[...] = jnp.concatenate(
        [
            jnp.where(holders[0] == at, first, 0.0) + jnp.where(holders[1] == at, 1.0 - first, 0.0)
            for at in (me, me ^ 1)
        ],
        axis=0,
    )
    expert_rows(rows, weights, active, stores)


def far_kernel(low_in, high_in, *rest):
    weights, (low_out, high_out, rows, active) = (rest[:3], rest[3:])
    part = low_in.shape[0]

    def stores(span, value):
        low_out[:, span] = value[:part].astype(bf16)
        high_out[:, span] = value[part:].astype(bf16)

    rows[:part, :] = low_in[...]
    rows[part:, :] = high_in[...]
    expert_rows(rows, weights, active, stores)


def direct_kernel(layers, *refs):
    packets, crossed, weights = (refs[:layers], refs[layers], refs[layers + 1 : layers + 4])
    near, far, rows, active = refs[layers + 4 :]
    cap = packets[0].shape[0] // 2
    half = layers * cap

    def stores(span, value):
        near[:, span] = value[:half].astype(bf16)
        far[:, span] = value[half:].astype(bf16)

    parts = [ref[...].astype(f32)[:cap] for ref in packets]
    rows[:half, :] = jnp.concatenate(parts, axis=0).astype(bf16)
    rows[half:, :] = crossed[...]
    expert_rows(rows, weights, active, stores)


def rejoin_kernel(near, far, *outs):
    cap = outs[0].shape[0] // 2
    both = [ref[...].astype(f32) for ref in (near, far)]
    for m, out in enumerate(outs):
        parts = [each[m * cap : (m + 1) * cap] for each in both]
        out[...] = jnp.concatenate(parts, axis=0).astype(bf16)


def partial_kernel(members, cap, columns, places, gates, near, far, *outs):
    at = iota((cap, places.shape[1]), 0)
    for n, m in enumerate(members):
        total = None
        near_rows = near[m * cap : (m + 1) * cap, :]
        far_rows = far[n * cap : (n + 1) * cap, :]
        for values, row in ((near_rows, m), (far_rows, columns + m)):
            spread = jnp.where(at == places[row : row + 1, :], gates[row : row + 1, :], 0.0)
            coarse = spread.astype(bf16)
            fine = (spread - coarse.astype(f32)).astype(bf16)
            for half in (coarse, fine):
                term = lax.dot_general(half, values, TN, preferred_element_type=f32)
                total = term if total is None else total + term
        outs[n][...] = total.astype(outs[n].dtype)


def fold_kernel(own, *rest):
    total = own[...]
    for ref in rest[:-1]:
        total = total + ref[...].astype(f32)
    rest[-1][...] = total.astype(rest[-1].dtype)


def final_kernel(layers, hidden, gates, rows, *rest):
    packets, ends, out = (rest[:layers], rest[layers:-1], rest[-1])
    at = iota((layers * packets[0].shape[0], hidden.shape[0]), 0)
    spread = jnp.where(at == rows[0:1, :], gates[0:1, :], 0.0)
    spread = spread + jnp.where(at == rows[1:2, :], gates[1:2, :], 0.0)
    coarse = spread.astype(bf16)
    fine = (spread - coarse.astype(f32)).astype(bf16)
    values = jnp.concatenate([ref[...].astype(f32) for ref in packets], axis=0).astype(bf16)
    total = hidden[...]
    for half in (coarse, fine):
        total = total + lax.dot_general(half, values, TN, preferred_element_type=f32)
    out[0, 0] = total.astype(bf16)
    total = ends[0][...]
    for ref in ends[1:]:
        total = total + ref[...].astype(f32)
    out[1, 0] = total.astype(bf16)


def local(
    tokens, queries, key_rows, value_rows, segments, bias_table, out_proj, router,
    gate_weight, up_weight, down_weight, old_table, new_table, routes_one, routes_two,
):
    tok_count, width = tokens.shape[2:]
    heads = bias_table.shape[0]
    experts = router.shape[1]
    columns = experts // 2
    inner = gate_weight.shape[2]
    seq_size = lax.axis_size("seq")
    seq_len = tok_count * seq_size
    capacity = tok_count * 2 * 5 // (4 * experts)
    longest = seq_len // 2
    hops = min(WIN_BLOCKS, (longest - 1 + tok_count - 1) // tok_count)
    relayed = seq_size == 4 and hops == 2
    sinks = seq_len > WIN_BLOCKS * tok_count
    weights = (gate_weight, up_weight, down_weight)
    router_t = router.T
    lower, upper = (range(columns // 2), range(columns // 2, columns))
    rows_bf16 = shaped((tok_count, width), bf16)
    rows_f32 = shaped((tok_count, width), f32)
    cap_two = capacity * MAX_SLOTS
    slots = columns * cap_two
    part_two = slots // 2
    packet = shaped((2 * capacity, width), bf16)
    stack_shape = shaped((2 * tok_count, width), bf16)
    latest = []

    def call(kernel, outs, ins, args, scratch=(), after=(), aliases=None, work=1):
        after = [*after, *latest]
        out_specs = jax.tree.map(lambda _: VMEM, outs)
        if aliases:
            out_specs = tuple(ANY if n in aliases.values() else VMEM for n in range(len(outs)))

        def body(*refs):
            kernel(*refs[: len(args)], *refs[len(args) + len(after) :])

        made = pl.pallas_call(
            body,
            out_shape=outs,
            in_specs=ins + [ANY] * len(after),
            out_specs=out_specs,
            scratch_shapes=list(scratch),
            input_output_aliases=aliases or {},
            compiler_params=pltpu.CompilerParams(vmem_limit_bytes=24 * 2**20),
            cost_estimate=pl.CostEstimate(flops=work, bytes_accessed=1, transcendentals=0),
        )(*args, *after)
        latest[:] = jax.tree.leaves(made)[:1]
        return made

    def multicast(own):
        blocks = {0: own}
        bit = columns // 2
        while bit:
            for m in sorted(blocks):
                blocks[m | bit] = swapped(blocks[m], "exp", 2 * bit)
            bit //= 2
        return blocks

    def chained(moving):
        moved = []
        for _ in range(hops):
            moving = passed_along(moving, "seq", 1)
            moved.append(moving)
        return moved

    def options(batch):
        extra = []
        if sinks:
            extra = latest_start(key_rows[batch, 0], value_rows[batch, 0], segments[batch, 0])
        return ((hops, relayed, heads, sinks), extra)

    def attend_column(moved):
        settings, extra = options(1)
        return call(
            functools.partial(attend_column_kernel, settings),
            (rows_f32, rows_bf16),
            [SMEM] + [VMEM] * (3 + 2 * len(moved)) + ([VMEM, SMEM] if sinks else [])
            + [VMEM] * 2,
            (bias_table, own, queries, stacks[1], *moved, *sent, *extra, tokens, out_proj),
            scratch=[pltpu.VMEM((tok_count, width), bf16)],
        )

    def attend_direct(moved):
        settings, extra = options(0)
        return call(
            functools.partial(attend_direct_kernel, settings, experts, capacity),
            (*[packet] * columns, rows_f32, shaped((2, tok_count), f32),
             shaped((2, tok_count), jnp.int32)),
            [SMEM] + [VMEM] * (4 + 2 * len(moved)) + ([VMEM, SMEM] if sinks else [])
            + [VMEM] * 2,
            (bias_table, router_t, own, queries, stacks[0], *moved, *sent, *extra, tokens,
             out_proj),
            scratch=[pltpu.VMEM((tok_count, width), bf16)],
        )

    def scratch_for(slots):
        return (pltpu.VMEM((slots, width), bf16), pltpu.VMEM((slots, inner), bf16))

    def pack(members, places, blocks):
        return call(
            functools.partial(pack_kernel, members, cap_two, columns),
            shaped((part_two, width), bf16),
            [VMEM] * (1 + len(members)),
            (places, *(blocks[m] for m in members)),
        )

    def partial(members, far):
        parts = call(
            functools.partial(partial_kernel, members, cap_two, columns),
            tuple(rows_bf16 if m % 2 else rows_f32 for m in members),
            [VMEM] * 4,
            (places, gates_two, near, far),
        )
        for m, value in zip(members, parts):
            totals.setdefault(m, []).insert(0, value)

    def send_down(members):
        for m in sorted(members, key=lambda m: (m & -m, -m)):
            parts = totals[m]
            value = parts[0]
            if len(parts) > 1:
                value = call(fold_kernel, rows_bf16, [VMEM] * len(parts), parts)
            totals.setdefault(m & (m - 1), []).append(swapped(value, "exp", 2 * (m & -m)))

    stacked = jnp.concatenate([key_rows[1, 0], value_rows[1, 0]], axis=0)
    first_hop = swapped(stacked, "seq", 1) if relayed else passed_along(stacked, "seq", 1)
    tables = [jnp.pad(table, (0, tok_count - experts))[None] for table in (new_table, old_table)]
    numbers = jnp.concatenate([segments[:, 0], routes_one[0].T, routes_two[0].T, *tables])
    own, own_routes, own_segs = call(
        numbers_kernel,
        tuple(shaped((rows, tok_count), jnp.int32) for rows in (8, 2, 2)),
        [VMEM], (numbers,), after=[first_hop],
    )
    routes = multicast(own_routes)
    if relayed:
        sent = [swapped(own_segs, "seq", mask) for mask in (1, 2, 3)]
        across = swapped(stacked, "seq", 2)
    else:
        sent = chained(own_segs)
        across = first_hop
    stack_one = call(
        stage_kernel, stack_shape, [VMEM] * 4, (key_rows, value_rows, queries, tokens),
        after=[routes[columns // 2]],
    )
    *routes, latest_seg = call(
        collect_kernel,
        tuple(shaped((2, tok_count), jnp.int32) for _ in range(columns + 1)),
        [VMEM] * (columns + 1),
        (*(routes[m] for m in range(columns)), sent[-1]),
        after=sent[:-1],
    )
    sent = [*sent[:-1], latest_seg]
    (across,) = call(pass_kernel, (stack_shape,), [ANY], (across,), aliases={0: 0})
    if relayed:
        moved_two = [first_hop, across, swapped(across, "seq", 1)]
    else:
        moved_two = [across]
        while len(moved_two) < hops:
            moved_two.append(passed_along(moved_two[-1], "seq", 1))
    stacks = [stack_one, stacked]
    hidden_two, normed_two = attend_column(moved_two)
    (stack_one,) = call(
        pass_kernel, (stack_shape,), [ANY], (stack_one,), aliases={0: 0}
    )
    stacks[0] = stack_one
    if relayed:
        moved_one = [
            swapped(stack_one, "seq", 1),
            swapped(stack_one, "seq", 2),
            lax.ppermute(stack_one, "seq", [(0, 0), (1, 2), (2, 1), (3, 3)]),
        ]
    else:
        moved_one = chained(stack_one)
    blocks = multicast(normed_two)
    places, low_in = call(
        functools.partial(first_pack_kernel, lower, cap_two, columns),
        (shaped((2 * columns, tok_count), jnp.int32), shaped((part_two, width), bf16)),
        [VMEM] * (1 + columns + len(lower)),
        (own, *routes, *(blocks[m] for m in lower)),
    )
    low_in = swapped(low_in, "exp", 1)
    high_in = swapped(pack(upper, places, blocks), "exp", 1)
    *packets, hidden_one, gates_one, rows_one = attend_direct(moved_one)
    arrived = [packets[0]] + [swapped(packets[m], "exp", 2 * m) for m in range(1, columns)]
    low_out, high_out = call(
        far_kernel,
        (shaped((part_two, width), bf16),) * 2,
        [VMEM] * 5,
        (low_in, high_in, *weights),
        scratch=scratch_for(slots),
    )
    high_far = swapped(high_out, "exp", 1)
    crossing = call(
        crossing_kernel, shaped((columns * capacity, width), bf16), [VMEM] * columns, arrived,
        work=2 * 10**10,
    )
    crossed_one = swapped(crossing, "exp", 1)
    near, gates_two, low_out = call(
        functools.partial(near_kernel, columns, experts, cap_two),
        (shaped((slots, width), bf16), shaped((2 * columns, tok_count), f32),
         shaped((part_two, width), bf16)),
        [VMEM] * (6 + 2 * columns) + [ANY],
        (own, places, router_t, *(blocks[m] for m in range(columns)), *routes,
         *weights, low_out),
        scratch=scratch_for(slots), work=4 * 10**9, aliases={6 + 2 * columns: 2},
    )
    low_far = swapped(low_out, "exp", 1)
    totals = {}
    partial(upper, high_far)
    send_down(m for m in upper if m % 2)
    near_one, far_one = call(
        functools.partial(direct_kernel, columns),
        (shaped((columns * capacity, width), bf16),) * 2,
        [VMEM] * (4 + columns),
        (*arrived, crossed_one, *weights),
        scratch=scratch_for(experts * capacity),
    )
    far_one = swapped(far_one, "exp", 1)
    send_down(m for m in upper if m % 2 == 0)
    partial(lower, low_far)
    send_down(m for m in lower if m)
    answers = call(rejoin_kernel, [packet] * columns, [VMEM] * 2, (near_one, far_one))
    returned = [answers[0]] + [swapped(answers[m], "exp", 2 * m) for m in range(1, columns)]
    far_part, rest = (totals[0][1], [hidden_two, totals[0][0], *totals[0][2:]])
    ends = (call(fold_kernel, rows_f32, [VMEM] * 2, (rest[0], far_part)), *rest[1:])
    return call(
        functools.partial(final_kernel, columns), shaped((2, 1, tok_count, width), bf16),
        [VMEM] * (3 + columns + len(ends)), (hidden_one, gates_one, rows_one, *returned, *ends),
    )


def solution(mesh):
    rows = P(None, "exp", "seq", None)
    placed = (
        rows, rows, rows, rows, P(None, "exp", "seq"), P(), P(), P(),
        P("exp", None, None), P("exp", None, None), P("exp", None, None), P(), P(),
        P("exp", "seq", None), P("exp", "seq", None),
    )
    return jax.shard_map(local, mesh=mesh, in_specs=placed, out_specs=rows, check_vma=False)
```

```python
import functools

import jax
import jax.numpy as jnp
from jax import lax
from jax.experimental import pallas as pl
from jax.experimental.pallas import tpu as pltpu
from jax.sharding import PartitionSpec as P

WIN_BLOCKS = 4
NBUCK = 32
MAX_SLOTS = 2
ONE_ROW, TWO_ROW, NEW_ROW, OLD_ROW = (2, 4, 6, 7)

score_scale = 0.125
epsilon = 1e-06
masked_score = -1e30

f32 = jnp.float32
bf16 = jnp.bfloat16
NT = (((1,), (1,)), ((), ()))
TN = (((0,), (0,)), ((), ()))
VMEM = pl.BlockSpec(memory_space=pltpu.VMEM)
SMEM = pl.BlockSpec(memory_space=pltpu.SMEM)
ANY = pl.BlockSpec(memory_space=pl.ANY)


def iota(shape, dim):
    return lax.broadcasted_iota(jnp.int32, shape, dim)


def shaped(shape, dtype):
    return jax.ShapeDtypeStruct(shape, dtype)


def passed_along(value, axis, steps):
    count = lax.axis_size(axis)
    return lax.ppermute(value, axis, [(source, source + steps) for source in range(count - steps)])


def swapped(value, axis, mask):
    count = lax.axis_size(axis)
    return lax.ppermute(value, axis, [(source, source ^ mask) for source in range(count)])


def merge_starts(former, latter):
    take_latter = (latter[4] > 0) & ((former[4] == 0) | (latter[3] != former[3]))
    return tuple((jnp.where(take_latter, newer, older) for older, newer in zip(former, latter)))


def latest_start(key_rows, value_rows, segments):
    tok_count, model_width = key_rows.shape
    length, index = (lax.axis_size("seq"), lax.axis_index("seq"))
    last_seg = segments[tok_count - 1]
    lead = jnp.sum((segments < last_seg).astype(jnp.int32))
    one = jnp.ones((), jnp.int32)
    found = (key_rows[lead], value_rows[lead], index * tok_count + lead, last_seg, one)
    everything = jax.tree.map(lambda part: lax.all_gather(part, "seq"), found)
    start = jax.tree.map(jnp.zeros_like, found)

    def lap(k, before):
        new = merge_starts(before, jax.tree.map(lambda part: part[k], everything))
        return jax.tree.map(lambda a, b: jnp.where(k < index, a, b), new, before)

    sink_key, sink_value, sink_pos, sink_seg, sink_has = lax.fori_loop(0, length, lap, start)
    block = jnp.zeros((2 * tok_count, model_width), key_rows.dtype)
    block = block.at[0].set(sink_key).at[tok_count].set(sink_value)
    return (block, jnp.stack([sink_pos, sink_seg, sink_has]))


def table_entry(own, row, entry):
    return own[row : row + 1, entry : entry + 1]


def holder_of(experts, own, pick):
    return sum(
        jnp.where(pick == table_entry(own, OLD_ROW, x), x, 0) for x in range(experts)
    )


def column_routes(experts, routes, own):
    members = len(routes)
    slots = jnp.concatenate([ref[c : c + 1, :] for c in range(2) for ref in routes], axis=0)
    chosen = sum(jnp.where(slots == s, table_entry(own, NEW_ROW, s), 0) for s in range(experts))
    holders = holder_of(experts, own, chosen)
    return tuple((each[:members], each[members:]) for each in (chosen, holders))


def attended(batch, hops, relayed, heads, sinks, bias, own, q, stack, rest, context):
    count = 3 if relayed else hops
    moved, sent, rest = (rest[:count], rest[count : 2 * count], rest[2 * count :])
    if sinks:
        sink_block, sink_info, rest = (rest[0], rest[1], rest[2:])
    tokens, proj = rest
    tok_count, width = tokens.shape[2:]
    window = WIN_BLOCKS * tok_count
    index = lax.axis_index("seq")
    grid = (tok_count, tok_count)

    own_seg = own[batch : batch + 1, :]
    key_segs = [own_seg]
    if relayed:
        pairwise, across, relay = moved
        paired = index % 2 == 1
        key_segs += [jnp.where(paired, sent[0][batch : batch + 1], sent[2][batch : batch + 1])]
        key_segs.append(sent[1][batch : batch + 1, :])
    else:
        key_segs += [ref[batch : batch + 1, :] for ref in sent]
    seg_col = jnp.broadcast_to(own_seg, grid).T
    visible, spans = ([], [])
    for j, key_seg in enumerate(key_segs):
        key_seg = jnp.where(index >= j, key_seg, -1)
        distance = iota(grid, 0) - iota(grid, 1) + tok_count * j
        seen = (seg_col == key_seg) & (distance >= 0) & (distance < window)
        visible.append(jnp.where(seen, 0.0, masked_score))
        low, high = (max(0, tok_count * (j - 1) + 1), min(window, tok_count * (j + 1)) - 1)
        spans.append((distance, low.bit_length(), high.bit_length()))
    if sinks:
        position = index * tok_count + iota(grid, 0)
        seen = (seg_col == sink_info[1]) & (sink_info[2] > 0) & (position - sink_info[0] >= window)
        visible.append(jnp.where(seen & (iota(grid, 1) == 0), 0.0, masked_score))
        spans.append((None, NBUCK - 1, NBUCK - 1))
    lane = iota((tok_count, 128), 1)
    half = width // heads
    keys_at, values_at = (slice(0, tok_count), slice(tok_count, 2 * tok_count))
    for pair in range(heads // 2):
        cols = slice(128 * pair, 128 * pair + 128)
        both = q[batch, 0, :, cols] * score_scale
        even = jnp.where(lane < half, both, jnp.zeros_like(both))
        odd = jnp.where(lane < half, jnp.zeros_like(both), both)
        stacked = jnp.concatenate([even, odd], axis=0)
        blocks = [(stack[keys_at, cols], stack[values_at, cols])]
        if relayed:
            blocks.append(tuple(
                jnp.where(paired, pairwise[at, cols], relay[at, cols])
                for at in (keys_at, values_at)
            ))
            blocks.append((across[keys_at, cols], across[values_at, cols]))
        else:
            for ref in moved:
                blocks.append((ref[keys_at, cols], ref[values_at, cols]))
        if sinks:
            blocks.append((sink_block[keys_at, cols], sink_block[values_at, cols]))
        scores = []
        for (keys, _), (distance, low, high), seen in zip(blocks, spans, visible):
            score = lax.dot_general(stacked, keys, NT, preferred_element_type=f32)
            parts = []
            for side in range(2):
                head = 2 * pair + side
                offset = jnp.full(grid, bias[head, low], f32)
                for bucket in range(low + 1, high + 1):
                    offset = jnp.where(distance >= 1 << (bucket - 1), bias[head, bucket], offset)
                parts.append(score[side * tok_count : (side + 1) * tok_count] + (offset + seen))
            scores.append(jnp.concatenate(parts, axis=0))
        peak = jnp.max(functools.reduce(jnp.maximum, scores), axis=1, keepdims=True)
        weights = [jnp.exp(score - peak) for score in scores]
        total = jnp.sum(functools.reduce(jnp.add, weights), axis=1, keepdims=True)
        scale = 1.0 / total
        mixed = sum(
            jnp.dot((weight * scale).astype(bf16), values, preferred_element_type=f32)
            for weight, (_, values) in zip(weights, blocks)
        )
        context[:, cols] = jnp.where(lane < half, mixed[:tok_count], mixed[tok_count:]).astype(bf16)
    hidden = tokens[batch, 0].astype(f32) + jnp.dot(
        context[...], proj[...], preferred_element_type=f32
    )
    mean = jnp.mean(hidden * hidden, axis=1, keepdims=True)
    return (hidden, (hidden * lax.rsqrt(mean + epsilon)).astype(bf16))


def ranks(member):
    grid = (member.shape[1], member.shape[1])
    earlier = jnp.where(iota(grid, 0) < iota(grid, 1), 1.0, 0.0).astype(bf16)
    return jnp.dot(member.astype(bf16), earlier, preferred_element_type=f32).astype(jnp.int32)


def attend_column_kernel(options, bias, own, q, stack, *rest):
    inputs, (hidden_out, normed_out, context) = (rest[:-3], rest[-3:])
    hidden, normed = attended(1, *options, bias, own, q, stack, inputs, context)
    hidden_out[...] = hidden
    normed_out[...] = normed


def column_places(experts, routes, own):
    me = lax.axis_index("exp")
    _, holders = column_routes(experts, routes, own)
    member = jnp.concatenate(
        [jnp.where((holders[0] == at) | (holders[1] == at), 1.0, 0.0) for at in (me, me ^ 1)],
        axis=0,
    )
    return jnp.where(member > 0.5, ranks(member), -1)


def attend_direct_kernel(options, experts, cap, bias, router_t, own, q, stack, *rest):
    layers = experts // 2
    inputs, rest = (rest[: -4 - layers], rest[-4 - layers :])
    outgoing, (hidden_out, gates_out, rows_out, context) = (rest[:layers], rest[layers:])
    hidden, normed = attended(0, *options, bias, own, q, stack, inputs, context)
    hidden_out[...] = hidden
    tok_count = hidden.shape[0]
    chosen = [own[ONE_ROW + c : ONE_ROW + c + 1, :] for c in range(2)]
    holders = [holder_of(experts, own, pick) for pick in chosen]
    expert = iota((experts, tok_count), 0)
    packet = expert ^ lax.axis_index("exp")
    member = jnp.where((packet == holders[0]) | (packet == holders[1]), 1.0, 0.0)
    place = ranks(member) + expert * cap
    rows = [
        jnp.sum(jnp.where(packet == holder, place, 0), axis=0, keepdims=True) for holder in holders
    ]
    rows_out[...] = jnp.concatenate(rows, axis=0)
    logits = lax.dot_general(router_t[...], normed, NT, preferred_element_type=f32)
    picked = [jnp.sum(jnp.where(expert == c, logits, 0.0), axis=0, keepdims=True) for c in chosen]
    first = jax.nn.sigmoid(picked[0] - picked[1])
    gates_out[...] = jnp.concatenate([first, 1.0 - first], axis=0)
    at = iota((experts * cap, tok_count), 0)
    plan = jnp.where((at == rows[0]) | (at == rows[1]), 1.0, 0.0).astype(bf16)
    packed = jnp.dot(plan, normed, preferred_element_type=f32)
    for m, ref in enumerate(outgoing):
        ref[...] = packed[2 * m * cap : 2 * (m + 1) * cap].astype(bf16)


def picked_rows(members, cap, first_row, places, blocks):
    at = iota((len(members) * cap, blocks[0].shape[0]), 0)
    plans = []
    for n, m in enumerate(members):
        place = places[first_row + m : first_row + m + 1, :]
        place = jnp.where(place >= 0, place + n * cap, -1)
        plans.append(jnp.where(at == place, 1.0, 0.0))
    plan = jnp.concatenate(plans, axis=1).astype(bf16)
    rows = jnp.concatenate([block[...] for block in blocks], axis=0)
    return (jnp.dot(plan, rows, preferred_element_type=f32).astype(bf16), rows)


def pack_kernel(members, cap, columns, places, *rest):
    blocks, out = (rest[:-1], rest[-1])
    out[...], _ = picked_rows(members, cap, columns, places, blocks)


def first_pack_kernel(members, cap, columns, own, *rest):
    routes, blocks, (places, out) = (rest[:columns], rest[columns:-2], rest[-2:])
    places[...] = column_places(2 * columns, routes, own)
    out[...], _ = picked_rows(members, cap, columns, places, blocks)


def numbers_kernel(numbers, own, routes_out, segs_out):
    own[...] = numbers[...]
    routes_out[...] = numbers[TWO_ROW : TWO_ROW + 2, :]
    segs_out[...] = numbers[:2, :]


def collect_kernel(*refs):
    count = len(refs) // 2
    for ref, out in zip(refs[:count], refs[count:]):
        out[...] = ref[...]


def stage_kernel(k, v, q, tokens, out):
    del q, tokens
    tok_count = k.shape[2]
    out[:tok_count, :] = k[0, 0]
    out[tok_count:, :] = v[0, 0]


def pass_kernel(*refs):
    del refs


def crossing_kernel(*refs):
    packets, out = (refs[:-1], refs[-1])
    cap = packets[0].shape[0] // 2
    parts = [ref[...].astype(f32)[cap:] for ref in packets]
    out[...] = jnp.concatenate(parts, axis=0).astype(bf16)


def expert_rows(rows, weights, active, stores):
    gate, up, down = weights
    inner, width = down.shape[1:]
    x = rows[...]
    for begin in range(0, inner, 256):
        span = slice(begin, min(inner, begin + 256))
        gate_part = jnp.dot(x, gate[0, :, span], preferred_element_type=f32)
        up_part = jnp.dot(x, up[0, :, span], preferred_element_type=f32)
        active[:, span] = (jax.nn.gelu(gate_part, approximate=True) * up_part).astype(bf16)
    for begin in range(0, width, 256):
        span = slice(begin, begin + 256)
        part = jnp.dot(active[...], down[0, :, span], preferred_element_type=f32)
        stores(span, part)


def near_kernel(columns, experts, cap, own, places, router_t, *rest):
    blocks, rest = (rest[:columns], rest[columns:])
    routes, rest = (rest[:columns], rest[columns:])
    weights, (out, gates_out, rows, active) = (rest[:3], rest[3:])

    def stores(span, value):
        out[:, span] = value.astype(bf16)

    rows[...], tokens = picked_rows(range(columns), cap, 0, places, blocks)
    logits = lax.dot_general(router_t[...], tokens, NT, preferred_element_type=f32)
    chosen, holders = column_routes(experts, routes, own)
    chosen = [
        jnp.concatenate([picks[m : m + 1, :] for m in range(columns)], axis=1) for picks in chosen
    ]
    expert = iota(logits.shape, 0)
    picked = [
        jnp.sum(jnp.where(expert == pick, logits, 0.0), axis=0, keepdims=True) for pick in chosen
    ]
    first = jax.nn.sigmoid(picked[0] - picked[1])
    tok_count = places.shape[1]
    first = jnp.concatenate(
        [first[:, m * tok_count : (m + 1) * tok_count] for m in range(columns)], axis=0
    )
    me = lax.axis_index("exp")
    gates_out[...] = jnp.concatenate(
        [
            jnp.where(holders[0] == at, first, 0.0) + jnp.where(holders[1] == at, 1.0 - first, 0.0)
            for at in (me, me ^ 1)
        ],
        axis=0,
    )
    expert_rows(rows, weights, active, stores)


def far_kernel(low_in, high_in, *rest):
    weights, (low_out, high_out, rows, active) = (rest[:3], rest[3:])
    part = low_in.shape[0]

    def stores(span, value):
        low_out[:, span] = value[:part].astype(bf16)
        high_out[:, span] = value[part:].astype(bf16)

    rows[:part, :] = low_in[...]
    rows[part:, :] = high_in[...]
    expert_rows(rows, weights, active, stores)


def direct_kernel(layers, *refs):
    packets, crossed, weights = (refs[:layers], refs[layers], refs[layers + 1 : layers + 4])
    near, far, rows, active = refs[layers + 4 :]
    cap = packets[0].shape[0] // 2
    half = layers * cap

    def stores(span, value):
        near[:, span] = value[:half].astype(bf16)
        far[:, span] = value[half:].astype(bf16)

    parts = [ref[...].astype(f32)[:cap] for ref in packets]
    rows[:half, :] = jnp.concatenate(parts, axis=0).astype(bf16)
    rows[half:, :] = crossed[...]
    expert_rows(rows, weights, active, stores)


def rejoin_kernel(near, far, *outs):
    cap = outs[0].shape[0] // 2
    both = [ref[...].astype(f32) for ref in (near, far)]
    for m, out in enumerate(outs):
        parts = [each[m * cap : (m + 1) * cap] for each in both]
        out[...] = jnp.concatenate(parts, axis=0).astype(bf16)


def partial_kernel(members, cap, columns, places, gates, near, far, *outs):
    at = iota((cap, places.shape[1]), 0)
    for n, m in enumerate(members):
        total = None
        near_rows = near[m * cap : (m + 1) * cap, :]
        far_rows = far[n * cap : (n + 1) * cap, :]
        for values, row in ((near_rows, m), (far_rows, columns + m)):
            spread = jnp.where(at == places[row : row + 1, :], gates[row : row + 1, :], 0.0)
            coarse = spread.astype(bf16)
            fine = (spread - coarse.astype(f32)).astype(bf16)
            for half in (coarse, fine):
                term = lax.dot_general(half, values, TN, preferred_element_type=f32)
                total = term if total is None else total + term
        outs[n][...] = total.astype(outs[n].dtype)


def fold_kernel(own, *rest):
    total = own[...]
    for ref in rest[:-1]:
        total = total + ref[...].astype(f32)
    rest[-1][...] = total.astype(rest[-1].dtype)


def final_kernel(layers, hidden, gates, rows, *rest):
    packets, ends, out = (rest[:layers], rest[layers:-1], rest[-1])
    at = iota((layers * packets[0].shape[0], hidden.shape[0]), 0)
    spread = jnp.where(at == rows[0:1, :], gates[0:1, :], 0.0)
    spread = spread + jnp.where(at == rows[1:2, :], gates[1:2, :], 0.0)
    coarse = spread.astype(bf16)
    fine = (spread - coarse.astype(f32)).astype(bf16)
    values = jnp.concatenate([ref[...].astype(f32) for ref in packets], axis=0).astype(bf16)
    total = hidden[...]
    for half in (coarse, fine):
        total = total + lax.dot_general(half, values, TN, preferred_element_type=f32)
    out[0, 0] = total.astype(bf16)
    total = ends[0][...]
    for ref in ends[1:]:
        total = total + ref[...].astype(f32)
    out[1, 0] = total.astype(bf16)


def local(
    tokens, queries, key_rows, value_rows, segments, bias_table, out_proj, router,
    gate_weight, up_weight, down_weight, old_table, new_table, routes_one, routes_two,
):
    tok_count, width = tokens.shape[2:]
    heads = bias_table.shape[0]
    experts = router.shape[1]
    columns = experts // 2
    inner = gate_weight.shape[2]
    seq_size = lax.axis_size("seq")
    seq_len = tok_count * seq_size
    capacity = tok_count * 2 * 5 // (4 * experts)
    longest = seq_len // 2
    hops = min(WIN_BLOCKS, (longest - 1 + tok_count - 1) // tok_count)
    relayed = seq_size == 4 and hops == 2
    sinks = seq_len > WIN_BLOCKS * tok_count
    weights = (gate_weight, up_weight, down_weight)
    router_t = router.T
    lower, upper = (range(columns // 2), range(columns // 2, columns))
    rows_bf16 = shaped((tok_count, width), bf16)
    rows_f32 = shaped((tok_count, width), f32)
    cap_two = capacity * MAX_SLOTS
    slots = columns * cap_two
    part_two = slots // 2
    packet = shaped((2 * capacity, width), bf16)
    stack_shape = shaped((2 * tok_count, width), bf16)
    latest = []

    def call(kernel, outs, ins, args, scratch=(), after=(), aliases=None, work=1):
        after = [*after, *latest]
        out_specs = jax.tree.map(lambda _: VMEM, outs)
        if aliases:
            out_specs = tuple(ANY if n in aliases.values() else VMEM for n in range(len(outs)))

        def body(*refs):
            kernel(*refs[: len(args)], *refs[len(args) + len(after) :])

        made = pl.pallas_call(
            body,
            out_shape=outs,
            in_specs=ins + [ANY] * len(after),
            out_specs=out_specs,
            scratch_shapes=list(scratch),
            input_output_aliases=aliases or {},
            compiler_params=pltpu.CompilerParams(vmem_limit_bytes=24 * 2**20),
            cost_estimate=pl.CostEstimate(flops=work, bytes_accessed=1, transcendentals=0),
        )(*args, *after)
        latest[:] = jax.tree.leaves(made)[:1]
        return made

    def multicast(own):
        blocks = {0: own}
        bit = columns // 2
        while bit:
            for m in sorted(blocks):
                blocks[m | bit] = swapped(blocks[m], "exp", 2 * bit)
            bit //= 2
        return blocks

    def chained(moving):
        moved = []
        for _ in range(hops):
            moving = passed_along(moving, "seq", 1)
            moved.append(moving)
        return moved

    def options(batch):
        extra = []
        if sinks:
            extra = latest_start(key_rows[batch, 0], value_rows[batch, 0], segments[batch, 0])
        return ((hops, relayed, heads, sinks), extra)

    def attend_column(moved):
        settings, extra = options(1)
        return call(
            functools.partial(attend_column_kernel, settings),
            (rows_f32, rows_bf16),
            [SMEM] + [VMEM] * (3 + 2 * len(moved)) + ([VMEM, SMEM] if sinks else [])
            + [VMEM] * 2,
            (bias_table, own, queries, stacks[1], *moved, *sent, *extra, tokens, out_proj),
            scratch=[pltpu.VMEM((tok_count, width), bf16)],
        )

    def attend_direct(moved):
        settings, extra = options(0)
        return call(
            functools.partial(attend_direct_kernel, settings, experts, capacity),
            (*[packet] * columns, rows_f32, shaped((2, tok_count), f32),
             shaped((2, tok_count), jnp.int32)),
            [SMEM] + [VMEM] * (4 + 2 * len(moved)) + ([VMEM, SMEM] if sinks else [])
            + [VMEM] * 2,
            (bias_table, router_t, own, queries, stacks[0], *moved, *sent, *extra, tokens,
             out_proj),
            scratch=[pltpu.VMEM((tok_count, width), bf16)],
        )

    def scratch_for(slots):
        return (pltpu.VMEM((slots, width), bf16), pltpu.VMEM((slots, inner), bf16))

    def pack(members, places, blocks):
        return call(
            functools.partial(pack_kernel, members, cap_two, columns),
            shaped((part_two, width), bf16),
            [VMEM] * (1 + len(members)),
            (places, *(blocks[m] for m in members)),
        )

    def partial(members, far, handed=None):
        more = [] if handed is None else [handed]

        def kernel(*refs):
            partial_kernel(members, cap_two, columns, *refs[:4], *refs[4 + len(more) :])

        *parts, last = call(
            kernel,
            (*(rows_bf16 if m % 2 else rows_f32 for m in members),
             *(shaped(each.shape, each.dtype) for each in more)),
            [VMEM] * 4 + [ANY] * len(more),
            (places, gates_two, near, far, *more),
            aliases={4: len(members)} if more else None,
        )
        for m, value in zip(members, [*parts, last]):
            totals.setdefault(m, []).insert(0, value)
        return last

    def send_down(members):
        for m in sorted(members, key=lambda m: (m & -m, -m)):
            parts = totals[m]
            value = parts[0]
            if len(parts) > 1:
                value = call(fold_kernel, rows_bf16, [VMEM] * len(parts), parts)
            totals.setdefault(m & (m - 1), []).append(swapped(value, "exp", 2 * (m & -m)))

    stacked = jnp.concatenate([key_rows[1, 0], value_rows[1, 0]], axis=0)
    first_hop = swapped(stacked, "seq", 1) if relayed else passed_along(stacked, "seq", 1)
    tables = [jnp.pad(table, (0, tok_count - experts))[None] for table in (new_table, old_table)]
    numbers = jnp.concatenate([segments[:, 0], routes_one[0].T, routes_two[0].T, *tables])
    own, own_routes, own_segs = call(
        numbers_kernel,
        tuple(shaped((rows, tok_count), jnp.int32) for rows in (8, 2, 2)),
        [VMEM], (numbers,), after=[first_hop],
    )
    routes = multicast(own_routes)
    if relayed:
        sent = [swapped(own_segs, "seq", mask) for mask in (1, 2, 3)]
        across = swapped(stacked, "seq", 2)
    else:
        sent = chained(own_segs)
        across = first_hop
    stack_one = call(
        stage_kernel, stack_shape, [VMEM] * 4, (key_rows, value_rows, queries, tokens),
        after=[routes[columns // 2]],
    )
    *routes, latest_seg = call(
        collect_kernel,
        tuple(shaped((2, tok_count), jnp.int32) for _ in range(columns + 1)),
        [VMEM] * (columns + 1),
        (*(routes[m] for m in range(columns)), sent[-1]),
        after=sent[:-1],
    )
    sent = [*sent[:-1], latest_seg]
    (across,) = call(pass_kernel, (stack_shape,), [ANY], (across,), aliases={0: 0})
    if relayed:
        moved_two = [first_hop, across, swapped(across, "seq", 1)]
    else:
        moved_two = [across]
        while len(moved_two) < hops:
            moved_two.append(passed_along(moved_two[-1], "seq", 1))
    stacks = [stack_one, stacked]
    hidden_two, normed_two = attend_column(moved_two)
    (stack_one,) = call(
        pass_kernel, (stack_shape,), [ANY], (stack_one,), aliases={0: 0}
    )
    stacks[0] = stack_one
    if relayed:
        moved_one = [
            swapped(stack_one, "seq", 1),
            swapped(stack_one, "seq", 2),
            lax.ppermute(stack_one, "seq", [(0, 0), (1, 2), (2, 1), (3, 3)]),
        ]
    else:
        moved_one = chained(stack_one)
    blocks = multicast(normed_two)
    places, low_in = call(
        functools.partial(first_pack_kernel, lower, cap_two, columns),
        (shaped((2 * columns, tok_count), jnp.int32), shaped((part_two, width), bf16)),
        [VMEM] * (1 + columns + len(lower)),
        (own, *routes, *(blocks[m] for m in lower)), work=4 * 10**9,
    )
    low_in = swapped(low_in, "exp", 1)
    high_in = swapped(pack(upper, places, blocks), "exp", 1)
    *packets, hidden_one, gates_one, rows_one = attend_direct(moved_one)
    arrived = [packets[0]] + [swapped(packets[m], "exp", 2 * m) for m in range(1, columns)]
    low_out, high_out = call(
        far_kernel,
        (shaped((part_two, width), bf16),) * 2,
        [VMEM] * 5,
        (low_in, high_in, *weights),
        scratch=scratch_for(slots),
    )
    high_far = swapped(high_out, "exp", 1)
    near, gates_two = call(
        functools.partial(near_kernel, columns, experts, cap_two),
        (shaped((slots, width), bf16), shaped((2 * columns, tok_count), f32)),
        [VMEM] * (6 + 2 * columns),
        (own, places, router_t, *(blocks[m] for m in range(columns)), *routes, *weights),
        scratch=scratch_for(slots), work=4 * 10**9,
    )
    crossing = call(
        crossing_kernel, shaped((columns * capacity, width), bf16), [VMEM] * columns, arrived,
        work=2 * 10**10,
    )
    crossed_one = swapped(crossing, "exp", 1)
    totals = {}
    low_far = swapped(partial(upper, high_far, low_out), "exp", 1)
    send_down(m for m in upper if m % 2)
    near_one, far_one = call(
        functools.partial(direct_kernel, columns),
        (shaped((columns * capacity, width), bf16),) * 2,
        [VMEM] * (4 + columns),
        (*arrived, crossed_one, *weights),
        scratch=scratch_for(experts * capacity),
    )
    far_one = swapped(far_one, "exp", 1)
    send_down(m for m in upper if m % 2 == 0)
    partial(lower, low_far)
    send_down(m for m in lower if m)
    answers = call(rejoin_kernel, [packet] * columns, [VMEM] * 2, (near_one, far_one))
    returned = [answers[0]] + [swapped(answers[m], "exp", 2 * m) for m in range(1, columns)]
    far_part, rest = (totals[0][1], [hidden_two, totals[0][0], *totals[0][2:]])
    ends = (call(fold_kernel, rows_f32, [VMEM] * 2, (rest[0], far_part)), *rest[1:])
    return call(
        functools.partial(final_kernel, columns), shaped((2, 1, tok_count, width), bf16),
        [VMEM] * (3 + columns + len(ends)), (hidden_one, gates_one, rows_one, *returned, *ends),
    )


def solution(mesh):
    rows = P(None, "exp", "seq", None)
    placed = (
        rows, rows, rows, rows, P(None, "exp", "seq"), P(), P(), P(),
        P("exp", None, None), P("exp", None, None), P("exp", None, None), P(), P(),
        P("exp", "seq", None), P("exp", "seq", None),
    )
    return jax.shard_map(local, mesh=mesh, in_specs=placed, out_specs=rows, check_vma=False)
```

```python
import functools

import jax
import jax.numpy as jnp
from jax import lax
from jax.experimental import pallas as pl
from jax.experimental.pallas import tpu as pltpu
from jax.sharding import PartitionSpec as P

WIN_BLOCKS = 4
NBUCK = 32
MAX_SLOTS = 2
ONE_ROW, TWO_ROW, NEW_ROW, OLD_ROW = (2, 4, 6, 7)

score_scale = 0.125
epsilon = 1e-06
masked_score = -1e30

f32 = jnp.float32
bf16 = jnp.bfloat16
NT = (((1,), (1,)), ((), ()))
TN = (((0,), (0,)), ((), ()))
VMEM = pl.BlockSpec(memory_space=pltpu.VMEM)
SMEM = pl.BlockSpec(memory_space=pltpu.SMEM)
ANY = pl.BlockSpec(memory_space=pl.ANY)


def iota(shape, dim):
    return lax.broadcasted_iota(jnp.int32, shape, dim)


def shaped(shape, dtype):
    return jax.ShapeDtypeStruct(shape, dtype)


def passed_along(value, axis, steps):
    count = lax.axis_size(axis)
    return lax.ppermute(value, axis, [(source, source + steps) for source in range(count - steps)])


def swapped(value, axis, mask):
    count = lax.axis_size(axis)
    return lax.ppermute(value, axis, [(source, source ^ mask) for source in range(count)])


def merge_starts(former, latter):
    take_latter = (latter[4] > 0) & ((former[4] == 0) | (latter[3] != former[3]))
    return tuple((jnp.where(take_latter, newer, older) for older, newer in zip(former, latter)))


def latest_start(key_rows, value_rows, segments):
    tok_count, model_width = key_rows.shape
    length, index = (lax.axis_size("seq"), lax.axis_index("seq"))
    last_seg = segments[tok_count - 1]
    lead = jnp.sum((segments < last_seg).astype(jnp.int32))
    one = jnp.ones((), jnp.int32)
    found = (key_rows[lead], value_rows[lead], index * tok_count + lead, last_seg, one)
    everything = jax.tree.map(lambda part: lax.all_gather(part, "seq"), found)
    start = jax.tree.map(jnp.zeros_like, found)

    def lap(k, before):
        new = merge_starts(before, jax.tree.map(lambda part: part[k], everything))
        return jax.tree.map(lambda a, b: jnp.where(k < index, a, b), new, before)

    sink_key, sink_value, sink_pos, sink_seg, sink_has = lax.fori_loop(0, length, lap, start)
    block = jnp.zeros((2 * tok_count, model_width), key_rows.dtype)
    block = block.at[0].set(sink_key).at[tok_count].set(sink_value)
    return (block, jnp.stack([sink_pos, sink_seg, sink_has]))


def table_entry(own, row, entry):
    return own[row : row + 1, entry : entry + 1]


def holder_of(experts, own, pick):
    return sum(
        jnp.where(pick == table_entry(own, OLD_ROW, x), x, 0) for x in range(experts)
    )


def column_routes(experts, routes, own):
    members = len(routes)
    slots = jnp.concatenate([ref[c : c + 1, :] for c in range(2) for ref in routes], axis=0)
    chosen = sum(jnp.where(slots == s, table_entry(own, NEW_ROW, s), 0) for s in range(experts))
    holders = holder_of(experts, own, chosen)
    return tuple((each[:members], each[members:]) for each in (chosen, holders))


def attended(batch, hops, relayed, heads, sinks, bias, own, q, stack, rest, context):
    count = 3 if relayed else hops
    moved, sent, rest = (rest[:count], rest[count : 2 * count], rest[2 * count :])
    if sinks:
        sink_block, sink_info, rest = (rest[0], rest[1], rest[2:])
    tokens, proj = rest
    tok_count, width = tokens.shape[2:]
    window = WIN_BLOCKS * tok_count
    index = lax.axis_index("seq")
    grid = (tok_count, tok_count)

    own_seg = own[batch : batch + 1, :]
    key_segs = [own_seg]
    if relayed:
        pairwise, across, relay = moved
        paired = index % 2 == 1
        key_segs += [jnp.where(paired, sent[0][batch : batch + 1], sent[2][batch : batch + 1])]
        key_segs.append(sent[1][batch : batch + 1, :])
    else:
        key_segs += [ref[batch : batch + 1, :] for ref in sent]
    seg_col = jnp.broadcast_to(own_seg, grid).T
    visible, spans = ([], [])
    for j, key_seg in enumerate(key_segs):
        key_seg = jnp.where(index >= j, key_seg, -1)
        distance = iota(grid, 0) - iota(grid, 1) + tok_count * j
        seen = (seg_col == key_seg) & (distance >= 0) & (distance < window)
        visible.append(jnp.where(seen, 0.0, masked_score))
        low, high = (max(0, tok_count * (j - 1) + 1), min(window, tok_count * (j + 1)) - 1)
        spans.append((distance, low.bit_length(), high.bit_length()))
    if sinks:
        position = index * tok_count + iota(grid, 0)
        seen = (seg_col == sink_info[1]) & (sink_info[2] > 0) & (position - sink_info[0] >= window)
        visible.append(jnp.where(seen & (iota(grid, 1) == 0), 0.0, masked_score))
        spans.append((None, NBUCK - 1, NBUCK - 1))
    lane = iota((tok_count, 128), 1)
    half = width // heads
    keys_at, values_at = (slice(0, tok_count), slice(tok_count, 2 * tok_count))
    for pair in range(heads // 2):
        cols = slice(128 * pair, 128 * pair + 128)
        both = q[batch, 0, :, cols] * score_scale
        even = jnp.where(lane < half, both, jnp.zeros_like(both))
        odd = jnp.where(lane < half, jnp.zeros_like(both), both)
        stacked = jnp.concatenate([even, odd], axis=0)
        blocks = [(stack[keys_at, cols], stack[values_at, cols])]
        if relayed:
            blocks.append(tuple(
                jnp.where(paired, pairwise[at, cols], relay[at, cols])
                for at in (keys_at, values_at)
            ))
            blocks.append((across[keys_at, cols], across[values_at, cols]))
        else:
            for ref in moved:
                blocks.append((ref[keys_at, cols], ref[values_at, cols]))
        if sinks:
            blocks.append((sink_block[keys_at, cols], sink_block[values_at, cols]))
        scores = []
        for (keys, _), (distance, low, high), seen in zip(blocks, spans, visible):
            score = lax.dot_general(stacked, keys, NT, preferred_element_type=f32)
            parts = []
            for side in range(2):
                head = 2 * pair + side
                offset = jnp.full(grid, bias[head, low], f32)
                for bucket in range(low + 1, high + 1):
                    offset = jnp.where(distance >= 1 << (bucket - 1), bias[head, bucket], offset)
                parts.append(score[side * tok_count : (side + 1) * tok_count] + (offset + seen))
            scores.append(jnp.concatenate(parts, axis=0))
        peak = jnp.max(functools.reduce(jnp.maximum, scores), axis=1, keepdims=True)
        weights = [jnp.exp(score - peak) for score in scores]
        total = jnp.sum(functools.reduce(jnp.add, weights), axis=1, keepdims=True)
        scale = 1.0 / total
        mixed = sum(
            jnp.dot((weight * scale).astype(bf16), values, preferred_element_type=f32)
            for weight, (_, values) in zip(weights, blocks)
        )
        context[:, cols] = jnp.where(lane < half, mixed[:tok_count], mixed[tok_count:]).astype(bf16)
    hidden = tokens[batch, 0].astype(f32) + jnp.dot(
        context[...], proj[...], preferred_element_type=f32
    )
    mean = jnp.mean(hidden * hidden, axis=1, keepdims=True)
    return (hidden, (hidden * lax.rsqrt(mean + epsilon)).astype(bf16))


def ranks(member):
    grid = (member.shape[1], member.shape[1])
    earlier = jnp.where(iota(grid, 0) < iota(grid, 1), 1.0, 0.0).astype(bf16)
    return jnp.dot(member.astype(bf16), earlier, preferred_element_type=f32).astype(jnp.int32)


def attend_column_kernel(options, bias, own, q, stack, *rest):
    inputs, (hidden_out, normed_out, context) = (rest[:-3], rest[-3:])
    hidden, normed = attended(1, *options, bias, own, q, stack, inputs, context)
    hidden_out[...] = hidden
    normed_out[...] = normed


def column_places(experts, routes, own):
    me = lax.axis_index("exp")
    _, holders = column_routes(experts, routes, own)
    member = jnp.concatenate(
        [jnp.where((holders[0] == at) | (holders[1] == at), 1.0, 0.0) for at in (me, me ^ 1)],
        axis=0,
    )
    return jnp.where(member > 0.5, ranks(member), -1)


def attend_direct_kernel(options, experts, cap, bias, router_t, own, q, stack, *rest):
    layers = experts // 2
    inputs, rest = (rest[: -4 - layers], rest[-4 - layers :])
    outgoing, (hidden_out, gates_out, rows_out, context) = (rest[:layers], rest[layers:])
    hidden, normed = attended(0, *options, bias, own, q, stack, inputs, context)
    hidden_out[...] = hidden
    tok_count = hidden.shape[0]
    chosen = [own[ONE_ROW + c : ONE_ROW + c + 1, :] for c in range(2)]
    holders = [holder_of(experts, own, pick) for pick in chosen]
    expert = iota((experts, tok_count), 0)
    packet = expert ^ lax.axis_index("exp")
    member = jnp.where((packet == holders[0]) | (packet == holders[1]), 1.0, 0.0)
    place = ranks(member) + expert * cap
    rows = [
        jnp.sum(jnp.where(packet == holder, place, 0), axis=0, keepdims=True) for holder in holders
    ]
    rows_out[...] = jnp.concatenate(rows, axis=0)
    logits = lax.dot_general(router_t[...], normed, NT, preferred_element_type=f32)
    picked = [jnp.sum(jnp.where(expert == c, logits, 0.0), axis=0, keepdims=True) for c in chosen]
    first = jax.nn.sigmoid(picked[0] - picked[1])
    gates_out[...] = jnp.concatenate([first, 1.0 - first], axis=0)
    at = iota((experts * cap, tok_count), 0)
    plan = jnp.where((at == rows[0]) | (at == rows[1]), 1.0, 0.0).astype(bf16)
    packed = jnp.dot(plan, normed, preferred_element_type=f32)
    for m, ref in enumerate(outgoing):
        ref[...] = packed[2 * m * cap : 2 * (m + 1) * cap].astype(bf16)


def picked_rows(members, cap, first_row, places, blocks):
    at = iota((len(members) * cap, blocks[0].shape[0]), 0)
    plans = []
    for n, m in enumerate(members):
        place = places[first_row + m : first_row + m + 1, :]
        place = jnp.where(place >= 0, place + n * cap, -1)
        plans.append(jnp.where(at == place, 1.0, 0.0))
    plan = jnp.concatenate(plans, axis=1).astype(bf16)
    rows = jnp.concatenate([block[...] for block in blocks], axis=0)
    return (jnp.dot(plan, rows, preferred_element_type=f32).astype(bf16), rows)


def pack_kernel(members, cap, columns, places, *rest):
    blocks, out = (rest[:-1], rest[-1])
    out[...], _ = picked_rows(members, cap, columns, places, blocks)


def first_pack_kernel(members, cap, columns, own, *rest):
    routes, blocks, (places, out) = (rest[:columns], rest[columns:-2], rest[-2:])
    places[...] = column_places(2 * columns, routes, own)
    out[...], _ = picked_rows(members, cap, columns, places, blocks)


def numbers_kernel(numbers, own, routes_out, segs_out):
    own[...] = numbers[...]
    routes_out[...] = numbers[TWO_ROW : TWO_ROW + 2, :]
    segs_out[...] = numbers[:2, :]


def collect_kernel(*refs):
    count = len(refs) // 2
    for ref, out in zip(refs[:count], refs[count:]):
        out[...] = ref[...]


def stage_kernel(k, v, q, tokens, out):
    del q, tokens
    tok_count = k.shape[2]
    out[:tok_count, :] = k[0, 0]
    out[tok_count:, :] = v[0, 0]


def join_kernel(k, v, out):
    tok_count = k.shape[0]
    out[:tok_count, :] = k[...]
    out[tok_count:, :] = v[...]


def pass_kernel(*refs):
    del refs


def crossing_kernel(*refs):
    packets, out = (refs[:-1][::-1], refs[-1])
    cap = packets[0].shape[0] // 2
    parts = [ref[...].astype(f32)[cap:] for ref in packets]
    out[...] = jnp.concatenate(parts, axis=0).astype(bf16)


def expert_rows(rows, weights, active, stores):
    gate, up, down = weights
    inner, width = down.shape[1:]
    x = rows[...]
    for begin in range(0, inner, 256):
        span = slice(begin, min(inner, begin + 256))
        gate_part = jnp.dot(x, gate[0, :, span], preferred_element_type=f32)
        up_part = jnp.dot(x, up[0, :, span], preferred_element_type=f32)
        active[:, span] = (jax.nn.gelu(gate_part, approximate=True) * up_part).astype(bf16)
    for begin in range(0, width, 256):
        span = slice(begin, begin + 256)
        part = jnp.dot(active[...], down[0, :, span], preferred_element_type=f32)
        stores(span, part)


def near_kernel(columns, experts, cap, own, places, router_t, *rest):
    blocks, rest = (rest[:columns], rest[columns:])
    routes, rest = (rest[:columns], rest[columns:])
    weights, (out, gates_out, rows, active) = (rest[:3], rest[3:])

    def stores(span, value):
        out[:, span] = value.astype(bf16)

    rows[...], tokens = picked_rows(range(columns), cap, 0, places, blocks)
    logits = lax.dot_general(router_t[...], tokens, NT, preferred_element_type=f32)
    chosen, holders = column_routes(experts, routes, own)
    chosen = [
        jnp.concatenate([picks[m : m + 1, :] for m in range(columns)], axis=1) for picks in chosen
    ]
    expert = iota(logits.shape, 0)
    picked = [
        jnp.sum(jnp.where(expert == pick, logits, 0.0), axis=0, keepdims=True) for pick in chosen
    ]
    first = jax.nn.sigmoid(picked[0] - picked[1])
    tok_count = places.shape[1]
    first = jnp.concatenate(
        [first[:, m * tok_count : (m + 1) * tok_count] for m in range(columns)], axis=0
    )
    me = lax.axis_index("exp")
    gates_out[...] = jnp.concatenate(
        [
            jnp.where(holders[0] == at, first, 0.0) + jnp.where(holders[1] == at, 1.0 - first, 0.0)
            for at in (me, me ^ 1)
        ],
        axis=0,
    )
    expert_rows(rows, weights, active, stores)


def far_kernel(low_in, high_in, *rest):
    weights, (low_out, high_out, rows, active) = (rest[:3], rest[3:])
    part = low_in.shape[0]

    def stores(span, value):
        low_out[:, span] = value[:part].astype(bf16)
        high_out[:, span] = value[part:].astype(bf16)

    rows[:part, :] = low_in[...]
    rows[part:, :] = high_in[...]
    expert_rows(rows, weights, active, stores)


def direct_kernel(layers, *refs):
    packets, crossed, weights = (refs[:layers][::-1], refs[layers], refs[layers + 1 : layers + 4])
    near, far, rows, active = refs[layers + 4 :]
    cap = packets[0].shape[0] // 2
    half = layers * cap

    def stores(span, value):
        near[:, span] = value[:half].astype(bf16)
        far[:, span] = value[half:].astype(bf16)

    parts = [ref[...].astype(f32)[:cap] for ref in packets]
    rows[:half, :] = jnp.concatenate(parts, axis=0).astype(bf16)
    rows[half:, :] = crossed[...]
    expert_rows(rows, weights, active, stores)


def rejoin_kernel(near, far, *outs):
    cap = outs[0].shape[0] // 2
    both = [ref[...].astype(f32) for ref in (near, far)]
    for m, out in enumerate(outs):
        parts = [each[m * cap : (m + 1) * cap] for each in both]
        out[...] = jnp.concatenate(parts, axis=0).astype(bf16)


def partial_kernel(members, cap, columns, places, gates, near, far, *outs):
    at = iota((cap, places.shape[1]), 0)
    for n, m in enumerate(members):
        total = None
        near_rows = near[m * cap : (m + 1) * cap, :]
        far_rows = far[n * cap : (n + 1) * cap, :]
        for values, row in ((near_rows, m), (far_rows, columns + m)):
            spread = jnp.where(at == places[row : row + 1, :], gates[row : row + 1, :], 0.0)
            coarse = spread.astype(bf16)
            fine = (spread - coarse.astype(f32)).astype(bf16)
            for half in (coarse, fine):
                term = lax.dot_general(half, values, TN, preferred_element_type=f32)
                total = term if total is None else total + term
        outs[n][...] = total.astype(outs[n].dtype)


def fold_kernel(own, *rest):
    total = own[...]
    for ref in rest[:-1]:
        total = total + ref[...].astype(f32)
    rest[-1][...] = total.astype(rest[-1].dtype)


def final_kernel(layers, hidden, gates, rows, *rest):
    packets, ends, out = (rest[:layers][::-1], rest[layers:-1], rest[-1])
    at = iota((layers * packets[0].shape[0], hidden.shape[0]), 0)
    spread = jnp.where(at == rows[0:1, :], gates[0:1, :], 0.0)
    spread = spread + jnp.where(at == rows[1:2, :], gates[1:2, :], 0.0)
    coarse = spread.astype(bf16)
    fine = (spread - coarse.astype(f32)).astype(bf16)
    values = jnp.concatenate([ref[...].astype(f32) for ref in packets], axis=0).astype(bf16)
    total = hidden[...]
    for half in (coarse, fine):
        total = total + lax.dot_general(half, values, TN, preferred_element_type=f32)
    out[0, 0] = total.astype(bf16)
    total = ends[0][...]
    for ref in ends[1:]:
        total = total + ref[...].astype(f32)
    out[1, 0] = total.astype(bf16)


def local(
    tokens, queries, key_rows, value_rows, segments, bias_table, out_proj, router,
    gate_weight, up_weight, down_weight, old_table, new_table, routes_one, routes_two,
):
    tok_count, width = tokens.shape[2:]
    heads = bias_table.shape[0]
    experts = router.shape[1]
    columns = experts // 2
    inner = gate_weight.shape[2]
    seq_size = lax.axis_size("seq")
    seq_len = tok_count * seq_size
    capacity = tok_count * 2 * 5 // (4 * experts)
    longest = seq_len // 2
    hops = min(WIN_BLOCKS, (longest - 1 + tok_count - 1) // tok_count)
    relayed = seq_size == 4 and hops == 2
    sinks = seq_len > WIN_BLOCKS * tok_count
    weights = (gate_weight, up_weight, down_weight)
    router_t = router.T
    lower, upper = (range(columns // 2), range(columns // 2, columns))
    rows_bf16 = shaped((tok_count, width), bf16)
    rows_f32 = shaped((tok_count, width), f32)
    cap_two = capacity * MAX_SLOTS
    slots = columns * cap_two
    part_two = slots // 2
    packet = shaped((2 * capacity, width), bf16)
    stack_shape = shaped((2 * tok_count, width), bf16)
    latest = []

    def call(kernel, outs, ins, args, scratch=(), after=(), aliases=None, work=1):
        after = [*after, *latest]
        out_specs = jax.tree.map(lambda _: VMEM, outs)
        if aliases:
            out_specs = tuple(ANY if n in aliases.values() else VMEM for n in range(len(outs)))

        def body(*refs):
            kernel(*refs[: len(args)], *refs[len(args) + len(after) :])

        made = pl.pallas_call(
            body,
            out_shape=outs,
            in_specs=ins + [ANY] * len(after),
            out_specs=out_specs,
            scratch_shapes=list(scratch),
            input_output_aliases=aliases or {},
            compiler_params=pltpu.CompilerParams(vmem_limit_bytes=24 * 2**20),
            cost_estimate=pl.CostEstimate(flops=work, bytes_accessed=1, transcendentals=0),
        )(*args, *after)
        latest[:] = jax.tree.leaves(made)[:1]
        return made

    def multicast(own):
        blocks = {0: own}
        bit = columns // 2
        while bit:
            for m in sorted(blocks):
                blocks[m | bit] = swapped(blocks[m], "exp", 2 * bit)
            bit //= 2
        return blocks

    def chained(moving):
        moved = []
        for _ in range(hops):
            moving = passed_along(moving, "seq", 1)
            moved.append(moving)
        return moved

    def options(batch):
        extra = []
        if sinks:
            extra = latest_start(key_rows[batch, 0], value_rows[batch, 0], segments[batch, 0])
        return ((hops, relayed, heads, sinks), extra)

    def attend_column(moved):
        settings, extra = options(1)
        return call(
            functools.partial(attend_column_kernel, settings),
            (rows_f32, rows_bf16),
            [SMEM] + [VMEM] * (3 + 2 * len(moved)) + ([VMEM, SMEM] if sinks else [])
            + [VMEM] * 2,
            (bias_table, own, queries, stacks[1], *moved, *sent, *extra, tokens, out_proj),
            scratch=[pltpu.VMEM((tok_count, width), bf16)],
        )

    def attend_direct(moved):
        settings, extra = options(0)
        return call(
            functools.partial(attend_direct_kernel, settings, experts, capacity),
            (*[packet] * columns, rows_f32, shaped((2, tok_count), f32),
             shaped((2, tok_count), jnp.int32)),
            [SMEM] + [VMEM] * (4 + 2 * len(moved)) + ([VMEM, SMEM] if sinks else [])
            + [VMEM] * 2,
            (bias_table, router_t, own, queries, stacks[0], *moved, *sent, *extra, tokens,
             out_proj),
            scratch=[pltpu.VMEM((tok_count, width), bf16)],
        )

    def scratch_for(slots):
        return (pltpu.VMEM((slots, width), bf16), pltpu.VMEM((slots, inner), bf16))

    def pack(members, places, blocks):
        return call(
            functools.partial(pack_kernel, members, cap_two, columns),
            shaped((part_two, width), bf16),
            [VMEM] * (1 + len(members)),
            (places, *(blocks[m] for m in members)),
        )

    def partial(members, far, handed=None):
        more = [] if handed is None else [handed]

        def kernel(*refs):
            partial_kernel(members, cap_two, columns, *refs[:4], *refs[4 + len(more) :])

        *parts, last = call(
            kernel,
            (*(rows_bf16 if m % 2 else rows_f32 for m in members),
             *(shaped(each.shape, each.dtype) for each in more)),
            [VMEM] * 4 + [ANY] * len(more),
            (places, gates_two, near, far, *more),
            aliases={4: len(members)} if more else None,
        )
        for m, value in zip(members, [*parts, last]):
            totals.setdefault(m, []).insert(0, value)
        return last

    def send_down(members):
        for m in sorted(members, key=lambda m: (m & -m, -m)):
            parts = totals[m]
            value = parts[0]
            if len(parts) > 1:
                value = call(fold_kernel, rows_bf16, [VMEM] * len(parts), parts)
            totals.setdefault(m & (m - 1), []).append(swapped(value, "exp", 2 * (m & -m)))

    stacked = call(join_kernel, stack_shape, [VMEM] * 2, (key_rows[1, 0], value_rows[1, 0]))
    first_hop = swapped(stacked, "seq", 1) if relayed else passed_along(stacked, "seq", 1)
    tables = [jnp.pad(table, (0, tok_count - experts))[None] for table in (new_table, old_table)]
    numbers = jnp.concatenate([segments[:, 0], routes_one[0].T, routes_two[0].T, *tables])
    own, own_routes, own_segs = call(
        numbers_kernel,
        tuple(shaped((rows, tok_count), jnp.int32) for rows in (8, 2, 2)),
        [VMEM], (numbers,), after=[first_hop],
    )
    routes = multicast(own_routes)
    if relayed:
        sent = [swapped(own_segs, "seq", mask) for mask in (1, 2, 3)]
        across = swapped(stacked, "seq", 2)
    else:
        sent = chained(own_segs)
        across = first_hop
    stack_one = call(
        stage_kernel, stack_shape, [VMEM] * 4, (key_rows, value_rows, queries, tokens),
        after=[routes[columns // 2]],
    )
    *routes, latest_seg = call(
        collect_kernel,
        tuple(shaped((2, tok_count), jnp.int32) for _ in range(columns + 1)),
        [VMEM] * (columns + 1),
        (*(routes[m] for m in range(columns)), sent[-1]),
        after=sent[:-1],
    )
    sent = [*sent[:-1], latest_seg]
    (across,) = call(pass_kernel, (stack_shape,), [ANY], (across,), aliases={0: 0})
    if relayed:
        moved_two = [first_hop, across, swapped(across, "seq", 1)]
    else:
        moved_two = [across]
        while len(moved_two) < hops:
            moved_two.append(passed_along(moved_two[-1], "seq", 1))
    stacks = [stack_one, stacked]
    hidden_two, normed_two = attend_column(moved_two)
    (stack_one,) = call(
        pass_kernel, (stack_shape,), [ANY], (stack_one,), aliases={0: 0}
    )
    stacks[0] = stack_one
    if relayed:
        moved_one = [
            swapped(stack_one, "seq", 1),
            swapped(stack_one, "seq", 2),
            lax.ppermute(stack_one, "seq", [(0, 0), (1, 2), (2, 1), (3, 3)]),
        ]
    else:
        moved_one = chained(stack_one)
    blocks = multicast(normed_two)
    places, low_in = call(
        functools.partial(first_pack_kernel, lower, cap_two, columns),
        (shaped((2 * columns, tok_count), jnp.int32), shaped((part_two, width), bf16)),
        [VMEM] * (1 + columns + len(lower)),
        (own, *routes, *(blocks[m] for m in lower)), work=4 * 10**9,
    )
    low_in = swapped(low_in, "exp", 1)
    high_in = swapped(pack(upper, places, blocks), "exp", 1)
    *packets, hidden_one, gates_one, rows_one = attend_direct(moved_one)
    arrived = [packets[0]] + [swapped(packets[m], "exp", 2 * m) for m in range(1, columns)]
    low_out, high_out = call(
        far_kernel,
        (shaped((part_two, width), bf16),) * 2,
        [VMEM] * 5,
        (low_in, high_in, *weights),
        scratch=scratch_for(slots),
    )
    high_far = swapped(high_out, "exp", 1)
    near, gates_two = call(
        functools.partial(near_kernel, columns, experts, cap_two),
        (shaped((slots, width), bf16), shaped((2 * columns, tok_count), f32)),
        [VMEM] * (6 + 2 * columns),
        (own, places, router_t, *(blocks[m] for m in range(columns)), *routes, *weights),
        scratch=scratch_for(slots), work=4 * 10**9,
    )
    crossing = call(
        crossing_kernel, shaped((columns * capacity, width), bf16), [VMEM] * columns, arrived[::-1],
        work=2 * 10**10,
    )
    crossed_one = swapped(crossing, "exp", 1)
    totals = {}
    low_far = swapped(partial(upper, high_far, low_out), "exp", 1)
    send_down(m for m in upper if m % 2)
    near_one, far_one = call(
        functools.partial(direct_kernel, columns),
        (shaped((columns * capacity, width), bf16),) * 2,
        [VMEM] * (4 + columns),
        (*arrived[::-1], crossed_one, *weights),
        scratch=scratch_for(experts * capacity),
    )
    far_one = swapped(far_one, "exp", 1)
    send_down(m for m in upper if m % 2 == 0)
    partial(lower, low_far)
    send_down(m for m in lower if m)
    answers = call(rejoin_kernel, [packet] * columns, [VMEM] * 2, (near_one, far_one))
    returned = [answers[0]] + [swapped(answers[m], "exp", 2 * m) for m in range(1, columns)]
    far_part, rest = (totals[0][1], [hidden_two, totals[0][0], *totals[0][2:]])
    ends = (call(fold_kernel, rows_f32, [VMEM] * 2, (rest[0], far_part)), *rest[1:])
    return call(
        functools.partial(final_kernel, columns), shaped((2, 1, tok_count, width), bf16),
        [VMEM] * (3 + columns + len(ends)), (hidden_one, gates_one, rows_one, *returned[::-1], *ends),
    )


def solution(mesh):
    rows = P(None, "exp", "seq", None)
    placed = (
        rows, rows, rows, rows, P(None, "exp", "seq"), P(), P(), P(),
        P("exp", None, None), P("exp", None, None), P("exp", None, None), P(), P(),
        P("exp", "seq", None), P("exp", "seq", None),
    )
    return jax.shard_map(local, mesh=mesh, in_specs=placed, out_specs=rows, check_vma=False)
```

```python
import functools

import jax
import jax.numpy as jnp
from jax import lax
from jax.experimental import pallas as pl
from jax.experimental.pallas import tpu as pltpu
from jax.sharding import PartitionSpec as P

WIN_BLOCKS = 4
NBUCK = 32
MAX_SLOTS = 2
ONE_ROW, TWO_ROW, NEW_ROW, OLD_ROW = (2, 4, 6, 7)

score_scale = 0.125
epsilon = 1e-06
masked_score = -1e30

f32 = jnp.float32
bf16 = jnp.bfloat16
NT = (((1,), (1,)), ((), ()))
TN = (((0,), (0,)), ((), ()))
VMEM = pl.BlockSpec(memory_space=pltpu.VMEM)
SMEM = pl.BlockSpec(memory_space=pltpu.SMEM)
ANY = pl.BlockSpec(memory_space=pl.ANY)


def iota(shape, dim):
    return lax.broadcasted_iota(jnp.int32, shape, dim)


def shaped(shape, dtype):
    return jax.ShapeDtypeStruct(shape, dtype)


def passed_along(value, axis, steps):
    count = lax.axis_size(axis)
    return lax.ppermute(value, axis, [(source, source + steps) for source in range(count - steps)])


def swapped(value, axis, mask):
    count = lax.axis_size(axis)
    return lax.ppermute(value, axis, [(source, source ^ mask) for source in range(count)])


def merge_starts(former, latter):
    take_latter = (latter[4] > 0) & ((former[4] == 0) | (latter[3] != former[3]))
    return tuple((jnp.where(take_latter, newer, older) for older, newer in zip(former, latter)))


def latest_start(key_rows, value_rows, segments):
    tok_count, model_width = key_rows.shape
    length, index = (lax.axis_size("seq"), lax.axis_index("seq"))
    last_seg = segments[tok_count - 1]
    lead = jnp.sum((segments < last_seg).astype(jnp.int32))
    one = jnp.ones((), jnp.int32)
    found = (key_rows[lead], value_rows[lead], index * tok_count + lead, last_seg, one)
    everything = jax.tree.map(lambda part: lax.all_gather(part, "seq"), found)
    start = jax.tree.map(jnp.zeros_like, found)

    def lap(k, before):
        new = merge_starts(before, jax.tree.map(lambda part: part[k], everything))
        return jax.tree.map(lambda a, b: jnp.where(k < index, a, b), new, before)

    sink_key, sink_value, sink_pos, sink_seg, sink_has = lax.fori_loop(0, length, lap, start)
    block = jnp.zeros((2 * tok_count, model_width), key_rows.dtype)
    block = block.at[0].set(sink_key).at[tok_count].set(sink_value)
    return (block, jnp.stack([sink_pos, sink_seg, sink_has]))


def table_entry(own, row, entry):
    return own[row : row + 1, entry : entry + 1]


def holder_of(experts, own, pick):
    return sum(
        jnp.where(pick == table_entry(own, OLD_ROW, x), x, 0) for x in range(experts)
    )


def column_routes(experts, routes, own):
    members = len(routes)
    slots = jnp.concatenate([ref[c : c + 1, :] for c in range(2) for ref in routes], axis=0)
    chosen = sum(jnp.where(slots == s, table_entry(own, NEW_ROW, s), 0) for s in range(experts))
    holders = holder_of(experts, own, chosen)
    return tuple((each[:members], each[members:]) for each in (chosen, holders))


def attended(batch, hops, relayed, heads, sinks, bias, own, q, stack, rest, context):
    count = 3 if relayed else hops
    moved, sent, rest = (rest[:count], rest[count : 2 * count], rest[2 * count :])
    if sinks:
        sink_block, sink_info, rest = (rest[0], rest[1], rest[2:])
    tokens, proj = rest
    tok_count, width = tokens.shape[2:]
    window = WIN_BLOCKS * tok_count
    index = lax.axis_index("seq")
    grid = (tok_count, tok_count)

    own_seg = own[batch : batch + 1, :]
    key_segs = [own_seg]
    if relayed:
        pairwise, across, relay = moved
        paired = index % 2 == 1
        key_segs += [jnp.where(paired, sent[0][batch : batch + 1], sent[2][batch : batch + 1])]
        key_segs.append(sent[1][batch : batch + 1, :])
    else:
        key_segs += [ref[batch : batch + 1, :] for ref in sent]
    seg_col = jnp.broadcast_to(own_seg, grid).T
    visible, spans = ([], [])
    for j, key_seg in enumerate(key_segs):
        key_seg = jnp.where(index >= j, key_seg, -1)
        distance = iota(grid, 0) - iota(grid, 1) + tok_count * j
        seen = (seg_col == key_seg) & (distance >= 0) & (distance < window)
        visible.append(jnp.where(seen, 0.0, masked_score))
        low, high = (max(0, tok_count * (j - 1) + 1), min(window, tok_count * (j + 1)) - 1)
        spans.append((distance, low.bit_length(), high.bit_length()))
    if sinks:
        position = index * tok_count + iota(grid, 0)
        seen = (seg_col == sink_info[1]) & (sink_info[2] > 0) & (position - sink_info[0] >= window)
        visible.append(jnp.where(seen & (iota(grid, 1) == 0), 0.0, masked_score))
        spans.append((None, NBUCK - 1, NBUCK - 1))
    lane = iota((tok_count, 128), 1)
    half = width // heads
    keys_at, values_at = (slice(0, tok_count), slice(tok_count, 2 * tok_count))
    for pair in range(heads // 2):
        cols = slice(128 * pair, 128 * pair + 128)
        both = q[batch, 0, :, cols] * score_scale
        even = jnp.where(lane < half, both, jnp.zeros_like(both))
        odd = jnp.where(lane < half, jnp.zeros_like(both), both)
        stacked = jnp.concatenate([even, odd], axis=0)
        blocks = [(stack[keys_at, cols], stack[values_at, cols])]
        if relayed:
            blocks.append(tuple(
                jnp.where(paired, pairwise[at, cols], relay[at, cols])
                for at in (keys_at, values_at)
            ))
            blocks.append((across[keys_at, cols], across[values_at, cols]))
        else:
            for ref in moved:
                blocks.append((ref[keys_at, cols], ref[values_at, cols]))
        if sinks:
            blocks.append((sink_block[keys_at, cols], sink_block[values_at, cols]))
        scores = []
        for (keys, _), (distance, low, high), seen in zip(blocks, spans, visible):
            score = lax.dot_general(stacked, keys, NT, preferred_element_type=f32)
            parts = []
            for side in range(2):
                head = 2 * pair + side
                offset = jnp.full(grid, bias[head, low], f32)
                for bucket in range(low + 1, high + 1):
                    offset = jnp.where(distance >= 1 << (bucket - 1), bias[head, bucket], offset)
                parts.append(score[side * tok_count : (side + 1) * tok_count] + (offset + seen))
            scores.append(jnp.concatenate(parts, axis=0))
        peak = jnp.max(functools.reduce(jnp.maximum, scores), axis=1, keepdims=True)
        weights = [jnp.exp(score - peak) for score in scores]
        total = jnp.sum(functools.reduce(jnp.add, weights), axis=1, keepdims=True)
        scale = 1.0 / total
        mixed = sum(
            jnp.dot((weight * scale).astype(bf16), values, preferred_element_type=f32)
            for weight, (_, values) in zip(weights, blocks)
        )
        context[:, cols] = jnp.where(lane < half, mixed[:tok_count], mixed[tok_count:]).astype(bf16)
    hidden = tokens[batch, 0].astype(f32) + jnp.dot(
        context[...], proj[...], preferred_element_type=f32
    )
    mean = jnp.mean(hidden * hidden, axis=1, keepdims=True)
    return (hidden, (hidden * lax.rsqrt(mean + epsilon)).astype(bf16))


def ranks(member):
    grid = (member.shape[1], member.shape[1])
    earlier = jnp.where(iota(grid, 0) < iota(grid, 1), 1.0, 0.0).astype(bf16)
    return jnp.dot(member.astype(bf16), earlier, preferred_element_type=f32).astype(jnp.int32)


def attend_column_kernel(options, bias, own, q, stack, *rest):
    inputs, (hidden_out, normed_out, context) = (rest[:-3], rest[-3:])
    hidden, normed = attended(1, *options, bias, own, q, stack, inputs, context)
    hidden_out[...] = hidden
    normed_out[...] = normed


def column_places(experts, routes, own):
    me = lax.axis_index("exp")
    _, holders = column_routes(experts, routes, own)
    member = jnp.concatenate(
        [jnp.where((holders[0] == at) | (holders[1] == at), 1.0, 0.0) for at in (me, me ^ 1)],
        axis=0,
    )
    return jnp.where(member > 0.5, ranks(member), -1)


def attend_direct_kernel(options, experts, cap, bias, router_t, own, q, stack, *rest):
    layers = experts // 2
    inputs, rest = (rest[: -4 - layers], rest[-4 - layers :])
    outgoing, (hidden_out, gates_out, rows_out, context) = (rest[:layers], rest[layers:])
    hidden, normed = attended(0, *options, bias, own, q, stack, inputs, context)
    hidden_out[...] = hidden
    tok_count = hidden.shape[0]
    chosen = [own[ONE_ROW + c : ONE_ROW + c + 1, :] for c in range(2)]
    holders = [holder_of(experts, own, pick) for pick in chosen]
    expert = iota((experts, tok_count), 0)
    packet = expert ^ lax.axis_index("exp")
    member = jnp.where((packet == holders[0]) | (packet == holders[1]), 1.0, 0.0)
    place = ranks(member) + expert * cap
    rows = [
        jnp.sum(jnp.where(packet == holder, place, 0), axis=0, keepdims=True) for holder in holders
    ]
    rows_out[...] = jnp.concatenate(rows, axis=0)
    logits = lax.dot_general(router_t[...], normed, NT, preferred_element_type=f32)
    picked = [jnp.sum(jnp.where(expert == c, logits, 0.0), axis=0, keepdims=True) for c in chosen]
    first = jax.nn.sigmoid(picked[0] - picked[1])
    gates_out[...] = jnp.concatenate([first, 1.0 - first], axis=0)
    at = iota((experts * cap, tok_count), 0)
    plan = jnp.where((at == rows[0]) | (at == rows[1]), 1.0, 0.0).astype(bf16)
    packed = jnp.dot(plan, normed, preferred_element_type=f32)
    for m, ref in enumerate(outgoing):
        ref[...] = packed[2 * m * cap : 2 * (m + 1) * cap].astype(bf16)


def picked_rows(members, cap, first_row, places, blocks):
    at = iota((len(members) * cap, blocks[0].shape[0]), 0)
    plans = []
    for n, m in enumerate(members):
        place = places[first_row + m : first_row + m + 1, :]
        place = jnp.where(place >= 0, place + n * cap, -1)
        plans.append(jnp.where(at == place, 1.0, 0.0))
    plan = jnp.concatenate(plans, axis=1).astype(bf16)
    rows = jnp.concatenate([block[...] for block in blocks], axis=0)
    return (jnp.dot(plan, rows, preferred_element_type=f32).astype(bf16), rows)


def pack_kernel(members, cap, columns, places, *rest):
    blocks, out = (rest[:-1], rest[-1])
    out[...], _ = picked_rows(members, cap, columns, places, blocks)


def first_pack_kernel(members, cap, columns, own, *rest):
    routes, blocks, (places, out) = (rest[:columns], rest[columns:-2], rest[-2:])
    places[...] = column_places(2 * columns, routes, own)
    out[...], _ = picked_rows(members, cap, columns, places, blocks)


def numbers_kernel(numbers, own, routes_out, segs_out):
    own[...] = numbers[...]
    routes_out[...] = numbers[TWO_ROW : TWO_ROW + 2, :]
    segs_out[...] = numbers[:2, :]


def collect_kernel(*refs):
    count = len(refs) // 2
    for ref, out in zip(refs[:count], refs[count:]):
        out[...] = ref[...]


def stage_kernel(k, v, q, tokens, out):
    del q, tokens
    tok_count = k.shape[2]
    out[:tok_count, :] = k[0, 0]
    out[tok_count:, :] = v[0, 0]


def join_kernel(k, v, out):
    tok_count = k.shape[0]
    out[:tok_count, :] = k[...]
    out[tok_count:, :] = v[...]


def pass_kernel(*refs):
    del refs


def crossing_kernel(*refs):
    packets, out = (refs[:-1][::-1], refs[-1])
    cap = packets[0].shape[0] // 2
    parts = [ref[...].astype(f32)[cap:] for ref in packets]
    out[...] = jnp.concatenate(parts, axis=0).astype(bf16)


def expert_rows(rows, weights, active, stores):
    gate, up, down = weights
    inner, width = down.shape[1:]
    x = rows[...]
    for begin in range(0, inner, 256):
        span = slice(begin, min(inner, begin + 256))
        gate_part = jnp.dot(x, gate[0, :, span], preferred_element_type=f32)
        up_part = jnp.dot(x, up[0, :, span], preferred_element_type=f32)
        active[:, span] = (jax.nn.gelu(gate_part, approximate=True) * up_part).astype(bf16)
    for begin in range(0, width, 256):
        span = slice(begin, begin + 256)
        part = jnp.dot(active[...], down[0, :, span], preferred_element_type=f32)
        stores(span, part)


def near_kernel(columns, experts, cap, own, places, router_t, *rest):
    blocks, rest = (rest[:columns], rest[columns:])
    routes, rest = (rest[:columns], rest[columns:])
    weights, (out, gates_out, rows, active) = (rest[:3], rest[3:])

    def stores(span, value):
        out[:, span] = value.astype(bf16)

    rows[...], tokens = picked_rows(range(columns), cap, 0, places, blocks)
    logits = lax.dot_general(router_t[...], tokens, NT, preferred_element_type=f32)
    chosen, holders = column_routes(experts, routes, own)
    chosen = [
        jnp.concatenate([picks[m : m + 1, :] for m in range(columns)], axis=1) for picks in chosen
    ]
    expert = iota(logits.shape, 0)
    picked = [
        jnp.sum(jnp.where(expert == pick, logits, 0.0), axis=0, keepdims=True) for pick in chosen
    ]
    first = jax.nn.sigmoid(picked[0] - picked[1])
    tok_count = places.shape[1]
    first = jnp.concatenate(
        [first[:, m * tok_count : (m + 1) * tok_count] for m in range(columns)], axis=0
    )
    me = lax.axis_index("exp")
    gates_out[...] = jnp.concatenate(
        [
            jnp.where(holders[0] == at, first, 0.0) + jnp.where(holders[1] == at, 1.0 - first, 0.0)
            for at in (me, me ^ 1)
        ],
        axis=0,
    )
    expert_rows(rows, weights, active, stores)


def far_kernel(low_in, high_in, *rest):
    weights, (low_out, high_out, rows, active) = (rest[:3], rest[3:])
    part = low_in.shape[0]

    def stores(span, value):
        low_out[:, span] = value[:part].astype(bf16)
        high_out[:, span] = value[part:].astype(bf16)

    rows[:part, :] = low_in[...]
    rows[part:, :] = high_in[...]
    expert_rows(rows, weights, active, stores)


def direct_kernel(layers, *refs):
    packets, crossed, weights = (refs[:layers][::-1], refs[layers], refs[layers + 1 : layers + 4])
    near, far, rows, active = refs[layers + 4 :]
    cap = packets[0].shape[0] // 2
    half = layers * cap

    def stores(span, value):
        near[:, span] = value[:half].astype(bf16)
        far[:, span] = value[half:].astype(bf16)

    parts = [ref[...].astype(f32)[:cap] for ref in packets]
    rows[:half, :] = jnp.concatenate(parts, axis=0).astype(bf16)
    rows[half:, :] = crossed[...]
    expert_rows(rows, weights, active, stores)


def rejoin_kernel(near, far, *outs):
    cap = outs[0].shape[0] // 2
    both = [ref[...].astype(f32) for ref in (near, far)]
    for m, out in enumerate(outs):
        parts = [each[m * cap : (m + 1) * cap] for each in both]
        out[...] = jnp.concatenate(parts, axis=0).astype(bf16)


def partial_kernel(members, cap, columns, places, gates, near, far, *outs):
    at = iota((cap, places.shape[1]), 0)
    for n, m in enumerate(members):
        total = None
        near_rows = near[m * cap : (m + 1) * cap, :]
        far_rows = far[n * cap : (n + 1) * cap, :]
        for values, row in ((near_rows, m), (far_rows, columns + m)):
            spread = jnp.where(at == places[row : row + 1, :], gates[row : row + 1, :], 0.0)
            coarse = spread.astype(bf16)
            fine = (spread - coarse.astype(f32)).astype(bf16)
            for half in (coarse, fine):
                term = lax.dot_general(half, values, TN, preferred_element_type=f32)
                total = term if total is None else total + term
        outs[n][...] = total.astype(outs[n].dtype)


def fold_kernel(own, *rest):
    total = own[...]
    for ref in rest[:-1]:
        total = total + ref[...].astype(f32)
    rest[-1][...] = total.astype(rest[-1].dtype)


def final_kernel(layers, hidden, gates, rows, *rest):
    packets, ends, out = (rest[:layers][::-1], rest[layers:-1], rest[-1])
    at = iota((layers * packets[0].shape[0], hidden.shape[0]), 0)
    spread = jnp.where(at == rows[0:1, :], gates[0:1, :], 0.0)
    spread = spread + jnp.where(at == rows[1:2, :], gates[1:2, :], 0.0)
    coarse = spread.astype(bf16)
    fine = (spread - coarse.astype(f32)).astype(bf16)
    values = jnp.concatenate([ref[...].astype(f32) for ref in packets], axis=0).astype(bf16)
    total = hidden[...]
    for half in (coarse, fine):
        total = total + lax.dot_general(half, values, TN, preferred_element_type=f32)
    out[0, 0] = total.astype(bf16)
    total = ends[0][...]
    for ref in ends[1:]:
        total = total + ref[...].astype(f32)
    out[1, 0] = total.astype(bf16)


def local(
    tokens, queries, key_rows, value_rows, segments, bias_table, out_proj, router,
    gate_weight, up_weight, down_weight, old_table, new_table, routes_one, routes_two,
):
    tok_count, width = tokens.shape[2:]
    heads = bias_table.shape[0]
    experts = router.shape[1]
    columns = experts // 2
    inner = gate_weight.shape[2]
    seq_size = lax.axis_size("seq")
    seq_len = tok_count * seq_size
    capacity = tok_count * 2 * 5 // (4 * experts)
    longest = seq_len // 2
    hops = min(WIN_BLOCKS, (longest - 1 + tok_count - 1) // tok_count)
    relayed = seq_size == 4 and hops == 2
    sinks = seq_len > WIN_BLOCKS * tok_count
    weights = (gate_weight, up_weight, down_weight)
    router_t = router.T
    lower, upper = (range(columns // 2), range(columns // 2, columns))
    rows_bf16 = shaped((tok_count, width), bf16)
    rows_f32 = shaped((tok_count, width), f32)
    cap_two = capacity * MAX_SLOTS
    slots = columns * cap_two
    part_two = slots // 2
    packet = shaped((2 * capacity, width), bf16)
    stack_shape = shaped((2 * tok_count, width), bf16)
    latest = []

    def call(kernel, outs, ins, args, scratch=(), after=(), aliases=None, work=1):
        after = [*after, *latest]
        out_specs = jax.tree.map(lambda _: VMEM, outs)
        if aliases:
            out_specs = tuple(ANY if n in aliases.values() else VMEM for n in range(len(outs)))

        def body(*refs):
            kernel(*refs[: len(args)], *refs[len(args) + len(after) :])

        made = pl.pallas_call(
            body,
            out_shape=outs,
            in_specs=ins + [ANY] * len(after),
            out_specs=out_specs,
            scratch_shapes=list(scratch),
            input_output_aliases=aliases or {},
            compiler_params=pltpu.CompilerParams(vmem_limit_bytes=24 * 2**20),
            cost_estimate=pl.CostEstimate(flops=work, bytes_accessed=1, transcendentals=0),
        )(*args, *after)
        latest[:] = jax.tree.leaves(made)[:1]
        return made

    def multicast(own):
        blocks = {0: own}
        bit = columns // 2
        while bit:
            for m in sorted(blocks):
                blocks[m | bit] = swapped(blocks[m], "exp", 2 * bit)
            bit //= 2
        return blocks

    def chained(moving):
        moved = []
        for _ in range(hops):
            moving = passed_along(moving, "seq", 1)
            moved.append(moving)
        return moved

    def options(batch):
        extra = []
        if sinks:
            extra = latest_start(key_rows[batch, 0], value_rows[batch, 0], segments[batch, 0])
        return ((hops, relayed, heads, sinks), extra)

    def attend_column(moved):
        settings, extra = options(1)
        return call(
            functools.partial(attend_column_kernel, settings),
            (rows_f32, rows_bf16),
            [SMEM] + [VMEM] * (3 + 2 * len(moved)) + ([VMEM, SMEM] if sinks else [])
            + [VMEM] * 2,
            (bias_table, own, queries, stacks[1], *moved, *sent, *extra, tokens, out_proj),
            scratch=[pltpu.VMEM((tok_count, width), bf16)],
        )

    def attend_direct(moved):
        settings, extra = options(0)
        return call(
            functools.partial(attend_direct_kernel, settings, experts, capacity),
            (*[packet] * columns, rows_f32, shaped((2, tok_count), f32),
             shaped((2, tok_count), jnp.int32)),
            [SMEM] + [VMEM] * (4 + 2 * len(moved)) + ([VMEM, SMEM] if sinks else [])
            + [VMEM] * 2,
            (bias_table, router_t, own, queries, stacks[0], *moved, *sent, *extra, tokens,
             out_proj),
            scratch=[pltpu.VMEM((tok_count, width), bf16)],
        )

    def scratch_for(slots):
        return (pltpu.VMEM((slots, width), bf16), pltpu.VMEM((slots, inner), bf16))

    def pack(members, places, blocks):
        return call(
            functools.partial(pack_kernel, members, cap_two, columns),
            shaped((part_two, width), bf16),
            [VMEM] * (1 + len(members)),
            (places, *(blocks[m] for m in members)),
        )

    def partial(members, far):
        parts = call(
            functools.partial(partial_kernel, members, cap_two, columns),
            tuple(rows_bf16 if m % 2 else rows_f32 for m in members),
            [VMEM] * 4,
            (places, gates_two, near, far),
        )
        for m, value in zip(members, parts):
            totals.setdefault(m, []).insert(0, value)

    def send_down(members):
        for m in sorted(members, key=lambda m: (m & -m, -m)):
            parts = totals[m]
            value = parts[0]
            if len(parts) > 1:
                value = call(
                    fold_kernel, rows_bf16, [VMEM] * len(parts), parts, work=6 * 10**9
                )
            totals.setdefault(m & (m - 1), []).append(swapped(value, "exp", 2 * (m & -m)))

    stacked = call(join_kernel, stack_shape, [VMEM] * 2, (key_rows[1, 0], value_rows[1, 0]))
    first_hop = swapped(stacked, "seq", 1) if relayed else passed_along(stacked, "seq", 1)
    tables = [jnp.pad(table, (0, tok_count - experts))[None] for table in (new_table, old_table)]
    numbers = jnp.concatenate([segments[:, 0], routes_one[0].T, routes_two[0].T, *tables])
    own, own_routes, own_segs = call(
        numbers_kernel,
        tuple(shaped((rows, tok_count), jnp.int32) for rows in (8, 2, 2)),
        [VMEM], (numbers,), after=[first_hop],
    )
    routes = multicast(own_routes)
    if relayed:
        sent = [swapped(own_segs, "seq", mask) for mask in (1, 2, 3)]
        across = swapped(stacked, "seq", 2)
    else:
        sent = chained(own_segs)
        across = first_hop
    stack_one = call(
        stage_kernel, stack_shape, [VMEM] * 4, (key_rows, value_rows, queries, tokens),
        after=[routes[columns // 2]],
    )
    *routes, latest_seg = call(
        collect_kernel,
        tuple(shaped((2, tok_count), jnp.int32) for _ in range(columns + 1)),
        [VMEM] * (columns + 1),
        (*(routes[m] for m in range(columns)), sent[-1]),
        after=sent[:-1],
    )
    sent = [*sent[:-1], latest_seg]
    (across,) = call(pass_kernel, (stack_shape,), [ANY], (across,), aliases={0: 0})
    if relayed:
        moved_two = [first_hop, across, swapped(across, "seq", 1)]
    else:
        moved_two = [across]
        while len(moved_two) < hops:
            moved_two.append(passed_along(moved_two[-1], "seq", 1))
    stacks = [stack_one, stacked]
    hidden_two, normed_two = attend_column(moved_two)
    (stack_one,) = call(
        pass_kernel, (stack_shape,), [ANY], (stack_one,), aliases={0: 0}
    )
    stacks[0] = stack_one
    if relayed:
        moved_one = [
            swapped(stack_one, "seq", 1),
            swapped(stack_one, "seq", 2),
            lax.ppermute(stack_one, "seq", [(0, 0), (1, 2), (2, 1), (3, 3)]),
        ]
    else:
        moved_one = chained(stack_one)
    blocks = multicast(normed_two)
    places, low_in = call(
        functools.partial(first_pack_kernel, lower, cap_two, columns),
        (shaped((2 * columns, tok_count), jnp.int32), shaped((part_two, width), bf16)),
        [VMEM] * (1 + columns + len(lower)),
        (own, *routes, *(blocks[m] for m in lower)), work=4 * 10**9,
    )
    low_in = swapped(low_in, "exp", 1)
    high_in = swapped(pack(upper, places, blocks), "exp", 1)
    *packets, hidden_one, gates_one, rows_one = attend_direct(moved_one)
    arrived = [packets[0]] + [swapped(packets[m], "exp", 2 * m) for m in range(1, columns)]
    low_out, high_out = call(
        far_kernel,
        (shaped((part_two, width), bf16),) * 2,
        [VMEM] * 5,
        (low_in, high_in, *weights),
        scratch=scratch_for(slots),
    )
    high_far = swapped(high_out, "exp", 1)
    near, gates_two = call(
        functools.partial(near_kernel, columns, experts, cap_two),
        (shaped((slots, width), bf16), shaped((2 * columns, tok_count), f32)),
        [VMEM] * (6 + 2 * columns),
        (own, places, router_t, *(blocks[m] for m in range(columns)), *routes, *weights),
        scratch=scratch_for(slots), work=4 * 10**9,
    )
    crossing = call(
        crossing_kernel, shaped((columns * capacity, width), bf16), [VMEM] * columns, arrived[::-1],
        work=2 * 10**10,
    )
    crossed_one = swapped(crossing, "exp", 1)
    totals = {}
    partial(upper, high_far)
    send_down(m for m in upper if m % 2)
    (low_out,) = call(
        pass_kernel, (shaped(low_out.shape, bf16),), [ANY], (low_out,), aliases={0: 0},
        after=[crossed_one],
    )
    low_far = swapped(low_out, "exp", 1)
    near_one, far_one = call(
        functools.partial(direct_kernel, columns),
        (shaped((columns * capacity, width), bf16),) * 2,
        [VMEM] * (4 + columns),
        (*arrived[::-1], crossed_one, *weights),
        scratch=scratch_for(experts * capacity),
    )
    far_one = swapped(far_one, "exp", 1)
    send_down(m for m in upper if m % 2 == 0)
    partial(lower, low_far)
    send_down(m for m in lower if m)
    answers = call(rejoin_kernel, [packet] * columns, [VMEM] * 2, (near_one, far_one))
    returned = [answers[0]] + [swapped(answers[m], "exp", 2 * m) for m in range(1, columns)]
    far_part, rest = (totals[0][1], [hidden_two, totals[0][0], *totals[0][2:]])
    ends = (call(fold_kernel, rows_f32, [VMEM] * 2, (rest[0], far_part)), *rest[1:])
    return call(
        functools.partial(final_kernel, columns), shaped((2, 1, tok_count, width), bf16),
        [VMEM] * (3 + columns + len(ends)), (hidden_one, gates_one, rows_one, *returned[::-1], *ends),
    )


def solution(mesh):
    rows = P(None, "exp", "seq", None)
    placed = (
        rows, rows, rows, rows, P(None, "exp", "seq"), P(), P(), P(),
        P("exp", None, None), P("exp", None, None), P("exp", None, None), P(), P(),
        P("exp", "seq", None), P("exp", "seq", None),
    )
    return jax.shard_map(local, mesh=mesh, in_specs=placed, out_specs=rows, check_vma=False)
```

```python
import functools

import jax
import jax.numpy as jnp
from jax import lax
from jax.experimental import pallas as pl
from jax.experimental.pallas import tpu as pltpu
from jax.sharding import PartitionSpec as P

WIN_BLOCKS = 4
NBUCK = 32
MAX_SLOTS = 2
ONE_ROW, TWO_ROW, NEW_ROW, OLD_ROW = (2, 4, 6, 7)

score_scale = 0.125
epsilon = 1e-06
masked_score = -1e30

f32 = jnp.float32
bf16 = jnp.bfloat16
NT = (((1,), (1,)), ((), ()))
TN = (((0,), (0,)), ((), ()))
VMEM = pl.BlockSpec(memory_space=pltpu.VMEM)
SMEM = pl.BlockSpec(memory_space=pltpu.SMEM)
ANY = pl.BlockSpec(memory_space=pl.ANY)


def iota(shape, dim):
    return lax.broadcasted_iota(jnp.int32, shape, dim)


def shaped(shape, dtype):
    return jax.ShapeDtypeStruct(shape, dtype)


def passed_along(value, axis, steps):
    count = lax.axis_size(axis)
    return lax.ppermute(value, axis, [(source, source + steps) for source in range(count - steps)])


def swapped(value, axis, mask):
    count = lax.axis_size(axis)
    return lax.ppermute(value, axis, [(source, source ^ mask) for source in range(count)])


def merge_starts(former, latter):
    take_latter = (latter[4] > 0) & ((former[4] == 0) | (latter[3] != former[3]))
    return tuple((jnp.where(take_latter, newer, older) for older, newer in zip(former, latter)))


def latest_start(key_rows, value_rows, segments):
    tok_count, model_width = key_rows.shape
    length, index = (lax.axis_size("seq"), lax.axis_index("seq"))
    last_seg = segments[tok_count - 1]
    lead = jnp.sum((segments < last_seg).astype(jnp.int32))
    one = jnp.ones((), jnp.int32)
    found = (key_rows[lead], value_rows[lead], index * tok_count + lead, last_seg, one)
    everything = jax.tree.map(lambda part: lax.all_gather(part, "seq"), found)
    start = jax.tree.map(jnp.zeros_like, found)

    def lap(k, before):
        new = merge_starts(before, jax.tree.map(lambda part: part[k], everything))
        return jax.tree.map(lambda a, b: jnp.where(k < index, a, b), new, before)

    sink_key, sink_value, sink_pos, sink_seg, sink_has = lax.fori_loop(0, length, lap, start)
    block = jnp.zeros((2 * tok_count, model_width), key_rows.dtype)
    block = block.at[0].set(sink_key).at[tok_count].set(sink_value)
    return (block, jnp.stack([sink_pos, sink_seg, sink_has]))


def table_entry(own, row, entry):
    return own[row : row + 1, entry : entry + 1]


def holder_of(experts, own, pick):
    return sum(
        jnp.where(pick == table_entry(own, OLD_ROW, x), x, 0) for x in range(experts)
    )


def column_routes(experts, routes, own):
    members = len(routes)
    slots = jnp.concatenate([ref[c : c + 1, :] for c in range(2) for ref in routes], axis=0)
    chosen = sum(jnp.where(slots == s, table_entry(own, NEW_ROW, s), 0) for s in range(experts))
    holders = holder_of(experts, own, chosen)
    return tuple((each[:members], each[members:]) for each in (chosen, holders))


def attended(batch, hops, relayed, heads, sinks, bias, own, q, stack, rest, context):
    count = 3 if relayed else hops
    moved, sent, rest = (rest[:count], rest[count : 2 * count], rest[2 * count :])
    if sinks:
        sink_block, sink_info, rest = (rest[0], rest[1], rest[2:])
    tokens, proj = rest
    tok_count, width = tokens.shape[2:]
    window = WIN_BLOCKS * tok_count
    index = lax.axis_index("seq")
    grid = (tok_count, tok_count)

    own_seg = own[batch : batch + 1, :]
    key_segs = [own_seg]
    if relayed:
        pairwise, across, relay = moved
        paired = index % 2 == 1
        key_segs += [jnp.where(paired, sent[0][batch : batch + 1], sent[2][batch : batch + 1])]
        key_segs.append(sent[1][batch : batch + 1, :])
    else:
        key_segs += [ref[batch : batch + 1, :] for ref in sent]
    seg_col = jnp.broadcast_to(own_seg, grid).T
    visible, spans = ([], [])
    for j, key_seg in enumerate(key_segs):
        key_seg = jnp.where(index >= j, key_seg, -1)
        distance = iota(grid, 0) - iota(grid, 1) + tok_count * j
        seen = (seg_col == key_seg) & (distance >= 0) & (distance < window)
        visible.append(jnp.where(seen, 0.0, masked_score))
        low, high = (max(0, tok_count * (j - 1) + 1), min(window, tok_count * (j + 1)) - 1)
        spans.append((distance, low.bit_length(), high.bit_length()))
    if sinks:
        position = index * tok_count + iota(grid, 0)
        seen = (seg_col == sink_info[1]) & (sink_info[2] > 0) & (position - sink_info[0] >= window)
        visible.append(jnp.where(seen & (iota(grid, 1) == 0), 0.0, masked_score))
        spans.append((None, NBUCK - 1, NBUCK - 1))
    lane = iota((tok_count, 128), 1)
    half = width // heads
    keys_at, values_at = (slice(0, tok_count), slice(tok_count, 2 * tok_count))
    for pair in range(heads // 2):
        cols = slice(128 * pair, 128 * pair + 128)
        both = q[batch, 0, :, cols] * score_scale
        even = jnp.where(lane < half, both, jnp.zeros_like(both))
        odd = jnp.where(lane < half, jnp.zeros_like(both), both)
        stacked = jnp.concatenate([even, odd], axis=0)
        blocks = [(stack[keys_at, cols], stack[values_at, cols])]
        if relayed:
            blocks.append(tuple(
                jnp.where(paired, pairwise[at, cols], relay[at, cols])
                for at in (keys_at, values_at)
            ))
            blocks.append((across[keys_at, cols], across[values_at, cols]))
        else:
            for ref in moved:
                blocks.append((ref[keys_at, cols], ref[values_at, cols]))
        if sinks:
            blocks.append((sink_block[keys_at, cols], sink_block[values_at, cols]))
        scores = []
        for (keys, _), (distance, low, high), seen in zip(blocks, spans, visible):
            score = lax.dot_general(stacked, keys, NT, preferred_element_type=f32)
            parts = []
            for side in range(2):
                head = 2 * pair + side
                offset = jnp.full(grid, bias[head, low], f32)
                for bucket in range(low + 1, high + 1):
                    offset = jnp.where(distance >= 1 << (bucket - 1), bias[head, bucket], offset)
                parts.append(score[side * tok_count : (side + 1) * tok_count] + (offset + seen))
            scores.append(jnp.concatenate(parts, axis=0))
        peak = jnp.max(functools.reduce(jnp.maximum, scores), axis=1, keepdims=True)
        weights = [jnp.exp(score - peak) for score in scores]
        total = jnp.sum(functools.reduce(jnp.add, weights), axis=1, keepdims=True)
        scale = 1.0 / total
        mixed = sum(
            jnp.dot((weight * scale).astype(bf16), values, preferred_element_type=f32)
            for weight, (_, values) in zip(weights, blocks)
        )
        context[:, cols] = jnp.where(lane < half, mixed[:tok_count], mixed[tok_count:]).astype(bf16)
    hidden = tokens[batch, 0].astype(f32) + jnp.dot(
        context[...], proj[...], preferred_element_type=f32
    )
    mean = jnp.mean(hidden * hidden, axis=1, keepdims=True)
    return (hidden, (hidden * lax.rsqrt(mean + epsilon)).astype(bf16))


def ranks(member):
    grid = (member.shape[1], member.shape[1])
    earlier = jnp.where(iota(grid, 0) < iota(grid, 1), 1.0, 0.0).astype(bf16)
    return jnp.dot(member.astype(bf16), earlier, preferred_element_type=f32).astype(jnp.int32)


def attend_column_kernel(options, bias, own, q, stack, *rest):
    inputs, (hidden_out, normed_out, context) = (rest[:-3], rest[-3:])
    hidden, normed = attended(1, *options, bias, own, q, stack, inputs, context)
    hidden_out[...] = hidden
    normed_out[...] = normed


def column_places(experts, routes, own):
    me = lax.axis_index("exp")
    _, holders = column_routes(experts, routes, own)
    member = jnp.concatenate(
        [jnp.where((holders[0] == at) | (holders[1] == at), 1.0, 0.0) for at in (me, me ^ 1)],
        axis=0,
    )
    return jnp.where(member > 0.5, ranks(member), -1)


def attend_direct_kernel(options, experts, cap, bias, router_t, own, q, stack, *rest):
    layers = experts // 2
    inputs, rest = (rest[: -4 - layers], rest[-4 - layers :])
    outgoing, (hidden_out, gates_out, rows_out, context) = (rest[:layers], rest[layers:])
    hidden, normed = attended(0, *options, bias, own, q, stack, inputs, context)
    hidden_out[...] = hidden
    tok_count = hidden.shape[0]
    chosen = [own[ONE_ROW + c : ONE_ROW + c + 1, :] for c in range(2)]
    holders = [holder_of(experts, own, pick) for pick in chosen]
    expert = iota((experts, tok_count), 0)
    packet = expert ^ lax.axis_index("exp")
    member = jnp.where((packet == holders[0]) | (packet == holders[1]), 1.0, 0.0)
    place = ranks(member) + expert * cap
    rows = [
        jnp.sum(jnp.where(packet == holder, place, 0), axis=0, keepdims=True) for holder in holders
    ]
    rows_out[...] = jnp.concatenate(rows, axis=0)
    logits = lax.dot_general(router_t[...], normed, NT, preferred_element_type=f32)
    picked = [jnp.sum(jnp.where(expert == c, logits, 0.0), axis=0, keepdims=True) for c in chosen]
    first = jax.nn.sigmoid(picked[0] - picked[1])
    gates_out[...] = jnp.concatenate([first, 1.0 - first], axis=0)
    at = iota((experts * cap, tok_count), 0)
    plan = jnp.where((at == rows[0]) | (at == rows[1]), 1.0, 0.0).astype(bf16)
    packed = jnp.dot(plan, normed, preferred_element_type=f32)
    for m, ref in enumerate(outgoing):
        ref[...] = packed[2 * m * cap : 2 * (m + 1) * cap].astype(bf16)


def picked_rows(members, cap, first_row, places, blocks):
    at = iota((len(members) * cap, blocks[0].shape[0]), 0)
    plans = []
    for n, m in enumerate(members):
        place = places[first_row + m : first_row + m + 1, :]
        place = jnp.where(place >= 0, place + n * cap, -1)
        plans.append(jnp.where(at == place, 1.0, 0.0))
    plan = jnp.concatenate(plans, axis=1).astype(bf16)
    rows = jnp.concatenate([block[...] for block in blocks], axis=0)
    return (jnp.dot(plan, rows, preferred_element_type=f32).astype(bf16), rows)


def pack_kernel(members, cap, columns, places, *rest):
    blocks, out = (rest[:-1], rest[-1])
    out[...], _ = picked_rows(members, cap, columns, places, blocks)


def first_pack_kernel(members, cap, columns, own, *rest):
    routes, blocks, (places, out) = (rest[:columns], rest[columns:-2], rest[-2:])
    places[...] = column_places(2 * columns, routes, own)
    out[...], _ = picked_rows(members, cap, columns, places, blocks)


def numbers_kernel(numbers, own, routes_out, segs_out):
    own[...] = numbers[...]
    routes_out[...] = numbers[TWO_ROW : TWO_ROW + 2, :]
    segs_out[...] = numbers[:2, :]


def collect_kernel(*refs):
    count = len(refs) // 2
    for ref, out in zip(refs[:count], refs[count:]):
        out[...] = ref[...]


def stage_kernel(k, v, q, tokens, out):
    del q, tokens
    tok_count = k.shape[2]
    out[:tok_count, :] = k[0, 0]
    out[tok_count:, :] = v[0, 0]


def join_kernel(k, v, out):
    tok_count = k.shape[0]
    out[:tok_count, :] = k[...]
    out[tok_count:, :] = v[...]


def pass_kernel(*refs):
    del refs


def crossing_kernel(*refs):
    packets, out = (refs[:-1][::-1], refs[-1])
    cap = packets[0].shape[0] // 2
    parts = [ref[...].astype(f32)[cap:] for ref in packets]
    out[...] = jnp.concatenate(parts, axis=0).astype(bf16)


def expert_rows(rows, weights, active, stores):
    gate, up, down = weights
    inner, width = down.shape[1:]
    x = rows[...]
    for begin in range(0, inner, 256):
        span = slice(begin, min(inner, begin + 256))
        gate_part = jnp.dot(x, gate[0, :, span], preferred_element_type=f32)
        up_part = jnp.dot(x, up[0, :, span], preferred_element_type=f32)
        active[:, span] = (jax.nn.gelu(gate_part, approximate=True) * up_part).astype(bf16)
    for begin in range(0, width, 256):
        span = slice(begin, begin + 256)
        part = jnp.dot(active[...], down[0, :, span], preferred_element_type=f32)
        stores(span, part)


def near_kernel(columns, experts, cap, own, places, router_t, *rest):
    blocks, rest = (rest[:columns], rest[columns:])
    routes, rest = (rest[:columns], rest[columns:])
    weights, (out, gates_out, rows, active) = (rest[:3], rest[3:])

    def stores(span, value):
        out[:, span] = value.astype(bf16)

    rows[...], tokens = picked_rows(range(columns), cap, 0, places, blocks)
    logits = lax.dot_general(router_t[...], tokens, NT, preferred_element_type=f32)
    chosen, holders = column_routes(experts, routes, own)
    chosen = [
        jnp.concatenate([picks[m : m + 1, :] for m in range(columns)], axis=1) for picks in chosen
    ]
    expert = iota(logits.shape, 0)
    picked = [
        jnp.sum(jnp.where(expert == pick, logits, 0.0), axis=0, keepdims=True) for pick in chosen
    ]
    first = jax.nn.sigmoid(picked[0] - picked[1])
    tok_count = places.shape[1]
    first = jnp.concatenate(
        [first[:, m * tok_count : (m + 1) * tok_count] for m in range(columns)], axis=0
    )
    me = lax.axis_index("exp")
    gates_out[...] = jnp.concatenate(
        [
            jnp.where(holders[0] == at, first, 0.0) + jnp.where(holders[1] == at, 1.0 - first, 0.0)
            for at in (me, me ^ 1)
        ],
        axis=0,
    )
    expert_rows(rows, weights, active, stores)


def far_kernel(low_in, high_in, *rest):
    weights, (low_out, high_out, rows, active) = (rest[:3], rest[3:])
    part = low_in.shape[0]

    def stores(span, value):
        low_out[:, span] = value[:part].astype(bf16)
        high_out[:, span] = value[part:].astype(bf16)

    rows[:part, :] = low_in[...]
    rows[part:, :] = high_in[...]
    expert_rows(rows, weights, active, stores)


def direct_near_kernel(layers, *refs):
    packets, weights = (refs[:layers][::-1], refs[layers : layers + 3])
    out, rows, active = refs[layers + 3 :]
    cap = packets[0].shape[0] // 2

    def stores(span, value):
        out[:, span] = value.astype(bf16)

    parts = [ref[...].astype(f32)[:cap] for ref in packets]
    rows[...] = jnp.concatenate(parts, axis=0).astype(bf16)
    expert_rows(rows, weights, active, stores)


def direct_far_kernel(crossed, gate, up, down, out, active):
    def stores(span, value):
        out[:, span] = value.astype(bf16)

    expert_rows(crossed, (gate, up, down), active, stores)


def rejoin_kernel(near, far, *outs):
    cap = outs[0].shape[0] // 2
    both = [ref[...].astype(f32) for ref in (near, far)]
    for m, out in enumerate(outs):
        parts = [each[m * cap : (m + 1) * cap] for each in both]
        out[...] = jnp.concatenate(parts, axis=0).astype(bf16)


def partial_kernel(members, cap, columns, places, gates, near, far, *outs):
    at = iota((cap, places.shape[1]), 0)
    for n, m in enumerate(members):
        total = None
        near_rows = near[m * cap : (m + 1) * cap, :]
        far_rows = far[n * cap : (n + 1) * cap, :]
        for values, row in ((near_rows, m), (far_rows, columns + m)):
            spread = jnp.where(at == places[row : row + 1, :], gates[row : row + 1, :], 0.0)
            coarse = spread.astype(bf16)
            fine = (spread - coarse.astype(f32)).astype(bf16)
            for half in (coarse, fine):
                term = lax.dot_general(half, values, TN, preferred_element_type=f32)
                total = term if total is None else total + term
        outs[n][...] = total.astype(outs[n].dtype)


def fold_kernel(own, *rest):
    total = own[...]
    for ref in rest[:-1]:
        total = total + ref[...].astype(f32)
    rest[-1][...] = total.astype(rest[-1].dtype)


def final_kernel(layers, hidden, gates, rows, *rest):
    packets, ends, out = (rest[:layers][::-1], rest[layers:-1], rest[-1])
    at = iota((layers * packets[0].shape[0], hidden.shape[0]), 0)
    spread = jnp.where(at == rows[0:1, :], gates[0:1, :], 0.0)
    spread = spread + jnp.where(at == rows[1:2, :], gates[1:2, :], 0.0)
    coarse = spread.astype(bf16)
    fine = (spread - coarse.astype(f32)).astype(bf16)
    values = jnp.concatenate([ref[...].astype(f32) for ref in packets], axis=0).astype(bf16)
    total = hidden[...]
    for half in (coarse, fine):
        total = total + lax.dot_general(half, values, TN, preferred_element_type=f32)
    out[0, 0] = total.astype(bf16)
    total = ends[0][...]
    for ref in ends[1:]:
        total = total + ref[...].astype(f32)
    out[1, 0] = total.astype(bf16)


def local(
    tokens, queries, key_rows, value_rows, segments, bias_table, out_proj, router,
    gate_weight, up_weight, down_weight, old_table, new_table, routes_one, routes_two,
):
    tok_count, width = tokens.shape[2:]
    heads = bias_table.shape[0]
    experts = router.shape[1]
    columns = experts // 2
    inner = gate_weight.shape[2]
    seq_size = lax.axis_size("seq")
    seq_len = tok_count * seq_size
    capacity = tok_count * 2 * 5 // (4 * experts)
    longest = seq_len // 2
    hops = min(WIN_BLOCKS, (longest - 1 + tok_count - 1) // tok_count)
    relayed = seq_size == 4 and hops == 2
    sinks = seq_len > WIN_BLOCKS * tok_count
    weights = (gate_weight, up_weight, down_weight)
    router_t = router.T
    lower, upper = (range(columns // 2), range(columns // 2, columns))
    rows_bf16 = shaped((tok_count, width), bf16)
    rows_f32 = shaped((tok_count, width), f32)
    cap_two = capacity * MAX_SLOTS
    slots = columns * cap_two
    part_two = slots // 2
    half_one = columns * capacity
    packet = shaped((2 * capacity, width), bf16)
    stack_shape = shaped((2 * tok_count, width), bf16)
    latest = []

    def call(kernel, outs, ins, args, scratch=(), after=(), aliases=None, work=1):
        after = [*after, *latest]
        out_specs = jax.tree.map(lambda _: VMEM, outs)
        if aliases:
            out_specs = tuple(ANY if n in aliases.values() else VMEM for n in range(len(outs)))

        def body(*refs):
            kernel(*refs[: len(args)], *refs[len(args) + len(after) :])

        made = pl.pallas_call(
            body,
            out_shape=outs,
            in_specs=ins + [ANY] * len(after),
            out_specs=out_specs,
            scratch_shapes=list(scratch),
            input_output_aliases=aliases or {},
            compiler_params=pltpu.CompilerParams(vmem_limit_bytes=24 * 2**20),
            cost_estimate=pl.CostEstimate(flops=work, bytes_accessed=1, transcendentals=0),
        )(*args, *after)
        latest[:] = jax.tree.leaves(made)[:1]
        return made

    def multicast(own):
        blocks = {0: own}
        bit = columns // 2
        while bit:
            for m in sorted(blocks):
                blocks[m | bit] = swapped(blocks[m], "exp", 2 * bit)
            bit //= 2
        return blocks

    def chained(moving):
        moved = []
        for _ in range(hops):
            moving = passed_along(moving, "seq", 1)
            moved.append(moving)
        return moved

    def options(batch):
        extra = []
        if sinks:
            extra = latest_start(key_rows[batch, 0], value_rows[batch, 0], segments[batch, 0])
        return ((hops, relayed, heads, sinks), extra)

    def attend_column(moved):
        settings, extra = options(1)
        return call(
            functools.partial(attend_column_kernel, settings),
            (rows_f32, rows_bf16),
            [SMEM] + [VMEM] * (3 + 2 * len(moved)) + ([VMEM, SMEM] if sinks else [])
            + [VMEM] * 2,
            (bias_table, own, queries, stacks[1], *moved, *sent, *extra, tokens, out_proj),
            scratch=[pltpu.VMEM((tok_count, width), bf16)],
        )

    def attend_direct(moved):
        settings, extra = options(0)
        return call(
            functools.partial(attend_direct_kernel, settings, experts, capacity),
            (*[packet] * columns, rows_f32, shaped((2, tok_count), f32),
             shaped((2, tok_count), jnp.int32)),
            [SMEM] + [VMEM] * (4 + 2 * len(moved)) + ([VMEM, SMEM] if sinks else [])
            + [VMEM] * 2,
            (bias_table, router_t, own, queries, stacks[0], *moved, *sent, *extra, tokens,
             out_proj),
            scratch=[pltpu.VMEM((tok_count, width), bf16)],
        )

    def scratch_for(slots):
        return (pltpu.VMEM((slots, width), bf16), pltpu.VMEM((slots, inner), bf16))

    def pack(members, places, blocks):
        return call(
            functools.partial(pack_kernel, members, cap_two, columns),
            shaped((part_two, width), bf16),
            [VMEM] * (1 + len(members)),
            (places, *(blocks[m] for m in members)),
        )

    def partial(members, far):
        parts = call(
            functools.partial(partial_kernel, members, cap_two, columns),
            tuple(rows_bf16 if m % 2 else rows_f32 for m in members),
            [VMEM] * 4,
            (places, gates_two, near, far),
        )
        for m, value in zip(members, parts):
            totals.setdefault(m, []).insert(0, value)

    def send_down(members):
        for m in sorted(members, key=lambda m: (m & -m, -m)):
            parts = totals[m]
            value = parts[0]
            if len(parts) > 1:
                value = call(
                    fold_kernel, rows_bf16, [VMEM] * len(parts), parts, work=6 * 10**9
                )
            totals.setdefault(m & (m - 1), []).append(swapped(value, "exp", 2 * (m & -m)))

    stacked = call(join_kernel, stack_shape, [VMEM] * 2, (key_rows[1, 0], value_rows[1, 0]))
    first_hop = swapped(stacked, "seq", 1) if relayed else passed_along(stacked, "seq", 1)
    tables = [jnp.pad(table, (0, tok_count - experts))[None] for table in (new_table, old_table)]
    numbers = jnp.concatenate([segments[:, 0], routes_one[0].T, routes_two[0].T, *tables])
    own, own_routes, own_segs = call(
        numbers_kernel,
        tuple(shaped((rows, tok_count), jnp.int32) for rows in (8, 2, 2)),
        [VMEM], (numbers,), after=[first_hop],
    )
    routes = multicast(own_routes)
    if relayed:
        sent = [swapped(own_segs, "seq", mask) for mask in (1, 2, 3)]
        across = swapped(stacked, "seq", 2)
    else:
        sent = chained(own_segs)
        across = first_hop
    stack_one = call(
        stage_kernel, stack_shape, [VMEM] * 4, (key_rows, value_rows, queries, tokens),
        after=[routes[columns // 2]],
    )
    *routes, latest_seg = call(
        collect_kernel,
        tuple(shaped((2, tok_count), jnp.int32) for _ in range(columns + 1)),
        [VMEM] * (columns + 1),
        (*(routes[m] for m in range(columns)), sent[-1]),
        after=sent[:-1],
    )
    sent = [*sent[:-1], latest_seg]
    (across,) = call(pass_kernel, (stack_shape,), [ANY], (across,), aliases={0: 0})
    if relayed:
        moved_two = [first_hop, across, swapped(across, "seq", 1)]
    else:
        moved_two = [across]
        while len(moved_two) < hops:
            moved_two.append(passed_along(moved_two[-1], "seq", 1))
    stacks = [stack_one, stacked]
    hidden_two, normed_two = attend_column(moved_two)
    (stack_one,) = call(
        pass_kernel, (stack_shape,), [ANY], (stack_one,), aliases={0: 0}
    )
    stacks[0] = stack_one
    if relayed:
        moved_one = [
            swapped(stack_one, "seq", 1),
            swapped(stack_one, "seq", 2),
            lax.ppermute(stack_one, "seq", [(0, 0), (1, 2), (2, 1), (3, 3)]),
        ]
    else:
        moved_one = chained(stack_one)
    blocks = multicast(normed_two)
    places, low_in = call(
        functools.partial(first_pack_kernel, lower, cap_two, columns),
        (shaped((2 * columns, tok_count), jnp.int32), shaped((part_two, width), bf16)),
        [VMEM] * (1 + columns + len(lower)),
        (own, *routes, *(blocks[m] for m in lower)), work=4 * 10**9,
    )
    low_in = swapped(low_in, "exp", 1)
    high_in = swapped(pack(upper, places, blocks), "exp", 1)
    *packets, hidden_one, gates_one, rows_one = attend_direct(moved_one)
    arrived = [packets[0]] + [swapped(packets[m], "exp", 2 * m) for m in range(1, columns)]
    low_out, high_out = call(
        far_kernel,
        (shaped((part_two, width), bf16),) * 2,
        [VMEM] * 5,
        (low_in, high_in, *weights),
        scratch=scratch_for(slots),
    )
    high_far = swapped(high_out, "exp", 1)
    near, gates_two = call(
        functools.partial(near_kernel, columns, experts, cap_two),
        (shaped((slots, width), bf16), shaped((2 * columns, tok_count), f32)),
        [VMEM] * (6 + 2 * columns),
        (own, places, router_t, *(blocks[m] for m in range(columns)), *routes, *weights),
        scratch=scratch_for(slots), work=4 * 10**9,
    )
    crossing = call(
        crossing_kernel, shaped((columns * capacity, width), bf16), [VMEM] * columns, arrived[::-1],
        work=2 * 10**10,
    )
    crossed_one = swapped(crossing, "exp", 1)
    totals = {}
    partial(upper, high_far)
    send_down(m for m in upper if m % 2)
    near_one = call(
        functools.partial(direct_near_kernel, columns), shaped((half_one, width), bf16),
        [VMEM] * (3 + columns), (*arrived[::-1], *weights), scratch=scratch_for(half_one),
    )
    (low_out,) = call(
        pass_kernel, (shaped(low_out.shape, bf16),), [ANY], (low_out,), aliases={0: 0},
        after=[crossed_one],
    )
    low_far = swapped(low_out, "exp", 1)
    far_one = call(
        direct_far_kernel, shaped((half_one, width), bf16), [VMEM] * 4, (crossed_one, *weights),
        scratch=scratch_for(half_one)[1:],
    )
    far_one = swapped(far_one, "exp", 1)
    send_down(m for m in upper if m % 2 == 0)
    partial(lower, low_far)
    send_down(m for m in lower if m)
    answers = call(rejoin_kernel, [packet] * columns, [VMEM] * 2, (near_one, far_one))
    returned = [answers[0]] + [swapped(answers[m], "exp", 2 * m) for m in range(1, columns)]
    far_part, rest = (totals[0][1], [hidden_two, totals[0][0], *totals[0][2:]])
    ends = (call(fold_kernel, rows_f32, [VMEM] * 2, (rest[0], far_part)), *rest[1:])
    return call(
        functools.partial(final_kernel, columns), shaped((2, 1, tok_count, width), bf16),
        [VMEM] * (3 + columns + len(ends)), (hidden_one, gates_one, rows_one, *returned[::-1], *ends),
    )


def solution(mesh):
    rows = P(None, "exp", "seq", None)
    placed = (
        rows, rows, rows, rows, P(None, "exp", "seq"), P(), P(), P(),
        P("exp", None, None), P("exp", None, None), P("exp", None, None), P(), P(),
        P("exp", "seq", None), P("exp", "seq", None),
    )
    return jax.shard_map(local, mesh=mesh, in_specs=placed, out_specs=rows, check_vma=False)
```

```python
import functools

import jax
import jax.numpy as jnp
from jax import lax
from jax.experimental import pallas as pl
from jax.experimental.pallas import tpu as pltpu
from jax.sharding import PartitionSpec as P

WIN_BLOCKS = 4
NBUCK = 32
MAX_SLOTS = 2
ONE_ROW, TWO_ROW, NEW_ROW, OLD_ROW = (2, 4, 6, 7)

score_scale = 0.125
epsilon = 1e-06
masked_score = -1e30

f32 = jnp.float32
bf16 = jnp.bfloat16
NT = (((1,), (1,)), ((), ()))
TN = (((0,), (0,)), ((), ()))
VMEM = pl.BlockSpec(memory_space=pltpu.VMEM)
SMEM = pl.BlockSpec(memory_space=pltpu.SMEM)
ANY = pl.BlockSpec(memory_space=pl.ANY)


def iota(shape, dim):
    return lax.broadcasted_iota(jnp.int32, shape, dim)


def shaped(shape, dtype):
    return jax.ShapeDtypeStruct(shape, dtype)


def passed_along(value, axis, steps):
    count = lax.axis_size(axis)
    return lax.ppermute(value, axis, [(source, source + steps) for source in range(count - steps)])


def swapped(value, axis, mask):
    count = lax.axis_size(axis)
    return lax.ppermute(value, axis, [(source, source ^ mask) for source in range(count)])


def merge_starts(former, latter):
    take_latter = (latter[4] > 0) & ((former[4] == 0) | (latter[3] != former[3]))
    return tuple((jnp.where(take_latter, newer, older) for older, newer in zip(former, latter)))


def latest_start(key_rows, value_rows, segments):
    tok_count, model_width = key_rows.shape
    length, index = (lax.axis_size("seq"), lax.axis_index("seq"))
    last_seg = segments[tok_count - 1]
    lead = jnp.sum((segments < last_seg).astype(jnp.int32))
    one = jnp.ones((), jnp.int32)
    found = (key_rows[lead], value_rows[lead], index * tok_count + lead, last_seg, one)
    everything = jax.tree.map(lambda part: lax.all_gather(part, "seq"), found)
    start = jax.tree.map(jnp.zeros_like, found)

    def lap(k, before):
        new = merge_starts(before, jax.tree.map(lambda part: part[k], everything))
        return jax.tree.map(lambda a, b: jnp.where(k < index, a, b), new, before)

    sink_key, sink_value, sink_pos, sink_seg, sink_has = lax.fori_loop(0, length, lap, start)
    block = jnp.zeros((2 * tok_count, model_width), key_rows.dtype)
    block = block.at[0].set(sink_key).at[tok_count].set(sink_value)
    return (block, jnp.stack([sink_pos, sink_seg, sink_has]))


def table_entry(own, row, entry):
    return own[row : row + 1, entry : entry + 1]


def holder_of(experts, own, pick):
    return sum(
        jnp.where(pick == table_entry(own, OLD_ROW, x), x, 0) for x in range(experts)
    )


def column_routes(experts, routes, own):
    members = len(routes)
    slots = jnp.concatenate([ref[c : c + 1, :] for c in range(2) for ref in routes], axis=0)
    chosen = sum(jnp.where(slots == s, table_entry(own, NEW_ROW, s), 0) for s in range(experts))
    holders = holder_of(experts, own, chosen)
    return tuple((each[:members], each[members:]) for each in (chosen, holders))


def attended(batch, hops, relayed, heads, sinks, bias, own, q, stack, rest, context):
    count = 3 if relayed else hops
    moved, sent, rest = (rest[:count], rest[count : 2 * count], rest[2 * count :])
    if sinks:
        sink_block, sink_info, rest = (rest[0], rest[1], rest[2:])
    tokens, proj = rest
    tok_count, width = tokens.shape[2:]
    window = WIN_BLOCKS * tok_count
    index = lax.axis_index("seq")
    grid = (tok_count, tok_count)

    own_seg = own[batch : batch + 1, :]
    key_segs = [own_seg]
    if relayed:
        pairwise, across, relay = moved
        paired = index % 2 == 1
        key_segs += [jnp.where(paired, sent[0][batch : batch + 1], sent[2][batch : batch + 1])]
        key_segs.append(sent[1][batch : batch + 1, :])
    else:
        key_segs += [ref[batch : batch + 1, :] for ref in sent]
    seg_col = jnp.broadcast_to(own_seg, grid).T
    visible, spans = ([], [])
    for j, key_seg in enumerate(key_segs):
        key_seg = jnp.where(index >= j, key_seg, -1)
        distance = iota(grid, 0) - iota(grid, 1) + tok_count * j
        seen = (seg_col == key_seg) & (distance >= 0) & (distance < window)
        visible.append(jnp.where(seen, 0.0, masked_score))
        low, high = (max(0, tok_count * (j - 1) + 1), min(window, tok_count * (j + 1)) - 1)
        spans.append((distance, low.bit_length(), high.bit_length()))
    if sinks:
        position = index * tok_count + iota(grid, 0)
        seen = (seg_col == sink_info[1]) & (sink_info[2] > 0) & (position - sink_info[0] >= window)
        visible.append(jnp.where(seen & (iota(grid, 1) == 0), 0.0, masked_score))
        spans.append((None, NBUCK - 1, NBUCK - 1))
    lane = iota((tok_count, 128), 1)
    half = width // heads
    keys_at, values_at = (slice(0, tok_count), slice(tok_count, 2 * tok_count))
    for pair in range(heads // 2):
        cols = slice(128 * pair, 128 * pair + 128)
        both = q[batch, 0, :, cols] * score_scale
        even = jnp.where(lane < half, both, jnp.zeros_like(both))
        odd = jnp.where(lane < half, jnp.zeros_like(both), both)
        stacked = jnp.concatenate([even, odd], axis=0)
        blocks = [(stack[keys_at, cols], stack[values_at, cols])]
        if relayed:
            blocks.append(tuple(
                jnp.where(paired, pairwise[at, cols], relay[at, cols])
                for at in (keys_at, values_at)
            ))
            blocks.append((across[keys_at, cols], across[values_at, cols]))
        else:
            for ref in moved:
                blocks.append((ref[keys_at, cols], ref[values_at, cols]))
        if sinks:
            blocks.append((sink_block[keys_at, cols], sink_block[values_at, cols]))
        scores = []
        for (keys, _), (distance, low, high), seen in zip(blocks, spans, visible):
            score = lax.dot_general(stacked, keys, NT, preferred_element_type=f32)
            parts = []
            for side in range(2):
                head = 2 * pair + side
                offset = jnp.full(grid, bias[head, low], f32)
                for bucket in range(low + 1, high + 1):
                    offset = jnp.where(distance >= 1 << (bucket - 1), bias[head, bucket], offset)
                parts.append(score[side * tok_count : (side + 1) * tok_count] + (offset + seen))
            scores.append(jnp.concatenate(parts, axis=0))
        peak = jnp.max(functools.reduce(jnp.maximum, scores), axis=1, keepdims=True)
        weights = [jnp.exp(score - peak) for score in scores]
        total = jnp.sum(functools.reduce(jnp.add, weights), axis=1, keepdims=True)
        scale = 1.0 / total
        mixed = sum(
            jnp.dot((weight * scale).astype(bf16), values, preferred_element_type=f32)
            for weight, (_, values) in zip(weights, blocks)
        )
        context[:, cols] = jnp.where(lane < half, mixed[:tok_count], mixed[tok_count:]).astype(bf16)
    hidden = tokens[batch, 0].astype(f32) + jnp.dot(
        context[...], proj[...], preferred_element_type=f32
    )
    mean = jnp.mean(hidden * hidden, axis=1, keepdims=True)
    return (hidden, (hidden * lax.rsqrt(mean + epsilon)).astype(bf16))


def ranks(member):
    grid = (member.shape[1], member.shape[1])
    earlier = jnp.where(iota(grid, 0) < iota(grid, 1), 1.0, 0.0).astype(bf16)
    return jnp.dot(member.astype(bf16), earlier, preferred_element_type=f32).astype(jnp.int32)


def attend_column_kernel(options, bias, own, q, stack, *rest):
    inputs, (hidden_out, normed_out, context) = (rest[:-3], rest[-3:])
    hidden, normed = attended(1, *options, bias, own, q, stack, inputs, context)
    hidden_out[...] = hidden
    normed_out[...] = normed


def column_places(experts, routes, own):
    me = lax.axis_index("exp")
    _, holders = column_routes(experts, routes, own)
    member = jnp.concatenate(
        [jnp.where((holders[0] == at) | (holders[1] == at), 1.0, 0.0) for at in (me, me ^ 1)],
        axis=0,
    )
    return jnp.where(member > 0.5, ranks(member), -1)


def attend_direct_kernel(options, experts, cap, bias, router_t, own, q, stack, *rest):
    layers = experts // 2
    inputs, rest = (rest[: -4 - layers], rest[-4 - layers :])
    outgoing, (hidden_out, gates_out, rows_out, context) = (rest[:layers], rest[layers:])
    hidden, normed = attended(0, *options, bias, own, q, stack, inputs, context)
    hidden_out[...] = hidden
    tok_count = hidden.shape[0]
    chosen = [own[ONE_ROW + c : ONE_ROW + c + 1, :] for c in range(2)]
    holders = [holder_of(experts, own, pick) for pick in chosen]
    expert = iota((experts, tok_count), 0)
    packet = expert ^ lax.axis_index("exp")
    member = jnp.where((packet == holders[0]) | (packet == holders[1]), 1.0, 0.0)
    place = ranks(member) + expert * cap
    rows = [
        jnp.sum(jnp.where(packet == holder, place, 0), axis=0, keepdims=True) for holder in holders
    ]
    rows_out[...] = jnp.concatenate(rows, axis=0)
    logits = lax.dot_general(router_t[...], normed, NT, preferred_element_type=f32)
    picked = [jnp.sum(jnp.where(expert == c, logits, 0.0), axis=0, keepdims=True) for c in chosen]
    first = jax.nn.sigmoid(picked[0] - picked[1])
    gates_out[...] = jnp.concatenate([first, 1.0 - first], axis=0)
    at = iota((experts * cap, tok_count), 0)
    plan = jnp.where((at == rows[0]) | (at == rows[1]), 1.0, 0.0).astype(bf16)
    packed = jnp.dot(plan, normed, preferred_element_type=f32)
    for m, ref in enumerate(outgoing):
        ref[...] = packed[2 * m * cap : 2 * (m + 1) * cap].astype(bf16)


def picked_rows(members, cap, first_row, places, blocks):
    at = iota((len(members) * cap, blocks[0].shape[0]), 0)
    plans = []
    for n, m in enumerate(members):
        place = places[first_row + m : first_row + m + 1, :]
        place = jnp.where(place >= 0, place + n * cap, -1)
        plans.append(jnp.where(at == place, 1.0, 0.0))
    plan = jnp.concatenate(plans, axis=1).astype(bf16)
    rows = jnp.concatenate([block[...] for block in blocks], axis=0)
    return (jnp.dot(plan, rows, preferred_element_type=f32).astype(bf16), rows)


def pack_kernel(members, cap, columns, places, *rest):
    blocks, out = (rest[:-1], rest[-1])
    out[...], _ = picked_rows(members, cap, columns, places, blocks)


def first_pack_kernel(members, cap, columns, own, *rest):
    routes, blocks, (places, out) = (rest[:columns], rest[columns:-2], rest[-2:])
    places[...] = column_places(2 * columns, routes, own)
    out[...], _ = picked_rows(members, cap, columns, places, blocks)


def numbers_kernel(numbers, own, routes_out, segs_out):
    own[...] = numbers[...]
    routes_out[...] = numbers[TWO_ROW : TWO_ROW + 2, :]
    segs_out[...] = numbers[:2, :]


def collect_kernel(*refs):
    count = len(refs) // 2
    for ref, out in zip(refs[:count], refs[count:]):
        out[...] = ref[...]


def stage_kernel(k, v, q, tokens, out):
    del q, tokens
    tok_count = k.shape[2]
    out[:tok_count, :] = k[0, 0]
    out[tok_count:, :] = v[0, 0]


def join_kernel(k, v, out):
    tok_count = k.shape[0]
    out[:tok_count, :] = k[...]
    out[tok_count:, :] = v[...]


def pass_kernel(*refs):
    del refs


def crossing_kernel(*refs):
    packets, out = (refs[:-1][::-1], refs[-1])
    cap = packets[0].shape[0] // 2
    parts = [ref[...].astype(f32)[cap:] for ref in packets]
    out[...] = jnp.concatenate(parts, axis=0).astype(bf16)


def expert_rows(rows, weights, active, stores):
    gate, up, down = weights
    inner, width = down.shape[1:]
    x = rows[...]
    for begin in range(0, inner, 256):
        span = slice(begin, min(inner, begin + 256))
        gate_part = jnp.dot(x, gate[0, :, span], preferred_element_type=f32)
        up_part = jnp.dot(x, up[0, :, span], preferred_element_type=f32)
        active[:, span] = (jax.nn.gelu(gate_part, approximate=True) * up_part).astype(bf16)
    for begin in range(0, width, 256):
        span = slice(begin, begin + 256)
        part = jnp.dot(active[...], down[0, :, span], preferred_element_type=f32)
        stores(span, part)


def near_kernel(columns, experts, cap, own, places, router_t, *rest):
    blocks, rest = (rest[:columns], rest[columns:])
    routes, rest = (rest[:columns], rest[columns:])
    weights, (out, gates_out, rows, active) = (rest[:3], rest[3:])

    def stores(span, value):
        out[:, span] = value.astype(bf16)

    rows[...], tokens = picked_rows(range(columns), cap, 0, places, blocks)
    logits = lax.dot_general(router_t[...], tokens, NT, preferred_element_type=f32)
    chosen, holders = column_routes(experts, routes, own)
    chosen = [
        jnp.concatenate([picks[m : m + 1, :] for m in range(columns)], axis=1) for picks in chosen
    ]
    expert = iota(logits.shape, 0)
    picked = [
        jnp.sum(jnp.where(expert == pick, logits, 0.0), axis=0, keepdims=True) for pick in chosen
    ]
    first = jax.nn.sigmoid(picked[0] - picked[1])
    tok_count = places.shape[1]
    first = jnp.concatenate(
        [first[:, m * tok_count : (m + 1) * tok_count] for m in range(columns)], axis=0
    )
    me = lax.axis_index("exp")
    gates_out[...] = jnp.concatenate(
        [
            jnp.where(holders[0] == at, first, 0.0) + jnp.where(holders[1] == at, 1.0 - first, 0.0)
            for at in (me, me ^ 1)
        ],
        axis=0,
    )
    expert_rows(rows, weights, active, stores)


def far_kernel(low_in, high_in, *rest):
    weights, (low_out, high_out, rows, active) = (rest[:3], rest[3:])
    part = low_in.shape[0]

    def stores(span, value):
        low_out[:, span] = value[:part].astype(bf16)
        high_out[:, span] = value[part:].astype(bf16)

    rows[:part, :] = low_in[...]
    rows[part:, :] = high_in[...]
    expert_rows(rows, weights, active, stores)


def direct_near_kernel(layers, *refs):
    packets, weights = (refs[:layers][::-1], refs[layers : layers + 3])
    out, rows, active = refs[layers + 3 :]
    cap = packets[0].shape[0] // 2

    def stores(span, value):
        out[:, span] = value.astype(bf16)

    parts = [ref[...].astype(f32)[:cap] for ref in packets]
    rows[...] = jnp.concatenate(parts, axis=0).astype(bf16)
    expert_rows(rows, weights, active, stores)


def direct_far_kernel(crossed, gate, up, down, out, active):
    def stores(span, value):
        out[:, span] = value.astype(bf16)

    expert_rows(crossed, (gate, up, down), active, stores)


def rejoin_kernel(near, far, *outs):
    cap = outs[0].shape[0] // 2
    both = [ref[...].astype(f32) for ref in (near, far)]
    for m, out in enumerate(outs):
        parts = [each[m * cap : (m + 1) * cap] for each in both]
        out[...] = jnp.concatenate(parts, axis=0).astype(bf16)


def partial_kernel(members, cap, columns, places, gates, near, far, *outs):
    at = iota((cap, places.shape[1]), 0)
    for n, m in enumerate(members):
        total = None
        near_rows = near[m * cap : (m + 1) * cap, :]
        far_rows = far[n * cap : (n + 1) * cap, :]
        for values, row in ((near_rows, m), (far_rows, columns + m)):
            spread = jnp.where(at == places[row : row + 1, :], gates[row : row + 1, :], 0.0)
            coarse = spread.astype(bf16)
            fine = (spread - coarse.astype(f32)).astype(bf16)
            for half in (coarse, fine):
                term = lax.dot_general(half, values, TN, preferred_element_type=f32)
                total = term if total is None else total + term
        outs[n][...] = total.astype(outs[n].dtype)


def fold_kernel(own, *rest):
    total = own[...]
    for ref in rest[:-1]:
        total = total + ref[...].astype(f32)
    rest[-1][...] = total.astype(rest[-1].dtype)


def final_kernel(layers, hidden, gates, rows, *rest):
    packets, ends, out = (rest[:layers][::-1], rest[layers:-1], rest[-1])
    at = iota((layers * packets[0].shape[0], hidden.shape[0]), 0)
    spread = jnp.where(at == rows[0:1, :], gates[0:1, :], 0.0)
    spread = spread + jnp.where(at == rows[1:2, :], gates[1:2, :], 0.0)
    coarse = spread.astype(bf16)
    fine = (spread - coarse.astype(f32)).astype(bf16)
    values = jnp.concatenate([ref[...].astype(f32) for ref in packets], axis=0).astype(bf16)
    total = hidden[...]
    for half in (coarse, fine):
        total = total + lax.dot_general(half, values, TN, preferred_element_type=f32)
    out[0, 0] = total.astype(bf16)
    total = ends[0][...]
    for ref in ends[1:]:
        total = total + ref[...].astype(f32)
    out[1, 0] = total.astype(bf16)


def local(
    tokens, queries, key_rows, value_rows, segments, bias_table, out_proj, router,
    gate_weight, up_weight, down_weight, old_table, new_table, routes_one, routes_two,
):
    tok_count, width = tokens.shape[2:]
    heads = bias_table.shape[0]
    experts = router.shape[1]
    columns = experts // 2
    inner = gate_weight.shape[2]
    seq_size = lax.axis_size("seq")
    seq_len = tok_count * seq_size
    capacity = tok_count * 2 * 5 // (4 * experts)
    longest = seq_len // 2
    hops = min(WIN_BLOCKS, (longest - 1 + tok_count - 1) // tok_count)
    relayed = seq_size == 4 and hops == 2
    sinks = seq_len > WIN_BLOCKS * tok_count
    weights = (gate_weight, up_weight, down_weight)
    router_t = router.T
    lower, upper = (range(columns // 2), range(columns // 2, columns))
    rows_bf16 = shaped((tok_count, width), bf16)
    rows_f32 = shaped((tok_count, width), f32)
    cap_two = capacity * MAX_SLOTS
    slots = columns * cap_two
    part_two = slots // 2
    half_one = columns * capacity
    packet = shaped((2 * capacity, width), bf16)
    stack_shape = shaped((2 * tok_count, width), bf16)
    latest = []

    def call(kernel, outs, ins, args, scratch=(), after=(), aliases=None, work=1):
        after = [*after, *latest]
        out_specs = jax.tree.map(lambda _: VMEM, outs)
        if aliases:
            out_specs = tuple(ANY if n in aliases.values() else VMEM for n in range(len(outs)))

        def body(*refs):
            kernel(*refs[: len(args)], *refs[len(args) + len(after) :])

        made = pl.pallas_call(
            body,
            out_shape=outs,
            in_specs=ins + [ANY] * len(after),
            out_specs=out_specs,
            scratch_shapes=list(scratch),
            input_output_aliases=aliases or {},
            compiler_params=pltpu.CompilerParams(vmem_limit_bytes=24 * 2**20),
            cost_estimate=pl.CostEstimate(flops=work, bytes_accessed=1, transcendentals=0),
        )(*args, *after)
        latest[:] = jax.tree.leaves(made)[:1]
        return made

    def multicast(own):
        blocks = {0: own}
        bit = columns // 2
        while bit:
            for m in sorted(blocks):
                blocks[m | bit] = swapped(blocks[m], "exp", 2 * bit)
            bit //= 2
        return blocks

    def chained(moving):
        moved = []
        for _ in range(hops):
            moving = passed_along(moving, "seq", 1)
            moved.append(moving)
        return moved

    def options(batch):
        extra = []
        if sinks:
            extra = latest_start(key_rows[batch, 0], value_rows[batch, 0], segments[batch, 0])
        return ((hops, relayed, heads, sinks), extra)

    def attend_column(moved):
        settings, extra = options(1)
        return call(
            functools.partial(attend_column_kernel, settings),
            (rows_f32, rows_bf16),
            [SMEM] + [VMEM] * (3 + 2 * len(moved)) + ([VMEM, SMEM] if sinks else [])
            + [VMEM] * 2,
            (bias_table, own, queries, stacks[1], *moved, *sent, *extra, tokens, out_proj),
            scratch=[pltpu.VMEM((tok_count, width), bf16)],
        )

    def attend_direct(moved):
        settings, extra = options(0)
        return call(
            functools.partial(attend_direct_kernel, settings, experts, capacity),
            (*[packet] * columns, rows_f32, shaped((2, tok_count), f32),
             shaped((2, tok_count), jnp.int32)),
            [SMEM] + [VMEM] * (4 + 2 * len(moved)) + ([VMEM, SMEM] if sinks else [])
            + [VMEM] * 2,
            (bias_table, router_t, own, queries, stacks[0], *moved, *sent, *extra, tokens,
             out_proj),
            scratch=[pltpu.VMEM((tok_count, width), bf16)],
        )

    def scratch_for(slots):
        return (pltpu.VMEM((slots, width), bf16), pltpu.VMEM((slots, inner), bf16))

    def pack(members, places, blocks):
        return call(
            functools.partial(pack_kernel, members, cap_two, columns),
            shaped((part_two, width), bf16),
            [VMEM] * (1 + len(members)),
            (places, *(blocks[m] for m in members)),
        )

    def partial(members, far):
        parts = call(
            functools.partial(partial_kernel, members, cap_two, columns),
            tuple(rows_bf16 if m % 2 else rows_f32 for m in members),
            [VMEM] * 4,
            (places, gates_two, near, far),
        )
        for m, value in zip(members, parts):
            totals.setdefault(m, []).insert(0, value)

    def send_down(members):
        for m in sorted(members, key=lambda m: (m & -m, -m)):
            parts = totals[m]
            value = parts[0]
            if len(parts) > 1:
                value = call(
                    fold_kernel, rows_bf16, [VMEM] * len(parts), parts, work=6 * 10**9
                )
            totals.setdefault(m & (m - 1), []).append(swapped(value, "exp", 2 * (m & -m)))

    stacked = call(join_kernel, stack_shape, [VMEM] * 2, (key_rows[1, 0], value_rows[1, 0]))
    first_hop = swapped(stacked, "seq", 1) if relayed else passed_along(stacked, "seq", 1)
    tables = [jnp.pad(table, (0, tok_count - experts))[None] for table in (new_table, old_table)]
    numbers = jnp.concatenate([segments[:, 0], routes_one[0].T, routes_two[0].T, *tables])
    own, own_routes, own_segs = call(
        numbers_kernel,
        tuple(shaped((rows, tok_count), jnp.int32) for rows in (8, 2, 2)),
        [VMEM], (numbers,), after=[first_hop],
    )
    routes = multicast(own_routes)
    if relayed:
        sent = [swapped(own_segs, "seq", mask) for mask in (1, 2, 3)]
        across = swapped(stacked, "seq", 2)
    else:
        sent = chained(own_segs)
        across = first_hop
    stack_one = call(
        stage_kernel, stack_shape, [VMEM] * 4, (key_rows, value_rows, queries, tokens),
        after=[routes[columns // 2]],
    )
    *routes, latest_seg = call(
        collect_kernel,
        tuple(shaped((2, tok_count), jnp.int32) for _ in range(columns + 1)),
        [VMEM] * (columns + 1),
        (*(routes[m] for m in range(columns)), sent[-1]),
        after=sent[:-1],
    )
    sent = [*sent[:-1], latest_seg]
    (across,) = call(pass_kernel, (stack_shape,), [ANY], (across,), aliases={0: 0})
    if relayed:
        moved_two = [first_hop, across, swapped(across, "seq", 1)]
    else:
        moved_two = [across]
        while len(moved_two) < hops:
            moved_two.append(passed_along(moved_two[-1], "seq", 1))
    stacks = [stack_one, stacked]
    hidden_two, normed_two = attend_column(moved_two)
    (stack_one,) = call(
        pass_kernel, (stack_shape,), [ANY], (stack_one,), aliases={0: 0}
    )
    stacks[0] = stack_one
    if relayed:
        moved_one = [
            swapped(stack_one, "seq", 1),
            swapped(stack_one, "seq", 2),
            lax.ppermute(stack_one, "seq", [(0, 0), (1, 2), (2, 1), (3, 3)]),
        ]
    else:
        moved_one = chained(stack_one)
    blocks = multicast(normed_two)
    places, low_in = call(
        functools.partial(first_pack_kernel, lower, cap_two, columns),
        (shaped((2 * columns, tok_count), jnp.int32), shaped((part_two, width), bf16)),
        [VMEM] * (1 + columns + len(lower)),
        (own, *routes, *(blocks[m] for m in lower)), work=4 * 10**9,
    )
    low_in = swapped(low_in, "exp", 1)
    high_in = swapped(pack(upper, places, blocks), "exp", 1)
    *packets, hidden_one, gates_one, rows_one = attend_direct(moved_one)
    arrived = [packets[0]] + [swapped(packets[m], "exp", 2 * m) for m in range(1, columns)]
    low_out, high_out = call(
        far_kernel,
        (shaped((part_two, width), bf16),) * 2,
        [VMEM] * 5,
        (low_in, high_in, *weights),
        scratch=scratch_for(slots),
    )
    high_far = swapped(high_out, "exp", 1)
    near, gates_two = call(
        functools.partial(near_kernel, columns, experts, cap_two),
        (shaped((slots, width), bf16), shaped((2 * columns, tok_count), f32)),
        [VMEM] * (6 + 2 * columns),
        (own, places, router_t, *(blocks[m] for m in range(columns)), *routes, *weights),
        scratch=scratch_for(slots), work=4 * 10**9,
    )
    crossing = call(
        crossing_kernel, shaped((columns * capacity, width), bf16), [VMEM] * columns, arrived[::-1],
        work=2 * 10**10,
    )
    crossed_one = swapped(crossing, "exp", 1)
    totals = {}
    partial(upper, high_far)
    send_down(m for m in upper if m % 2)
    near_one = call(
        functools.partial(direct_near_kernel, columns), shaped((half_one, width), bf16),
        [VMEM] * (3 + columns), (*arrived[::-1], *weights), scratch=scratch_for(half_one),
    )
    (low_out,) = call(
        pass_kernel, (shaped(low_out.shape, bf16),), [ANY], (low_out,), aliases={0: 0},
        after=[crossed_one],
    )
    low_far = swapped(low_out, "exp", 1)
    send_down(m for m in upper if m % 2 == 0)
    far_one = call(
        direct_far_kernel, shaped((half_one, width), bf16), [VMEM] * 4, (crossed_one, *weights),
        scratch=scratch_for(half_one)[1:],
    )
    far_one = swapped(far_one, "exp", 1)
    partial(lower, low_far)
    send_down(m for m in lower if m)
    answers = call(rejoin_kernel, [packet] * columns, [VMEM] * 2, (near_one, far_one))
    returned = [answers[0]] + [swapped(answers[m], "exp", 2 * m) for m in range(1, columns)]
    far_part, rest = (totals[0][1], [hidden_two, totals[0][0], *totals[0][2:]])
    ends = (call(fold_kernel, rows_f32, [VMEM] * 2, (rest[0], far_part)), *rest[1:])
    return call(
        functools.partial(final_kernel, columns), shaped((2, 1, tok_count, width), bf16),
        [VMEM] * (3 + columns + len(ends)), (hidden_one, gates_one, rows_one, *returned[::-1], *ends),
    )


def solution(mesh):
    rows = P(None, "exp", "seq", None)
    placed = (
        rows, rows, rows, rows, P(None, "exp", "seq"), P(), P(), P(),
        P("exp", None, None), P("exp", None, None), P("exp", None, None), P(), P(),
        P("exp", "seq", None), P("exp", "seq", None),
    )
    return jax.shard_map(local, mesh=mesh, in_specs=placed, out_specs=rows, check_vma=False)
```
